32 devices in a mesh: pool: 4 (over x, core), dp: 8 (over z, y).
Axes of the slice: x: 2, y: 2, z: 4, core: 2. Of those that a mesh axis runs over, the one named last changes fastest.
Arguments:
- queries: bfloat16 [4, 8, 256, 2048], P('pool', 'dp'), may hold values from -48 to 48
- cotangent: bfloat16 [4, 8, 256, 2048], P('pool', 'dp'), may hold values from -6 to 6
- cond: bfloat16 [4, 8, 4, 512], P('pool', 'dp'), may hold values from -6 to 6
- nbr_owner: int32 [4, 8, 4, 2], P('pool', 'dp'), may hold values from 0 to 7, as said below
- nbr_block: int32 [4, 8, 4, 2], P('pool', 'dp'), may hold values from 0 to 15
- database: bfloat16 [4, 8, 16, 128, 512], P('pool', 'dp'), may hold values from -6 to 6
- lengths: int32 [4, 8, 16], P('pool', 'dp'), may hold values from 1 to 128, as said below
- gain: float32 [512], replicated, may hold values from 0.25 to 1.75
- w_down: bfloat16 [512, 256], replicated, may hold values from -0.25 to 0.25
- w_up: bfloat16 [256, 512], replicated, may hold values from -0.375 to 0.375
- w_kv: bfloat16 [512, 4096], replicated, may hold values from -0.25 to 0.25
Outputs:
- attn_out: bfloat16 [4, 8, 256, 2048], P('pool', 'dp')
- q_grad: bfloat16 [4, 8, 256, 2048], P('pool', 'dp')
- cond_grad: float32 [4, 8, 4, 512], P('pool', 'dp')
- adapter_grad: float32 [512, 512], P(('pool', 'dp'))
The draws below stay inside these ranges and needn't reach their ends.
Inputs may be any that keep to these rules, and one draw needn't show every extreme that they name: `nbr_owner`: among the 8 neighbours of each of the decoder devices (pool index below 4-1) that share one index of dp, no encoder device is named more than 4 times, and one encoder device, the same for every index of dp, is named exactly 4 times. Entries at pool index 4-1 are not read. `lengths`: every encoder device holds a block of length 128.
All inputs are finite; a program needn't handle non-finite values.
Results may differ from the reference program's by a relative error of at most 0.013.
The reference program's roundings to bfloat16 on the way count: a program that leaves them out, or rounds other values in their place, can miss the bound.
Values may be sent and summed in bfloat16 or wider, within the bound.
No kernel may reach another device: no remote copies, remote signals or barrier semaphores. Data moves between devices by JAX's collectives and lax.ppermute only.
A program may use at most 192 MiB of HBM per device.

```python
import jax
import jax.numpy as jnp
from jax import lax

HEADS = 16
HEAD = 128
E = 512
RANK = 256
SPAN = 64
NBR = 2
NLEN = 128
SPANS_DEV = 4
BLK_DEV = 16
HQ = 2048
TOK_DEV = 256
NB_DEV = 8
CAP = 4
N_POOL = 4
N_DP = 8


def draw_queries(key, part):
    normal_part = jnp.clip(jax.random.normal(jax.random.fold_in(key, 1), (N_POOL, N_DP, TOK_DEV, HEADS, HEAD), jnp.float32), -6.0, 6.0)
    return normal_part.reshape(N_POOL, N_DP, TOK_DEV, HEADS * HEAD).astype(jnp.bfloat16)


def draw_nbr_owner(key, part):
    live_count = (N_POOL - 1) * SPANS_DEV * NBR
    slot_count = N_DP * CAP
    full_owner = jax.random.randint(jax.random.fold_in(key, 11), (), 0, N_DP)
    slot_ids = jnp.arange(slot_count, dtype=jnp.int32)

    def column(column_key):
        shuffled = jax.random.permutation(jax.random.fold_in(column_key, 1), slot_count)
        ranked = jnp.argsort(shuffled).astype(jnp.int32)
        priority = jnp.where(slot_ids // CAP == full_owner, slot_ids % CAP, CAP + ranked)
        chosen = jnp.argsort(priority)[:live_count].astype(jnp.int32)
        placed = jax.random.permutation(jax.random.fold_in(column_key, 2), live_count)
        owners_live = (chosen // CAP)[placed]
        spare_rows = jax.random.randint(jax.random.fold_in(column_key, 3), (SPANS_DEV * NBR,), 0, N_DP)
        return jnp.concatenate([owners_live, spare_rows]).astype(jnp.int32).reshape(N_POOL, SPANS_DEV, NBR)
    column_keys = jax.random.split(jax.random.fold_in(key, 5), N_DP)
    return jnp.transpose(jax.vmap(column)(column_keys), (1, 0, 2, 3))


def draw_lengths(key, part):
    drawn = jax.random.randint(jax.random.fold_in(key, 1), (N_POOL, N_DP, BLK_DEV), 1, NLEN + 1)
    longest = jax.random.randint(jax.random.fold_in(key, 2), (N_POOL, N_DP, 1), 0, BLK_DEV)
    position = jnp.arange(BLK_DEV, dtype=jnp.int32)[None, None, :]
    return jnp.where(position == longest, NLEN, drawn).astype(jnp.int32)


def set_ends(array, rng, least, largest):
    dims = array.shape
    spot = [jax.random.randint(jax.random.fold_in(rng, axis), (), 0, dims[axis]) for axis in range(len(dims))]
    array = array.at[tuple(spot)].set(least)
    longest = dims.index(max(dims))
    spot[longest] = (spot[longest] + 1) % dims[longest]
    return array.at[tuple(spot)].set(largest)


def block_scale(key, dims, cuts, low, top_value):
    factor_of = 1.0
    for dim, parts in cuts:
        draws = jax.random.uniform(jax.random.fold_in(jax.random.fold_in(key, 6), dim), (parts,), jnp.float32, low / len(cuts), top_value / len(cuts))
        factor_of = factor_of * jnp.repeat(jnp.exp(draws), dims[dim] // parts).reshape((-1,) + (1,) * (len(dims) - 1 - dim))
    return factor_of


def centred(rng, dims, spread, most, pieces=(), kind=jnp.bfloat16):
    level = block_scale(rng, dims, pieces, -0.22, 0.18) if pieces else 1.0
    entries = jax.random.normal(rng, dims, jnp.float32) * spread * level
    return jnp.minimum(jnp.maximum(entries, -most), most).astype(kind)


def setup_inputs(seed: int = 0) -> dict:
    key_list = jax.random.split(jax.random.key(seed), 12)
    return {
        "queries": draw_queries(jax.random.fold_in(key_list[11], 71), 0),
        "cotangent": centred(key_list[1], (N_POOL, N_DP, TOK_DEV, HQ), 1.0, 6.0, ((0, 4), (1, 8))),
        "cond": centred(key_list[2], (N_POOL, N_DP, SPANS_DEV, E), 1.0, 6.0, ((0, 4), (1, 8))),
        "nbr_owner": draw_nbr_owner(jax.random.fold_in(key_list[11], 71), 0),
        "nbr_block": set_ends(jax.random.randint(key_list[4], (N_POOL, N_DP, SPANS_DEV, NBR), 0, BLK_DEV), jax.random.fold_in(key_list[4], 1), 0, BLK_DEV - 1).astype(jnp.int32),
        "database": centred(key_list[5], (N_POOL, N_DP, BLK_DEV, NLEN, E), 1.0, 6.0, ((0, 4), (1, 8))),
        "lengths": draw_lengths(jax.random.fold_in(key_list[11], 71), 0),
        "gain": jnp.clip(1.0 + 0.15 * jax.random.normal(key_list[7], (E,), jnp.float32), 0.25, 1.75),
        "w_down": centred(key_list[8], (E, RANK), E ** -0.5, 0.25),
        "w_up": centred(key_list[9], (RANK, E), RANK ** -0.5, 0.375),
        "w_kv": centred(key_list[10], (E, 2 * HQ), E ** -0.5, 0.25),
    }


EPSILON = 1e-06
FLOOR = -1e+30

def encode_rows(block_rows, cond_rows, gain, w_down, w_up):
    x_full = block_rows.astype(jnp.float32) + cond_rows.astype(jnp.float32)[:, None, :]
    inv_rms = lax.rsqrt(lax.optimization_barrier(jnp.mean(x_full * x_full, axis=-1, keepdims=True)) + EPSILON)
    hidden = (x_full * inv_rms * gain).astype(jnp.bfloat16)
    flat_hidden = hidden.reshape(-1, hidden.shape[-1])
    latent = jnp.dot(flat_hidden, w_down, preferred_element_type=jnp.float32).astype(jnp.bfloat16)
    branch = jnp.dot(latent, w_up, preferred_element_type=jnp.float32).reshape(x_full.shape)
    encoded = (x_full + branch).astype(jnp.bfloat16)
    return (encoded, x_full, inv_rms, hidden, latent.reshape(x_full.shape[:-1] + (latent.shape[-1],)))

def encode_back(enc_grad, x_full, inv_rms, gain, w_down, w_up):
    flat_grad = enc_grad.reshape(-1, enc_grad.shape[-1])
    lat_grad = jnp.dot(flat_grad, w_up.T, preferred_element_type=jnp.float32).astype(jnp.bfloat16)
    hid_grad = jnp.dot(lat_grad, w_down.T, preferred_element_type=jnp.float32).reshape(x_full.shape)
    scaled = hid_grad * gain
    normed = x_full * inv_rms
    x_grad = enc_grad.astype(jnp.float32) + inv_rms * (scaled - normed * lax.optimization_barrier(jnp.mean(scaled * normed, axis=-1, keepdims=True)))
    return (lax.optimization_barrier(jnp.sum(x_grad, axis=-2)), lat_grad)

def attend(query_rows, cot_rows, encoded, block_len, w_kv):
    token_count = query_rows.shape[0]
    block_count = encoded.shape[0]
    span_count = token_count // SPAN
    key_count = NBR * NLEN
    scaling = HEAD ** (-0.5)
    key_value = jnp.dot(encoded.reshape(block_count * NLEN, E), w_kv, preferred_element_type=jnp.float32).astype(jnp.bfloat16)
    key_rows = key_value[:, :HQ].reshape(span_count, key_count, HEADS, HEAD).astype(jnp.float32)
    value_rows = key_value[:, HQ:].reshape(span_count, key_count, HEADS, HEAD).astype(jnp.float32)
    q_heads = query_rows.reshape(span_count, SPAN, HEADS, HEAD).astype(jnp.float32)
    out_grad = cot_rows.reshape(span_count, SPAN, HEADS, HEAD).astype(jnp.float32)
    usable = (jnp.arange(NLEN, dtype=jnp.int32)[None, :] < block_len[:, None]).reshape(span_count, 1, 1, key_count)
    scores = jnp.einsum('cqhd,ckhd->chqk', q_heads, key_rows) * scaling
    scores = jnp.where(usable, scores, FLOOR)
    row_max = lax.optimization_barrier(jnp.max(scores, axis=-1, keepdims=True))
    raised = jnp.exp(scores - row_max)
    probs = raised / lax.optimization_barrier(jnp.sum(raised, axis=-1, keepdims=True))
    probs_b = probs.astype(jnp.bfloat16).astype(jnp.float32)
    attn_out = jnp.einsum('chqk,ckhd->cqhd', probs_b, value_rows).astype(jnp.bfloat16).reshape(token_count, HQ)
    d_probs = jnp.einsum('cqhd,ckhd->chqk', out_grad, value_rows)
    delta = lax.optimization_barrier(jnp.sum(probs * d_probs, axis=-1, keepdims=True))
    d_scores = (probs * (d_probs - delta)).astype(jnp.bfloat16).astype(jnp.float32)
    q_grad = (jnp.einsum('chqk,ckhd->cqhd', d_scores, key_rows) * scaling).astype(jnp.bfloat16).reshape(token_count, HQ)
    key_grad = (jnp.einsum('chqk,cqhd->ckhd', d_scores, q_heads) * scaling).astype(jnp.bfloat16)
    value_grad = jnp.einsum('chqk,cqhd->ckhd', probs_b, out_grad).astype(jnp.bfloat16)
    kv_grad = jnp.concatenate([key_grad.reshape(block_count * NLEN, HQ), value_grad.reshape(block_count * NLEN, HQ)], axis=1)
    enc_grad = jnp.dot(kv_grad, w_kv.T, preferred_element_type=jnp.float32).astype(jnp.bfloat16)
    return (attn_out, q_grad, enc_grad.reshape(block_count, NLEN, E))

def reference(queries, cotangent, cond, nbr_owner, nbr_block, database, lengths, gain, w_down, w_up, w_kv):
    decoder_count = (N_POOL - 1) * N_DP
    store_rows = database[N_POOL - 1]
    store_len = lengths[N_POOL - 1]
    items = (queries[:N_POOL - 1].reshape(decoder_count, TOK_DEV, HQ), cotangent[:N_POOL - 1].reshape(decoder_count, TOK_DEV, HQ), cond[:N_POOL - 1].reshape(decoder_count, SPANS_DEV, E), nbr_owner[:N_POOL - 1].reshape(decoder_count, NB_DEV), nbr_block[:N_POOL - 1].reshape(decoder_count, NB_DEV))

    def one_device(carry, item):
        query_rows, cot_rows, cond_rows, owner_ids, block_ids = item
        block_rows = store_rows[owner_ids, block_ids]
        block_len = store_len[owner_ids, block_ids].astype(jnp.int32)
        cond_rep = jnp.repeat(cond_rows, NBR, axis=0)
        encoded, x_full, inv_rms, hidden, latent = encode_rows(block_rows, cond_rep, gain, w_down, w_up)
        attn_out, q_grad, enc_grad = attend(query_rows, cot_rows, encoded, block_len, w_kv)
        cond_rows_grad, lat_grad = encode_back(enc_grad, x_full, inv_rms, gain, w_down, w_up)
        down_term = jnp.dot(hidden.reshape(-1, E).T, lat_grad, preferred_element_type=jnp.float32)
        up_term = jnp.dot(enc_grad.reshape(-1, E).T, latent.reshape(-1, RANK), preferred_element_type=jnp.float32)
        span_grad = lax.optimization_barrier(jnp.sum(cond_rows_grad.reshape(SPANS_DEV, NBR, E), axis=1))
        return ((carry[0] + down_term, carry[1] + up_term), (attn_out, q_grad, span_grad))
    start = (jnp.zeros((E, RANK), jnp.float32), jnp.zeros((E, RANK), jnp.float32))
    sums, stacked = lax.scan(one_device, start, items)
    attn_all = jnp.concatenate([stacked[0].reshape(N_POOL - 1, N_DP, TOK_DEV, HQ), jnp.zeros((1, N_DP, TOK_DEV, HQ), jnp.bfloat16)], axis=0)
    qgrad_all = jnp.concatenate([stacked[1].reshape(N_POOL - 1, N_DP, TOK_DEV, HQ), jnp.zeros((1, N_DP, TOK_DEV, HQ), jnp.bfloat16)], axis=0)
    cgrad_all = jnp.concatenate([stacked[2].reshape(N_POOL - 1, N_DP, SPANS_DEV, E), jnp.zeros((1, N_DP, SPANS_DEV, E), jnp.float32)], axis=0)
    adapter_grad = jnp.concatenate([sums[0], sums[1]], axis=1)
    return (attn_all, qgrad_all, cgrad_all, adapter_grad)
```

```python
import functools

import jax
import jax.numpy as jnp
from jax import lax
from jax.experimental import pallas as pl
from jax.experimental.pallas import tpu as pltpu
from jax.sharding import PartitionSpec as P

HEADS = 16
HEAD = 128
SPAN = 64

EPSILON = 1e-06
FLOOR = -1e30
LOG2E = 1.4426950408889634

NT = (((1,), (1,)), ((), ()))
TN = (((0,), (0,)), ((), ()))


def dot(a, b, dims=(((1,), (0,)), ((), ()))):
    return lax.dot_general(a, b, dims, preferred_element_type=jnp.float32)


def two_heads(rows):
    blank = jnp.zeros((rows.shape[0], HEAD), rows.dtype)
    return jnp.concatenate(
        [
            jnp.concatenate([rows[:, :HEAD], blank], axis=1),
            jnp.concatenate([blank, rows[:, HEAD:]], axis=1),
        ],
        axis=0,
    )


def span_kernel(
    raw_count, nbr_count, meta,
    q_ref, cot_ref, cond_ref, *rest,
):
    raw_refs = rest[:raw_count]
    (gain_ref, down_ref, up_ref, kv_ref, kvt_ref, upt_ref, downt_ref,
     out_ref, qg_ref, cg_ref, ad_ref, kvg_ref, acc_ref) = rest[raw_count:]
    span = pl.program_id(0)
    slot_len, width = raw_refs[0].shape[1:]
    key_count = nbr_count * slot_len
    head_cols = q_ref.shape[1]
    rank = down_ref.shape[1]
    scaling = HEAD ** (-0.5)
    pool_index = meta[0]
    live = pool_index < raw_count

    raw = raw_refs[raw_count - 1][...]
    for p in range(raw_count - 1):
        raw = jnp.where(pool_index == p, raw_refs[p][...], raw)
    x_full = raw.reshape(key_count, width).astype(jnp.float32) + cond_ref[
        pl.ds(span, 1), :
    ]
    inv_rms = lax.rsqrt(jnp.mean(x_full * x_full, axis=-1, keepdims=True) + EPSILON)
    gain = gain_ref[...]
    hidden = (x_full * inv_rms * gain).astype(jnp.bfloat16)
    latent = dot(hidden, down_ref[...]).astype(jnp.bfloat16)
    encoded = (x_full + dot(latent, up_ref[...])).astype(jnp.bfloat16)

    slot = lax.broadcasted_iota(jnp.int32, (key_count, 2 * SPAN), 0)
    limit = jnp.zeros((key_count, 2 * SPAN), jnp.int32)
    for n in range(nbr_count):
        here = jnp.logical_and(slot >= n * slot_len, slot < (n + 1) * slot_len)
        limit = jnp.where(here, n * slot_len + meta[1 + span * nbr_count + n], limit)
    usable = slot < limit

    for pair in range(HEADS // 2):
        cols = pl.ds(pair * 2 * HEAD, 2 * HEAD)
        vcols = pl.ds(head_cols + pair * 2 * HEAD, 2 * HEAD)
        keys = dot(encoded, kv_ref[:, cols]).astype(jnp.bfloat16)
        values = dot(encoded, kv_ref[:, vcols]).astype(jnp.bfloat16)
        q2 = two_heads(q_ref[:, cols])
        cot2 = two_heads(cot_ref[:, cols])
        scores = jnp.where(usable, dot(keys, q2, NT), FLOOR)
        row_max = jnp.max(scores, axis=0, keepdims=True)
        raised = jnp.exp2((scores - row_max) * (scaling * LOG2E))
        inv_sum = 1.0 / jnp.sum(raised, axis=0, keepdims=True)
        probs = raised * inv_sum
        probs_b = probs.astype(jnp.bfloat16)
        d_probs = dot(values, cot2, NT)
        delta = jnp.sum(probs * d_probs, axis=0, keepdims=True)
        d_scores = (probs * (d_probs - delta) * scaling).astype(jnp.bfloat16)
        kvg_ref[:, cols] = dot(d_scores, q2).astype(jnp.bfloat16)
        kvg_ref[:, vcols] = dot(probs_b, cot2).astype(jnp.bfloat16)
        probs_t = probs_b.T
        d_scores_t = d_scores.T
        outs, grads = [], []
        for h in range(2):
            lanes = slice(h * HEAD, (h + 1) * HEAD)
            tokens = slice(h * SPAN, (h + 1) * SPAN)
            outs.append(dot(probs_t[tokens], values[:, lanes]))
            grads.append(dot(d_scores_t[tokens], keys[:, lanes]))
        out_ref[:, cols] = jnp.where(live, jnp.concatenate(outs, axis=1), 0.0).astype(jnp.bfloat16)
        qg_ref[:, cols] = jnp.where(live, jnp.concatenate(grads, axis=1), 0.0).astype(jnp.bfloat16)

    enc_grad = dot(kvg_ref[...], kvt_ref[...]).astype(jnp.bfloat16)
    lat_grad = dot(enc_grad, upt_ref[...]).astype(jnp.bfloat16)
    scaled = dot(lat_grad, downt_ref[...]) * gain
    normed = x_full * inv_rms
    x_grad = enc_grad.astype(jnp.float32) + inv_rms * (
        scaled - normed * jnp.mean(scaled * normed, axis=-1, keepdims=True)
    )
    span_grad = jnp.sum(x_grad, axis=0, keepdims=True)
    cg_ref[pl.ds(span, 1), :] = jnp.where(live, span_grad, 0.0)

    @pl.when(span == 0)
    def _():
        acc_ref[...] = jnp.zeros_like(acc_ref)

    acc_ref[:, :rank] += dot(hidden, lat_grad, TN)
    acc_ref[:, rank:] += dot(enc_grad, latent, TN)

    @pl.when(span == pl.num_programs(0) - 1)
    def _():
        ad_ref[...] = jnp.where(live, acc_ref[...], 0.0).astype(ad_ref.dtype)


def run_spans(meta, query, cot, cond, raws, gain, w_down, w_up, w_kv, nbr_count):
    span_count, width = cond.shape
    token_count, head_cols = query.shape
    slot_len = raws[0].shape[1]
    rank = w_down.shape[1]
    whole = lambda a: pl.BlockSpec(a.shape, lambda s, m: (0,) * a.ndim, pipeline_mode=pl.Buffered(1))
    tokens = pl.BlockSpec((SPAN, head_cols), lambda s, m: (s, 0))
    weights = [gain.reshape(1, width), w_down, w_up, w_kv, w_kv.T, w_up.T, w_down.T]
    rows = span_count * nbr_count * slot_len
    flops = 2 * rows * (2 * width * 2 * head_cols + 6 * width * rank + 6 * SPAN * head_cols)
    return pl.pallas_call(
        functools.partial(span_kernel, len(raws), nbr_count),
        grid_spec=pltpu.PrefetchScalarGridSpec(
            num_scalar_prefetch=1,
            grid=(span_count,),
            in_specs=[tokens, tokens, whole(cond)]
            + [pl.BlockSpec((nbr_count, slot_len, width), lambda s, m: (s, 0, 0))] * len(raws)
            + [whole(w) for w in weights],
            out_specs=[
                tokens,
                tokens,
                pl.BlockSpec((span_count, width), lambda s, m: (0, 0)),
                pl.BlockSpec((width, 2 * rank), lambda s, m: (0, 0)),
            ],
            scratch_shapes=[
                pltpu.VMEM((nbr_count * slot_len, 2 * head_cols), jnp.bfloat16),
                pltpu.VMEM((width, 2 * rank), jnp.float32),
            ],
        ),
        out_shape=[
            jax.ShapeDtypeStruct((token_count, head_cols), jnp.bfloat16),
            jax.ShapeDtypeStruct((token_count, head_cols), jnp.bfloat16),
            jax.ShapeDtypeStruct((span_count, width), jnp.float32),
            jax.ShapeDtypeStruct((width, 2 * rank), jnp.bfloat16),
        ],
        compiler_params=pltpu.CompilerParams(vmem_limit_bytes=48 * 2**20),
        cost_estimate=pl.CostEstimate(
            flops=flops, bytes_accessed=16 * 2**20, transcendentals=rows * SPAN * HEADS
        ),
    )(meta, query, cot, cond, *raws, *weights)


def body(
    queries, cotangent, cond, nbr_owner, nbr_block, database, lengths, gain, w_down, w_up, w_kv
):
    axes = ("pool", "dp")
    pool_count = lax.axis_size("pool")
    columns = lax.axis_size("dp")
    relay_row = pool_count - 1
    pool_index = lax.axis_index("pool")
    me = lax.axis_index("dp")
    span_count, width = cond.shape[2:]
    nbr_count = nbr_owner.shape[3]
    per_device = span_count * nbr_count
    block_count, slot_len = database.shape[2:4]
    live_count = relay_row * per_device
    capacity = max(2, live_count // columns + 1)
    slot_count = columns * capacity
    token_count, head_cols = queries.shape[2:]

    def at(pool, dp):
        return pool * columns + dp % columns

    info = jnp.concatenate([nbr_owner.reshape(-1), nbr_block.reshape(-1), lengths.reshape(-1)])
    table = lax.all_gather(info, axes, axis=0).reshape(pool_count, columns, -1)
    by_column = jnp.swapaxes(table[:relay_row], 0, 1)
    owners = by_column[:, :, :per_device].reshape(columns, live_count)
    blocks = by_column[:, :, per_device : 2 * per_device].reshape(columns, live_count)
    store_len = table[relay_row, :, 2 * per_device :]
    order = jnp.arange(live_count, dtype=jnp.int32)
    same = owners[:, :, None] == owners[:, None, :]
    rank = jnp.sum(jnp.where(same & (order[None, :] < order[:, None])[None], 1, 0), axis=2)

    target = (me + jnp.arange(columns, dtype=jnp.int32)) % columns
    ring = jnp.arange(capacity, dtype=jnp.int32)
    mine = (owners == me)[:, None, :] & (rank[:, None, :] == ring[None, :, None])
    slot_block = jnp.sum(jnp.where(mine, blocks[:, None, :], 0), axis=2)
    slot_block = jnp.take(slot_block, target, axis=0).reshape(slot_count)
    store = database.reshape(block_count, slot_len, width)
    sends = jnp.take(store, slot_block, axis=0).reshape(columns, capacity, slot_len, width)

    arrived = [sends[0]]
    for shift in range(1, columns):
        hops = [(at(relay_row, j), at(relay_row, j + shift)) for j in range(columns)]
        arrived.append(lax.ppermute(sends[shift], axes, hops))
    arrived = jnp.concatenate(arrived, axis=0)

    my_owner = lax.dynamic_index_in_dim(owners, me, 0, keepdims=False)
    my_block = lax.dynamic_index_in_dim(blocks, me, 0, keepdims=False)
    my_rank = lax.dynamic_index_in_dim(rank, me, 0, keepdims=False)
    position = ((me - my_owner) % columns) * capacity + my_rank
    wanted = jnp.take(arrived, position, axis=0).reshape(relay_row, per_device, slot_len, width)
    raws = [
        lax.ppermute(
            wanted[p], axes, [(at(relay_row, j), at(p, j)) for j in range(columns)]
        )
        for p in range(relay_row)
    ]

    own_row = jnp.minimum(pool_index, relay_row - 1)
    pick = my_owner * block_count + my_block
    hot = pick[:, None] == jnp.arange(columns * block_count, dtype=jnp.int32)[None, :]
    wanted_len = jnp.sum(jnp.where(hot, store_len.reshape(1, -1), 0), axis=1)
    my_len = lax.dynamic_index_in_dim(
        wanted_len.reshape(relay_row, per_device), own_row, 0, keepdims=False
    )
    meta = jnp.concatenate([pool_index[None], my_len]).astype(jnp.int32)

    attn_out, q_grad, cond_grad, terms = run_spans(
        meta,
        queries.reshape(token_count, head_cols),
        cotangent.reshape(token_count, head_cols),
        cond.reshape(span_count, width).astype(jnp.float32),
        raws,
        gain,
        w_down,
        w_up,
        w_kv,
        nbr_count,
    )
    parts = lax.all_to_all(terms, axes, split_axis=0, concat_axis=0, tiled=True)
    adapter_grad = jnp.sum(
        parts.reshape(pool_count * columns, -1, terms.shape[1]).astype(jnp.float32), axis=0
    )
    return (
        attn_out.reshape(1, 1, token_count, head_cols),
        q_grad.reshape(1, 1, token_count, head_cols),
        cond_grad.reshape(1, 1, span_count, width),
        adapter_grad,
    )


def solution(mesh):
    return jax.shard_map(
        body,
        mesh=mesh,
        in_specs=(
            P("pool", "dp", None, None),
            P("pool", "dp", None, None),
            P("pool", "dp", None, None),
            P("pool", "dp", None, None),
            P("pool", "dp", None, None),
            P("pool", "dp", None, None, None),
            P("pool", "dp", None),
            P(),
            P(),
            P(),
            P(),
        ),
        out_specs=(
            P("pool", "dp", None, None),
            P("pool", "dp", None, None),
            P("pool", "dp", None, None),
            P(("pool", "dp"), None),
        ),
        check_vma=False,
    )
```

```python
import functools

import jax
import jax.numpy as jnp
from jax import lax
from jax.experimental import pallas as pl
from jax.experimental.pallas import tpu as pltpu
from jax.sharding import PartitionSpec as P

HEADS = 16
HEAD = 128
SPAN = 64

EPSILON = 1e-06
FLOOR = -1e30
LOG2E = 1.4426950408889634

NT = (((1,), (1,)), ((), ()))
TN = (((0,), (0,)), ((), ()))


def dot(a, b, dims=(((1,), (0,)), ((), ()))):
    return lax.dot_general(a, b, dims, preferred_element_type=jnp.float32)


def two_heads(rows):
    blank = jnp.zeros((rows.shape[0], HEAD), rows.dtype)
    return jnp.concatenate(
        [
            jnp.concatenate([rows[:, :HEAD], blank], axis=1),
            jnp.concatenate([blank, rows[:, HEAD:]], axis=1),
        ],
        axis=0,
    )


def span_kernel(
    held_count, nbr_count, meta,
    q_ref, cot_ref, cond_ref, *rest,
):
    held_refs = rest[:held_count]
    (gain_ref, down_ref, up_ref, kv_ref, kvt_ref, upt_ref, downt_ref,
     out_ref, qg_ref, cg_ref, ad_ref, kvg_ref, acc_ref, raw_ref, sems) = rest[held_count:]
    span = pl.program_id(0)
    per_device, slot_len, width = raw_ref.shape
    key_count = nbr_count * slot_len
    head_cols = q_ref.shape[1]
    rank = down_ref.shape[1]
    scaling = HEAD ** (-0.5)
    live = meta[0] == 1
    lens, which, index = 1, 1 + per_device, 1 + 2 * per_device

    @pl.when(span == 0)
    def _():
        for n in range(per_device):
            for b, held in enumerate(held_refs):
                @pl.when(meta[which + n] == b)
                def _():
                    pltpu.make_async_copy(
                        held.at[meta[index + n]], raw_ref.at[n], sems.at[n]
                    ).start()

    for n in range(nbr_count):
        item = span * nbr_count + n
        pltpu.make_async_copy(held_refs[0].at[0], raw_ref.at[item], sems.at[item]).wait()
    raw = raw_ref[pl.ds(span * nbr_count, nbr_count)]
    x_full = raw.reshape(key_count, width).astype(jnp.float32) + cond_ref[
        pl.ds(span, 1), :
    ]
    inv_rms = lax.rsqrt(jnp.mean(x_full * x_full, axis=-1, keepdims=True) + EPSILON)
    gain = gain_ref[...]
    hidden = (x_full * inv_rms * gain).astype(jnp.bfloat16)
    latent = dot(hidden, down_ref[...]).astype(jnp.bfloat16)
    encoded = (x_full + dot(latent, up_ref[...])).astype(jnp.bfloat16)

    slot = lax.broadcasted_iota(jnp.int32, (key_count, 2 * SPAN), 0)
    limit = jnp.zeros((key_count, 2 * SPAN), jnp.int32)
    for n in range(nbr_count):
        here = jnp.logical_and(slot >= n * slot_len, slot < (n + 1) * slot_len)
        limit = jnp.where(here, n * slot_len + meta[lens + span * nbr_count + n], limit)
    usable = slot < limit

    for pair in range(HEADS // 2):
        cols = pl.ds(pair * 2 * HEAD, 2 * HEAD)
        vcols = pl.ds(head_cols + pair * 2 * HEAD, 2 * HEAD)
        keys = dot(encoded, kv_ref[:, cols]).astype(jnp.bfloat16)
        values = dot(encoded, kv_ref[:, vcols]).astype(jnp.bfloat16)
        q2 = two_heads(q_ref[:, cols])
        cot2 = two_heads(cot_ref[:, cols])
        scores = jnp.where(usable, dot(keys, q2, NT), FLOOR)
        row_max = jnp.max(scores, axis=0, keepdims=True)
        raised = jnp.exp2((scores - row_max) * (scaling * LOG2E))
        inv_sum = 1.0 / jnp.sum(raised, axis=0, keepdims=True)
        probs = raised * inv_sum
        probs_b = probs.astype(jnp.bfloat16)
        d_probs = dot(values, cot2, NT)
        delta = jnp.sum(probs * d_probs, axis=0, keepdims=True)
        d_scores = (probs * (d_probs - delta) * scaling).astype(jnp.bfloat16)
        kvg_ref[:, cols] = dot(d_scores, q2).astype(jnp.bfloat16)
        kvg_ref[:, vcols] = dot(probs_b, cot2).astype(jnp.bfloat16)
        probs_t = probs_b.T
        d_scores_t = d_scores.T
        outs, grads = [], []
        for h in range(2):
            lanes = slice(h * HEAD, (h + 1) * HEAD)
            tokens = slice(h * SPAN, (h + 1) * SPAN)
            outs.append(dot(probs_t[tokens], values[:, lanes]))
            grads.append(dot(d_scores_t[tokens], keys[:, lanes]))
        out_ref[:, cols] = jnp.where(live, jnp.concatenate(outs, axis=1), 0.0).astype(jnp.bfloat16)
        qg_ref[:, cols] = jnp.where(live, jnp.concatenate(grads, axis=1), 0.0).astype(jnp.bfloat16)

    enc_grad = dot(kvg_ref[...], kvt_ref[...]).astype(jnp.bfloat16)
    lat_grad = dot(enc_grad, upt_ref[...]).astype(jnp.bfloat16)
    scaled = dot(lat_grad, downt_ref[...]) * gain
    normed = x_full * inv_rms
    x_grad = enc_grad.astype(jnp.float32) + inv_rms * (
        scaled - normed * jnp.mean(scaled * normed, axis=-1, keepdims=True)
    )
    span_grad = jnp.sum(x_grad, axis=0, keepdims=True)
    cg_ref[pl.ds(span, 1), :] = jnp.where(live, span_grad, 0.0)

    @pl.when(span == 0)
    def _():
        acc_ref[...] = jnp.zeros_like(acc_ref)

    acc_ref[:, :rank] += dot(hidden, lat_grad, TN)
    acc_ref[:, rank:] += dot(enc_grad, latent, TN)

    @pl.when(span == pl.num_programs(0) - 1)
    def _():
        ad_ref[...] = jnp.where(live, acc_ref[...], 0.0).astype(ad_ref.dtype)


def run_spans(meta, query, cot, cond, held, gain, w_down, w_up, w_kv, nbr_count):
    span_count, width = cond.shape
    token_count, head_cols = query.shape
    slot_len = held[0].shape[1]
    rank = w_down.shape[1]
    whole = lambda a: pl.BlockSpec(a.shape, lambda s, m: (0,) * a.ndim, pipeline_mode=pl.Buffered(1))
    tokens = pl.BlockSpec((SPAN, head_cols), lambda s, m: (s, 0))
    weights = [gain.reshape(1, width), w_down, w_up, w_kv, w_kv.T, w_up.T, w_down.T]
    per_device = span_count * nbr_count
    rows = per_device * slot_len
    flops = 2 * rows * (2 * width * 2 * head_cols + 6 * width * rank + 6 * SPAN * head_cols)
    return pl.pallas_call(
        functools.partial(span_kernel, len(held), nbr_count),
        grid_spec=pltpu.PrefetchScalarGridSpec(
            num_scalar_prefetch=1,
            grid=(span_count,),
            in_specs=[tokens, tokens, whole(cond)]
            + [pl.BlockSpec(memory_space=pl.ANY)] * len(held)
            + [whole(w) for w in weights],
            out_specs=[
                tokens,
                tokens,
                pl.BlockSpec((span_count, width), lambda s, m: (0, 0)),
                pl.BlockSpec((width, 2 * rank), lambda s, m: (0, 0)),
            ],
            scratch_shapes=[
                pltpu.VMEM((nbr_count * slot_len, 2 * head_cols), jnp.bfloat16),
                pltpu.VMEM((width, 2 * rank), jnp.float32),
                pltpu.VMEM((per_device, slot_len, width), jnp.bfloat16),
                pltpu.SemaphoreType.DMA((per_device,)),
            ],
        ),
        out_shape=[
            jax.ShapeDtypeStruct((token_count, head_cols), jnp.bfloat16),
            jax.ShapeDtypeStruct((token_count, head_cols), jnp.bfloat16),
            jax.ShapeDtypeStruct((span_count, width), jnp.float32),
            jax.ShapeDtypeStruct((width, 2 * rank), jnp.bfloat16),
        ],
        compiler_params=pltpu.CompilerParams(vmem_limit_bytes=48 * 2**20),
        cost_estimate=pl.CostEstimate(
            flops=flops, bytes_accessed=16 * 2**20, transcendentals=rows * SPAN * HEADS
        ),
    )(meta, query, cot, cond, *held, *weights)


def pick_kernel(held_count, meta, *refs):
    held_refs, out_ref, sems = refs[:held_count], refs[held_count], refs[held_count + 1]
    for b, held in enumerate(held_refs):
        @pl.when(meta[0] == b)
        def _():
            for n in range(out_ref.shape[0]):
                pltpu.make_async_copy(held.at[meta[1 + n]], out_ref.at[n], sems.at[n]).start()
    for n in range(out_ref.shape[0]):
        pltpu.make_async_copy(held_refs[0].at[0], out_ref.at[n], sems.at[n]).wait()


def pick(which, index, held):
    count = index.shape[0]
    meta = jnp.concatenate([jnp.reshape(which, (1,)), index]).astype(jnp.int32)
    return pl.pallas_call(
        functools.partial(pick_kernel, len(held)),
        grid_spec=pltpu.PrefetchScalarGridSpec(
            num_scalar_prefetch=1,
            grid=(1,),
            in_specs=[pl.BlockSpec(memory_space=pl.ANY)] * len(held),
            out_specs=pl.BlockSpec(memory_space=pl.ANY),
            scratch_shapes=[pltpu.SemaphoreType.DMA((count,))],
        ),
        out_shape=jax.ShapeDtypeStruct((count,) + held[0].shape[1:], held[0].dtype),
    )(meta, *held)


def place_requests(owners, per_device, pool_count, lanes):
    half = pool_count // 2
    count = owners.shape[1]
    order = jnp.arange(count, dtype=jnp.int32)
    side = (order // per_device) // half
    mate = side[:, None] == side[None, :]
    before = order[None, :] < order[:, None]
    same = owners[:, :, None] == owners[:, None, :]
    lower = owners[:, None, :] < owners[:, :, None]
    total = lambda mask: jnp.sum(mask.astype(jnp.int32), axis=2)
    rank = total(same & (mate & before)[None])
    crosses = rank >= lanes
    far = crosses[:, None, :]
    number = total(far & mate[None] & (lower | (same & before[None])))
    first = total(far & ~mate[None] & lower)
    guests = total(far & ~mate[None] & same)
    lane = jnp.where(crosses, number, first + guests + rank) % lanes
    row = jnp.where(crosses, 1 - side[None, :], side[None, :]) * half + lane % half
    return row, lane // half, crosses, number // half


def body(
    queries, cotangent, cond, nbr_owner, nbr_block, database, lengths, gain, w_down, w_up, w_kv
):
    axes = ("pool", "dp")
    pool_count = lax.axis_size("pool")
    columns = lax.axis_size("dp")
    relay_row = pool_count - 1
    half = pool_count // 2
    row = lax.axis_index("pool")
    me = lax.axis_index("dp")
    span_count, width = cond.shape[2:]
    nbr_count = nbr_owner.shape[3]
    per_device = span_count * nbr_count
    block_count, slot_len = database.shape[2:4]
    live_count = relay_row * per_device
    capacity = max(2, live_count // columns + 1)
    slots = -(-capacity // pool_count)
    lanes = half * slots
    most = 0
    if capacity > lanes:
        for rows in (half, relay_row - half):
            full, left = divmod(rows * per_device, capacity)
            most = max(most, full * (capacity - lanes) + max(0, left - lanes))
    crossing = -(-most // half)
    token_count, head_cols = queries.shape[2:]

    def hop(array, pairs):
        return lax.ppermute(
            array, axes, [(a * columns + j, b * columns + j) for a, b in pairs for j in range(columns)]
        )

    store = database.reshape(block_count, slot_len, width)
    across = hop(store, [(relay_row, relay_row - half)])
    stores = [store, across]
    held_by = jnp.where(row == relay_row, 0, 1)
    for step in range(1, half):
        stores.append(hop(store, [(relay_row, relay_row - step)]))
        held_by = jnp.where(row == relay_row - step, len(stores) - 1, held_by)
        stores.append(hop(across, [(relay_row - half, relay_row - half - step)]))
        held_by = jnp.where(row == relay_row - half - step, len(stores) - 1, held_by)

    info = jnp.concatenate([nbr_owner.reshape(-1), nbr_block.reshape(-1), lengths.reshape(-1)])
    info = jnp.pad(info, (0, -info.shape[0] % 128))
    table = lax.all_gather(info.reshape(1, -1, 128), "dp", axis=0, tiled=True)
    table = lax.all_gather(table.reshape(1, columns, -1, 128), "pool", axis=0, tiled=True)
    table = table.reshape(pool_count, columns, -1)
    by_column = jnp.swapaxes(table[:relay_row], 0, 1)
    owners = by_column[:, :, :per_device].reshape(columns, live_count)
    blocks = by_column[:, :, per_device : 2 * per_device].reshape(columns, live_count)
    store_len = table[relay_row, :, 2 * per_device : 2 * per_device + block_count]
    carrier, slot, crosses, number = place_requests(owners, per_device, pool_count, lanes)

    ring = jnp.arange(slots, dtype=jnp.int32)
    mine = ((owners == me) & (carrier == row))[:, None, :] & (slot[:, None, :] == ring[None, :, None])
    slot_block = jnp.sum(jnp.where(mine, blocks[:, None, :], 0), axis=2).reshape(-1)
    sends = pick(held_by, slot_block, stores)
    arrived = lax.all_to_all(sends, "dp", split_axis=0, concat_axis=0, tiled=True)

    mine_of = lambda a: lax.dynamic_index_in_dim(a, me, 0, keepdims=False)
    my_owner, my_block, my_carrier, my_slot, my_cross, my_number = map(
        mine_of, (owners, blocks, carrier, slot, crosses, number)
    )
    place = my_owner * slots + my_slot
    share = lambda a, step: hop(
        a,
        [(p, p // half * half + (p + step) % half) for p in range(pool_count)],
    )
    held = [arrived] + [share(arrived, step) for step in range(1, half)]
    if crossing:
        ring = jnp.arange(crossing, dtype=jnp.int32)
        mine = (my_cross & (my_carrier == row))[None, :] & (my_number[None, :] == ring[:, None])
        leaving = pick(0, jnp.sum(jnp.where(mine, place[None, :], 0), axis=1), [arrived])
        landed = hop(leaving, [(p, (p + half) % pool_count) for p in range(pool_count)])
        held += [landed] + [share(landed, step) for step in range(1, half)]
    origin = jnp.where(my_cross, (my_carrier + half) % pool_count, my_carrier)
    which = (row - origin) % half + jnp.where(my_cross, half, 0)
    index = jnp.where(my_cross, my_number, place)

    own_row = jnp.minimum(row, relay_row - 1)
    hot = (my_owner * block_count + my_block)[:, None] == jnp.arange(
        columns * block_count, dtype=jnp.int32
    )[None, :]
    wanted_len = jnp.sum(jnp.where(hot, store_len.reshape(1, -1), 0), axis=1)
    own = lambda a: lax.dynamic_index_in_dim(
        a.reshape(relay_row, per_device), own_row, 0, keepdims=False
    )
    live = (row < relay_row).astype(jnp.int32)
    meta = jnp.concatenate([live[None], own(wanted_len), own(which), own(index)]).astype(jnp.int32)

    attn_out, q_grad, cond_grad, terms = run_spans(
        meta,
        queries.reshape(token_count, head_cols),
        cotangent.reshape(token_count, head_cols),
        cond.reshape(span_count, width).astype(jnp.float32),
        held,
        gain,
        w_down,
        w_up,
        w_kv,
        nbr_count,
    )

    def scatter_sum(array, axis):
        parts = lax.all_to_all(array, axis, split_axis=0, concat_axis=0, tiled=True)
        return jnp.sum(
            parts.reshape(lax.axis_size(axis), -1, array.shape[1]).astype(jnp.float32), axis=0
        )

    adapter_grad = scatter_sum(scatter_sum(terms, "pool").astype(jnp.bfloat16), "dp")
    return (
        attn_out.reshape(1, 1, token_count, head_cols),
        q_grad.reshape(1, 1, token_count, head_cols),
        cond_grad.reshape(1, 1, span_count, width),
        adapter_grad,
    )


def solution(mesh):
    return jax.shard_map(
        body,
        mesh=mesh,
        in_specs=(
            P("pool", "dp", None, None),
            P("pool", "dp", None, None),
            P("pool", "dp", None, None),
            P("pool", "dp", None, None),
            P("pool", "dp", None, None),
            P("pool", "dp", None, None, None),
            P("pool", "dp", None),
            P(),
            P(),
            P(),
            P(),
        ),
        out_specs=(
            P("pool", "dp", None, None),
            P("pool", "dp", None, None),
            P("pool", "dp", None, None),
            P(("pool", "dp"), None),
        ),
        check_vma=False,
    )
```

```python
import functools

import jax
import jax.numpy as jnp
from jax import lax
from jax.experimental import pallas as pl
from jax.experimental.pallas import tpu as pltpu
from jax.sharding import PartitionSpec as P

HEADS = 16
HEAD = 128
SPAN = 64
PARTS = 1

EPSILON = 1e-06
FLOOR = -1e30
LOG2E = 1.4426950408889634

NT = (((1,), (1,)), ((), ()))
TN = (((0,), (0,)), ((), ()))


def dot(a, b, dims=(((1,), (0,)), ((), ()))):
    return lax.dot_general(a, b, dims, preferred_element_type=jnp.float32)


def two_heads(rows):
    blank = jnp.zeros((rows.shape[0], HEAD), rows.dtype)
    return jnp.concatenate(
        [
            jnp.concatenate([rows[:, :HEAD], blank], axis=1),
            jnp.concatenate([blank, rows[:, HEAD:]], axis=1),
        ],
        axis=0,
    )


def span_kernel(
    held_count, nbr_count, parts, meta,
    q_ref, cot_ref, cond_ref, *rest,
):
    held_refs = rest[:held_count]
    (gain_ref, down_ref, up_ref, kv_ref, kvt_ref, upt_ref, downt_ref,
     out_ref, qg_ref, cg_ref, ad_ref, kvg_ref, acc_ref, raw_ref) = rest[held_count:]
    span = pl.program_id(0)
    per_device = pl.num_programs(0) * nbr_count
    slot_len, width = raw_ref.shape[1:]
    key_count = nbr_count * slot_len
    head_cols = q_ref.shape[1]
    rank = down_ref.shape[1]
    scaling = HEAD ** (-0.5)
    live = meta[0] == 1
    lens, which, index = 1, 1 + per_device, 1 + 2 * per_device

    for n in range(nbr_count):
        item = span * nbr_count + n
        for b, held in enumerate(held_refs):
            part, source = b % parts, b // parts
            piece = held.shape[1]

            @pl.when(meta[which + item] == source)
            def _():
                raw_ref[n, part * piece : (part + 1) * piece] = held[meta[index + item]]

    raw = raw_ref[...]
    x_full = raw.reshape(key_count, width).astype(jnp.float32) + cond_ref[
        pl.ds(span, 1), :
    ]
    inv_rms = lax.rsqrt(jnp.mean(x_full * x_full, axis=-1, keepdims=True) + EPSILON)
    gain = gain_ref[...]
    hidden = (x_full * inv_rms * gain).astype(jnp.bfloat16)
    latent = dot(hidden, down_ref[...]).astype(jnp.bfloat16)
    encoded = (x_full + dot(latent, up_ref[...])).astype(jnp.bfloat16)

    slot = lax.broadcasted_iota(jnp.int32, (key_count, 2 * SPAN), 0)
    limit = jnp.zeros((key_count, 2 * SPAN), jnp.int32)
    for n in range(nbr_count):
        here = jnp.logical_and(slot >= n * slot_len, slot < (n + 1) * slot_len)
        limit = jnp.where(here, n * slot_len + meta[lens + span * nbr_count + n], limit)
    usable = slot < limit

    for pair in range(HEADS // 2):
        cols = pl.ds(pair * 2 * HEAD, 2 * HEAD)
        vcols = pl.ds(head_cols + pair * 2 * HEAD, 2 * HEAD)
        keys = dot(encoded, kv_ref[:, cols]).astype(jnp.bfloat16)
        values = dot(encoded, kv_ref[:, vcols]).astype(jnp.bfloat16)
        q2 = two_heads(q_ref[:, cols])
        cot2 = two_heads(cot_ref[:, cols])
        scores = jnp.where(usable, dot(keys, q2, NT), FLOOR)
        row_max = jnp.max(scores, axis=0, keepdims=True)
        raised = jnp.exp2((scores - row_max) * (scaling * LOG2E))
        inv_sum = 1.0 / jnp.sum(raised, axis=0, keepdims=True)
        probs = raised * inv_sum
        probs_b = probs.astype(jnp.bfloat16)
        d_probs = dot(values, cot2, NT)
        delta = jnp.sum(probs * d_probs, axis=0, keepdims=True)
        d_scores = (probs * (d_probs - delta) * scaling).astype(jnp.bfloat16)
        kvg_ref[:, cols] = dot(d_scores, q2).astype(jnp.bfloat16)
        kvg_ref[:, vcols] = dot(probs_b, cot2).astype(jnp.bfloat16)
        probs_t = probs_b.T
        d_scores_t = d_scores.T
        outs, grads = [], []
        for h in range(2):
            lanes = slice(h * HEAD, (h + 1) * HEAD)
            tokens = slice(h * SPAN, (h + 1) * SPAN)
            outs.append(dot(probs_t[tokens], values[:, lanes]))
            grads.append(dot(d_scores_t[tokens], keys[:, lanes]))
        out_ref[:, cols] = jnp.where(live, jnp.concatenate(outs, axis=1), 0.0).astype(jnp.bfloat16)
        qg_ref[:, cols] = jnp.where(live, jnp.concatenate(grads, axis=1), 0.0).astype(jnp.bfloat16)

    enc_grad = dot(kvg_ref[...], kvt_ref[...]).astype(jnp.bfloat16)
    lat_grad = dot(enc_grad, upt_ref[...]).astype(jnp.bfloat16)
    scaled = dot(lat_grad, downt_ref[...]) * gain
    normed = x_full * inv_rms
    x_grad = enc_grad.astype(jnp.float32) + inv_rms * (
        scaled - normed * jnp.mean(scaled * normed, axis=-1, keepdims=True)
    )
    span_grad = jnp.sum(x_grad, axis=0, keepdims=True)
    cg_ref[pl.ds(span, 1), :] = jnp.where(live, span_grad, 0.0)

    @pl.when(span == 0)
    def _():
        acc_ref[...] = jnp.zeros_like(acc_ref)

    acc_ref[:, :rank] += dot(hidden, lat_grad, TN)
    acc_ref[:, rank:] += dot(enc_grad, latent, TN)

    @pl.when(span == pl.num_programs(0) - 1)
    def _():
        ad_ref[...] = jnp.where(live, acc_ref[...], 0.0).astype(ad_ref.dtype)


def run_spans(meta, query, cot, cond, held, parts, gain, w_down, w_up, w_kv, nbr_count):
    span_count, width = cond.shape
    token_count, head_cols = query.shape
    slot_len = held[0].shape[1] * parts
    rank = w_down.shape[1]
    whole = lambda a: pl.BlockSpec(a.shape, lambda s, m: (0,) * a.ndim, pipeline_mode=pl.Buffered(1))
    tokens = pl.BlockSpec((SPAN, head_cols), lambda s, m: (s, 0))
    weights = [gain.reshape(1, width), w_down, w_up, w_kv, w_kv.T, w_up.T, w_down.T]
    per_device = span_count * nbr_count
    rows = per_device * slot_len
    flops = 2 * rows * (2 * width * 2 * head_cols + 6 * width * rank + 6 * SPAN * head_cols)
    return pl.pallas_call(
        functools.partial(span_kernel, len(held), nbr_count, parts),
        grid_spec=pltpu.PrefetchScalarGridSpec(
            num_scalar_prefetch=1,
            grid=(span_count,),
            in_specs=[tokens, tokens, whole(cond)]
            + [pl.BlockSpec(memory_space=pltpu.VMEM)] * len(held)
            + [whole(w) for w in weights],
            out_specs=[
                tokens,
                tokens,
                pl.BlockSpec((span_count, width), lambda s, m: (0, 0)),
                pl.BlockSpec((width, 2 * rank), lambda s, m: (0, 0)),
            ],
            scratch_shapes=[
                pltpu.VMEM((nbr_count * slot_len, 2 * head_cols), jnp.bfloat16),
                pltpu.VMEM((width, 2 * rank), jnp.float32),
                pltpu.VMEM((nbr_count, slot_len, width), jnp.bfloat16),
            ],
        ),
        out_shape=[
            jax.ShapeDtypeStruct((token_count, head_cols), jnp.bfloat16),
            jax.ShapeDtypeStruct((token_count, head_cols), jnp.bfloat16),
            jax.ShapeDtypeStruct((span_count, width), jnp.float32),
            jax.ShapeDtypeStruct((width, 2 * rank), jnp.bfloat16),
        ],
        compiler_params=pltpu.CompilerParams(vmem_limit_bytes=40 * 2**20),
        cost_estimate=pl.CostEstimate(
            flops=flops, bytes_accessed=16 * 2**20, transcendentals=rows * SPAN * HEADS
        ),
    )(meta, query, cot, cond, *held, *weights)


def pick_kernel(held_count, meta, *refs):
    held_refs, out_ref = refs[:held_count], refs[held_count]
    for b, held in enumerate(held_refs):
        @pl.when(meta[0] == b)
        def _():
            for n in range(out_ref.shape[0]):
                out_ref[n] = held[meta[1 + n]]


def pick(which, index, held):
    count = index.shape[0]
    meta = jnp.concatenate([jnp.reshape(which, (1,)), index]).astype(jnp.int32)
    return pl.pallas_call(
        functools.partial(pick_kernel, len(held)),
        grid_spec=pltpu.PrefetchScalarGridSpec(
            num_scalar_prefetch=1,
            grid=(1,),
            in_specs=[pl.BlockSpec(memory_space=pltpu.VMEM)] * len(held),
            out_specs=pl.BlockSpec(memory_space=pltpu.VMEM),
        ),
        out_shape=jax.ShapeDtypeStruct((count,) + held[0].shape[1:], held[0].dtype),
        compiler_params=pltpu.CompilerParams(vmem_limit_bytes=24 * 2**20),
    )(meta, *held)


def place_requests(owners, per_device, pool_count, lanes):
    half = pool_count // 2
    count = owners.shape[1]
    order = jnp.arange(count, dtype=jnp.int32)
    side = (order // per_device) // half
    mate = side[:, None] == side[None, :]
    before = order[None, :] < order[:, None]
    same = owners[:, :, None] == owners[:, None, :]
    lower = owners[:, None, :] < owners[:, :, None]
    total = lambda mask: jnp.sum(mask.astype(jnp.int32), axis=2)
    rank = total(same & (mate & before)[None])
    crosses = rank >= lanes
    far = crosses[:, None, :]
    number = total(far & mate[None] & (lower | (same & before[None])))
    first = total(far & ~mate[None] & lower)
    guests = total(far & ~mate[None] & same)
    lane = jnp.where(crosses, number, first + guests + rank) % lanes
    row = jnp.where(crosses, 1 - side[None, :], side[None, :]) * half + lane % half
    return row, lane // half, crosses, number // half


def body(
    queries, cotangent, cond, nbr_owner, nbr_block, database, lengths, gain, w_down, w_up, w_kv
):
    axes = ("pool", "dp")
    pool_count = lax.axis_size("pool")
    columns = lax.axis_size("dp")
    relay_row = pool_count - 1
    half = pool_count // 2
    row = lax.axis_index("pool")
    me = lax.axis_index("dp")
    span_count, width = cond.shape[2:]
    nbr_count = nbr_owner.shape[3]
    per_device = span_count * nbr_count
    block_count, slot_len = database.shape[2:4]
    live_count = relay_row * per_device
    capacity = max(2, live_count // columns + 1)
    slots = -(-capacity // pool_count)
    lanes = half * slots
    most = 0
    if capacity > lanes:
        for rows in (half, relay_row - half):
            full, left = divmod(rows * per_device, capacity)
            most = max(most, full * (capacity - lanes) + max(0, left - lanes))
    crossing = -(-most // half)
    token_count, head_cols = queries.shape[2:]

    def hop(array, pairs):
        return lax.ppermute(
            array, axes, [(a * columns + j, b * columns + j) for a, b in pairs for j in range(columns)]
        )

    parts = PARTS if slot_len % (PARTS * 16) == 0 else 1
    piece = slot_len // parts
    full_store = database.reshape(block_count, slot_len, width)
    store = [full_store[:, i * piece : (i + 1) * piece] for i in range(parts)]

    across = [hop(a, [(relay_row, relay_row - half)]) for a in store]

    info = jnp.concatenate([nbr_owner.reshape(-1), nbr_block.reshape(-1), lengths.reshape(-1)])
    info = jnp.pad(info, (0, -info.shape[0] % 128))
    table = lax.all_gather(info.reshape(1, -1, 128), "dp", axis=0, tiled=True)
    table = lax.all_gather(table.reshape(1, columns, -1, 128), "pool", axis=0, tiled=True)
    across, table = lax.optimization_barrier((across, table))
    table = table.reshape(pool_count, columns, -1)
    by_column = jnp.swapaxes(table[:relay_row], 0, 1)
    owners = by_column[:, :, :per_device].reshape(columns, live_count)
    blocks = by_column[:, :, per_device : 2 * per_device].reshape(columns, live_count)
    store_len = table[relay_row, :, 2 * per_device : 2 * per_device + block_count]
    carrier, slot, crosses, number = place_requests(owners, per_device, pool_count, lanes)

    ring = jnp.arange(slots, dtype=jnp.int32)
    mine = ((owners == me) & (carrier == row))[:, None, :] & (slot[:, None, :] == ring[None, :, None])
    slot_block = jnp.sum(jnp.where(mine, blocks[:, None, :], 0), axis=2).reshape(-1)

    mine_of = lambda a: lax.dynamic_index_in_dim(a, me, 0, keepdims=False)
    my_owner, my_block, my_carrier, my_slot, my_cross, my_number = map(
        mine_of, (owners, blocks, carrier, slot, crosses, number)
    )
    place = my_owner * slots + my_slot
    ring = jnp.arange(crossing, dtype=jnp.int32)
    mine = (my_cross & (my_carrier == row))[None, :] & (my_number[None, :] == ring[:, None])
    leaving_place = jnp.sum(jnp.where(mine, place[None, :], 0), axis=1)

    def share(array, step):
        return hop(array, [(p, p // half * half + (p + step) % half) for p in range(pool_count)])

    held = []
    for i in range(parts):
        stores = [store[i], across[i]]
        held_by = jnp.where(row == relay_row, 0, 1)
        for step in range(1, half):
            for near, array in ((relay_row, store[i]), (relay_row - half, across[i])):
                stores.append(hop(array, [(near, near - step)]))
                held_by = jnp.where(row == near - step, len(stores) - 1, held_by)
        sends = pick(held_by, slot_block, stores)
        arrived = lax.all_to_all(sends, "dp", split_axis=0, concat_axis=0, tiled=True)
        here = [arrived] + [share(arrived, step) for step in range(1, half)]
        if crossing:
            leaving = pick(0, leaving_place, [arrived])
            landed = hop(leaving, [(p, (p + half) % pool_count) for p in range(pool_count)])
            here += [landed] + [share(landed, step) for step in range(1, half)]
        held.append(here)
    origin = jnp.where(my_cross, (my_carrier + half) % pool_count, my_carrier)
    which = (row - origin) % half + jnp.where(my_cross, half, 0)
    index = jnp.where(my_cross, my_number, place)
    held = [here[b] for b in range(len(held[0])) for here in held]

    own_row = jnp.minimum(row, relay_row - 1)
    hot = (my_owner * block_count + my_block)[:, None] == jnp.arange(
        columns * block_count, dtype=jnp.int32
    )[None, :]
    wanted_len = jnp.sum(jnp.where(hot, store_len.reshape(1, -1), 0), axis=1)
    own = lambda a: lax.dynamic_index_in_dim(
        a.reshape(relay_row, per_device), own_row, 0, keepdims=False
    )
    live = (row < relay_row).astype(jnp.int32)
    meta = jnp.concatenate([live[None], own(wanted_len), own(which), own(index)]).astype(jnp.int32)

    attn_out, q_grad, cond_grad, terms = run_spans(
        meta,
        queries.reshape(token_count, head_cols),
        cotangent.reshape(token_count, head_cols),
        cond.reshape(span_count, width).astype(jnp.float32),
        held,
        parts,
        gain,
        w_down,
        w_up,
        w_kv,
        nbr_count,
    )

    def scatter_sum(array, axis):
        parts = lax.all_to_all(array, axis, split_axis=0, concat_axis=0, tiled=True)
        return jnp.sum(
            parts.reshape(lax.axis_size(axis), -1, array.shape[1]).astype(jnp.float32), axis=0
        )

    adapter_grad = scatter_sum(scatter_sum(terms, "pool").astype(jnp.bfloat16), "dp")
    return (
        attn_out.reshape(1, 1, token_count, head_cols),
        q_grad.reshape(1, 1, token_count, head_cols),
        cond_grad.reshape(1, 1, span_count, width),
        adapter_grad,
    )


def solution(mesh):
    return jax.shard_map(
        body,
        mesh=mesh,
        in_specs=(
            P("pool", "dp", None, None),
            P("pool", "dp", None, None),
            P("pool", "dp", None, None),
            P("pool", "dp", None, None),
            P("pool", "dp", None, None),
            P("pool", "dp", None, None, None),
            P("pool", "dp", None),
            P(),
            P(),
            P(),
            P(),
        ),
        out_specs=(
            P("pool", "dp", None, None),
            P("pool", "dp", None, None),
            P("pool", "dp", None, None),
            P(("pool", "dp"), None),
        ),
        check_vma=False,
    )
```

```python
import functools

import jax
import jax.numpy as jnp
from jax import lax
from jax.experimental import pallas as pl
from jax.experimental.pallas import tpu as pltpu
from jax.sharding import PartitionSpec as P

HEADS = 16
HEAD = 128
SPAN = 64
PARTS = 2

EPSILON = 1e-06
FLOOR = -1e30
LOG2E = 1.4426950408889634

NT = (((1,), (1,)), ((), ()))
TN = (((0,), (0,)), ((), ()))


def dot(a, b, dims=(((1,), (0,)), ((), ()))):
    return lax.dot_general(a, b, dims, preferred_element_type=jnp.float32)


def two_heads(rows):
    blank = jnp.zeros((rows.shape[0], HEAD), rows.dtype)
    return jnp.concatenate(
        [
            jnp.concatenate([rows[:, :HEAD], blank], axis=1),
            jnp.concatenate([blank, rows[:, HEAD:]], axis=1),
        ],
        axis=0,
    )


def span_kernel(
    held_count, nbr_count, parts, meta,
    q_ref, cot_ref, cond_ref, *rest,
):
    held_refs = rest[:held_count]
    (gain_ref, down_ref, up_ref, kv_ref, kvt_ref, upt_ref, downt_ref,
     out_ref, qg_ref, cg_ref, ad_ref, kvg_ref, acc_ref, raw_ref) = rest[held_count:]
    span = pl.program_id(0)
    per_device = pl.num_programs(0) * nbr_count
    slot_len, width = raw_ref.shape[1:]
    key_count = nbr_count * slot_len
    head_cols = q_ref.shape[1]
    rank = down_ref.shape[1]
    scaling = HEAD ** (-0.5)
    live = meta[0] == 1
    lens, which, index = 1, 1 + per_device, 1 + 2 * per_device

    for n in range(nbr_count):
        item = span * nbr_count + n
        for b, held in enumerate(held_refs):
            part, source = b % parts, b // parts
            piece = held.shape[1]

            @pl.when(meta[which + item] == source)
            def _():
                raw_ref[n, part * piece : (part + 1) * piece] = held[meta[index + item]]

    raw = raw_ref[...]
    x_full = raw.reshape(key_count, width).astype(jnp.float32) + cond_ref[
        pl.ds(span, 1), :
    ]
    inv_rms = lax.rsqrt(jnp.mean(x_full * x_full, axis=-1, keepdims=True) + EPSILON)
    gain = gain_ref[...]
    hidden = (x_full * inv_rms * gain).astype(jnp.bfloat16)
    latent = dot(hidden, down_ref[...]).astype(jnp.bfloat16)
    encoded = (x_full + dot(latent, up_ref[...])).astype(jnp.bfloat16)

    slot = lax.broadcasted_iota(jnp.int32, (key_count, 2 * SPAN), 0)
    limit = jnp.zeros((key_count, 2 * SPAN), jnp.int32)
    for n in range(nbr_count):
        here = jnp.logical_and(slot >= n * slot_len, slot < (n + 1) * slot_len)
        limit = jnp.where(here, n * slot_len + meta[lens + span * nbr_count + n], limit)
    usable = slot < limit

    for pair in range(HEADS // 2):
        cols = pl.ds(pair * 2 * HEAD, 2 * HEAD)
        vcols = pl.ds(head_cols + pair * 2 * HEAD, 2 * HEAD)
        keys = dot(encoded, kv_ref[:, cols]).astype(jnp.bfloat16)
        values = dot(encoded, kv_ref[:, vcols]).astype(jnp.bfloat16)
        q2 = two_heads(q_ref[:, cols])
        cot2 = two_heads(cot_ref[:, cols])
        scores = jnp.where(usable, dot(keys, q2, NT), FLOOR)
        row_max = jnp.max(scores, axis=0, keepdims=True)
        raised = jnp.exp2((scores - row_max) * (scaling * LOG2E))
        inv_sum = 1.0 / jnp.sum(raised, axis=0, keepdims=True)
        probs = raised * inv_sum
        probs_b = probs.astype(jnp.bfloat16)
        d_probs = dot(values, cot2, NT)
        delta = jnp.sum(probs * d_probs, axis=0, keepdims=True)
        d_scores = (probs * (d_probs - delta) * scaling).astype(jnp.bfloat16)
        kvg_ref[:, cols] = dot(d_scores, q2).astype(jnp.bfloat16)
        kvg_ref[:, vcols] = dot(probs_b, cot2).astype(jnp.bfloat16)
        probs_t = probs_b.T
        d_scores_t = d_scores.T
        outs, grads = [], []
        for h in range(2):
            lanes = slice(h * HEAD, (h + 1) * HEAD)
            tokens = slice(h * SPAN, (h + 1) * SPAN)
            outs.append(dot(probs_t[tokens], values[:, lanes]))
            grads.append(dot(d_scores_t[tokens], keys[:, lanes]))
        out_ref[:, cols] = jnp.where(live, jnp.concatenate(outs, axis=1), 0.0).astype(jnp.bfloat16)
        qg_ref[:, cols] = jnp.where(live, jnp.concatenate(grads, axis=1), 0.0).astype(jnp.bfloat16)

    enc_grad = dot(kvg_ref[...], kvt_ref[...]).astype(jnp.bfloat16)
    lat_grad = dot(enc_grad, upt_ref[...]).astype(jnp.bfloat16)
    scaled = dot(lat_grad, downt_ref[...]) * gain
    normed = x_full * inv_rms
    x_grad = enc_grad.astype(jnp.float32) + inv_rms * (
        scaled - normed * jnp.mean(scaled * normed, axis=-1, keepdims=True)
    )
    span_grad = jnp.sum(x_grad, axis=0, keepdims=True)
    cg_ref[pl.ds(span, 1), :] = jnp.where(live, span_grad, 0.0)

    @pl.when(span == 0)
    def _():
        acc_ref[...] = jnp.zeros_like(acc_ref)

    acc_ref[:, :rank] += dot(hidden, lat_grad, TN)
    acc_ref[:, rank:] += dot(enc_grad, latent, TN)

    @pl.when(span == pl.num_programs(0) - 1)
    def _():
        ad_ref[...] = jnp.where(live, acc_ref[...], 0.0).astype(ad_ref.dtype)


def run_spans(meta, query, cot, cond, held, parts, gain, w_down, w_up, w_kv, nbr_count):
    span_count, width = cond.shape
    token_count, head_cols = query.shape
    slot_len = held[0].shape[1] * parts
    rank = w_down.shape[1]
    whole = lambda a: pl.BlockSpec(a.shape, lambda s, m: (0,) * a.ndim, pipeline_mode=pl.Buffered(1))
    tokens = pl.BlockSpec((SPAN, head_cols), lambda s, m: (s, 0))
    weights = [gain.reshape(1, width), w_down, w_up, w_kv, w_kv.T, w_up.T, w_down.T]
    per_device = span_count * nbr_count
    rows = per_device * slot_len
    flops = 2 * rows * (2 * width * 2 * head_cols + 6 * width * rank + 6 * SPAN * head_cols)
    return pl.pallas_call(
        functools.partial(span_kernel, len(held), nbr_count, parts),
        grid_spec=pltpu.PrefetchScalarGridSpec(
            num_scalar_prefetch=1,
            grid=(span_count,),
            in_specs=[tokens, tokens, whole(cond)]
            + [pl.BlockSpec(memory_space=pltpu.VMEM)] * len(held)
            + [whole(w) for w in weights],
            out_specs=[
                tokens,
                tokens,
                pl.BlockSpec((span_count, width), lambda s, m: (0, 0)),
                pl.BlockSpec((width, 2 * rank), lambda s, m: (0, 0)),
            ],
            scratch_shapes=[
                pltpu.VMEM((nbr_count * slot_len, 2 * head_cols), jnp.bfloat16),
                pltpu.VMEM((width, 2 * rank), jnp.float32),
                pltpu.VMEM((nbr_count, slot_len, width), jnp.bfloat16),
            ],
        ),
        out_shape=[
            jax.ShapeDtypeStruct((token_count, head_cols), jnp.bfloat16),
            jax.ShapeDtypeStruct((token_count, head_cols), jnp.bfloat16),
            jax.ShapeDtypeStruct((span_count, width), jnp.float32),
            jax.ShapeDtypeStruct((width, 2 * rank), jnp.bfloat16),
        ],
        compiler_params=pltpu.CompilerParams(vmem_limit_bytes=40 * 2**20),
        cost_estimate=pl.CostEstimate(
            flops=flops, bytes_accessed=16 * 2**20, transcendentals=rows * SPAN * HEADS
        ),
    )(meta, query, cot, cond, *held, *weights)


def pick_kernel(held_count, meta, *refs):
    held_refs, out_ref = refs[:held_count], refs[held_count]
    for b, held in enumerate(held_refs):
        @pl.when(meta[0] == b)
        def _():
            for n in range(out_ref.shape[0]):
                out_ref[n] = held[meta[1 + n]]


def pick(which, index, held):
    count = index.shape[0]
    meta = jnp.concatenate([jnp.reshape(which, (1,)), index]).astype(jnp.int32)
    return pl.pallas_call(
        functools.partial(pick_kernel, len(held)),
        grid_spec=pltpu.PrefetchScalarGridSpec(
            num_scalar_prefetch=1,
            grid=(1,),
            in_specs=[pl.BlockSpec(memory_space=pltpu.VMEM)] * len(held),
            out_specs=pl.BlockSpec(memory_space=pltpu.VMEM),
        ),
        out_shape=jax.ShapeDtypeStruct((count,) + held[0].shape[1:], held[0].dtype),
        compiler_params=pltpu.CompilerParams(vmem_limit_bytes=24 * 2**20),
    )(meta, *held)


def place_requests(owners, per_device, pool_count, lanes):
    half = pool_count // 2
    count = owners.shape[1]
    order = jnp.arange(count, dtype=jnp.int32)
    side = (order // per_device) // half
    mate = side[:, None] == side[None, :]
    before = order[None, :] < order[:, None]
    same = owners[:, :, None] == owners[:, None, :]
    lower = owners[:, None, :] < owners[:, :, None]
    total = lambda mask: jnp.sum(mask.astype(jnp.int32), axis=2)
    rank = total(same & (mate & before)[None])
    crosses = rank >= lanes
    far = crosses[:, None, :]
    number = total(far & mate[None] & (lower | (same & before[None])))
    first = total(far & ~mate[None] & lower)
    guests = total(far & ~mate[None] & same)
    lane = jnp.where(crosses, number, first + guests + rank) % lanes
    row = jnp.where(crosses, 1 - side[None, :], side[None, :]) * half + lane % half
    return row, lane // half, crosses, number // half


def body(
    queries, cotangent, cond, nbr_owner, nbr_block, database, lengths, gain, w_down, w_up, w_kv
):
    axes = ("pool", "dp")
    pool_count = lax.axis_size("pool")
    columns = lax.axis_size("dp")
    relay_row = pool_count - 1
    half = pool_count // 2
    row = lax.axis_index("pool")
    me = lax.axis_index("dp")
    span_count, width = cond.shape[2:]
    nbr_count = nbr_owner.shape[3]
    per_device = span_count * nbr_count
    block_count, slot_len = database.shape[2:4]
    live_count = relay_row * per_device
    capacity = max(2, live_count // columns + 1)
    slots = -(-capacity // pool_count)
    lanes = half * slots
    most = 0
    if capacity > lanes:
        for rows in (half, relay_row - half):
            full, left = divmod(rows * per_device, capacity)
            most = max(most, full * (capacity - lanes) + max(0, left - lanes))
    crossing = -(-most // half)
    token_count, head_cols = queries.shape[2:]

    def hop(array, pairs):
        return lax.ppermute(
            array, axes, [(a * columns + j, b * columns + j) for a, b in pairs for j in range(columns)]
        )

    parts = PARTS if slot_len % (PARTS * 16) == 0 else 1
    piece = slot_len // parts
    full_store = database.reshape(block_count, slot_len, width)
    store = [full_store[:, i * piece : (i + 1) * piece] for i in range(parts)]

    across = [hop(a, [(relay_row, relay_row - half)]) for a in store]

    info = jnp.concatenate([nbr_owner.reshape(-1), nbr_block.reshape(-1), lengths.reshape(-1)])
    info = jnp.pad(info, (0, -info.shape[0] % 128))
    table = lax.all_gather(info.reshape(1, -1, 128), "dp", axis=0, tiled=True)
    table = lax.all_gather(table.reshape(1, columns, -1, 128), "pool", axis=0, tiled=True)
    across, table = lax.optimization_barrier((across, table))
    table = table.reshape(pool_count, columns, -1)
    by_column = jnp.swapaxes(table[:relay_row], 0, 1)
    owners = by_column[:, :, :per_device].reshape(columns, live_count)
    blocks = by_column[:, :, per_device : 2 * per_device].reshape(columns, live_count)
    store_len = table[relay_row, :, 2 * per_device : 2 * per_device + block_count]
    carrier, slot, crosses, number = place_requests(owners, per_device, pool_count, lanes)

    ring = jnp.arange(slots, dtype=jnp.int32)
    mine = ((owners == me) & (carrier == row))[:, None, :] & (slot[:, None, :] == ring[None, :, None])
    slot_block = jnp.sum(jnp.where(mine, blocks[:, None, :], 0), axis=2).reshape(-1)

    mine_of = lambda a: lax.dynamic_index_in_dim(a, me, 0, keepdims=False)
    my_owner, my_block, my_carrier, my_slot, my_cross, my_number = map(
        mine_of, (owners, blocks, carrier, slot, crosses, number)
    )
    place = my_owner * slots + my_slot
    ring = jnp.arange(crossing, dtype=jnp.int32)
    mine = (my_cross & (my_carrier == row))[None, :] & (my_number[None, :] == ring[:, None])
    leaving_place = jnp.sum(jnp.where(mine, place[None, :], 0), axis=1)

    def share(array, step):
        return hop(array, [(p, p // half * half + (p + step) % half) for p in range(pool_count)])

    held = []
    for i in range(parts):
        stores = [store[i], across[i]]
        held_by = jnp.where(row == relay_row, 0, 1)
        for step in range(1, half):
            for near, array in ((relay_row, store[i]), (relay_row - half, across[i])):
                stores.append(hop(array, [(near, near - step)]))
                held_by = jnp.where(row == near - step, len(stores) - 1, held_by)
        sends = pick(held_by, slot_block, stores)
        arrived = lax.all_to_all(sends, "dp", split_axis=0, concat_axis=0, tiled=True)
        here = [arrived] + [share(arrived, step) for step in range(1, half)]
        if crossing:
            leaving = pick(0, leaving_place, [arrived])
            landed = hop(leaving, [(p, (p + half) % pool_count) for p in range(pool_count)])
            here += [landed] + [share(landed, step) for step in range(1, half)]
        held.append(here)
    origin = jnp.where(my_cross, (my_carrier + half) % pool_count, my_carrier)
    which = (row - origin) % half + jnp.where(my_cross, half, 0)
    index = jnp.where(my_cross, my_number, place)
    held = [here[b] for b in range(len(held[0])) for here in held]

    own_row = jnp.minimum(row, relay_row - 1)
    hot = (my_owner * block_count + my_block)[:, None] == jnp.arange(
        columns * block_count, dtype=jnp.int32
    )[None, :]
    wanted_len = jnp.sum(jnp.where(hot, store_len.reshape(1, -1), 0), axis=1)
    own = lambda a: lax.dynamic_index_in_dim(
        a.reshape(relay_row, per_device), own_row, 0, keepdims=False
    )
    live = (row < relay_row).astype(jnp.int32)
    meta = jnp.concatenate([live[None], own(wanted_len), own(which), own(index)]).astype(jnp.int32)

    attn_out, q_grad, cond_grad, terms = run_spans(
        meta,
        queries.reshape(token_count, head_cols),
        cotangent.reshape(token_count, head_cols),
        cond.reshape(span_count, width).astype(jnp.float32),
        held,
        parts,
        gain,
        w_down,
        w_up,
        w_kv,
        nbr_count,
    )

    def scatter_sum(array, axis):
        parts = lax.all_to_all(array, axis, split_axis=0, concat_axis=0, tiled=True)
        return jnp.sum(
            parts.reshape(lax.axis_size(axis), -1, array.shape[1]).astype(jnp.float32), axis=0
        )

    adapter_grad = scatter_sum(scatter_sum(terms, "pool").astype(jnp.bfloat16), "dp")
    return (
        attn_out.reshape(1, 1, token_count, head_cols),
        q_grad.reshape(1, 1, token_count, head_cols),
        cond_grad.reshape(1, 1, span_count, width),
        adapter_grad,
    )


def solution(mesh):
    return jax.shard_map(
        body,
        mesh=mesh,
        in_specs=(
            P("pool", "dp", None, None),
            P("pool", "dp", None, None),
            P("pool", "dp", None, None),
            P("pool", "dp", None, None),
            P("pool", "dp", None, None),
            P("pool", "dp", None, None, None),
            P("pool", "dp", None),
            P(),
            P(),
            P(),
            P(),
        ),
        out_specs=(
            P("pool", "dp", None, None),
            P("pool", "dp", None, None),
            P("pool", "dp", None, None),
            P(("pool", "dp"), None),
        ),
        check_vma=False,
    )
```

```python
import functools

import jax
import jax.numpy as jnp
from jax import lax
from jax.experimental import pallas as pl
from jax.experimental.pallas import tpu as pltpu
from jax.sharding import PartitionSpec as P

HEADS = 16
HEAD = 128
SPAN = 64
PARTS = 1

EPSILON = 1e-06
FLOOR = -1e30
LOG2E = 1.4426950408889634

NT = (((1,), (1,)), ((), ()))
TN = (((0,), (0,)), ((), ()))


def dot(a, b, dims=(((1,), (0,)), ((), ()))):
    return lax.dot_general(a, b, dims, preferred_element_type=jnp.float32)


def span_kernel(
    held_count, nbr_count, parts, meta,
    q_ref, cot_ref, cond_ref, gain_ref, down_ref, up_ref, upt_ref, downt_ref, *rest,
):
    held_refs = rest[:held_count]
    (kv_hbm, kvt_hbm, out_ref, qg_ref, cg_ref, ad_ref,
     raw_ref, kv_ref, kvt_ref, proj_ref, grad_ref, score_ref, dprob_ref, prob_ref, dscore_ref,
     q2_ref, cot2_ref, acc_ref, sems, kv_sem) = rest[held_count:]
    span = pl.program_id(0)
    per_device, slot_len, width = raw_ref.shape
    key_count = nbr_count * slot_len
    head_cols = q_ref.shape[1]
    rank = down_ref.shape[1]
    scaling = HEAD ** (-0.5)
    live = meta[0] == 1
    lens, which, index = 1, 1 + per_device, 1 + 2 * per_device
    piece = slot_len // parts
    pairs = [pl.ds(i * 2 * HEAD, 2 * HEAD) for i in range(HEADS // 2)]
    value_pairs = [pl.ds(head_cols + i * 2 * HEAD, 2 * HEAD) for i in range(HEADS // 2)]
    lanes = [pl.ds(i * 2 * SPAN, 2 * SPAN) for i in range(HEADS // 2)]
    kv_copy = pltpu.make_async_copy(kv_hbm, kv_ref, kv_sem.at[0])
    kvt_copy = pltpu.make_async_copy(kvt_hbm, kvt_ref, kv_sem.at[1])

    @pl.when(span == 0)
    def _():
        for n in range(per_device):
            for b, held in enumerate(held_refs):
                @pl.when(meta[which + n] == b // parts)
                def _():
                    part = b % parts
                    pltpu.make_async_copy(
                        held.at[meta[index + n]],
                        raw_ref.at[n, pl.ds(part * piece, piece)],
                        sems.at[n * parts + part],
                    ).start()
        kv_copy.start()
        kvt_copy.start()

    q2_ref[...] = jnp.zeros_like(q2_ref)
    cot2_ref[...] = jnp.zeros_like(cot2_ref)
    for i in range(HEADS):
        cols = pl.ds(i * HEAD, HEAD)
        tokens = pl.ds(i % 2 * SPAN, SPAN)
        q2_ref[tokens, cols] = q_ref[:, cols]
        cot2_ref[tokens, cols] = cot_ref[:, cols]

    for n in range(nbr_count):
        for part in range(parts):
            item = span * nbr_count + n
            pltpu.make_async_copy(
                held_refs[0].at[0],
                raw_ref.at[item, pl.ds(part * piece, piece)],
                sems.at[item * parts + part],
            ).wait()
    raw = raw_ref[pl.ds(span * nbr_count, nbr_count)]
    x_full = raw.reshape(key_count, width).astype(jnp.float32) + cond_ref[pl.ds(span, 1), :]
    inv_rms = lax.rsqrt(jnp.mean(x_full * x_full, axis=-1, keepdims=True) + EPSILON)
    gain = gain_ref[...]
    hidden = (x_full * inv_rms * gain).astype(jnp.bfloat16)
    latent = dot(hidden, down_ref[...]).astype(jnp.bfloat16)
    encoded = (x_full + dot(latent, up_ref[...])).astype(jnp.bfloat16)

    @pl.when(span == 0)
    def _():
        kv_copy.wait()

    for cols in pairs + value_pairs:
        proj_ref[:, cols] = dot(encoded, kv_ref[:, cols]).astype(jnp.bfloat16)

    for cols, value_cols, lane in zip(pairs, value_pairs, lanes):
        score_ref[:, lane] = dot(proj_ref[:, cols], q2_ref[:, cols], NT)
        dprob_ref[:, lane] = dot(proj_ref[:, value_cols], cot2_ref[:, cols], NT)

    slot = lax.broadcasted_iota(jnp.int32, (key_count, 2 * SPAN), 0)
    limit = jnp.zeros((key_count, 2 * SPAN), jnp.int32)
    for n in range(nbr_count):
        here = jnp.logical_and(slot >= n * slot_len, slot < (n + 1) * slot_len)
        limit = jnp.where(here, n * slot_len + meta[lens + span * nbr_count + n], limit)
    usable = slot < limit
    for lane in lanes:
        scores = jnp.where(usable, score_ref[:, lane], FLOOR)
        row_max = jnp.max(scores, axis=0, keepdims=True)
        raised = jnp.exp2((scores - row_max) * (scaling * LOG2E))
        probs = raised * (1.0 / jnp.sum(raised, axis=0, keepdims=True))
        d_probs = dprob_ref[:, lane]
        delta = jnp.sum(probs * d_probs, axis=0, keepdims=True)
        prob_ref[:, lane] = probs.astype(jnp.bfloat16)
        dscore_ref[:, lane] = (probs * (d_probs - delta) * scaling).astype(jnp.bfloat16)

    for cols, value_cols, lane in zip(pairs, value_pairs, lanes):
        grad_ref[:, cols] = dot(dscore_ref[:, lane], q2_ref[:, cols]).astype(jnp.bfloat16)
        grad_ref[:, value_cols] = dot(prob_ref[:, lane], cot2_ref[:, cols]).astype(jnp.bfloat16)

    def diagonal(both):
        return jnp.concatenate([both[:SPAN, :HEAD], both[SPAN:, HEAD:]], axis=1)

    for cols, value_cols, lane in zip(pairs, value_pairs, lanes):
        out = diagonal(dot(prob_ref[:, lane].T, proj_ref[:, value_cols]))
        grad = diagonal(dot(dscore_ref[:, lane].T, proj_ref[:, cols]))
        out_ref[:, cols] = jnp.where(live, out, 0.0).astype(jnp.bfloat16)
        qg_ref[:, cols] = jnp.where(live, grad, 0.0).astype(jnp.bfloat16)

    @pl.when(span == 0)
    def _():
        kvt_copy.wait()
        acc_ref[...] = jnp.zeros_like(acc_ref)

    enc_grad = dot(grad_ref[...], kvt_ref[...]).astype(jnp.bfloat16)
    lat_grad = dot(enc_grad, upt_ref[...]).astype(jnp.bfloat16)
    scaled = dot(lat_grad, downt_ref[...]) * gain
    normed = x_full * inv_rms
    x_grad = enc_grad.astype(jnp.float32) + inv_rms * (
        scaled - normed * jnp.mean(scaled * normed, axis=-1, keepdims=True)
    )
    span_grad = jnp.sum(x_grad, axis=0, keepdims=True)
    cg_ref[pl.ds(span, 1), :] = jnp.where(live, span_grad, 0.0)
    acc_ref[:, :rank] += dot(hidden, lat_grad, TN)
    acc_ref[:, rank:] += dot(enc_grad, latent, TN)

    @pl.when(span == pl.num_programs(0) - 1)
    def _():
        ad_ref[...] = jnp.where(live, acc_ref[...], 0.0).astype(ad_ref.dtype)


def run_spans(meta, query, cot, cond, held, parts, gain, w_down, w_up, w_kv, nbr_count):
    span_count, width = cond.shape
    token_count, head_cols = query.shape
    slot_len = held[0].shape[1] * parts
    rank = w_down.shape[1]
    whole = lambda a: pl.BlockSpec(a.shape, lambda s, m: (0,) * a.ndim, pipeline_mode=pl.Buffered(1))
    tokens = pl.BlockSpec((SPAN, head_cols), lambda s, m: (s, 0))
    small = [cond, gain.reshape(1, width), w_down, w_up, w_up.T, w_down.T]
    large = list(held) + [w_kv, w_kv.T]
    per_device = span_count * nbr_count
    keys = nbr_count * slot_len
    rows = per_device * slot_len
    lanes = SPAN * HEADS
    flops = 2 * rows * (2 * width * 2 * head_cols + 6 * width * rank + 6 * SPAN * head_cols)
    return pl.pallas_call(
        functools.partial(span_kernel, len(held), nbr_count, parts),
        grid_spec=pltpu.PrefetchScalarGridSpec(
            num_scalar_prefetch=1,
            grid=(span_count,),
            in_specs=[tokens, tokens]
            + [whole(a) for a in small]
            + [pl.BlockSpec(memory_space=pltpu.HBM)] * len(large),
            out_specs=[
                tokens,
                tokens,
                pl.BlockSpec((span_count, width), lambda s, m: (0, 0)),
                pl.BlockSpec((width, 2 * rank), lambda s, m: (0, 0)),
            ],
            scratch_shapes=[
                pltpu.VMEM((per_device, slot_len, width), jnp.bfloat16),
                pltpu.VMEM((width, 2 * head_cols), jnp.bfloat16),
                pltpu.VMEM((2 * head_cols, width), jnp.bfloat16),
                pltpu.VMEM((keys, 2 * head_cols), jnp.bfloat16),
                pltpu.VMEM((keys, 2 * head_cols), jnp.bfloat16),
                pltpu.VMEM((keys, lanes), jnp.float32),
                pltpu.VMEM((keys, lanes), jnp.float32),
                pltpu.VMEM((keys, lanes), jnp.bfloat16),
                pltpu.VMEM((keys, lanes), jnp.bfloat16),
                pltpu.VMEM((2 * SPAN, head_cols), jnp.bfloat16),
                pltpu.VMEM((2 * SPAN, head_cols), jnp.bfloat16),
                pltpu.VMEM((width, 2 * rank), jnp.float32),
                pltpu.SemaphoreType.DMA((per_device * parts,)),
                pltpu.SemaphoreType.DMA((2,)),
            ],
        ),
        out_shape=[
            jax.ShapeDtypeStruct((token_count, head_cols), jnp.bfloat16),
            jax.ShapeDtypeStruct((token_count, head_cols), jnp.bfloat16),
            jax.ShapeDtypeStruct((span_count, width), jnp.float32),
            jax.ShapeDtypeStruct((width, 2 * rank), jnp.bfloat16),
        ],
        compiler_params=pltpu.CompilerParams(vmem_limit_bytes=60 * 2**20),
        cost_estimate=pl.CostEstimate(
            flops=flops, bytes_accessed=16 * 2**20, transcendentals=rows * SPAN * HEADS
        ),
    )(meta, query, cot, *small, *large)


def pick_kernel(held_count, meta, *refs):
    held_refs, out_ref, sems = refs[:held_count], refs[held_count], refs[held_count + 1]
    for b, held in enumerate(held_refs):
        @pl.when(meta[0] == b)
        def _():
            for n in range(out_ref.shape[0]):
                pltpu.make_async_copy(held.at[meta[1 + n]], out_ref.at[n], sems.at[n]).start()
    for n in range(out_ref.shape[0]):
        pltpu.make_async_copy(held_refs[0].at[0], out_ref.at[n], sems.at[n]).wait()


def pick(which, index, held):
    count = index.shape[0]
    meta = jnp.concatenate([jnp.reshape(which, (1,)), index]).astype(jnp.int32)
    return pl.pallas_call(
        functools.partial(pick_kernel, len(held)),
        grid_spec=pltpu.PrefetchScalarGridSpec(
            num_scalar_prefetch=1,
            grid=(1,),
            in_specs=[pl.BlockSpec(memory_space=pltpu.HBM)] * len(held),
            out_specs=pl.BlockSpec(memory_space=pltpu.VMEM),
            scratch_shapes=[pltpu.SemaphoreType.DMA((count,))],
        ),
        out_shape=jax.ShapeDtypeStruct((count,) + held[0].shape[1:], held[0].dtype),
        compiler_params=pltpu.CompilerParams(vmem_limit_bytes=60 * 2**20),
    )(meta, *held)


def place_requests(owners, per_device, pool_count, lanes):
    half = pool_count // 2
    count = owners.shape[1]
    order = jnp.arange(count, dtype=jnp.int32)
    side = (order // per_device) // half
    mate = side[:, None] == side[None, :]
    before = order[None, :] < order[:, None]
    same = owners[:, :, None] == owners[:, None, :]
    lower = owners[:, None, :] < owners[:, :, None]
    total = lambda mask: jnp.sum(mask.astype(jnp.int32), axis=2)
    rank = total(same & (mate & before)[None])
    crosses = rank >= lanes
    far = crosses[:, None, :]
    number = total(far & mate[None] & (lower | (same & before[None])))
    first = total(far & ~mate[None] & lower)
    guests = total(far & ~mate[None] & same)
    lane = jnp.where(crosses, number, first + guests + rank) % lanes
    row = jnp.where(crosses, 1 - side[None, :], side[None, :]) * half + lane % half
    return row, lane // half, crosses, number // half


def body(
    queries, cotangent, cond, nbr_owner, nbr_block, database, lengths, gain, w_down, w_up, w_kv
):
    axes = ("pool", "dp")
    pool_count = lax.axis_size("pool")
    columns = lax.axis_size("dp")
    relay_row = pool_count - 1
    half = pool_count // 2
    row = lax.axis_index("pool")
    me = lax.axis_index("dp")
    span_count, width = cond.shape[2:]
    nbr_count = nbr_owner.shape[3]
    per_device = span_count * nbr_count
    block_count, slot_len = database.shape[2:4]
    live_count = relay_row * per_device
    capacity = max(2, live_count // columns + 1)
    slots = -(-capacity // pool_count)
    lanes = half * slots
    most = 0
    if capacity > lanes:
        for rows in (half, relay_row - half):
            full, left = divmod(rows * per_device, capacity)
            most = max(most, full * (capacity - lanes) + max(0, left - lanes))
    crossing = -(-most // half)
    token_count, head_cols = queries.shape[2:]

    def hop(array, pairs):
        return lax.ppermute(
            array, axes, [(a * columns + j, b * columns + j) for a, b in pairs for j in range(columns)]
        )

    parts = PARTS if slot_len % (PARTS * 16) == 0 else 1
    piece = slot_len // parts
    full_store = database.reshape(block_count, slot_len, width)
    store = [full_store[:, i * piece : (i + 1) * piece] for i in range(parts)]

    across = [hop(a, [(relay_row, relay_row - half)]) for a in store]

    info = jnp.concatenate([nbr_owner.reshape(-1), nbr_block.reshape(-1), lengths.reshape(-1)])
    info = jnp.pad(info, (0, -info.shape[0] % 128))
    table = lax.all_gather(info.reshape(1, -1, 128), axes, axis=0, tiled=True)
    across, table = lax.optimization_barrier((across, table))
    table = table.reshape(pool_count, columns, -1)
    by_column = jnp.swapaxes(table[:relay_row], 0, 1)
    owners = by_column[:, :, :per_device].reshape(columns, live_count)
    blocks = by_column[:, :, per_device : 2 * per_device].reshape(columns, live_count)
    store_len = table[relay_row, :, 2 * per_device : 2 * per_device + block_count]
    carrier, slot, crosses, number = place_requests(owners, per_device, pool_count, lanes)

    ring = jnp.arange(slots, dtype=jnp.int32)
    mine = ((owners == me) & (carrier == row))[:, None, :] & (slot[:, None, :] == ring[None, :, None])
    slot_block = jnp.sum(jnp.where(mine, blocks[:, None, :], 0), axis=2).reshape(-1)

    mine_of = lambda a: lax.dynamic_index_in_dim(a, me, 0, keepdims=False)
    my_owner, my_block, my_carrier, my_slot, my_cross, my_number = map(
        mine_of, (owners, blocks, carrier, slot, crosses, number)
    )
    place = my_owner * slots + my_slot
    ring = jnp.arange(crossing, dtype=jnp.int32)
    mine = (my_cross & (my_carrier == row))[None, :] & (my_number[None, :] == ring[:, None])
    leaving_place = jnp.sum(jnp.where(mine, place[None, :], 0), axis=1)

    def share(array, step):
        return hop(array, [(p, p // half * half + (p + step) % half) for p in range(pool_count)])

    held = []
    for i in range(parts):
        stores = [store[i], across[i]]
        held_by = jnp.where(row == relay_row, 0, 1)
        for step in range(1, half):
            for near, array in ((relay_row, store[i]), (relay_row - half, across[i])):
                stores.append(hop(array, [(near, near - step)]))
                held_by = jnp.where(row == near - step, len(stores) - 1, held_by)
        sends = pick(held_by, slot_block, stores)
        arrived = lax.all_to_all(sends, "dp", split_axis=0, concat_axis=0, tiled=True)
        here = [arrived] + [share(arrived, step) for step in range(1, half)]
        if crossing:
            leaving = pick(0, leaving_place, [arrived])
            landed = hop(leaving, [(p, (p + half) % pool_count) for p in range(pool_count)])
            here += [landed] + [share(landed, step) for step in range(1, half)]
        held.append(here)
    origin = jnp.where(my_cross, (my_carrier + half) % pool_count, my_carrier)
    which = (row - origin) % half + jnp.where(my_cross, half, 0)
    index = jnp.where(my_cross, my_number, place)
    held = [here[b] for b in range(len(held[0])) for here in held]

    own_row = jnp.minimum(row, relay_row - 1)
    hot = (my_owner * block_count + my_block)[:, None] == jnp.arange(
        columns * block_count, dtype=jnp.int32
    )[None, :]
    wanted_len = jnp.sum(jnp.where(hot, store_len.reshape(1, -1), 0), axis=1)
    own = lambda a: lax.dynamic_index_in_dim(
        a.reshape(relay_row, per_device), own_row, 0, keepdims=False
    )
    live = (row < relay_row).astype(jnp.int32)
    meta = jnp.concatenate([live[None], own(wanted_len), own(which), own(index)]).astype(jnp.int32)

    attn_out, q_grad, cond_grad, terms = run_spans(
        meta,
        queries.reshape(token_count, head_cols),
        cotangent.reshape(token_count, head_cols),
        cond.reshape(span_count, width).astype(jnp.float32),
        held,
        parts,
        gain,
        w_down,
        w_up,
        w_kv,
        nbr_count,
    )

    def scatter_sum(array, axis):
        parts = lax.all_to_all(array, axis, split_axis=0, concat_axis=0, tiled=True)
        return jnp.sum(
            parts.reshape(lax.axis_size(axis), -1, array.shape[1]).astype(jnp.float32), axis=0
        )

    adapter_grad = scatter_sum(scatter_sum(terms, "pool").astype(jnp.bfloat16), "dp")
    return (
        attn_out.reshape(1, 1, token_count, head_cols),
        q_grad.reshape(1, 1, token_count, head_cols),
        cond_grad.reshape(1, 1, span_count, width),
        adapter_grad,
    )


def solution(mesh):
    return jax.shard_map(
        body,
        mesh=mesh,
        in_specs=(
            P("pool", "dp", None, None),
            P("pool", "dp", None, None),
            P("pool", "dp", None, None),
            P("pool", "dp", None, None),
            P("pool", "dp", None, None),
            P("pool", "dp", None, None, None),
            P("pool", "dp", None),
            P(),
            P(),
            P(),
            P(),
        ),
        out_specs=(
            P("pool", "dp", None, None),
            P("pool", "dp", None, None),
            P("pool", "dp", None, None),
            P(("pool", "dp"), None),
        ),
        check_vma=False,
    )
```

```python
import functools

import jax
import jax.numpy as jnp
from jax import lax
from jax.experimental import pallas as pl
from jax.experimental.pallas import tpu as pltpu
from jax.sharding import PartitionSpec as P

HEADS = 16
HEAD = 128
SPAN = 64
PARTS = 2

EPSILON = 1e-06
FLOOR = -1e30
LOG2E = 1.4426950408889634

NT = (((1,), (1,)), ((), ()))
TN = (((0,), (0,)), ((), ()))


def dot(a, b, dims=(((1,), (0,)), ((), ()))):
    return lax.dot_general(a, b, dims, preferred_element_type=jnp.float32)


def span_kernel(
    held_count, nbr_count, parts, meta,
    q_ref, cot_ref, cond_ref, gain_ref, down_ref, up_ref, upt_ref, downt_ref, *rest,
):
    held_refs = rest[:held_count]
    (kv_hbm, kvt_hbm, out_ref, qg_ref, cg_ref, ad_ref,
     raw_ref, kv_ref, kvt_ref, proj_ref, grad_ref, score_ref, dprob_ref, prob_ref, dscore_ref,
     q2_ref, cot2_ref, acc_ref, sems, kv_sem) = rest[held_count:]
    span = pl.program_id(0)
    per_device, slot_len, width = raw_ref.shape
    key_count = nbr_count * slot_len
    head_cols = q_ref.shape[1]
    rank = down_ref.shape[1]
    scaling = HEAD ** (-0.5)
    live = meta[0] == 1
    lens, which, index = 1, 1 + per_device, 1 + 2 * per_device
    piece = slot_len // parts
    pairs = [pl.ds(i * 2 * HEAD, 2 * HEAD) for i in range(HEADS // 2)]
    value_pairs = [pl.ds(head_cols + i * 2 * HEAD, 2 * HEAD) for i in range(HEADS // 2)]
    lanes = [pl.ds(i * 2 * SPAN, 2 * SPAN) for i in range(HEADS // 2)]
    kv_copy = pltpu.make_async_copy(kv_hbm, kv_ref, kv_sem.at[0])
    kvt_copy = pltpu.make_async_copy(kvt_hbm, kvt_ref, kv_sem.at[1])

    @pl.when(span == 0)
    def _():
        for n in range(per_device):
            for b, held in enumerate(held_refs):
                @pl.when(meta[which + n] == b // parts)
                def _():
                    part = b % parts
                    pltpu.make_async_copy(
                        held.at[meta[index + n]],
                        raw_ref.at[n, pl.ds(part * piece, piece)],
                        sems.at[n * parts + part],
                    ).start()
        kv_copy.start()
        kvt_copy.start()

    q2_ref[...] = jnp.zeros_like(q2_ref)
    cot2_ref[...] = jnp.zeros_like(cot2_ref)
    for i in range(HEADS):
        cols = pl.ds(i * HEAD, HEAD)
        tokens = pl.ds(i % 2 * SPAN, SPAN)
        q2_ref[tokens, cols] = q_ref[:, cols]
        cot2_ref[tokens, cols] = cot_ref[:, cols]

    for n in range(nbr_count):
        for part in range(parts):
            item = span * nbr_count + n
            pltpu.make_async_copy(
                held_refs[0].at[0],
                raw_ref.at[item, pl.ds(part * piece, piece)],
                sems.at[item * parts + part],
            ).wait()
    raw = raw_ref[pl.ds(span * nbr_count, nbr_count)]
    x_full = raw.reshape(key_count, width).astype(jnp.float32) + cond_ref[pl.ds(span, 1), :]
    inv_rms = lax.rsqrt(jnp.mean(x_full * x_full, axis=-1, keepdims=True) + EPSILON)
    gain = gain_ref[...]
    hidden = (x_full * inv_rms * gain).astype(jnp.bfloat16)
    latent = dot(hidden, down_ref[...]).astype(jnp.bfloat16)
    encoded = (x_full + dot(latent, up_ref[...])).astype(jnp.bfloat16)

    @pl.when(span == 0)
    def _():
        kv_copy.wait()

    for cols in pairs + value_pairs:
        proj_ref[:, cols] = dot(encoded, kv_ref[:, cols]).astype(jnp.bfloat16)

    for cols, value_cols, lane in zip(pairs, value_pairs, lanes):
        score_ref[:, lane] = dot(proj_ref[:, cols], q2_ref[:, cols], NT)
        dprob_ref[:, lane] = dot(proj_ref[:, value_cols], cot2_ref[:, cols], NT)

    slot = lax.broadcasted_iota(jnp.int32, (key_count, 2 * SPAN), 0)
    limit = jnp.zeros((key_count, 2 * SPAN), jnp.int32)
    for n in range(nbr_count):
        here = jnp.logical_and(slot >= n * slot_len, slot < (n + 1) * slot_len)
        limit = jnp.where(here, n * slot_len + meta[lens + span * nbr_count + n], limit)
    usable = slot < limit
    for lane in lanes:
        scores = jnp.where(usable, score_ref[:, lane], FLOOR)
        row_max = jnp.max(scores, axis=0, keepdims=True)
        raised = jnp.exp2((scores - row_max) * (scaling * LOG2E))
        probs = raised * (1.0 / jnp.sum(raised, axis=0, keepdims=True))
        d_probs = dprob_ref[:, lane]
        delta = jnp.sum(probs * d_probs, axis=0, keepdims=True)
        prob_ref[:, lane] = probs.astype(jnp.bfloat16)
        dscore_ref[:, lane] = (probs * (d_probs - delta) * scaling).astype(jnp.bfloat16)

    for cols, value_cols, lane in zip(pairs, value_pairs, lanes):
        grad_ref[:, cols] = dot(dscore_ref[:, lane], q2_ref[:, cols]).astype(jnp.bfloat16)
        grad_ref[:, value_cols] = dot(prob_ref[:, lane], cot2_ref[:, cols]).astype(jnp.bfloat16)

    def diagonal(both):
        return jnp.concatenate([both[:SPAN, :HEAD], both[SPAN:, HEAD:]], axis=1)

    for cols, value_cols, lane in zip(pairs, value_pairs, lanes):
        out = diagonal(dot(prob_ref[:, lane].T, proj_ref[:, value_cols]))
        grad = diagonal(dot(dscore_ref[:, lane].T, proj_ref[:, cols]))
        out_ref[:, cols] = jnp.where(live, out, 0.0).astype(jnp.bfloat16)
        qg_ref[:, cols] = jnp.where(live, grad, 0.0).astype(jnp.bfloat16)

    @pl.when(span == 0)
    def _():
        kvt_copy.wait()
        acc_ref[...] = jnp.zeros_like(acc_ref)

    enc_grad = dot(grad_ref[...], kvt_ref[...]).astype(jnp.bfloat16)
    lat_grad = dot(enc_grad, upt_ref[...]).astype(jnp.bfloat16)
    scaled = dot(lat_grad, downt_ref[...]) * gain
    normed = x_full * inv_rms
    x_grad = enc_grad.astype(jnp.float32) + inv_rms * (
        scaled - normed * jnp.mean(scaled * normed, axis=-1, keepdims=True)
    )
    span_grad = jnp.sum(x_grad, axis=0, keepdims=True)
    cg_ref[pl.ds(span, 1), :] = jnp.where(live, span_grad, 0.0)
    acc_ref[:, :rank] += dot(hidden, lat_grad, TN)
    acc_ref[:, rank:] += dot(enc_grad, latent, TN)

    @pl.when(span == pl.num_programs(0) - 1)
    def _():
        ad_ref[...] = jnp.where(live, acc_ref[...], 0.0).astype(ad_ref.dtype)


def run_spans(meta, query, cot, cond, held, parts, gain, w_down, w_up, w_kv, nbr_count):
    span_count, width = cond.shape
    token_count, head_cols = query.shape
    slot_len = held[0].shape[1] * parts
    rank = w_down.shape[1]
    whole = lambda a: pl.BlockSpec(a.shape, lambda s, m: (0,) * a.ndim, pipeline_mode=pl.Buffered(1))
    tokens = pl.BlockSpec((SPAN, head_cols), lambda s, m: (s, 0))
    small = [cond, gain.reshape(1, width), w_down, w_up, w_up.T, w_down.T]
    large = list(held) + [w_kv, w_kv.T]
    per_device = span_count * nbr_count
    keys = nbr_count * slot_len
    rows = per_device * slot_len
    lanes = SPAN * HEADS
    flops = 2 * rows * (2 * width * 2 * head_cols + 6 * width * rank + 6 * SPAN * head_cols)
    return pl.pallas_call(
        functools.partial(span_kernel, len(held), nbr_count, parts),
        grid_spec=pltpu.PrefetchScalarGridSpec(
            num_scalar_prefetch=1,
            grid=(span_count,),
            in_specs=[tokens, tokens]
            + [whole(a) for a in small]
            + [pl.BlockSpec(memory_space=pltpu.HBM)] * len(large),
            out_specs=[
                tokens,
                tokens,
                pl.BlockSpec((span_count, width), lambda s, m: (0, 0)),
                pl.BlockSpec((width, 2 * rank), lambda s, m: (0, 0)),
            ],
            scratch_shapes=[
                pltpu.VMEM((per_device, slot_len, width), jnp.bfloat16),
                pltpu.VMEM((width, 2 * head_cols), jnp.bfloat16),
                pltpu.VMEM((2 * head_cols, width), jnp.bfloat16),
                pltpu.VMEM((keys, 2 * head_cols), jnp.bfloat16),
                pltpu.VMEM((keys, 2 * head_cols), jnp.bfloat16),
                pltpu.VMEM((keys, lanes), jnp.float32),
                pltpu.VMEM((keys, lanes), jnp.float32),
                pltpu.VMEM((keys, lanes), jnp.bfloat16),
                pltpu.VMEM((keys, lanes), jnp.bfloat16),
                pltpu.VMEM((2 * SPAN, head_cols), jnp.bfloat16),
                pltpu.VMEM((2 * SPAN, head_cols), jnp.bfloat16),
                pltpu.VMEM((width, 2 * rank), jnp.float32),
                pltpu.SemaphoreType.DMA((per_device * parts,)),
                pltpu.SemaphoreType.DMA((2,)),
            ],
        ),
        out_shape=[
            jax.ShapeDtypeStruct((token_count, head_cols), jnp.bfloat16),
            jax.ShapeDtypeStruct((token_count, head_cols), jnp.bfloat16),
            jax.ShapeDtypeStruct((span_count, width), jnp.float32),
            jax.ShapeDtypeStruct((width, 2 * rank), jnp.float32),
        ],
        compiler_params=pltpu.CompilerParams(vmem_limit_bytes=60 * 2**20),
        cost_estimate=pl.CostEstimate(
            flops=flops, bytes_accessed=16 * 2**20, transcendentals=rows * SPAN * HEADS
        ),
    )(meta, query, cot, *small, *large)


def pick_kernel(held_count, meta, *refs):
    held_refs, out_ref, sems = refs[:held_count], refs[held_count], refs[held_count + 1]
    for b, held in enumerate(held_refs):
        @pl.when(meta[0] == b)
        def _():
            for n in range(out_ref.shape[0]):
                pltpu.make_async_copy(held.at[meta[1 + n]], out_ref.at[n], sems.at[n]).start()
    for n in range(out_ref.shape[0]):
        pltpu.make_async_copy(held_refs[0].at[0], out_ref.at[n], sems.at[n]).wait()


def pick(which, index, held):
    count = index.shape[0]
    meta = jnp.concatenate([jnp.reshape(which, (1,)), index]).astype(jnp.int32)
    return pl.pallas_call(
        functools.partial(pick_kernel, len(held)),
        grid_spec=pltpu.PrefetchScalarGridSpec(
            num_scalar_prefetch=1,
            grid=(1,),
            in_specs=[pl.BlockSpec(memory_space=pltpu.HBM)] * len(held),
            out_specs=pl.BlockSpec(memory_space=pltpu.VMEM),
            scratch_shapes=[pltpu.SemaphoreType.DMA((count,))],
        ),
        out_shape=jax.ShapeDtypeStruct((count,) + held[0].shape[1:], held[0].dtype),
        compiler_params=pltpu.CompilerParams(vmem_limit_bytes=60 * 2**20),
    )(meta, *held)


def place_requests(owners, per_device, pool_count, lanes):
    half = pool_count // 2
    count = owners.shape[1]
    order = jnp.arange(count, dtype=jnp.int32)
    side = (order // per_device) // half
    mate = side[:, None] == side[None, :]
    before = order[None, :] < order[:, None]
    same = owners[:, :, None] == owners[:, None, :]
    lower = owners[:, None, :] < owners[:, :, None]
    total = lambda mask: jnp.sum(mask.astype(jnp.int32), axis=2)
    rank = total(same & (mate & before)[None])
    crosses = rank >= lanes
    far = crosses[:, None, :]
    number = total(far & mate[None] & (lower | (same & before[None])))
    first = total(far & ~mate[None] & lower)
    guests = total(far & ~mate[None] & same)
    lane = jnp.where(crosses, number, first + guests + rank) % lanes
    row = jnp.where(crosses, 1 - side[None, :], side[None, :]) * half + lane % half
    return row, lane // half, crosses, number // half


def scatter_sum(total, axes):
    width = total.shape[1]
    sizes = [lax.axis_size(axis) for axis in axes]
    total = total.reshape(tuple(sizes) + (-1, width)).astype(jnp.float32)
    for at, axis in enumerate(axes):
        size, index = sizes[at], lax.axis_index(axis)
        if size & (size - 1):
            lead = (size,) + tuple(d for i, d in enumerate(total.shape) if i != at)
            parts = jnp.moveaxis(total, at, 0).astype(jnp.bfloat16)
            parts = lax.all_to_all(parts, axis, split_axis=0, concat_axis=0, tiled=True)
            total = jnp.sum(parts.reshape(lead).astype(jnp.float32), axis=0)
            total = jnp.expand_dims(total, at)
            continue
        bit = 1
        while bit < size:
            shape = total.shape
            split = total.reshape(shape[:at] + (shape[at] // 2, 2) + shape[at + 1 :])
            mine = (index // bit) % 2
            keep = lax.dynamic_index_in_dim(split, mine, at + 1, keepdims=False)
            give = lax.dynamic_index_in_dim(split, 1 - mine, at + 1, keepdims=False)
            got = lax.ppermute(
                give.astype(jnp.bfloat16), axis, [(i, i ^ bit) for i in range(size)]
            )
            total = keep + got.astype(jnp.float32)
            bit *= 2
    return total.reshape(-1, width)


def body(
    queries, cotangent, cond, nbr_owner, nbr_block, database, lengths, gain, w_down, w_up, w_kv
):
    axes = ("pool", "dp")
    pool_count = lax.axis_size("pool")
    columns = lax.axis_size("dp")
    relay_row = pool_count - 1
    half = pool_count // 2
    row = lax.axis_index("pool")
    me = lax.axis_index("dp")
    span_count, width = cond.shape[2:]
    nbr_count = nbr_owner.shape[3]
    per_device = span_count * nbr_count
    block_count, slot_len = database.shape[2:4]
    live_count = relay_row * per_device
    capacity = max(2, live_count // columns + 1)
    slots = -(-capacity // pool_count)
    lanes = half * slots
    most = 0
    if capacity > lanes:
        for rows in (half, relay_row - half):
            full, left = divmod(rows * per_device, capacity)
            most = max(most, full * (capacity - lanes) + max(0, left - lanes))
    crossing = -(-most // half)
    token_count, head_cols = queries.shape[2:]

    def hop(array, pairs):
        return lax.ppermute(
            array, axes, [(a * columns + j, b * columns + j) for a, b in pairs for j in range(columns)]
        )

    parts = PARTS if slot_len % (PARTS * 16) == 0 else 1
    piece = slot_len // parts
    full_store = database.reshape(block_count, slot_len, width)
    store = [full_store[:, i * piece : (i + 1) * piece] for i in range(parts)]

    def to_all(array, axis):
        copies = jnp.broadcast_to(array[None], (lax.axis_size(axis),) + array.shape)
        return lax.all_to_all(copies, axis, split_axis=0, concat_axis=0, tiled=True)

    across = [hop(a, [(relay_row, relay_row - half)]) for a in store]

    info = jnp.concatenate([nbr_owner.reshape(-1), nbr_block.reshape(-1), lengths.reshape(-1)])
    info = jnp.pad(info, (0, -info.shape[0] % 128))
    table = to_all(to_all(info.reshape(-1, 128), "dp"), "pool")
    across, table = lax.optimization_barrier((across, table))
    table = table.reshape(pool_count, columns, -1)
    by_column = jnp.swapaxes(table[:relay_row], 0, 1)
    owners = by_column[:, :, :per_device].reshape(columns, live_count)
    blocks = by_column[:, :, per_device : 2 * per_device].reshape(columns, live_count)
    store_len = table[relay_row, :, 2 * per_device : 2 * per_device + block_count]
    carrier, slot, crosses, number = place_requests(owners, per_device, pool_count, lanes)

    ring = jnp.arange(slots, dtype=jnp.int32)
    mine = ((owners == me) & (carrier == row))[:, None, :] & (slot[:, None, :] == ring[None, :, None])
    slot_block = jnp.sum(jnp.where(mine, blocks[:, None, :], 0), axis=2).reshape(-1)

    mine_of = lambda a: lax.dynamic_index_in_dim(a, me, 0, keepdims=False)
    my_owner, my_block, my_carrier, my_slot, my_cross, my_number = map(
        mine_of, (owners, blocks, carrier, slot, crosses, number)
    )
    place = my_owner * slots + my_slot
    ring = jnp.arange(crossing, dtype=jnp.int32)
    mine = (my_cross & (my_carrier == row))[None, :] & (my_number[None, :] == ring[:, None])
    leaving_place = jnp.sum(jnp.where(mine, place[None, :], 0), axis=1)

    def share(array, step):
        return hop(array, [(p, p // half * half + (p + step) % half) for p in range(pool_count)])

    held = []
    for i in range(parts):
        stores = [store[i], across[i]]
        held_by = jnp.where(row == relay_row, 0, 1)
        for step in range(1, half):
            for near, array in ((relay_row, store[i]), (relay_row - half, across[i])):
                stores.append(hop(array, [(near, near - step)]))
                held_by = jnp.where(row == near - step, len(stores) - 1, held_by)
        sends = pick(held_by, slot_block, stores)
        arrived = lax.all_to_all(sends, "dp", split_axis=0, concat_axis=0, tiled=True)
        here = [arrived] + [share(arrived, step) for step in range(1, half)]
        if crossing:
            leaving = pick(0, leaving_place, [arrived])
            landed = hop(leaving, [(p, (p + half) % pool_count) for p in range(pool_count)])
            here += [landed] + [share(landed, step) for step in range(1, half)]
        held.append(here)
    origin = jnp.where(my_cross, (my_carrier + half) % pool_count, my_carrier)
    which = (row - origin) % half + jnp.where(my_cross, half, 0)
    index = jnp.where(my_cross, my_number, place)
    held = [here[b] for b in range(len(held[0])) for here in held]

    own_row = jnp.minimum(row, relay_row - 1)
    hot = (my_owner * block_count + my_block)[:, None] == jnp.arange(
        columns * block_count, dtype=jnp.int32
    )[None, :]
    wanted_len = jnp.sum(jnp.where(hot, store_len.reshape(1, -1), 0), axis=1)
    own = lambda a: lax.dynamic_index_in_dim(
        a.reshape(relay_row, per_device), own_row, 0, keepdims=False
    )
    live = (row < relay_row).astype(jnp.int32)
    meta = jnp.concatenate([live[None], own(wanted_len), own(which), own(index)]).astype(jnp.int32)

    attn_out, q_grad, cond_grad, terms = run_spans(
        meta,
        queries.reshape(token_count, head_cols),
        cotangent.reshape(token_count, head_cols),
        cond.reshape(span_count, width).astype(jnp.float32),
        held,
        parts,
        gain,
        w_down,
        w_up,
        w_kv,
        nbr_count,
    )

    adapter_grad = scatter_sum(terms, axes)
    return (
        attn_out.reshape(1, 1, token_count, head_cols),
        q_grad.reshape(1, 1, token_count, head_cols),
        cond_grad.reshape(1, 1, span_count, width),
        adapter_grad,
    )


def solution(mesh):
    return jax.shard_map(
        body,
        mesh=mesh,
        in_specs=(
            P("pool", "dp", None, None),
            P("pool", "dp", None, None),
            P("pool", "dp", None, None),
            P("pool", "dp", None, None),
            P("pool", "dp", None, None),
            P("pool", "dp", None, None, None),
            P("pool", "dp", None),
            P(),
            P(),
            P(),
            P(),
        ),
        out_specs=(
            P("pool", "dp", None, None),
            P("pool", "dp", None, None),
            P("pool", "dp", None, None),
            P(("pool", "dp"), None),
        ),
        check_vma=False,
    )
```

```python
import functools

import jax
import jax.numpy as jnp
from jax import lax
from jax.experimental import pallas as pl
from jax.experimental.pallas import tpu as pltpu
from jax.sharding import PartitionSpec as P

HEADS = 16
HEAD = 128
SPAN = 64
PARTS = 2

EPSILON = 1e-06
FLOOR = -1e30
LOG2E = 1.4426950408889634

NT = (((1,), (1,)), ((), ()))
TN = (((0,), (0,)), ((), ()))


def dot(a, b, dims=(((1,), (0,)), ((), ()))):
    return lax.dot_general(a, b, dims, preferred_element_type=jnp.float32)


def span_kernel(
    held_count, nbr_count, parts, meta,
    q_ref, cot_ref, cond_ref, gain_ref, down_ref, up_ref, upt_ref, downt_ref, *rest,
):
    held_refs = rest[:held_count]
    (kv_hbm, kvt_hbm, out_ref, qg_ref, cg_ref, ad_ref,
     raw_ref, kv_ref, kvt_ref, proj_ref, grad_ref, score_ref, dprob_ref, prob_ref, dscore_ref,
     q2_ref, cot2_ref, acc_ref, sems, kv_sem) = rest[held_count:]
    span = pl.program_id(0)
    per_device, slot_len, width = raw_ref.shape
    key_count = nbr_count * slot_len
    head_cols = q_ref.shape[1]
    rank = down_ref.shape[1]
    scaling = HEAD ** (-0.5)
    live = meta[0] == 1
    lens, which, index = 1, 1 + per_device, 1 + 2 * per_device
    piece = slot_len // parts
    pairs = [pl.ds(i * 2 * HEAD, 2 * HEAD) for i in range(HEADS // 2)]
    value_pairs = [pl.ds(head_cols + i * 2 * HEAD, 2 * HEAD) for i in range(HEADS // 2)]
    lanes = [pl.ds(i * 2 * SPAN, 2 * SPAN) for i in range(HEADS // 2)]
    kv_copy = pltpu.make_async_copy(kv_hbm, kv_ref, kv_sem.at[0])
    kvt_copy = pltpu.make_async_copy(kvt_hbm, kvt_ref, kv_sem.at[1])

    @pl.when(span == 0)
    def _():
        for n in range(per_device):
            for b, held in enumerate(held_refs):
                @pl.when(meta[which + n] == b // parts)
                def _():
                    part = b % parts
                    pltpu.make_async_copy(
                        held.at[meta[index + n]],
                        raw_ref.at[n, pl.ds(part * piece, piece)],
                        sems.at[n * parts + part],
                    ).start()
        kv_copy.start()
        kvt_copy.start()

    q2_ref[...] = jnp.zeros_like(q2_ref)
    cot2_ref[...] = jnp.zeros_like(cot2_ref)
    for i in range(HEADS):
        cols = pl.ds(i * HEAD, HEAD)
        tokens = pl.ds(i % 2 * SPAN, SPAN)
        q2_ref[tokens, cols] = q_ref[:, cols]
        cot2_ref[tokens, cols] = cot_ref[:, cols]

    for n in range(nbr_count):
        for part in range(parts):
            item = span * nbr_count + n
            pltpu.make_async_copy(
                held_refs[0].at[0],
                raw_ref.at[item, pl.ds(part * piece, piece)],
                sems.at[item * parts + part],
            ).wait()
    raw = raw_ref[pl.ds(span * nbr_count, nbr_count)]
    x_full = raw.reshape(key_count, width).astype(jnp.float32) + cond_ref[pl.ds(span, 1), :]
    inv_rms = lax.rsqrt(jnp.mean(x_full * x_full, axis=-1, keepdims=True) + EPSILON)
    gain = gain_ref[...]
    hidden = (x_full * inv_rms * gain).astype(jnp.bfloat16)
    latent = dot(hidden, down_ref[...]).astype(jnp.bfloat16)
    encoded = (x_full + dot(latent, up_ref[...])).astype(jnp.bfloat16)

    @pl.when(span == 0)
    def _():
        kv_copy.wait()

    for cols in pairs + value_pairs:
        proj_ref[:, cols] = dot(encoded, kv_ref[:, cols]).astype(jnp.bfloat16)

    for cols, value_cols, lane in zip(pairs, value_pairs, lanes):
        score_ref[:, lane] = dot(proj_ref[:, cols], q2_ref[:, cols], NT)
        dprob_ref[:, lane] = dot(proj_ref[:, value_cols], cot2_ref[:, cols], NT)

    slot = lax.broadcasted_iota(jnp.int32, (key_count, 2 * SPAN), 0)
    limit = jnp.zeros((key_count, 2 * SPAN), jnp.int32)
    for n in range(nbr_count):
        here = jnp.logical_and(slot >= n * slot_len, slot < (n + 1) * slot_len)
        limit = jnp.where(here, n * slot_len + meta[lens + span * nbr_count + n], limit)
    usable = slot < limit
    for lane in lanes:
        scores = jnp.where(usable, score_ref[:, lane], FLOOR)
        row_max = jnp.max(scores, axis=0, keepdims=True)
        raised = jnp.exp2((scores - row_max) * (scaling * LOG2E))
        probs = raised * (1.0 / jnp.sum(raised, axis=0, keepdims=True))
        d_probs = dprob_ref[:, lane]
        delta = jnp.sum(probs * d_probs, axis=0, keepdims=True)
        prob_ref[:, lane] = probs.astype(jnp.bfloat16)
        dscore_ref[:, lane] = (probs * (d_probs - delta) * scaling).astype(jnp.bfloat16)

    for cols, value_cols, lane in zip(pairs, value_pairs, lanes):
        grad_ref[:, cols] = dot(dscore_ref[:, lane], q2_ref[:, cols]).astype(jnp.bfloat16)
        grad_ref[:, value_cols] = dot(prob_ref[:, lane], cot2_ref[:, cols]).astype(jnp.bfloat16)

    def diagonal(both):
        return jnp.concatenate([both[:SPAN, :HEAD], both[SPAN:, HEAD:]], axis=1)

    for cols, value_cols, lane in zip(pairs, value_pairs, lanes):
        out = diagonal(dot(prob_ref[:, lane].T, proj_ref[:, value_cols]))
        grad = diagonal(dot(dscore_ref[:, lane].T, proj_ref[:, cols]))
        out_ref[:, cols] = jnp.where(live, out, 0.0).astype(jnp.bfloat16)
        qg_ref[:, cols] = jnp.where(live, grad, 0.0).astype(jnp.bfloat16)

    @pl.when(span == 0)
    def _():
        kvt_copy.wait()
        acc_ref[...] = jnp.zeros_like(acc_ref)

    enc_grad = dot(grad_ref[...], kvt_ref[...]).astype(jnp.bfloat16)
    lat_grad = dot(enc_grad, upt_ref[...]).astype(jnp.bfloat16)
    scaled = dot(lat_grad, downt_ref[...]) * gain
    normed = x_full * inv_rms
    x_grad = enc_grad.astype(jnp.float32) + inv_rms * (
        scaled - normed * jnp.mean(scaled * normed, axis=-1, keepdims=True)
    )
    span_grad = jnp.sum(x_grad, axis=0, keepdims=True)
    cg_ref[pl.ds(span, 1), :] = jnp.where(live, span_grad, 0.0)
    acc_ref[:, :rank] += dot(hidden, lat_grad, TN)
    acc_ref[:, rank:] += dot(enc_grad, latent, TN)

    @pl.when(span == pl.num_programs(0) - 1)
    def _():
        ad_ref[...] = jnp.where(live, acc_ref[...], 0.0).astype(ad_ref.dtype)


def run_spans(meta, query, cot, cond, held, parts, gain, w_down, w_up, w_kv, w_kv_t, nbr_count):
    span_count, width = cond.shape
    token_count, head_cols = query.shape
    slot_len = held[0].shape[1] * parts
    rank = w_down.shape[1]
    whole = lambda a: pl.BlockSpec(a.shape, lambda s, m: (0,) * a.ndim, pipeline_mode=pl.Buffered(1))
    tokens = pl.BlockSpec((SPAN, head_cols), lambda s, m: (s, 0))
    small = [cond, gain.reshape(1, width), w_down, w_up, w_up.T, w_down.T]
    large = list(held) + [w_kv, w_kv_t]
    per_device = span_count * nbr_count
    keys = nbr_count * slot_len
    rows = per_device * slot_len
    lanes = SPAN * HEADS
    flops = 2 * rows * (2 * width * 2 * head_cols + 6 * width * rank + 6 * SPAN * head_cols)
    return pl.pallas_call(
        functools.partial(span_kernel, len(held), nbr_count, parts),
        grid_spec=pltpu.PrefetchScalarGridSpec(
            num_scalar_prefetch=1,
            grid=(span_count,),
            in_specs=[tokens, tokens]
            + [whole(a) for a in small]
            + [pl.BlockSpec(memory_space=pltpu.HBM)] * len(large),
            out_specs=[
                tokens,
                tokens,
                pl.BlockSpec((span_count, width), lambda s, m: (0, 0)),
                pl.BlockSpec((width, 2 * rank), lambda s, m: (0, 0)),
            ],
            scratch_shapes=[
                pltpu.VMEM((per_device, slot_len, width), jnp.bfloat16),
                pltpu.VMEM((width, 2 * head_cols), jnp.bfloat16),
                pltpu.VMEM((2 * head_cols, width), jnp.bfloat16),
                pltpu.VMEM((keys, 2 * head_cols), jnp.bfloat16),
                pltpu.VMEM((keys, 2 * head_cols), jnp.bfloat16),
                pltpu.VMEM((keys, lanes), jnp.float32),
                pltpu.VMEM((keys, lanes), jnp.float32),
                pltpu.VMEM((keys, lanes), jnp.bfloat16),
                pltpu.VMEM((keys, lanes), jnp.bfloat16),
                pltpu.VMEM((2 * SPAN, head_cols), jnp.bfloat16),
                pltpu.VMEM((2 * SPAN, head_cols), jnp.bfloat16),
                pltpu.VMEM((width, 2 * rank), jnp.float32),
                pltpu.SemaphoreType.DMA((per_device * parts,)),
                pltpu.SemaphoreType.DMA((2,)),
            ],
        ),
        out_shape=[
            jax.ShapeDtypeStruct((token_count, head_cols), jnp.bfloat16),
            jax.ShapeDtypeStruct((token_count, head_cols), jnp.bfloat16),
            jax.ShapeDtypeStruct((span_count, width), jnp.float32),
            jax.ShapeDtypeStruct((width, 2 * rank), jnp.float32),
        ],
        compiler_params=pltpu.CompilerParams(vmem_limit_bytes=60 * 2**20),
        cost_estimate=pl.CostEstimate(
            flops=flops, bytes_accessed=16 * 2**20, transcendentals=rows * SPAN * HEADS
        ),
    )(meta, query, cot, *small, *large)


def pick_kernel(held_count, meta, *refs):
    held_refs, out_ref = refs[:held_count], refs[held_count]
    for b, held in enumerate(held_refs):
        @pl.when(meta[0] == b)
        def _():
            for n in range(out_ref.shape[0]):
                out_ref[n] = held[meta[1 + n]]


def pick(which, index, held):
    count = index.shape[0]
    meta = jnp.concatenate([jnp.reshape(which, (1,)), index]).astype(jnp.int32)
    return pl.pallas_call(
        functools.partial(pick_kernel, len(held)),
        grid_spec=pltpu.PrefetchScalarGridSpec(
            num_scalar_prefetch=1,
            grid=(1,),
            in_specs=[pl.BlockSpec(memory_space=pltpu.VMEM)] * len(held),
            out_specs=pl.BlockSpec(memory_space=pltpu.VMEM),
        ),
        out_shape=jax.ShapeDtypeStruct((count,) + held[0].shape[1:], held[0].dtype),
        compiler_params=pltpu.CompilerParams(vmem_limit_bytes=16 * 2**20),
    )(meta, *held)


def place_requests(owners, per_device, pool_count, lanes):
    half = pool_count // 2
    count = owners.shape[1]
    order = jnp.arange(count, dtype=jnp.int32)
    side = (order // per_device) // half
    mate = side[:, None] == side[None, :]
    before = order[None, :] < order[:, None]
    same = owners[:, :, None] == owners[:, None, :]
    lower = owners[:, None, :] < owners[:, :, None]
    total = lambda mask: jnp.sum(mask.astype(jnp.int32), axis=2)
    rank = total(same & (mate & before)[None])
    crosses = rank >= lanes
    far = crosses[:, None, :]
    number = total(far & mate[None] & (lower | (same & before[None])))
    first = total(far & ~mate[None] & lower)
    guests = total(far & ~mate[None] & same)
    lane = jnp.where(crosses, number, first + guests + rank) % lanes
    row = jnp.where(crosses, 1 - side[None, :], side[None, :]) * half + lane % half
    return row, lane // half, crosses, number // half


def scatter_sum(total, axes):
    width = total.shape[1]
    sizes = [lax.axis_size(axis) for axis in axes]
    total = total.reshape(tuple(sizes) + (-1, width)).astype(jnp.float32)
    for at, axis in enumerate(axes):
        size, index = sizes[at], lax.axis_index(axis)
        if size & (size - 1):
            lead = (size,) + tuple(d for i, d in enumerate(total.shape) if i != at)
            parts = jnp.moveaxis(total, at, 0).astype(jnp.bfloat16)
            parts = lax.all_to_all(parts, axis, split_axis=0, concat_axis=0, tiled=True)
            total = jnp.sum(parts.reshape(lead).astype(jnp.float32), axis=0)
            total = jnp.expand_dims(total, at)
            continue
        bit = 1
        while bit < size:
            shape = total.shape
            split = total.reshape(shape[:at] + (shape[at] // 2, 2) + shape[at + 1 :])
            mine = (index // bit) % 2
            keep = lax.dynamic_index_in_dim(split, mine, at + 1, keepdims=False)
            give = lax.dynamic_index_in_dim(split, 1 - mine, at + 1, keepdims=False)
            got = lax.ppermute(
                give.astype(jnp.bfloat16), axis, [(i, i ^ bit) for i in range(size)]
            )
            total = keep + got.astype(jnp.float32)
            bit *= 2
    return total.reshape(-1, width)


def body(
    queries, cotangent, cond, nbr_owner, nbr_block, database, lengths, gain, w_down, w_up, w_kv
):
    axes = ("pool", "dp")
    pool_count = lax.axis_size("pool")
    columns = lax.axis_size("dp")
    relay_row = pool_count - 1
    half = pool_count // 2
    row = lax.axis_index("pool")
    me = lax.axis_index("dp")
    span_count, width = cond.shape[2:]
    nbr_count = nbr_owner.shape[3]
    per_device = span_count * nbr_count
    block_count, slot_len = database.shape[2:4]
    live_count = relay_row * per_device
    capacity = max(2, live_count // columns + 1)
    slots = -(-capacity // pool_count)
    lanes = half * slots
    most = 0
    if capacity > lanes:
        for rows in (half, relay_row - half):
            full, left = divmod(rows * per_device, capacity)
            most = max(most, full * (capacity - lanes) + max(0, left - lanes))
    crossing = -(-most // half)
    token_count, head_cols = queries.shape[2:]

    def hop(array, pairs):
        return lax.ppermute(
            array, axes, [(a * columns + j, b * columns + j) for a, b in pairs for j in range(columns)]
        )

    parts = PARTS if slot_len % (PARTS * 16) == 0 else 1
    piece = slot_len // parts
    full_store = database.reshape(block_count, slot_len, width)
    store = [full_store[:, i * piece : (i + 1) * piece] for i in range(parts)]

    def to_all(array, axis):
        copies = jnp.broadcast_to(array[None], (lax.axis_size(axis),) + array.shape)
        return lax.all_to_all(copies, axis, split_axis=0, concat_axis=0, tiled=True)

    info = jnp.concatenate([nbr_owner.reshape(-1), nbr_block.reshape(-1), lengths.reshape(-1)])
    info = jnp.pad(info, (0, -info.shape[0] % 128))
    over = lambda a: hop(a, [(relay_row, relay_row - half)])
    across = [over(store[0])]
    table = to_all(info.reshape(-1, 128), "dp")
    store[1:], table = lax.optimization_barrier((store[1:], table))
    across += [over(a) for a in store[1:]]
    table = to_all(table, "pool")
    table = table.reshape(pool_count, columns, -1)
    by_column = jnp.swapaxes(table[:relay_row], 0, 1)
    owners = by_column[:, :, :per_device].reshape(columns, live_count)
    blocks = by_column[:, :, per_device : 2 * per_device].reshape(columns, live_count)
    store_len = table[relay_row, :, 2 * per_device : 2 * per_device + block_count]
    carrier, slot, crosses, number = place_requests(owners, per_device, pool_count, lanes)

    ring = jnp.arange(slots, dtype=jnp.int32)
    mine = ((owners == me) & (carrier == row))[:, None, :] & (slot[:, None, :] == ring[None, :, None])
    slot_block = jnp.sum(jnp.where(mine, blocks[:, None, :], 0), axis=2).reshape(-1)

    mine_of = lambda a: lax.dynamic_index_in_dim(a, me, 0, keepdims=False)
    my_owner, my_block, my_carrier, my_slot, my_cross, my_number = map(
        mine_of, (owners, blocks, carrier, slot, crosses, number)
    )
    place = my_owner * slots + my_slot
    ring = jnp.arange(crossing, dtype=jnp.int32)
    mine = (my_cross & (my_carrier == row))[None, :] & (my_number[None, :] == ring[:, None])
    leaving_place = jnp.sum(jnp.where(mine, place[None, :], 0), axis=1)

    def share(array, step):
        return hop(array, [(p, p // half * half + (p + step) % half) for p in range(pool_count)])

    held = []
    weight, weight_t = w_kv, None
    for i in range(parts):
        near = jnp.where(row == relay_row, store[i], across[i])
        stores = [near]
        held_by = jnp.where(row % half == half - 1, 0, 1)
        for step in range(1, half):
            stores.append(hop(near, [(p, p - step) for p in (relay_row, relay_row - half)]))
            held_by = jnp.where(row % half == half - 1 - step, step, held_by)
        wanted = slot_block
        if i == 1:
            weight_t, wanted = lax.optimization_barrier((weight.T, wanted))
        sends = pick(held_by, wanted, stores)
        if i == 0:
            weight, sends = lax.optimization_barrier((weight, sends))
        arrived = lax.all_to_all(sends, "dp", split_axis=0, concat_axis=0, tiled=True)
        here = [arrived] + [share(arrived, step) for step in range(1, half)]
        if crossing:
            leaving = pick(0, leaving_place, [arrived])
            landed = hop(leaving, [(p, (p + half) % pool_count) for p in range(pool_count)])
            here += [landed] + [share(landed, step) for step in range(1, half)]
        held.append(here)
    weight_t = weight.T if weight_t is None else weight_t
    origin = jnp.where(my_cross, (my_carrier + half) % pool_count, my_carrier)
    which = (row - origin) % half + jnp.where(my_cross, half, 0)
    index = jnp.where(my_cross, my_number, place)
    held = [here[b] for b in range(len(held[0])) for here in held]

    own_row = jnp.minimum(row, relay_row - 1)
    hot = (my_owner * block_count + my_block)[:, None] == jnp.arange(
        columns * block_count, dtype=jnp.int32
    )[None, :]
    wanted_len = jnp.sum(jnp.where(hot, store_len.reshape(1, -1), 0), axis=1)
    own = lambda a: lax.dynamic_index_in_dim(
        a.reshape(relay_row, per_device), own_row, 0, keepdims=False
    )
    live = (row < relay_row).astype(jnp.int32)
    meta = jnp.concatenate([live[None], own(wanted_len), own(which), own(index)]).astype(jnp.int32)

    attn_out, q_grad, cond_grad, terms = run_spans(
        meta,
        queries.reshape(token_count, head_cols),
        cotangent.reshape(token_count, head_cols),
        cond.reshape(span_count, width).astype(jnp.float32),
        held,
        parts,
        gain,
        w_down,
        w_up,
        w_kv,
        weight_t,
        nbr_count,
    )

    adapter_grad = scatter_sum(terms, axes)
    return (
        attn_out.reshape(1, 1, token_count, head_cols),
        q_grad.reshape(1, 1, token_count, head_cols),
        cond_grad.reshape(1, 1, span_count, width),
        adapter_grad,
    )


def solution(mesh):
    return jax.shard_map(
        body,
        mesh=mesh,
        in_specs=(
            P("pool", "dp", None, None),
            P("pool", "dp", None, None),
            P("pool", "dp", None, None),
            P("pool", "dp", None, None),
            P("pool", "dp", None, None),
            P("pool", "dp", None, None, None),
            P("pool", "dp", None),
            P(),
            P(),
            P(),
            P(),
        ),
        out_specs=(
            P("pool", "dp", None, None),
            P("pool", "dp", None, None),
            P("pool", "dp", None, None),
            P(("pool", "dp"), None),
        ),
        check_vma=False,
    )
```

```python
import functools

import jax
import jax.numpy as jnp
from jax import lax
from jax.experimental import pallas as pl
from jax.experimental.pallas import tpu as pltpu
from jax.sharding import PartitionSpec as P

HEADS = 16
HEAD = 128
SPAN = 64

EPSILON = 1e-06
FLOOR = -1e30
LOG2E = 1.4426950408889634

NT = (((1,), (1,)), ((), ()))
TN = (((0,), (0,)), ((), ()))


def dot(a, b, dims=(((1,), (0,)), ((), ()))):
    return lax.dot_general(a, b, dims, preferred_element_type=jnp.float32)


def span_kernel(
    nbr_count, meta,
    q_ref, cot_ref, own_ref, got_ref, cond_ref, gain_ref, down_ref, up_ref, upt_ref, downt_ref,
    kv_hbm, kvt_hbm, out_ref, qg_ref, cg_ref, ad_ref,
    kv_ref, kvt_ref, proj_ref, grad_ref, score_ref, dprob_ref, prob_ref, dscore_ref,
    q2_ref, cot2_ref, acc_ref, kv_sem,
):
    span = pl.program_id(0)
    slot_len, width = own_ref.shape[1:]
    key_count = nbr_count * slot_len
    head_cols = q_ref.shape[1]
    rank = down_ref.shape[1]
    scaling = HEAD ** (-0.5)
    live = meta[0] == 1
    carrier = meta[1] == 1
    lens = 2
    pairs = [pl.ds(i * 2 * HEAD, 2 * HEAD) for i in range(HEADS // 2)]
    value_pairs = [pl.ds(head_cols + i * 2 * HEAD, 2 * HEAD) for i in range(HEADS // 2)]
    lanes = [pl.ds(i * 2 * SPAN, 2 * SPAN) for i in range(HEADS // 2)]
    kv_copy = pltpu.make_async_copy(kv_hbm, kv_ref, kv_sem.at[0])
    kvt_copy = pltpu.make_async_copy(kvt_hbm, kvt_ref, kv_sem.at[1])

    @pl.when(span == 0)
    def _():
        kv_copy.start()
        kvt_copy.start()

    q2_ref[...] = jnp.zeros_like(q2_ref)
    cot2_ref[...] = jnp.zeros_like(cot2_ref)
    for i in range(HEADS):
        cols = pl.ds(i * HEAD, HEAD)
        tokens = pl.ds(i % 2 * SPAN, SPAN)
        q2_ref[tokens, cols] = q_ref[:, cols]
        cot2_ref[tokens, cols] = cot_ref[:, cols]

    raw = jnp.where(carrier, own_ref[...], got_ref[...])
    x_full = raw.reshape(key_count, width).astype(jnp.float32) + cond_ref[pl.ds(span, 1), :]
    inv_rms = lax.rsqrt(jnp.mean(x_full * x_full, axis=-1, keepdims=True) + EPSILON)
    gain = gain_ref[...]
    hidden = (x_full * inv_rms * gain).astype(jnp.bfloat16)
    latent = dot(hidden, down_ref[...]).astype(jnp.bfloat16)
    encoded = (x_full + dot(latent, up_ref[...])).astype(jnp.bfloat16)

    @pl.when(span == 0)
    def _():
        kv_copy.wait()

    for cols in pairs + value_pairs:
        proj_ref[:, cols] = dot(encoded, kv_ref[:, cols]).astype(jnp.bfloat16)

    for cols, value_cols, lane in zip(pairs, value_pairs, lanes):
        score_ref[:, lane] = dot(proj_ref[:, cols], q2_ref[:, cols], NT)
        dprob_ref[:, lane] = dot(proj_ref[:, value_cols], cot2_ref[:, cols], NT)

    slot = lax.broadcasted_iota(jnp.int32, (key_count, 2 * SPAN), 0)
    limit = jnp.zeros((key_count, 2 * SPAN), jnp.int32)
    for n in range(nbr_count):
        here = jnp.logical_and(slot >= n * slot_len, slot < (n + 1) * slot_len)
        limit = jnp.where(here, n * slot_len + meta[lens + span * nbr_count + n], limit)
    usable = slot < limit
    for lane in lanes:
        scores = jnp.where(usable, score_ref[:, lane], FLOOR)
        row_max = jnp.max(scores, axis=0, keepdims=True)
        raised = jnp.exp2((scores - row_max) * (scaling * LOG2E))
        probs = raised * (1.0 / jnp.sum(raised, axis=0, keepdims=True))
        d_probs = dprob_ref[:, lane]
        delta = jnp.sum(probs * d_probs, axis=0, keepdims=True)
        prob_ref[:, lane] = probs.astype(jnp.bfloat16)
        dscore_ref[:, lane] = (probs * (d_probs - delta) * scaling).astype(jnp.bfloat16)

    for cols, value_cols, lane in zip(pairs, value_pairs, lanes):
        grad_ref[:, cols] = dot(dscore_ref[:, lane], q2_ref[:, cols]).astype(jnp.bfloat16)
        grad_ref[:, value_cols] = dot(prob_ref[:, lane], cot2_ref[:, cols]).astype(jnp.bfloat16)

    def diagonal(both):
        return jnp.concatenate([both[:SPAN, :HEAD], both[SPAN:, HEAD:]], axis=1)

    for cols, value_cols, lane in zip(pairs, value_pairs, lanes):
        out = diagonal(dot(prob_ref[:, lane].T, proj_ref[:, value_cols]))
        grad = diagonal(dot(dscore_ref[:, lane].T, proj_ref[:, cols]))
        out_ref[:, cols] = jnp.where(live, out, 0.0).astype(jnp.bfloat16)
        qg_ref[:, cols] = jnp.where(live, grad, 0.0).astype(jnp.bfloat16)

    @pl.when(span == 0)
    def _():
        kvt_copy.wait()
        acc_ref[...] = jnp.zeros_like(acc_ref)

    enc_grad = dot(grad_ref[...], kvt_ref[...]).astype(jnp.bfloat16)
    lat_grad = dot(enc_grad, upt_ref[...]).astype(jnp.bfloat16)
    scaled = dot(lat_grad, downt_ref[...]) * gain
    normed = x_full * inv_rms
    x_grad = enc_grad.astype(jnp.float32) + inv_rms * (
        scaled - normed * jnp.mean(scaled * normed, axis=-1, keepdims=True)
    )
    span_grad = jnp.sum(x_grad, axis=0, keepdims=True)
    cg_ref[pl.ds(span, 1), :] = jnp.where(live, span_grad, 0.0)
    acc_ref[:, :rank] += dot(hidden, lat_grad, TN)
    acc_ref[:, rank:] += dot(enc_grad, latent, TN)

    @pl.when(span == pl.num_programs(0) - 1)
    def _():
        ad_ref[...] = jnp.where(live, acc_ref[...], 0.0).astype(ad_ref.dtype)


def run_spans(meta, query, cot, own, got, cond, gain, w_down, w_up, w_kv, w_kv_t, nbr_count):
    span_count, width = cond.shape
    token_count, head_cols = query.shape
    slot_len = own.shape[1]
    rank = w_down.shape[1]
    whole = lambda a: pl.BlockSpec(a.shape, lambda s, m: (0,) * a.ndim, pipeline_mode=pl.Buffered(1))
    tokens = pl.BlockSpec((SPAN, head_cols), lambda s, m: (s, 0))
    small = [cond, gain.reshape(1, width), w_down, w_up, w_up.T, w_down.T]
    blocks = pl.BlockSpec((nbr_count, slot_len, width), lambda s, m: (s, 0, 0))
    large = [w_kv, w_kv_t]
    per_device = span_count * nbr_count
    keys = nbr_count * slot_len
    rows = per_device * slot_len
    lanes = SPAN * HEADS
    flops = 2 * rows * (2 * width * 2 * head_cols + 6 * width * rank + 6 * SPAN * head_cols)
    return pl.pallas_call(
        functools.partial(span_kernel, nbr_count),
        grid_spec=pltpu.PrefetchScalarGridSpec(
            num_scalar_prefetch=1,
            grid=(span_count,),
            in_specs=[tokens, tokens, blocks, blocks]
            + [whole(a) for a in small]
            + [pl.BlockSpec(memory_space=pltpu.HBM)] * len(large),
            out_specs=[
                tokens,
                tokens,
                pl.BlockSpec((span_count, width), lambda s, m: (0, 0)),
                pl.BlockSpec((width, 2 * rank), lambda s, m: (0, 0)),
            ],
            scratch_shapes=[
                pltpu.VMEM((width, 2 * head_cols), jnp.bfloat16),
                pltpu.VMEM((2 * head_cols, width), jnp.bfloat16),
                pltpu.VMEM((keys, 2 * head_cols), jnp.bfloat16),
                pltpu.VMEM((keys, 2 * head_cols), jnp.bfloat16),
                pltpu.VMEM((keys, lanes), jnp.float32),
                pltpu.VMEM((keys, lanes), jnp.float32),
                pltpu.VMEM((keys, lanes), jnp.bfloat16),
                pltpu.VMEM((keys, lanes), jnp.bfloat16),
                pltpu.VMEM((2 * SPAN, head_cols), jnp.bfloat16),
                pltpu.VMEM((2 * SPAN, head_cols), jnp.bfloat16),
                pltpu.VMEM((width, 2 * rank), jnp.float32),
                pltpu.SemaphoreType.DMA((2,)),
            ],
        ),
        out_shape=[
            jax.ShapeDtypeStruct((token_count, head_cols), jnp.bfloat16),
            jax.ShapeDtypeStruct((token_count, head_cols), jnp.bfloat16),
            jax.ShapeDtypeStruct((span_count, width), jnp.float32),
            jax.ShapeDtypeStruct((width, 2 * rank), jnp.float32),
        ],
        compiler_params=pltpu.CompilerParams(vmem_limit_bytes=60 * 2**20),
        cost_estimate=pl.CostEstimate(
            flops=flops, bytes_accessed=16 * 2**20, transcendentals=rows * SPAN * HEADS
        ),
    )(meta, query, cot, own, got, *small, *large)


def pick_kernel(held_count, meta, *refs):
    held_refs, out_refs = refs[:held_count], refs[held_count:]
    count = sum(out.shape[0] for out in out_refs)
    start = 0
    for out in out_refs:
        def one(n, _, out=out, start=start):
            for b, held in enumerate(held_refs):
                @pl.when(meta[start + n] == b)
                def _():
                    out[n] = held[meta[count + start + n]]
            return 0

        lax.fori_loop(0, out.shape[0], one, 0)
        start += out.shape[0]


def pick(which, index, held, outs):
    count = index.shape[0]
    meta = jnp.concatenate([which, index]).astype(jnp.int32)
    shape = jax.ShapeDtypeStruct((count // outs,) + held[0].shape[1:], held[0].dtype)
    return pl.pallas_call(
        functools.partial(pick_kernel, len(held)),
        grid_spec=pltpu.PrefetchScalarGridSpec(
            num_scalar_prefetch=1,
            grid=(1,),
            in_specs=[pl.BlockSpec(memory_space=pltpu.VMEM)] * len(held),
            out_specs=[pl.BlockSpec(memory_space=pltpu.VMEM)] * outs,
        ),
        out_shape=[shape] * outs,
        compiler_params=pltpu.CompilerParams(vmem_limit_bytes=20 * 2**20),
    )(meta, *held)


def place_requests(owners, per_device, half, lanes):
    count = owners.shape[1]
    order = jnp.arange(count, dtype=jnp.int32)
    side = (order // per_device) // half
    mate = side[:, None] == side[None, :]
    before = order[None, :] < order[:, None]
    same = owners[:, :, None] == owners[:, None, :]
    lower = owners[:, None, :] < owners[:, :, None]
    total = lambda mask: jnp.sum(mask.astype(jnp.int32), axis=2)
    rank = total(same & (mate & before)[None])
    crosses = rank >= lanes
    far = crosses[:, None, :]
    number = total(far & mate[None] & (lower | (same & before[None])))
    guests = total(far & ~mate[None] & same)
    slot = jnp.where(crosses, rank - lanes, guests + rank)
    return slot, crosses, number, jnp.broadcast_to(side[None], owners.shape)


def scatter_sum(total, axes):
    width = total.shape[1]
    sizes = [lax.axis_size(axis) for axis in axes]
    total = total.reshape(tuple(sizes) + (-1, width)).astype(jnp.float32)
    for at, axis in enumerate(axes):
        size, index = sizes[at], lax.axis_index(axis)
        if size & (size - 1):
            lead = (size,) + tuple(d for i, d in enumerate(total.shape) if i != at)
            parts = jnp.moveaxis(total, at, 0).astype(jnp.bfloat16)
            parts = lax.all_to_all(parts, axis, split_axis=0, concat_axis=0, tiled=True)
            total = jnp.sum(parts.reshape(lead).astype(jnp.float32), axis=0)
            total = jnp.expand_dims(total, at)
            continue
        bit = 1
        while bit < size:
            shape = total.shape
            split = total.reshape(shape[:at] + (shape[at] // 2, 2) + shape[at + 1 :])
            mine = (index // bit) % 2
            keep = lax.dynamic_index_in_dim(split, mine, at + 1, keepdims=False)
            give = lax.dynamic_index_in_dim(split, 1 - mine, at + 1, keepdims=False)
            got = lax.ppermute(
                give.astype(jnp.bfloat16), axis, [(i, i ^ bit) for i in range(size)]
            )
            total = keep + got.astype(jnp.float32)
            bit *= 2
    return total.reshape(-1, width)


def body(
    queries, cotangent, cond, nbr_owner, nbr_block, database, lengths, gain, w_down, w_up, w_kv
):
    axes = ("pool", "dp")
    pool_count = lax.axis_size("pool")
    columns = lax.axis_size("dp")
    relay_row = pool_count - 1
    half = pool_count // 2
    row = lax.axis_index("pool")
    me = lax.axis_index("dp")
    span_count, width = cond.shape[2:]
    nbr_count = nbr_owner.shape[3]
    per_device = span_count * nbr_count
    block_count, slot_len = database.shape[2:4]
    live_count = relay_row * per_device
    capacity = max(2, live_count // columns + 1)
    lanes = -(-capacity // 2)
    crossing = 0
    for rows in (half, relay_row - half):
        full, left = divmod(rows * per_device, capacity)
        crossing = max(crossing, full * (capacity - lanes) + max(0, left - lanes))
    token_count, head_cols = queries.shape[2:]
    carriers = (half - 1, relay_row)

    def hop(array, pairs, shift=0):
        return lax.ppermute(
            array,
            axes,
            [(a * columns + j, b * columns + (j + shift) % columns) for a, b in pairs for j in range(columns)],
        )

    def to_all(array, axis):
        copies = jnp.broadcast_to(array[None], (lax.axis_size(axis),) + array.shape)
        return lax.all_to_all(copies, axis, split_axis=0, concat_axis=0, tiled=True)

    store = database.reshape(block_count, slot_len, width)
    across = hop(store, [(relay_row, half - 1)])

    info = jnp.concatenate([nbr_owner.reshape(-1), nbr_block.reshape(-1), lengths.reshape(-1)])
    info = jnp.pad(info, (0, -info.shape[0] % 128))
    table = to_all(to_all(info.reshape(-1, 128), "dp"), "pool")
    across, table = lax.optimization_barrier((across, table))
    table = table.reshape(pool_count, columns, -1)
    by_column = jnp.swapaxes(table[:relay_row], 0, 1)
    owners = by_column[:, :, :per_device].reshape(columns, live_count)
    blocks = by_column[:, :, per_device : 2 * per_device].reshape(columns, live_count)
    store_len = table[relay_row, :, 2 * per_device : 2 * per_device + block_count]
    slot, crosses, number, side = place_requests(owners, per_device, half, lanes)
    held_side = jnp.where(crosses, 1 - side, side)
    my_side = row // half

    target = (me + jnp.arange(columns, dtype=jnp.int32)) % columns
    ring = jnp.arange(lanes, dtype=jnp.int32)
    mine = ((owners == me) & (held_side == my_side))[:, None, :] & (
        slot[:, None, :] == ring[None, :, None]
    )
    slot_block = jnp.sum(jnp.where(mine, blocks[:, None, :], 0), axis=2)
    slot_block = jnp.take(slot_block, target, axis=0).reshape(-1)
    source = jnp.broadcast_to(jnp.where(row == relay_row, 0, 1), slot_block.shape)
    sends = pick(source, slot_block, [store, across], columns)
    w_kv, sends = lax.optimization_barrier((w_kv, sends))
    arrived = [sends[0]] + [
        hop(sends[shift], [(c, c) for c in carriers], shift) for shift in range(1, columns)
    ]

    mine_of = lambda a: lax.dynamic_index_in_dim(a, me, 0, keepdims=False)
    my_owner, my_block, my_slot, my_cross, my_number, my_held = map(
        mine_of, (owners, blocks, slot, crosses, number, held_side)
    )
    shift = (me - my_owner) % columns
    w_kv_t = w_kv.T
    if crossing:
        ring = jnp.arange(crossing, dtype=jnp.int32)
        mine = (my_cross & (my_held == my_side))[None, :] & (my_number[None, :] == ring[:, None])
        chosen = lambda a: jnp.sum(jnp.where(mine, a[None, :], 0), axis=1)
        w_kv_t, leaving = lax.optimization_barrier((w_kv_t, (chosen(shift), chosen(my_slot))))
        (leaving,) = pick(*leaving, arrived, 1)
        arrived.append(hop(leaving, [carriers, carriers[::-1]]))
    source = jnp.where(my_cross, columns, shift).reshape(relay_row, per_device)
    index = jnp.where(my_cross, my_number, my_slot).reshape(relay_row, per_device)
    order = jnp.minimum(my_side * half + jnp.arange(half, dtype=jnp.int32), relay_row - 1)
    sorted_rows = pick(
        jnp.take(source, order, axis=0).reshape(-1),
        jnp.take(index, order, axis=0).reshape(-1),
        arrived,
        half,
    )
    got = jnp.zeros_like(sorted_rows[0])
    for place in range(half - 1):
        passed = hop(sorted_rows[place], [(c, c - (half - 1 - place)) for c in carriers])
        got = passed if half == 2 else jnp.where(row % half == place, passed, got)
    own = sorted_rows[half - 1]

    own_row = jnp.minimum(row, relay_row - 1)
    hot = (my_owner * block_count + my_block)[:, None] == jnp.arange(
        columns * block_count, dtype=jnp.int32
    )[None, :]
    wanted_len = jnp.sum(jnp.where(hot, store_len.reshape(1, -1), 0), axis=1)
    my_len = lax.dynamic_index_in_dim(
        wanted_len.reshape(relay_row, per_device), own_row, 0, keepdims=False
    )
    flags = jnp.stack([row < relay_row, row % half == half - 1])
    meta = jnp.concatenate([flags.astype(jnp.int32), my_len])

    attn_out, q_grad, cond_grad, terms = run_spans(
        meta,
        queries.reshape(token_count, head_cols),
        cotangent.reshape(token_count, head_cols),
        own,
        got,
        cond.reshape(span_count, width).astype(jnp.float32),
        gain,
        w_down,
        w_up,
        w_kv,
        w_kv_t,
        nbr_count,
    )
    adapter_grad = scatter_sum(terms, axes)
    return (
        attn_out.reshape(1, 1, token_count, head_cols),
        q_grad.reshape(1, 1, token_count, head_cols),
        cond_grad.reshape(1, 1, span_count, width),
        adapter_grad,
    )


def solution(mesh):
    return jax.shard_map(
        body,
        mesh=mesh,
        in_specs=(
            P("pool", "dp", None, None),
            P("pool", "dp", None, None),
            P("pool", "dp", None, None),
            P("pool", "dp", None, None),
            P("pool", "dp", None, None),
            P("pool", "dp", None, None, None),
            P("pool", "dp", None),
            P(),
            P(),
            P(),
            P(),
        ),
        out_specs=(
            P("pool", "dp", None, None),
            P("pool", "dp", None, None),
            P("pool", "dp", None, None),
            P(("pool", "dp"), None),
        ),
        check_vma=False,
    )
```

```python
import functools

import jax
import jax.numpy as jnp
from jax import lax
from jax.experimental import pallas as pl
from jax.experimental.pallas import tpu as pltpu
from jax.sharding import PartitionSpec as P

HEADS = 16
HEAD = 128
SPAN = 64
PARTS = 2

EPSILON = 1e-06
FLOOR = -1e30
LOG2E = 1.4426950408889634

NT = (((1,), (1,)), ((), ()))
TN = (((0,), (0,)), ((), ()))


def dot(a, b, dims=(((1,), (0,)), ((), ()))):
    return lax.dot_general(a, b, dims, preferred_element_type=jnp.float32)


def span_kernel(
    held_count, nbr_count, parts, meta,
    q_ref, cot_ref, cond_ref, gain_ref, down_ref, up_ref, upt_ref, downt_ref, *rest,
):
    held_refs = rest[:held_count]
    (kv_hbm, kvt_hbm, out_ref, qg_ref, cg_ref, ad_ref,
     raw_ref, kv_ref, kvt_ref, proj_ref, grad_ref, score_ref, dprob_ref, prob_ref, dscore_ref,
     q2_ref, cot2_ref, acc_ref, sems, kv_sem) = rest[held_count:]
    span = pl.program_id(0)
    per_device, slot_len, width = raw_ref.shape
    key_count = nbr_count * slot_len
    head_cols = q_ref.shape[1]
    rank = down_ref.shape[1]
    scaling = HEAD ** (-0.5)
    live = meta[0] == 1
    lens, which, index = 1, 1 + per_device, 1 + 2 * per_device
    piece = slot_len // parts
    pairs = [pl.ds(i * 2 * HEAD, 2 * HEAD) for i in range(HEADS // 2)]
    value_pairs = [pl.ds(head_cols + i * 2 * HEAD, 2 * HEAD) for i in range(HEADS // 2)]
    lanes = [pl.ds(i * 2 * SPAN, 2 * SPAN) for i in range(HEADS // 2)]
    kv_copy = pltpu.make_async_copy(kv_hbm, kv_ref, kv_sem.at[0])
    kvt_copy = pltpu.make_async_copy(kvt_hbm, kvt_ref, kv_sem.at[1])

    @pl.when(span == 0)
    def _():
        for n in range(per_device):
            for b, held in enumerate(held_refs):
                @pl.when(meta[which + n] == b // parts)
                def _():
                    part = b % parts
                    pltpu.make_async_copy(
                        held.at[meta[index + n]],
                        raw_ref.at[n, pl.ds(part * piece, piece)],
                        sems.at[n * parts + part],
                    ).start()
        kv_copy.start()
        kvt_copy.start()

    q2_ref[...] = jnp.zeros_like(q2_ref)
    cot2_ref[...] = jnp.zeros_like(cot2_ref)
    for i in range(HEADS):
        cols = pl.ds(i * HEAD, HEAD)
        tokens = pl.ds(i % 2 * SPAN, SPAN)
        q2_ref[tokens, cols] = q_ref[:, cols]
        cot2_ref[tokens, cols] = cot_ref[:, cols]

    for n in range(nbr_count):
        for part in range(parts):
            item = span * nbr_count + n
            pltpu.make_async_copy(
                held_refs[0].at[0],
                raw_ref.at[item, pl.ds(part * piece, piece)],
                sems.at[item * parts + part],
            ).wait()
    raw = raw_ref[pl.ds(span * nbr_count, nbr_count)]
    x_full = raw.reshape(key_count, width).astype(jnp.float32) + cond_ref[pl.ds(span, 1), :]
    inv_rms = lax.rsqrt(jnp.mean(x_full * x_full, axis=-1, keepdims=True) + EPSILON)
    gain = gain_ref[...]
    hidden = (x_full * inv_rms * gain).astype(jnp.bfloat16)
    latent = dot(hidden, down_ref[...]).astype(jnp.bfloat16)
    encoded = (x_full + dot(latent, up_ref[...])).astype(jnp.bfloat16)

    @pl.when(span == 0)
    def _():
        kv_copy.wait()

    for cols in pairs + value_pairs:
        proj_ref[:, cols] = dot(encoded, kv_ref[:, cols]).astype(jnp.bfloat16)

    for cols, value_cols, lane in zip(pairs, value_pairs, lanes):
        score_ref[:, lane] = dot(proj_ref[:, cols], q2_ref[:, cols], NT)
        dprob_ref[:, lane] = dot(proj_ref[:, value_cols], cot2_ref[:, cols], NT)

    slot = lax.broadcasted_iota(jnp.int32, (key_count, 2 * SPAN), 0)
    limit = jnp.zeros((key_count, 2 * SPAN), jnp.int32)
    for n in range(nbr_count):
        here = jnp.logical_and(slot >= n * slot_len, slot < (n + 1) * slot_len)
        limit = jnp.where(here, n * slot_len + meta[lens + span * nbr_count + n], limit)
    usable = slot < limit
    for lane in lanes:
        scores = jnp.where(usable, score_ref[:, lane], FLOOR)
        row_max = jnp.max(scores, axis=0, keepdims=True)
        raised = jnp.exp2((scores - row_max) * (scaling * LOG2E))
        probs = raised * (1.0 / jnp.sum(raised, axis=0, keepdims=True))
        d_probs = dprob_ref[:, lane]
        delta = jnp.sum(probs * d_probs, axis=0, keepdims=True)
        prob_ref[:, lane] = probs.astype(jnp.bfloat16)
        dscore_ref[:, lane] = (probs * (d_probs - delta) * scaling).astype(jnp.bfloat16)

    for cols, value_cols, lane in zip(pairs, value_pairs, lanes):
        grad_ref[:, cols] = dot(dscore_ref[:, lane], q2_ref[:, cols]).astype(jnp.bfloat16)
        grad_ref[:, value_cols] = dot(prob_ref[:, lane], cot2_ref[:, cols]).astype(jnp.bfloat16)

    def diagonal(both):
        return jnp.concatenate([both[:SPAN, :HEAD], both[SPAN:, HEAD:]], axis=1)

    for cols, value_cols, lane in zip(pairs, value_pairs, lanes):
        out = diagonal(dot(prob_ref[:, lane].T, proj_ref[:, value_cols]))
        grad = diagonal(dot(dscore_ref[:, lane].T, proj_ref[:, cols]))
        out_ref[:, cols] = jnp.where(live, out, 0.0).astype(jnp.bfloat16)
        qg_ref[:, cols] = jnp.where(live, grad, 0.0).astype(jnp.bfloat16)

    @pl.when(span == 0)
    def _():
        kvt_copy.wait()
        acc_ref[...] = jnp.zeros_like(acc_ref)

    enc_grad = dot(grad_ref[...], kvt_ref[...]).astype(jnp.bfloat16)
    lat_grad = dot(enc_grad, upt_ref[...]).astype(jnp.bfloat16)
    scaled = dot(lat_grad, downt_ref[...]) * gain
    normed = x_full * inv_rms
    x_grad = enc_grad.astype(jnp.float32) + inv_rms * (
        scaled - normed * jnp.mean(scaled * normed, axis=-1, keepdims=True)
    )
    span_grad = jnp.sum(x_grad, axis=0, keepdims=True)
    cg_ref[pl.ds(span, 1), :] = jnp.where(live, span_grad, 0.0)
    acc_ref[:, :rank] += dot(hidden, lat_grad, TN)
    acc_ref[:, rank:] += dot(enc_grad, latent, TN)

    @pl.when(span == pl.num_programs(0) - 1)
    def _():
        ad_ref[...] = jnp.where(live, acc_ref[...], 0.0).astype(ad_ref.dtype)


def run_spans(meta, query, cot, cond, held, parts, gain, w_down, w_up, w_kv, w_kv_t, nbr_count):
    span_count, width = cond.shape
    token_count, head_cols = query.shape
    slot_len = held[0].shape[1] * parts
    rank = w_down.shape[1]
    whole = lambda a: pl.BlockSpec(a.shape, lambda s, m: (0,) * a.ndim, pipeline_mode=pl.Buffered(1))
    tokens = pl.BlockSpec((SPAN, head_cols), lambda s, m: (s, 0))
    small = [cond, gain.reshape(1, width), w_down, w_up, w_up.T, w_down.T]
    large = list(held) + [w_kv, w_kv_t]
    per_device = span_count * nbr_count
    keys = nbr_count * slot_len
    rows = per_device * slot_len
    lanes = SPAN * HEADS
    flops = 2 * rows * (2 * width * 2 * head_cols + 6 * width * rank + 6 * SPAN * head_cols)
    return pl.pallas_call(
        functools.partial(span_kernel, len(held), nbr_count, parts),
        grid_spec=pltpu.PrefetchScalarGridSpec(
            num_scalar_prefetch=1,
            grid=(span_count,),
            in_specs=[tokens, tokens]
            + [whole(a) for a in small]
            + [pl.BlockSpec(memory_space=pltpu.HBM)] * len(large),
            out_specs=[
                tokens,
                tokens,
                pl.BlockSpec((span_count, width), lambda s, m: (0, 0)),
                pl.BlockSpec((width, 2 * rank), lambda s, m: (0, 0)),
            ],
            scratch_shapes=[
                pltpu.VMEM((per_device, slot_len, width), jnp.bfloat16),
                pltpu.VMEM((width, 2 * head_cols), jnp.bfloat16),
                pltpu.VMEM((2 * head_cols, width), jnp.bfloat16),
                pltpu.VMEM((keys, 2 * head_cols), jnp.bfloat16),
                pltpu.VMEM((keys, 2 * head_cols), jnp.bfloat16),
                pltpu.VMEM((keys, lanes), jnp.float32),
                pltpu.VMEM((keys, lanes), jnp.float32),
                pltpu.VMEM((keys, lanes), jnp.bfloat16),
                pltpu.VMEM((keys, lanes), jnp.bfloat16),
                pltpu.VMEM((2 * SPAN, head_cols), jnp.bfloat16),
                pltpu.VMEM((2 * SPAN, head_cols), jnp.bfloat16),
                pltpu.VMEM((width, 2 * rank), jnp.float32),
                pltpu.SemaphoreType.DMA((per_device * parts,)),
                pltpu.SemaphoreType.DMA((2,)),
            ],
        ),
        out_shape=[
            jax.ShapeDtypeStruct((token_count, head_cols), jnp.bfloat16),
            jax.ShapeDtypeStruct((token_count, head_cols), jnp.bfloat16),
            jax.ShapeDtypeStruct((span_count, width), jnp.float32),
            jax.ShapeDtypeStruct((width, 2 * rank), jnp.float32),
        ],
        compiler_params=pltpu.CompilerParams(vmem_limit_bytes=60 * 2**20),
        cost_estimate=pl.CostEstimate(
            flops=flops, bytes_accessed=16 * 2**20, transcendentals=rows * SPAN * HEADS
        ),
    )(meta, query, cot, *small, *large)


def pick_kernel(held_count, meta, *refs):
    held_refs, out_ref = refs[:held_count], refs[held_count]
    for b, held in enumerate(held_refs):
        @pl.when(meta[0] == b)
        def _():
            for n in range(out_ref.shape[0]):
                out_ref[n] = held[meta[1 + n]]


def pick(which, index, held):
    count = index.shape[0]
    meta = jnp.concatenate([jnp.reshape(which, (1,)), index]).astype(jnp.int32)
    return pl.pallas_call(
        functools.partial(pick_kernel, len(held)),
        grid_spec=pltpu.PrefetchScalarGridSpec(
            num_scalar_prefetch=1,
            grid=(1,),
            in_specs=[pl.BlockSpec(memory_space=pltpu.VMEM)] * len(held),
            out_specs=pl.BlockSpec(memory_space=pltpu.VMEM),
        ),
        out_shape=jax.ShapeDtypeStruct((count,) + held[0].shape[1:], held[0].dtype),
        compiler_params=pltpu.CompilerParams(vmem_limit_bytes=16 * 2**20),
    )(meta, *held)


def place_requests(owners, per_device, pool_count, lanes):
    half = pool_count // 2
    count = owners.shape[1]
    order = jnp.arange(count, dtype=jnp.int32)
    side = (order // per_device) // half
    mate = side[:, None] == side[None, :]
    before = order[None, :] < order[:, None]
    same = owners[:, :, None] == owners[:, None, :]
    lower = owners[:, None, :] < owners[:, :, None]
    total = lambda mask: jnp.sum(mask.astype(jnp.int32), axis=2)
    rank = total(same & (mate & before)[None])
    crosses = rank >= lanes
    far = crosses[:, None, :]
    number = total(far & mate[None] & (lower | (same & before[None])))
    first = total(far & ~mate[None] & lower)
    guests = total(far & ~mate[None] & same)
    lane = jnp.where(crosses, number, first + guests + rank) % lanes
    row = jnp.where(crosses, 1 - side[None, :], side[None, :]) * half + lane % half
    return row, lane // half, crosses, number // half


def scatter_sum(total, axes):
    width = total.shape[1]
    sizes = [lax.axis_size(axis) for axis in axes]
    total = total.reshape(tuple(sizes) + (-1, width)).astype(jnp.float32)
    for at, axis in enumerate(axes):
        size, index = sizes[at], lax.axis_index(axis)
        if size & (size - 1):
            lead = (size,) + tuple(d for i, d in enumerate(total.shape) if i != at)
            parts = jnp.moveaxis(total, at, 0).astype(jnp.bfloat16)
            parts = lax.all_to_all(parts, axis, split_axis=0, concat_axis=0, tiled=True)
            total = jnp.sum(parts.reshape(lead).astype(jnp.float32), axis=0)
            total = jnp.expand_dims(total, at)
            continue
        bit = 1
        while bit < size:
            shape = total.shape
            split = total.reshape(shape[:at] + (shape[at] // 2, 2) + shape[at + 1 :])
            mine = (index // bit) % 2
            keep = lax.dynamic_index_in_dim(split, mine, at + 1, keepdims=False)
            give = lax.dynamic_index_in_dim(split, 1 - mine, at + 1, keepdims=False)
            got = lax.ppermute(
                give.astype(jnp.bfloat16), axis, [(i, i ^ bit) for i in range(size)]
            )
            total = keep + got.astype(jnp.float32)
            bit *= 2
    return total.reshape(-1, width)


def body(
    queries, cotangent, cond, nbr_owner, nbr_block, database, lengths, gain, w_down, w_up, w_kv
):
    axes = ("pool", "dp")
    pool_count = lax.axis_size("pool")
    columns = lax.axis_size("dp")
    relay_row = pool_count - 1
    half = pool_count // 2
    row = lax.axis_index("pool")
    me = lax.axis_index("dp")
    span_count, width = cond.shape[2:]
    nbr_count = nbr_owner.shape[3]
    per_device = span_count * nbr_count
    block_count, slot_len = database.shape[2:4]
    live_count = relay_row * per_device
    capacity = max(2, live_count // columns + 1)
    slots = -(-capacity // pool_count)
    lanes = half * slots
    most = 0
    if capacity > lanes:
        for rows in (half, relay_row - half):
            full, left = divmod(rows * per_device, capacity)
            most = max(most, full * (capacity - lanes) + max(0, left - lanes))
    crossing = -(-most // half)
    token_count, head_cols = queries.shape[2:]

    def hop(array, pairs):
        return lax.ppermute(
            array, axes, [(a * columns + j, b * columns + j) for a, b in pairs for j in range(columns)]
        )

    parts = PARTS if slot_len % (PARTS * 16) == 0 else 1
    piece = slot_len // parts
    full_store = database.reshape(block_count, slot_len, width)
    store = [full_store[:, i * piece : (i + 1) * piece] for i in range(parts)]

    def to_all(array, axis):
        copies = jnp.broadcast_to(array[None], (lax.axis_size(axis),) + array.shape)
        return lax.all_to_all(copies, axis, split_axis=0, concat_axis=0, tiled=True)

    info = jnp.concatenate([nbr_owner.reshape(-1), nbr_block.reshape(-1), lengths.reshape(-1)])
    info = jnp.pad(info, (0, -info.shape[0] % 128))
    over = lambda a: hop(a, [(relay_row, relay_row - half)])
    across = [over(store[0])]
    table = to_all(info.reshape(-1, 128), axes)
    store[1:], across, table = lax.optimization_barrier((store[1:], across, table))
    across += [over(a) for a in store[1:]]
    table = table.reshape(pool_count, columns, -1)
    by_column = jnp.swapaxes(table[:relay_row], 0, 1)
    owners = by_column[:, :, :per_device].reshape(columns, live_count)
    blocks = by_column[:, :, per_device : 2 * per_device].reshape(columns, live_count)
    store_len = table[relay_row, :, 2 * per_device : 2 * per_device + block_count]
    carrier, slot, crosses, number = place_requests(owners, per_device, pool_count, lanes)

    ring = jnp.arange(slots, dtype=jnp.int32)
    mine = ((owners == me) & (carrier == row))[:, None, :] & (slot[:, None, :] == ring[None, :, None])
    slot_block = jnp.sum(jnp.where(mine, blocks[:, None, :], 0), axis=2).reshape(-1)

    mine_of = lambda a: lax.dynamic_index_in_dim(a, me, 0, keepdims=False)
    my_owner, my_block, my_carrier, my_slot, my_cross, my_number = map(
        mine_of, (owners, blocks, carrier, slot, crosses, number)
    )
    place = my_owner * slots + my_slot
    ring = jnp.arange(crossing, dtype=jnp.int32)
    mine = (my_cross & (my_carrier == row))[None, :] & (my_number[None, :] == ring[:, None])
    leaving_place = jnp.sum(jnp.where(mine, place[None, :], 0), axis=1)

    def share(array, step):
        return hop(array, [(p, p // half * half + (p + step) % half) for p in range(pool_count)])

    held = []
    weight, weight_t = w_kv, None
    for i in range(parts):
        near = jnp.where(row == relay_row, store[i], across[i])
        stores = [near]
        held_by = jnp.where(row % half == half - 1, 0, 1)
        for step in range(1, half):
            stores.append(hop(near, [(p, p - step) for p in (relay_row, relay_row - half)]))
            held_by = jnp.where(row % half == half - 1 - step, step, held_by)
        wanted = slot_block
        if i == 1:
            weight_t, wanted = lax.optimization_barrier((weight.T, wanted))
        sends = pick(held_by, wanted, stores)
        if i == 0:
            weight, sends = lax.optimization_barrier((weight, sends))
        arrived = lax.all_to_all(sends, "dp", split_axis=0, concat_axis=0, tiled=True)
        here = [arrived] + [share(arrived, step) for step in range(1, half)]
        if crossing:
            leaving = pick(0, leaving_place, [arrived])
            landed = hop(leaving, [(p, (p + half) % pool_count) for p in range(pool_count)])
            here += [landed] + [share(landed, step) for step in range(1, half)]
        held.append(here)
    weight_t = weight.T if weight_t is None else weight_t
    origin = jnp.where(my_cross, (my_carrier + half) % pool_count, my_carrier)
    which = (row - origin) % half + jnp.where(my_cross, half, 0)
    index = jnp.where(my_cross, my_number, place)
    held = [here[b] for b in range(len(held[0])) for here in held]

    own_row = jnp.minimum(row, relay_row - 1)
    hot = (my_owner * block_count + my_block)[:, None] == jnp.arange(
        columns * block_count, dtype=jnp.int32
    )[None, :]
    wanted_len = jnp.sum(jnp.where(hot, store_len.reshape(1, -1), 0), axis=1)
    own = lambda a: lax.dynamic_index_in_dim(
        a.reshape(relay_row, per_device), own_row, 0, keepdims=False
    )
    live = (row < relay_row).astype(jnp.int32)
    meta = jnp.concatenate([live[None], own(wanted_len), own(which), own(index)]).astype(jnp.int32)

    attn_out, q_grad, cond_grad, terms = run_spans(
        meta,
        queries.reshape(token_count, head_cols),
        cotangent.reshape(token_count, head_cols),
        cond.reshape(span_count, width).astype(jnp.float32),
        held,
        parts,
        gain,
        w_down,
        w_up,
        w_kv,
        weight_t,
        nbr_count,
    )

    adapter_grad = scatter_sum(terms, axes)
    return (
        attn_out.reshape(1, 1, token_count, head_cols),
        q_grad.reshape(1, 1, token_count, head_cols),
        cond_grad.reshape(1, 1, span_count, width),
        adapter_grad,
    )


def solution(mesh):
    return jax.shard_map(
        body,
        mesh=mesh,
        in_specs=(
            P("pool", "dp", None, None),
            P("pool", "dp", None, None),
            P("pool", "dp", None, None),
            P("pool", "dp", None, None),
            P("pool", "dp", None, None),
            P("pool", "dp", None, None, None),
            P("pool", "dp", None),
            P(),
            P(),
            P(),
            P(),
        ),
        out_specs=(
            P("pool", "dp", None, None),
            P("pool", "dp", None, None),
            P("pool", "dp", None, None),
            P(("pool", "dp"), None),
        ),
        check_vma=False,
    )
```

```python
import functools

import jax
import jax.numpy as jnp
from jax import lax
from jax.experimental import pallas as pl
from jax.experimental.pallas import tpu as pltpu
from jax.sharding import PartitionSpec as P

HEADS = 16
HEAD = 128
SPAN = 64
PARTS = 2
GROUP = 2

EPSILON = 1e-06
FLOOR = -1e30
LOG2E = 1.4426950408889634

NT = (((1,), (1,)), ((), ()))
TN = (((0,), (0,)), ((), ()))


def dot(a, b, dims=(((1,), (0,)), ((), ()))):
    return lax.dot_general(a, b, dims, preferred_element_type=jnp.float32)


def span_kernel(
    held_count, nbr_count, parts, meta,
    q_ref, cot_ref, cond_ref, gain_ref, down_ref, up_ref, upt_ref, downt_ref, *rest,
):
    held_refs = rest[:held_count]
    (kv_hbm, kvt_hbm, out_ref, qg_ref, cg_ref, ad_ref,
     raw_ref, kv_ref, kvt_ref, proj_ref, grad_ref, score_ref, dprob_ref, prob_ref, dscore_ref,
     q2_ref, cot2_ref, acc_ref, sems, kv_sem) = rest[held_count:]
    step = pl.program_id(0)
    per_device, slot_len, width = raw_ref.shape
    key_count = nbr_count * slot_len
    span_count = per_device // nbr_count
    group = span_count // pl.num_programs(0)
    head_cols = q_ref.shape[1]
    rank = down_ref.shape[1]
    scaling = HEAD ** (-0.5)
    live = meta[0] == 1
    lens, which, index = 1, 1 + per_device, 1 + 2 * per_device
    piece = slot_len // parts
    pairs = [pl.ds(i * 2 * HEAD, 2 * HEAD) for i in range(HEADS // 2)]
    value_pairs = [pl.ds(head_cols + i * 2 * HEAD, 2 * HEAD) for i in range(HEADS // 2)]
    lanes = [pl.ds(i * 2 * SPAN, 2 * SPAN) for i in range(HEADS // 2)]
    keys = [pl.ds(g * key_count, key_count) for g in range(group)]
    tokens = [pl.ds(g * SPAN, SPAN) for g in range(group)]
    double = [pl.ds(g * 2 * SPAN, 2 * SPAN) for g in range(group)]
    spots = [
        (g, cols, value_cols, lane)
        for g in range(group)
        for cols, value_cols, lane in zip(pairs, value_pairs, lanes)
    ]
    kv_copy = pltpu.make_async_copy(kv_hbm, kv_ref, kv_sem.at[0])
    kvt_copy = pltpu.make_async_copy(kvt_hbm, kvt_ref, kv_sem.at[1])

    @pl.when(step == 0)
    def _():
        for n in range(per_device):
            for b, held in enumerate(held_refs):
                @pl.when(meta[which + n] == b // parts)
                def _():
                    part = b % parts
                    pltpu.make_async_copy(
                        held.at[meta[index + n]],
                        raw_ref.at[n, pl.ds(part * piece, piece)],
                        sems.at[n * parts + part],
                    ).start()
        kv_copy.start()
        kvt_copy.start()
        q2_ref[...] = jnp.zeros_like(q2_ref)
        cot2_ref[...] = jnp.zeros_like(cot2_ref)

    for g in range(group):
        for i in range(HEADS):
            cols = pl.ds(i * HEAD, HEAD)
            part = pl.ds((2 * g + i % 2) * SPAN, SPAN)
            q2_ref[part, cols] = q_ref[tokens[g], cols]
            cot2_ref[part, cols] = cot_ref[tokens[g], cols]

    for n in range(group * nbr_count):
        for part in range(parts):
            item = step * group * nbr_count + n
            pltpu.make_async_copy(
                held_refs[0].at[0],
                raw_ref.at[item, pl.ds(part * piece, piece)],
                sems.at[item * parts + part],
            ).wait()
    x_full = jnp.concatenate(
        [
            raw_ref[pl.ds((step * group + g) * nbr_count, nbr_count)]
            .reshape(key_count, width)
            .astype(jnp.float32)
            + cond_ref[pl.ds(step * group + g, 1), :]
            for g in range(group)
        ],
        axis=0,
    )
    inv_rms = lax.rsqrt(jnp.mean(x_full * x_full, axis=-1, keepdims=True) + EPSILON)
    gain = gain_ref[...]
    hidden = (x_full * inv_rms * gain).astype(jnp.bfloat16)
    latent = dot(hidden, down_ref[...]).astype(jnp.bfloat16)
    encoded = (x_full + dot(latent, up_ref[...])).astype(jnp.bfloat16)

    @pl.when(step == 0)
    def _():
        kv_copy.wait()

    for cols in pairs + value_pairs:
        proj_ref[:, cols] = dot(encoded, kv_ref[:, cols]).astype(jnp.bfloat16)

    for g, cols, value_cols, lane in spots:
        score_ref[keys[g], lane] = dot(proj_ref[keys[g], cols], q2_ref[double[g], cols], NT)
        dprob_ref[keys[g], lane] = dot(proj_ref[keys[g], value_cols], cot2_ref[double[g], cols], NT)

    slot = lax.broadcasted_iota(jnp.int32, (key_count, 2 * SPAN), 0)
    for g in range(group):
        limit = jnp.zeros((key_count, 2 * SPAN), jnp.int32)
        for n in range(nbr_count):
            here = jnp.logical_and(slot >= n * slot_len, slot < (n + 1) * slot_len)
            item = (step * group + g) * nbr_count + n
            limit = jnp.where(here, n * slot_len + meta[lens + item], limit)
        usable = slot < limit
        for lane in lanes:
            scores = jnp.where(usable, score_ref[keys[g], lane], FLOOR)
            row_max = jnp.max(scores, axis=0, keepdims=True)
            raised = jnp.exp2((scores - row_max) * (scaling * LOG2E))
            probs = raised * (1.0 / jnp.sum(raised, axis=0, keepdims=True))
            d_probs = dprob_ref[keys[g], lane]
            delta = jnp.sum(probs * d_probs, axis=0, keepdims=True)
            prob_ref[keys[g], lane] = probs.astype(jnp.bfloat16)
            dscore_ref[keys[g], lane] = (probs * (d_probs - delta) * scaling).astype(jnp.bfloat16)

    for g, cols, value_cols, lane in spots:
        grad_ref[keys[g], cols] = dot(
            dscore_ref[keys[g], lane], q2_ref[double[g], cols]
        ).astype(jnp.bfloat16)
        grad_ref[keys[g], value_cols] = dot(
            prob_ref[keys[g], lane], cot2_ref[double[g], cols]
        ).astype(jnp.bfloat16)

    def diagonal(both):
        return jnp.concatenate([both[:SPAN, :HEAD], both[SPAN:, HEAD:]], axis=1)

    for g, cols, value_cols, lane in spots:
        out = diagonal(dot(prob_ref[keys[g], lane].T, proj_ref[keys[g], value_cols]))
        grad = diagonal(dot(dscore_ref[keys[g], lane].T, proj_ref[keys[g], cols]))
        out_ref[tokens[g], cols] = jnp.where(live, out, 0.0).astype(jnp.bfloat16)
        qg_ref[tokens[g], cols] = jnp.where(live, grad, 0.0).astype(jnp.bfloat16)

    @pl.when(step == 0)
    def _():
        kvt_copy.wait()
        acc_ref[...] = jnp.zeros_like(acc_ref)

    enc_grad = dot(grad_ref[...], kvt_ref[...]).astype(jnp.bfloat16)
    lat_grad = dot(enc_grad, upt_ref[...]).astype(jnp.bfloat16)
    scaled = dot(lat_grad, downt_ref[...]) * gain
    normed = x_full * inv_rms
    x_grad = enc_grad.astype(jnp.float32) + inv_rms * (
        scaled - normed * jnp.mean(scaled * normed, axis=-1, keepdims=True)
    )
    for g in range(group):
        span_grad = jnp.sum(
            x_grad[g * key_count : (g + 1) * key_count], axis=0, keepdims=True
        )
        cg_ref[pl.ds(step * group + g, 1), :] = jnp.where(live, span_grad, 0.0)
    acc_ref[:, :rank] += dot(hidden, lat_grad, TN)
    acc_ref[:, rank:] += dot(enc_grad, latent, TN)

    @pl.when(step == pl.num_programs(0) - 1)
    def _():
        ad_ref[...] = jnp.where(live, acc_ref[...], 0.0).astype(ad_ref.dtype)


def run_spans(meta, query, cot, cond, held, parts, gain, w_down, w_up, w_kv, w_kv_t, nbr_count):
    span_count, width = cond.shape
    token_count, head_cols = query.shape
    slot_len = held[0].shape[1] * parts
    rank = w_down.shape[1]
    whole = lambda a: pl.BlockSpec(a.shape, lambda s, m: (0,) * a.ndim, pipeline_mode=pl.Buffered(1))
    group = GROUP if span_count % GROUP == 0 else 1
    tokens = pl.BlockSpec((group * SPAN, head_cols), lambda s, m: (s, 0))
    small = [cond, gain.reshape(1, width), w_down, w_up, w_up.T, w_down.T]
    large = list(held) + [w_kv, w_kv_t]
    per_device = span_count * nbr_count
    keys = group * nbr_count * slot_len
    rows = per_device * slot_len
    lanes = SPAN * HEADS
    flops = 2 * rows * (2 * width * 2 * head_cols + 6 * width * rank + 6 * SPAN * head_cols)
    return pl.pallas_call(
        functools.partial(span_kernel, len(held), nbr_count, parts),
        grid_spec=pltpu.PrefetchScalarGridSpec(
            num_scalar_prefetch=1,
            grid=(span_count // group,),
            in_specs=[tokens, tokens]
            + [whole(a) for a in small]
            + [pl.BlockSpec(memory_space=pltpu.HBM)] * len(large),
            out_specs=[
                tokens,
                tokens,
                pl.BlockSpec((span_count, width), lambda s, m: (0, 0)),
                pl.BlockSpec((width, 2 * rank), lambda s, m: (0, 0)),
            ],
            scratch_shapes=[
                pltpu.VMEM((per_device, slot_len, width), jnp.bfloat16),
                pltpu.VMEM((width, 2 * head_cols), jnp.bfloat16),
                pltpu.VMEM((2 * head_cols, width), jnp.bfloat16),
                pltpu.VMEM((keys, 2 * head_cols), jnp.bfloat16),
                pltpu.VMEM((keys, 2 * head_cols), jnp.bfloat16),
                pltpu.VMEM((keys, lanes), jnp.float32),
                pltpu.VMEM((keys, lanes), jnp.float32),
                pltpu.VMEM((keys, lanes), jnp.bfloat16),
                pltpu.VMEM((keys, lanes), jnp.bfloat16),
                pltpu.VMEM((group * 2 * SPAN, head_cols), jnp.bfloat16),
                pltpu.VMEM((group * 2 * SPAN, head_cols), jnp.bfloat16),
                pltpu.VMEM((width, 2 * rank), jnp.float32),
                pltpu.SemaphoreType.DMA((per_device * parts,)),
                pltpu.SemaphoreType.DMA((2,)),
            ],
        ),
        out_shape=[
            jax.ShapeDtypeStruct((token_count, head_cols), jnp.bfloat16),
            jax.ShapeDtypeStruct((token_count, head_cols), jnp.bfloat16),
            jax.ShapeDtypeStruct((span_count, width), jnp.float32),
            jax.ShapeDtypeStruct((width, 2 * rank), jnp.float32),
        ],
        compiler_params=pltpu.CompilerParams(vmem_limit_bytes=60 * 2**20),
        cost_estimate=pl.CostEstimate(
            flops=flops, bytes_accessed=16 * 2**20, transcendentals=rows * SPAN * HEADS
        ),
    )(meta, query, cot, *small, *large)


def pick_kernel(held_count, meta, *refs):
    held_refs, out_ref = refs[:held_count], refs[held_count]
    for b, held in enumerate(held_refs):
        @pl.when(meta[0] == b)
        def _():
            for n in range(out_ref.shape[0]):
                out_ref[n] = held[meta[1 + n]]


def pick(which, index, held):
    count = index.shape[0]
    meta = jnp.concatenate([jnp.reshape(which, (1,)), index]).astype(jnp.int32)
    return pl.pallas_call(
        functools.partial(pick_kernel, len(held)),
        grid_spec=pltpu.PrefetchScalarGridSpec(
            num_scalar_prefetch=1,
            grid=(1,),
            in_specs=[pl.BlockSpec(memory_space=pltpu.VMEM)] * len(held),
            out_specs=pl.BlockSpec(memory_space=pltpu.VMEM),
        ),
        out_shape=jax.ShapeDtypeStruct((count,) + held[0].shape[1:], held[0].dtype),
        compiler_params=pltpu.CompilerParams(vmem_limit_bytes=16 * 2**20),
    )(meta, *held)


def place_requests(owners, per_device, pool_count, lanes):
    half = pool_count // 2
    count = owners.shape[1]
    order = jnp.arange(count, dtype=jnp.int32)
    side = (order // per_device) // half
    mate = side[:, None] == side[None, :]
    before = order[None, :] < order[:, None]
    same = owners[:, :, None] == owners[:, None, :]
    lower = owners[:, None, :] < owners[:, :, None]
    total = lambda mask: jnp.sum(mask.astype(jnp.int32), axis=2)
    rank = total(same & (mate & before)[None])
    crosses = rank >= lanes
    far = crosses[:, None, :]
    number = total(far & mate[None] & (lower | (same & before[None])))
    first = total(far & ~mate[None] & lower)
    guests = total(far & ~mate[None] & same)
    lane = jnp.where(crosses, number, first + guests + rank) % lanes
    row = jnp.where(crosses, 1 - side[None, :], side[None, :]) * half + lane % half
    return row, lane // half, crosses, number // half


def scatter_sum(total, axes):
    width = total.shape[1]
    sizes = [lax.axis_size(axis) for axis in axes]
    total = total.reshape(tuple(sizes) + (-1, width)).astype(jnp.float32)
    for at, axis in enumerate(axes):
        size, index = sizes[at], lax.axis_index(axis)
        if size & (size - 1):
            lead = (size,) + tuple(d for i, d in enumerate(total.shape) if i != at)
            parts = jnp.moveaxis(total, at, 0).astype(jnp.bfloat16)
            parts = lax.all_to_all(parts, axis, split_axis=0, concat_axis=0, tiled=True)
            total = jnp.sum(parts.reshape(lead).astype(jnp.float32), axis=0)
            total = jnp.expand_dims(total, at)
            continue
        bit = 1
        while bit < size:
            shape = total.shape
            split = total.reshape(shape[:at] + (shape[at] // 2, 2) + shape[at + 1 :])
            mine = (index // bit) % 2
            keep = lax.dynamic_index_in_dim(split, mine, at + 1, keepdims=False)
            give = lax.dynamic_index_in_dim(split, 1 - mine, at + 1, keepdims=False)
            got = lax.ppermute(
                give.astype(jnp.bfloat16), axis, [(i, i ^ bit) for i in range(size)]
            )
            total = keep + got.astype(jnp.float32)
            bit *= 2
    return total.reshape(-1, width)


def body(
    queries, cotangent, cond, nbr_owner, nbr_block, database, lengths, gain, w_down, w_up, w_kv
):
    axes = ("pool", "dp")
    pool_count = lax.axis_size("pool")
    columns = lax.axis_size("dp")
    relay_row = pool_count - 1
    half = pool_count // 2
    row = lax.axis_index("pool")
    me = lax.axis_index("dp")
    span_count, width = cond.shape[2:]
    nbr_count = nbr_owner.shape[3]
    per_device = span_count * nbr_count
    block_count, slot_len = database.shape[2:4]
    live_count = relay_row * per_device
    capacity = max(2, live_count // columns + 1)
    slots = -(-capacity // pool_count)
    lanes = half * slots
    most = 0
    if capacity > lanes:
        for rows in (half, relay_row - half):
            full, left = divmod(rows * per_device, capacity)
            most = max(most, full * (capacity - lanes) + max(0, left - lanes))
    crossing = -(-most // half)
    token_count, head_cols = queries.shape[2:]

    def hop(array, pairs):
        return lax.ppermute(
            array, axes, [(a * columns + j, b * columns + j) for a, b in pairs for j in range(columns)]
        )

    parts = PARTS if slot_len % (PARTS * 16) == 0 else 1
    piece = slot_len // parts
    full_store = database.reshape(block_count, slot_len, width)
    cut = lambda i: full_store[:, i * piece : (i + 1) * piece]
    store = [cut(0)]

    def to_all(array, axis):
        copies = jnp.broadcast_to(array[None], (lax.axis_size(axis),) + array.shape)
        return lax.all_to_all(copies, axis, split_axis=0, concat_axis=0, tiled=True)

    info = jnp.concatenate([nbr_owner.reshape(-1), nbr_block.reshape(-1), lengths.reshape(-1)])
    info = jnp.pad(info, (0, -info.shape[0] % 128))
    over = lambda a: hop(a, [(relay_row, relay_row - half)])
    across = [over(store[0])]
    table = to_all(info.reshape(-1, 128), axes)
    full_store, across, table = lax.optimization_barrier((full_store, across, table))
    store += [cut(i) for i in range(1, parts)]
    across += [over(a) for a in store[1:]]
    table = table.reshape(pool_count, columns, -1)
    by_column = jnp.swapaxes(table[:relay_row], 0, 1)
    owners = by_column[:, :, :per_device].reshape(columns, live_count)
    blocks = by_column[:, :, per_device : 2 * per_device].reshape(columns, live_count)
    store_len = table[relay_row, :, 2 * per_device : 2 * per_device + block_count]
    carrier, slot, crosses, number = place_requests(owners, per_device, pool_count, lanes)

    ring = jnp.arange(slots, dtype=jnp.int32)
    mine = ((owners == me) & (carrier == row))[:, None, :] & (slot[:, None, :] == ring[None, :, None])
    slot_block = jnp.sum(jnp.where(mine, blocks[:, None, :], 0), axis=2).reshape(-1)

    mine_of = lambda a: lax.dynamic_index_in_dim(a, me, 0, keepdims=False)
    my_owner, my_block, my_carrier, my_slot, my_cross, my_number = map(
        mine_of, (owners, blocks, carrier, slot, crosses, number)
    )
    place = my_owner * slots + my_slot
    ring = jnp.arange(crossing, dtype=jnp.int32)
    mine = (my_cross & (my_carrier == row))[None, :] & (my_number[None, :] == ring[:, None])
    leaving_place = jnp.sum(jnp.where(mine, place[None, :], 0), axis=1)

    def share(array, step):
        return hop(array, [(p, p // half * half + (p + step) % half) for p in range(pool_count)])

    held = []
    weight, weight_t = w_kv, None
    for i in range(parts):
        if i == 1:
            weight_t, across[i] = lax.optimization_barrier((weight.T, across[i]))
        near = jnp.where(row == relay_row, store[i], across[i])
        stores = [near]
        held_by = jnp.where(row % half == half - 1, 0, 1)
        for step in range(1, half):
            stores.append(hop(near, [(p, p - step) for p in (relay_row, relay_row - half)]))
            held_by = jnp.where(row % half == half - 1 - step, step, held_by)
        sends = pick(held_by, slot_block, stores)
        if i == 0:
            weight, sends = lax.optimization_barrier((weight, sends))
        arrived = lax.all_to_all(sends, "dp", split_axis=0, concat_axis=0, tiled=True)
        here = [arrived] + [share(arrived, step) for step in range(1, half)]
        if crossing:
            leaving = pick(0, leaving_place, [arrived])
            landed = hop(leaving, [(p, (p + half) % pool_count) for p in range(pool_count)])
            here += [landed] + [share(landed, step) for step in range(1, half)]
        held.append(here)
    weight_t = weight.T if weight_t is None else weight_t
    origin = jnp.where(my_cross, (my_carrier + half) % pool_count, my_carrier)
    which = (row - origin) % half + jnp.where(my_cross, half, 0)
    index = jnp.where(my_cross, my_number, place)
    held = [here[b] for b in range(len(held[0])) for here in held]

    own_row = jnp.minimum(row, relay_row - 1)
    hot = (my_owner * block_count + my_block)[:, None] == jnp.arange(
        columns * block_count, dtype=jnp.int32
    )[None, :]
    wanted_len = jnp.sum(jnp.where(hot, store_len.reshape(1, -1), 0), axis=1)
    own = lambda a: lax.dynamic_index_in_dim(
        a.reshape(relay_row, per_device), own_row, 0, keepdims=False
    )
    live = (row < relay_row).astype(jnp.int32)
    meta = jnp.concatenate([live[None], own(wanted_len), own(which), own(index)]).astype(jnp.int32)

    attn_out, q_grad, cond_grad, terms = run_spans(
        meta,
        queries.reshape(token_count, head_cols),
        cotangent.reshape(token_count, head_cols),
        cond.reshape(span_count, width).astype(jnp.float32),
        held,
        parts,
        gain,
        w_down,
        w_up,
        w_kv,
        weight_t,
        nbr_count,
    )

    adapter_grad = scatter_sum(terms, axes)
    return (
        attn_out.reshape(1, 1, token_count, head_cols),
        q_grad.reshape(1, 1, token_count, head_cols),
        cond_grad.reshape(1, 1, span_count, width),
        adapter_grad,
    )


def solution(mesh):
    return jax.shard_map(
        body,
        mesh=mesh,
        in_specs=(
            P("pool", "dp", None, None),
            P("pool", "dp", None, None),
            P("pool", "dp", None, None),
            P("pool", "dp", None, None),
            P("pool", "dp", None, None),
            P("pool", "dp", None, None, None),
            P("pool", "dp", None),
            P(),
            P(),
            P(),
            P(),
        ),
        out_specs=(
            P("pool", "dp", None, None),
            P("pool", "dp", None, None),
            P("pool", "dp", None, None),
            P(("pool", "dp"), None),
        ),
        check_vma=False,
    )
```

```python
import functools

import jax
import jax.numpy as jnp
from jax import lax
from jax.experimental import pallas as pl
from jax.experimental.pallas import tpu as pltpu
from jax.sharding import PartitionSpec as P

HEADS = 16
HEAD = 128
SPAN = 64
PARTS = 2
GROUP = 2

EPSILON = 1e-06
FLOOR = -1e30
LOG2E = 1.4426950408889634

NT = (((1,), (1,)), ((), ()))
TN = (((0,), (0,)), ((), ()))


def dot(a, b, dims=(((1,), (0,)), ((), ()))):
    return lax.dot_general(a, b, dims, preferred_element_type=jnp.float32)


def span_kernel(
    held_count, nbr_count, parts, meta,
    q_ref, cot_ref, cond_ref, gain_ref, down_ref, up_ref, upt_ref, downt_ref, *rest,
):
    held_refs = rest[:held_count]
    (kv_hbm, kvt_hbm, out_ref, qg_ref, cg_ref, ad_ref,
     raw_ref, kv_ref, kvt_ref, proj_ref, grad_ref, score_ref, dprob_ref, prob_ref, dscore_ref,
     q2_ref, cot2_ref, acc_ref, sems, kv_sem) = rest[held_count:]
    step = pl.program_id(0)
    per_device, slot_len, width = raw_ref.shape
    key_count = nbr_count * slot_len
    span_count = per_device // nbr_count
    group = span_count // pl.num_programs(0)
    head_cols = q_ref.shape[1]
    rank = down_ref.shape[1]
    scaling = HEAD ** (-0.5)
    live = meta[0] == 1
    lens, which, index = 1, 1 + per_device, 1 + 2 * per_device
    piece = slot_len // parts
    pairs = [pl.ds(i * 2 * HEAD, 2 * HEAD) for i in range(HEADS // 2)]
    value_pairs = [pl.ds(head_cols + i * 2 * HEAD, 2 * HEAD) for i in range(HEADS // 2)]
    lanes = [pl.ds(i * 2 * SPAN, 2 * SPAN) for i in range(HEADS // 2)]
    keys = [pl.ds(g * key_count, key_count) for g in range(group)]
    tokens = [pl.ds(g * SPAN, SPAN) for g in range(group)]
    double = [pl.ds(g * 2 * SPAN, 2 * SPAN) for g in range(group)]
    spots = [
        (g, cols, value_cols, lane)
        for g in range(group)
        for cols, value_cols, lane in zip(pairs, value_pairs, lanes)
    ]
    kv_copy = pltpu.make_async_copy(kv_hbm, kv_ref, kv_sem.at[0])
    kvt_copy = pltpu.make_async_copy(kvt_hbm, kvt_ref, kv_sem.at[1])

    @pl.when(step == 0)
    def _():
        for n in range(per_device):
            for b, held in enumerate(held_refs):
                @pl.when(meta[which + n] == b // parts)
                def _():
                    part = b % parts
                    pltpu.make_async_copy(
                        held.at[meta[index + n]],
                        raw_ref.at[n, pl.ds(part * piece, piece)],
                        sems.at[n * parts + part],
                    ).start()
        kv_copy.start()
        kvt_copy.start()
        q2_ref[...] = jnp.zeros_like(q2_ref)
        cot2_ref[...] = jnp.zeros_like(cot2_ref)

    for g in range(group):
        for i in range(HEADS):
            cols = pl.ds(i * HEAD, HEAD)
            part = pl.ds((2 * g + i % 2) * SPAN, SPAN)
            q2_ref[part, cols] = q_ref[tokens[g], cols]
            cot2_ref[part, cols] = cot_ref[tokens[g], cols]

    for n in range(group * nbr_count):
        for part in range(parts):
            item = step * group * nbr_count + n
            pltpu.make_async_copy(
                held_refs[0].at[0],
                raw_ref.at[item, pl.ds(part * piece, piece)],
                sems.at[item * parts + part],
            ).wait()
    x_full = jnp.concatenate(
        [
            raw_ref[pl.ds((step * group + g) * nbr_count, nbr_count)]
            .reshape(key_count, width)
            .astype(jnp.float32)
            + cond_ref[pl.ds(step * group + g, 1), :]
            for g in range(group)
        ],
        axis=0,
    )
    inv_rms = lax.rsqrt(jnp.mean(x_full * x_full, axis=-1, keepdims=True) + EPSILON)
    gain = gain_ref[...]
    hidden = (x_full * inv_rms * gain).astype(jnp.bfloat16)
    latent = dot(hidden, down_ref[...]).astype(jnp.bfloat16)
    encoded = (x_full + dot(latent, up_ref[...])).astype(jnp.bfloat16)

    @pl.when(step == 0)
    def _():
        kv_copy.wait()

    for cols in pairs + value_pairs:
        proj_ref[:, cols] = dot(encoded, kv_ref[:, cols]).astype(jnp.bfloat16)

    for g, cols, value_cols, lane in spots:
        score_ref[keys[g], lane] = dot(proj_ref[keys[g], cols], q2_ref[double[g], cols], NT)
        dprob_ref[keys[g], lane] = dot(proj_ref[keys[g], value_cols], cot2_ref[double[g], cols], NT)

    slot = lax.broadcasted_iota(jnp.int32, (key_count, 2 * SPAN), 0)
    for g in range(group):
        limit = jnp.zeros((key_count, 2 * SPAN), jnp.int32)
        for n in range(nbr_count):
            here = jnp.logical_and(slot >= n * slot_len, slot < (n + 1) * slot_len)
            item = (step * group + g) * nbr_count + n
            limit = jnp.where(here, n * slot_len + meta[lens + item], limit)
        usable = slot < limit
        for lane in lanes:
            scores = jnp.where(usable, score_ref[keys[g], lane], FLOOR)
            row_max = jnp.max(scores, axis=0, keepdims=True)
            raised = jnp.exp2((scores - row_max) * (scaling * LOG2E))
            probs = raised * (1.0 / jnp.sum(raised, axis=0, keepdims=True))
            d_probs = dprob_ref[keys[g], lane]
            delta = jnp.sum(probs * d_probs, axis=0, keepdims=True)
            prob_ref[keys[g], lane] = probs.astype(jnp.bfloat16)
            dscore_ref[keys[g], lane] = (probs * (d_probs - delta) * scaling).astype(jnp.bfloat16)

    for g, cols, value_cols, lane in spots:
        grad_ref[keys[g], cols] = dot(
            dscore_ref[keys[g], lane], q2_ref[double[g], cols]
        ).astype(jnp.bfloat16)
        grad_ref[keys[g], value_cols] = dot(
            prob_ref[keys[g], lane], cot2_ref[double[g], cols]
        ).astype(jnp.bfloat16)

    def diagonal(both):
        return jnp.concatenate([both[:SPAN, :HEAD], both[SPAN:, HEAD:]], axis=1)

    for g, cols, value_cols, lane in spots:
        out = diagonal(dot(prob_ref[keys[g], lane].T, proj_ref[keys[g], value_cols]))
        grad = diagonal(dot(dscore_ref[keys[g], lane].T, proj_ref[keys[g], cols]))
        out_ref[tokens[g], cols] = jnp.where(live, out, 0.0).astype(jnp.bfloat16)
        qg_ref[tokens[g], cols] = jnp.where(live, grad, 0.0).astype(jnp.bfloat16)

    @pl.when(step == 0)
    def _():
        kvt_copy.wait()
        acc_ref[...] = jnp.zeros_like(acc_ref)

    enc_grad = dot(grad_ref[...], kvt_ref[...]).astype(jnp.bfloat16)
    lat_grad = dot(enc_grad, upt_ref[...]).astype(jnp.bfloat16)
    scaled = dot(lat_grad, downt_ref[...]) * gain
    normed = x_full * inv_rms
    x_grad = enc_grad.astype(jnp.float32) + inv_rms * (
        scaled - normed * jnp.mean(scaled * normed, axis=-1, keepdims=True)
    )
    for g in range(group):
        span_grad = jnp.sum(
            x_grad[g * key_count : (g + 1) * key_count], axis=0, keepdims=True
        )
        cg_ref[pl.ds(step * group + g, 1), :] = jnp.where(live, span_grad, 0.0)
    acc_ref[:, :rank] += dot(hidden, lat_grad, TN)
    acc_ref[:, rank:] += dot(enc_grad, latent, TN)

    @pl.when(step == pl.num_programs(0) - 1)
    def _():
        ad_ref[...] = jnp.where(live, acc_ref[...], 0.0).astype(ad_ref.dtype)


def run_spans(meta, query, cot, cond, held, parts, gain, w_down, w_up, w_kv, w_kv_t, nbr_count):
    span_count, width = cond.shape
    token_count, head_cols = query.shape
    slot_len = held[0].shape[1] * parts
    rank = w_down.shape[1]
    whole = lambda a: pl.BlockSpec(a.shape, lambda s, m: (0,) * a.ndim, pipeline_mode=pl.Buffered(1))
    group = GROUP if span_count % GROUP == 0 else 1
    tokens = pl.BlockSpec((group * SPAN, head_cols), lambda s, m: (s, 0))
    small = [cond, gain.reshape(1, width), w_down, w_up, w_up.T, w_down.T]
    large = list(held) + [w_kv, w_kv_t]
    per_device = span_count * nbr_count
    keys = group * nbr_count * slot_len
    rows = per_device * slot_len
    lanes = SPAN * HEADS
    flops = 2 * rows * (2 * width * 2 * head_cols + 6 * width * rank + 6 * SPAN * head_cols)
    return pl.pallas_call(
        functools.partial(span_kernel, len(held), nbr_count, parts),
        grid_spec=pltpu.PrefetchScalarGridSpec(
            num_scalar_prefetch=1,
            grid=(span_count // group,),
            in_specs=[tokens, tokens]
            + [whole(a) for a in small]
            + [pl.BlockSpec(memory_space=pltpu.HBM)] * len(large),
            out_specs=[
                tokens,
                tokens,
                pl.BlockSpec((span_count, width), lambda s, m: (0, 0)),
                pl.BlockSpec((width, 2 * rank), lambda s, m: (0, 0)),
            ],
            scratch_shapes=[
                pltpu.VMEM((per_device, slot_len, width), jnp.bfloat16),
                pltpu.VMEM((width, 2 * head_cols), jnp.bfloat16),
                pltpu.VMEM((2 * head_cols, width), jnp.bfloat16),
                pltpu.VMEM((keys, 2 * head_cols), jnp.bfloat16),
                pltpu.VMEM((keys, 2 * head_cols), jnp.bfloat16),
                pltpu.VMEM((keys, lanes), jnp.float32),
                pltpu.VMEM((keys, lanes), jnp.float32),
                pltpu.VMEM((keys, lanes), jnp.bfloat16),
                pltpu.VMEM((keys, lanes), jnp.bfloat16),
                pltpu.VMEM((group * 2 * SPAN, head_cols), jnp.bfloat16),
                pltpu.VMEM((group * 2 * SPAN, head_cols), jnp.bfloat16),
                pltpu.VMEM((width, 2 * rank), jnp.float32),
                pltpu.SemaphoreType.DMA((per_device * parts,)),
                pltpu.SemaphoreType.DMA((2,)),
            ],
        ),
        out_shape=[
            jax.ShapeDtypeStruct((token_count, head_cols), jnp.bfloat16),
            jax.ShapeDtypeStruct((token_count, head_cols), jnp.bfloat16),
            jax.ShapeDtypeStruct((span_count, width), jnp.float32),
            jax.ShapeDtypeStruct((width, 2 * rank), jnp.float32),
        ],
        compiler_params=pltpu.CompilerParams(vmem_limit_bytes=60 * 2**20),
        cost_estimate=pl.CostEstimate(
            flops=flops, bytes_accessed=16 * 2**20, transcendentals=rows * SPAN * HEADS
        ),
    )(meta, query, cot, *small, *large)


def pick_kernel(held_count, meta, *refs):
    held_refs, out_ref = refs[:held_count], refs[held_count]
    for b, held in enumerate(held_refs):
        @pl.when(meta[0] == b)
        def _():
            for n in range(out_ref.shape[0]):
                out_ref[n] = held[meta[1 + n]]


def pick(which, index, held):
    count = index.shape[0]
    meta = jnp.concatenate([jnp.reshape(which, (1,)), index]).astype(jnp.int32)
    return pl.pallas_call(
        functools.partial(pick_kernel, len(held)),
        grid_spec=pltpu.PrefetchScalarGridSpec(
            num_scalar_prefetch=1,
            grid=(1,),
            in_specs=[pl.BlockSpec(memory_space=pltpu.VMEM)] * len(held),
            out_specs=pl.BlockSpec(memory_space=pltpu.VMEM),
        ),
        out_shape=jax.ShapeDtypeStruct((count,) + held[0].shape[1:], held[0].dtype),
        compiler_params=pltpu.CompilerParams(vmem_limit_bytes=16 * 2**20),
    )(meta, *held)


def cut_kernel(held_count, low, meta, *refs):
    held_refs, out_ref, sems = refs[:held_count], refs[held_count], refs[held_count + 1]
    count, piece = out_ref.shape[:2]
    rows = pl.ds(low, piece)
    for b, held in enumerate(held_refs):
        @pl.when(meta[0] == b)
        def _():
            for n in range(count):
                pltpu.make_async_copy(held.at[meta[1 + n], rows], out_ref.at[n], sems.at[n]).start()
    for n in range(count):
        pltpu.make_async_copy(held_refs[0].at[0, rows], out_ref.at[n], sems.at[n]).wait()


def cut(which, index, held, low, piece):
    count = index.shape[0]
    meta = jnp.concatenate([jnp.reshape(which, (1,)), index]).astype(jnp.int32)
    return pl.pallas_call(
        functools.partial(cut_kernel, len(held), low),
        grid_spec=pltpu.PrefetchScalarGridSpec(
            num_scalar_prefetch=1,
            grid=(1,),
            in_specs=[pl.BlockSpec(memory_space=pltpu.HBM)] * len(held),
            out_specs=pl.BlockSpec(memory_space=pltpu.VMEM),
            scratch_shapes=[pltpu.SemaphoreType.DMA((count,))],
        ),
        out_shape=jax.ShapeDtypeStruct((count, piece, held[0].shape[2]), held[0].dtype),
        compiler_params=pltpu.CompilerParams(vmem_limit_bytes=60 * 2**20),
    )(meta, *held)


def place_requests(owners, per_device, pool_count, lanes):
    half = pool_count // 2
    count = owners.shape[1]
    order = jnp.arange(count, dtype=jnp.int32)
    side = (order // per_device) // half
    mate = side[:, None] == side[None, :]
    before = order[None, :] < order[:, None]
    same = owners[:, :, None] == owners[:, None, :]
    lower = owners[:, None, :] < owners[:, :, None]
    total = lambda mask: jnp.sum(mask.astype(jnp.int32), axis=2)
    rank = total(same & (mate & before)[None])
    crosses = rank >= lanes
    far = crosses[:, None, :]
    number = total(far & mate[None] & (lower | (same & before[None])))
    first = total(far & ~mate[None] & lower)
    guests = total(far & ~mate[None] & same)
    lane = jnp.where(crosses, number, first + guests + rank) % lanes
    row = jnp.where(crosses, 1 - side[None, :], side[None, :]) * half + lane % half
    return row, lane // half, crosses, number // half


def scatter_sum(total, axes):
    width = total.shape[1]
    sizes = [lax.axis_size(axis) for axis in axes]
    total = total.reshape(tuple(sizes) + (-1, width)).astype(jnp.float32)
    for at, axis in enumerate(axes):
        size, index = sizes[at], lax.axis_index(axis)
        if size & (size - 1):
            lead = (size,) + tuple(d for i, d in enumerate(total.shape) if i != at)
            parts = jnp.moveaxis(total, at, 0).astype(jnp.bfloat16)
            parts = lax.all_to_all(parts, axis, split_axis=0, concat_axis=0, tiled=True)
            total = jnp.sum(parts.reshape(lead).astype(jnp.float32), axis=0)
            total = jnp.expand_dims(total, at)
            continue
        bit = 1
        while bit < size:
            shape = total.shape
            split = total.reshape(shape[:at] + (shape[at] // 2, 2) + shape[at + 1 :])
            mine = (index // bit) % 2
            keep = lax.dynamic_index_in_dim(split, mine, at + 1, keepdims=False)
            give = lax.dynamic_index_in_dim(split, 1 - mine, at + 1, keepdims=False)
            got = lax.ppermute(
                give.astype(jnp.bfloat16), axis, [(i, i ^ bit) for i in range(size)]
            )
            total = keep + got.astype(jnp.float32)
            bit *= 2
    return total.reshape(-1, width)


def body(
    queries, cotangent, cond, nbr_owner, nbr_block, database, lengths, gain, w_down, w_up, w_kv
):
    axes = ("pool", "dp")
    pool_count = lax.axis_size("pool")
    columns = lax.axis_size("dp")
    relay_row = pool_count - 1
    half = pool_count // 2
    row = lax.axis_index("pool")
    me = lax.axis_index("dp")
    span_count, width = cond.shape[2:]
    nbr_count = nbr_owner.shape[3]
    per_device = span_count * nbr_count
    block_count, slot_len = database.shape[2:4]
    live_count = relay_row * per_device
    capacity = max(2, live_count // columns + 1)
    slots = -(-capacity // pool_count)
    lanes = half * slots
    most = 0
    if capacity > lanes:
        for rows in (half, relay_row - half):
            full, left = divmod(rows * per_device, capacity)
            most = max(most, full * (capacity - lanes) + max(0, left - lanes))
    crossing = -(-most // half)
    token_count, head_cols = queries.shape[2:]

    def hop(array, pairs):
        return lax.ppermute(
            array, axes, [(a * columns + j, b * columns + j) for a, b in pairs for j in range(columns)]
        )

    parts = PARTS if slot_len % (PARTS * 16) == 0 else 1
    piece = slot_len // parts
    store = database.reshape(block_count, slot_len, width)

    def to_all(array, axis):
        copies = jnp.broadcast_to(array[None], (lax.axis_size(axis),) + array.shape)
        return lax.all_to_all(copies, axis, split_axis=0, concat_axis=0, tiled=True)

    across = hop(store, [(relay_row, relay_row - half)])
    info = jnp.concatenate([nbr_owner.reshape(-1), nbr_block.reshape(-1), lengths.reshape(-1)])
    info = jnp.pad(info, (0, -info.shape[0] % 128))
    table = to_all(info.reshape(-1, 128), axes)
    store, across, table = lax.optimization_barrier((store, across, table))
    stores = [store, across]
    held_by = jnp.where(row == relay_row, 0, 1)
    for step in range(1, half):
        for near, array in ((relay_row, store), (relay_row - half, across)):
            held_by = jnp.where(row == near - step, len(stores), held_by)
            stores.append(hop(array, [(near, near - step)]))
    table = table.reshape(pool_count, columns, -1)
    by_column = jnp.swapaxes(table[:relay_row], 0, 1)
    owners = by_column[:, :, :per_device].reshape(columns, live_count)
    blocks = by_column[:, :, per_device : 2 * per_device].reshape(columns, live_count)
    store_len = table[relay_row, :, 2 * per_device : 2 * per_device + block_count]
    carrier, slot, crosses, number = place_requests(owners, per_device, pool_count, lanes)

    ring = jnp.arange(slots, dtype=jnp.int32)
    mine = ((owners == me) & (carrier == row))[:, None, :] & (slot[:, None, :] == ring[None, :, None])
    slot_block = jnp.sum(jnp.where(mine, blocks[:, None, :], 0), axis=2).reshape(-1)

    mine_of = lambda a: lax.dynamic_index_in_dim(a, me, 0, keepdims=False)
    my_owner, my_block, my_carrier, my_slot, my_cross, my_number = map(
        mine_of, (owners, blocks, carrier, slot, crosses, number)
    )
    place = my_owner * slots + my_slot
    ring = jnp.arange(crossing, dtype=jnp.int32)
    mine = (my_cross & (my_carrier == row))[None, :] & (my_number[None, :] == ring[:, None])
    leaving_place = jnp.sum(jnp.where(mine, place[None, :], 0), axis=1)

    def share(array, step):
        return hop(array, [(p, p // half * half + (p + step) % half) for p in range(pool_count)])

    held = []
    weight, weight_t = w_kv, None
    for i in range(parts):
        wanted = slot_block
        if i == 1:
            weight_t, wanted = lax.optimization_barrier((weight.T, wanted))
        sends = cut(held_by, wanted, stores, i * piece, piece)
        if i == 0:
            weight, sends = lax.optimization_barrier((weight, sends))
        arrived = lax.all_to_all(sends, "dp", split_axis=0, concat_axis=0, tiled=True)
        here = [arrived] + [share(arrived, step) for step in range(1, half)]
        if crossing:
            leaving = pick(0, leaving_place, [arrived])
            landed = hop(leaving, [(p, (p + half) % pool_count) for p in range(pool_count)])
            here += [landed] + [share(landed, step) for step in range(1, half)]
        held.append(here)
    weight_t = weight.T if weight_t is None else weight_t
    origin = jnp.where(my_cross, (my_carrier + half) % pool_count, my_carrier)
    which = (row - origin) % half + jnp.where(my_cross, half, 0)
    index = jnp.where(my_cross, my_number, place)
    held = [here[b] for b in range(len(held[0])) for here in held]

    own_row = jnp.minimum(row, relay_row - 1)
    hot = (my_owner * block_count + my_block)[:, None] == jnp.arange(
        columns * block_count, dtype=jnp.int32
    )[None, :]
    wanted_len = jnp.sum(jnp.where(hot, store_len.reshape(1, -1), 0), axis=1)
    own = lambda a: lax.dynamic_index_in_dim(
        a.reshape(relay_row, per_device), own_row, 0, keepdims=False
    )
    live = (row < relay_row).astype(jnp.int32)
    meta = jnp.concatenate([live[None], own(wanted_len), own(which), own(index)]).astype(jnp.int32)

    attn_out, q_grad, cond_grad, terms = run_spans(
        meta,
        queries.reshape(token_count, head_cols),
        cotangent.reshape(token_count, head_cols),
        cond.reshape(span_count, width).astype(jnp.float32),
        held,
        parts,
        gain,
        w_down,
        w_up,
        w_kv,
        weight_t,
        nbr_count,
    )

    adapter_grad = scatter_sum(terms, axes)
    return (
        attn_out.reshape(1, 1, token_count, head_cols),
        q_grad.reshape(1, 1, token_count, head_cols),
        cond_grad.reshape(1, 1, span_count, width),
        adapter_grad,
    )


def solution(mesh):
    return jax.shard_map(
        body,
        mesh=mesh,
        in_specs=(
            P("pool", "dp", None, None),
            P("pool", "dp", None, None),
            P("pool", "dp", None, None),
            P("pool", "dp", None, None),
            P("pool", "dp", None, None),
            P("pool", "dp", None, None, None),
            P("pool", "dp", None),
            P(),
            P(),
            P(),
            P(),
        ),
        out_specs=(
            P("pool", "dp", None, None),
            P("pool", "dp", None, None),
            P("pool", "dp", None, None),
            P(("pool", "dp"), None),
        ),
        check_vma=False,
    )
```

```python
import functools

import jax
import jax.numpy as jnp
from jax import lax
from jax.experimental import pallas as pl
from jax.experimental.pallas import tpu as pltpu
from jax.sharding import PartitionSpec as P

HEADS = 16
HEAD = 128
SPAN = 64
GROUP = 2

EPSILON = 1e-06
FLOOR = -1e30
LOG2E = 1.4426950408889634

NT = (((1,), (1,)), ((), ()))
TN = (((0,), (0,)), ((), ()))


def dot(a, b, dims=(((1,), (0,)), ((), ()))):
    return lax.dot_general(a, b, dims, preferred_element_type=jnp.float32)


def span_kernel(
    held_count, nbr_count, bounds, meta,
    q_ref, cot_ref, cond_ref, gain_ref, down_ref, up_ref, upt_ref, downt_ref, *rest,
):
    held_refs = rest[:held_count]
    (kv_hbm, kvt_hbm, out_ref, qg_ref, cg_ref, ad_ref,
     raw_ref, kv_ref, kvt_ref, proj_ref, grad_ref, score_ref, dprob_ref, prob_ref, dscore_ref,
     q2_ref, cot2_ref, acc_ref, sems, kv_sem) = rest[held_count:]
    step = pl.program_id(0)
    per_device, slot_len, width = raw_ref.shape
    key_count = nbr_count * slot_len
    span_count = per_device // nbr_count
    group = span_count // pl.num_programs(0)
    head_cols = q_ref.shape[1]
    rank = down_ref.shape[1]
    scaling = HEAD ** (-0.5)
    live = meta[0] == 1
    lens, which, index = 1, 1 + per_device, 1 + 2 * per_device
    parts = len(bounds) - 1
    cuts = [pl.ds(low, high - low) for low, high in zip(bounds, bounds[1:])]
    pairs = [pl.ds(i * 2 * HEAD, 2 * HEAD) for i in range(HEADS // 2)]
    value_pairs = [pl.ds(head_cols + i * 2 * HEAD, 2 * HEAD) for i in range(HEADS // 2)]
    lanes = [pl.ds(i * 2 * SPAN, 2 * SPAN) for i in range(HEADS // 2)]
    keys = [pl.ds(g * key_count, key_count) for g in range(group)]
    tokens = [pl.ds(g * SPAN, SPAN) for g in range(group)]
    double = [pl.ds(g * 2 * SPAN, 2 * SPAN) for g in range(group)]
    spots = [
        (g, cols, value_cols, lane)
        for g in range(group)
        for cols, value_cols, lane in zip(pairs, value_pairs, lanes)
    ]
    kv_copy = pltpu.make_async_copy(kv_hbm, kv_ref, kv_sem.at[0])
    kvt_copy = pltpu.make_async_copy(kvt_hbm, kvt_ref, kv_sem.at[1])

    @pl.when(step == 0)
    def _():
        for n in range(per_device):
            for b, held in enumerate(held_refs):
                @pl.when(meta[which + n] == b // parts)
                def _():
                    part = b % parts
                    pltpu.make_async_copy(
                        held.at[meta[index + n]],
                        raw_ref.at[n, cuts[part]],
                        sems.at[n * parts + part],
                    ).start()
        kv_copy.start()
        kvt_copy.start()
        q2_ref[...] = jnp.zeros_like(q2_ref)
        cot2_ref[...] = jnp.zeros_like(cot2_ref)

    for g in range(group):
        for i in range(HEADS):
            cols = pl.ds(i * HEAD, HEAD)
            part = pl.ds((2 * g + i % 2) * SPAN, SPAN)
            q2_ref[part, cols] = q_ref[tokens[g], cols]
            cot2_ref[part, cols] = cot_ref[tokens[g], cols]

    for n in range(group * nbr_count):
        for part in range(parts):
            item = step * group * nbr_count + n
            pltpu.make_async_copy(
                held_refs[part].at[0],
                raw_ref.at[item, cuts[part]],
                sems.at[item * parts + part],
            ).wait()
    x_full = jnp.concatenate(
        [
            raw_ref[pl.ds((step * group + g) * nbr_count, nbr_count)]
            .reshape(key_count, width)
            .astype(jnp.float32)
            + cond_ref[pl.ds(step * group + g, 1), :]
            for g in range(group)
        ],
        axis=0,
    )
    inv_rms = lax.rsqrt(jnp.mean(x_full * x_full, axis=-1, keepdims=True) + EPSILON)
    gain = gain_ref[...]
    hidden = (x_full * inv_rms * gain).astype(jnp.bfloat16)
    latent = dot(hidden, down_ref[...]).astype(jnp.bfloat16)
    encoded = (x_full + dot(latent, up_ref[...])).astype(jnp.bfloat16)

    @pl.when(step == 0)
    def _():
        kv_copy.wait()

    for cols in pairs + value_pairs:
        proj_ref[:, cols] = dot(encoded, kv_ref[:, cols]).astype(jnp.bfloat16)

    for g, cols, value_cols, lane in spots:
        score_ref[keys[g], lane] = dot(proj_ref[keys[g], cols], q2_ref[double[g], cols], NT)
        dprob_ref[keys[g], lane] = dot(proj_ref[keys[g], value_cols], cot2_ref[double[g], cols], NT)

    slot = lax.broadcasted_iota(jnp.int32, (key_count, 2 * SPAN), 0)
    for g in range(group):
        limit = jnp.zeros((key_count, 2 * SPAN), jnp.int32)
        for n in range(nbr_count):
            here = jnp.logical_and(slot >= n * slot_len, slot < (n + 1) * slot_len)
            item = (step * group + g) * nbr_count + n
            limit = jnp.where(here, n * slot_len + meta[lens + item], limit)
        usable = slot < limit
        for lane in lanes:
            scores = jnp.where(usable, score_ref[keys[g], lane], FLOOR)
            row_max = jnp.max(scores, axis=0, keepdims=True)
            raised = jnp.exp2((scores - row_max) * (scaling * LOG2E))
            probs = raised * (1.0 / jnp.sum(raised, axis=0, keepdims=True))
            d_probs = dprob_ref[keys[g], lane]
            delta = jnp.sum(probs * d_probs, axis=0, keepdims=True)
            prob_ref[keys[g], lane] = probs.astype(jnp.bfloat16)
            dscore_ref[keys[g], lane] = (probs * (d_probs - delta) * scaling).astype(jnp.bfloat16)

    for g, cols, value_cols, lane in spots:
        grad_ref[keys[g], cols] = dot(
            dscore_ref[keys[g], lane], q2_ref[double[g], cols]
        ).astype(jnp.bfloat16)
        grad_ref[keys[g], value_cols] = dot(
            prob_ref[keys[g], lane], cot2_ref[double[g], cols]
        ).astype(jnp.bfloat16)

    def diagonal(both):
        return jnp.concatenate([both[:SPAN, :HEAD], both[SPAN:, HEAD:]], axis=1)

    for g, cols, value_cols, lane in spots:
        out = diagonal(dot(prob_ref[keys[g], lane].T, proj_ref[keys[g], value_cols]))
        grad = diagonal(dot(dscore_ref[keys[g], lane].T, proj_ref[keys[g], cols]))
        out_ref[tokens[g], cols] = jnp.where(live, out, 0.0).astype(jnp.bfloat16)
        qg_ref[tokens[g], cols] = jnp.where(live, grad, 0.0).astype(jnp.bfloat16)

    @pl.when(step == 0)
    def _():
        kvt_copy.wait()
        acc_ref[...] = jnp.zeros_like(acc_ref)

    enc_grad = dot(grad_ref[...], kvt_ref[...]).astype(jnp.bfloat16)
    lat_grad = dot(enc_grad, upt_ref[...]).astype(jnp.bfloat16)
    scaled = dot(lat_grad, downt_ref[...]) * gain
    normed = x_full * inv_rms
    x_grad = enc_grad.astype(jnp.float32) + inv_rms * (
        scaled - normed * jnp.mean(scaled * normed, axis=-1, keepdims=True)
    )
    for g in range(group):
        span_grad = jnp.sum(
            x_grad[g * key_count : (g + 1) * key_count], axis=0, keepdims=True
        )
        cg_ref[pl.ds(step * group + g, 1), :] = jnp.where(live, span_grad, 0.0)
    acc_ref[:, :rank] += dot(hidden, lat_grad, TN)
    acc_ref[:, rank:] += dot(enc_grad, latent, TN)

    @pl.when(step == pl.num_programs(0) - 1)
    def _():
        ad_ref[...] = jnp.where(live, acc_ref[...], 0.0).astype(ad_ref.dtype)


def run_spans(meta, query, cot, cond, held, bounds, gain, w_down, w_up, w_kv, w_kv_t, nbr_count):
    span_count, width = cond.shape
    token_count, head_cols = query.shape
    slot_len = bounds[-1]
    parts = len(bounds) - 1
    rank = w_down.shape[1]
    whole = lambda a: pl.BlockSpec(a.shape, lambda s, m: (0,) * a.ndim, pipeline_mode=pl.Buffered(1))
    group = GROUP if span_count % GROUP == 0 else 1
    tokens = pl.BlockSpec((group * SPAN, head_cols), lambda s, m: (s, 0))
    small = [cond, gain.reshape(1, width), w_down, w_up, w_up.T, w_down.T]
    large = list(held) + [w_kv, w_kv_t]
    per_device = span_count * nbr_count
    keys = group * nbr_count * slot_len
    rows = per_device * slot_len
    lanes = SPAN * HEADS
    flops = 2 * rows * (2 * width * 2 * head_cols + 6 * width * rank + 6 * SPAN * head_cols)
    return pl.pallas_call(
        functools.partial(span_kernel, len(held), nbr_count, bounds),
        grid_spec=pltpu.PrefetchScalarGridSpec(
            num_scalar_prefetch=1,
            grid=(span_count // group,),
            in_specs=[tokens, tokens]
            + [whole(a) for a in small]
            + [pl.BlockSpec(memory_space=pltpu.HBM)] * len(large),
            out_specs=[
                tokens,
                tokens,
                pl.BlockSpec((span_count, width), lambda s, m: (0, 0)),
                pl.BlockSpec((width, 2 * rank), lambda s, m: (0, 0)),
            ],
            scratch_shapes=[
                pltpu.VMEM((per_device, slot_len, width), jnp.bfloat16),
                pltpu.VMEM((width, 2 * head_cols), jnp.bfloat16),
                pltpu.VMEM((2 * head_cols, width), jnp.bfloat16),
                pltpu.VMEM((keys, 2 * head_cols), jnp.bfloat16),
                pltpu.VMEM((keys, 2 * head_cols), jnp.bfloat16),
                pltpu.VMEM((keys, lanes), jnp.float32),
                pltpu.VMEM((keys, lanes), jnp.float32),
                pltpu.VMEM((keys, lanes), jnp.bfloat16),
                pltpu.VMEM((keys, lanes), jnp.bfloat16),
                pltpu.VMEM((group * 2 * SPAN, head_cols), jnp.bfloat16),
                pltpu.VMEM((group * 2 * SPAN, head_cols), jnp.bfloat16),
                pltpu.VMEM((width, 2 * rank), jnp.float32),
                pltpu.SemaphoreType.DMA((per_device * parts,)),
                pltpu.SemaphoreType.DMA((2,)),
            ],
        ),
        out_shape=[
            jax.ShapeDtypeStruct((token_count, head_cols), jnp.bfloat16),
            jax.ShapeDtypeStruct((token_count, head_cols), jnp.bfloat16),
            jax.ShapeDtypeStruct((span_count, width), jnp.float32),
            jax.ShapeDtypeStruct((width, 2 * rank), jnp.float32),
        ],
        compiler_params=pltpu.CompilerParams(vmem_limit_bytes=60 * 2**20),
        cost_estimate=pl.CostEstimate(
            flops=flops, bytes_accessed=16 * 2**20, transcendentals=rows * SPAN * HEADS
        ),
    )(meta, query, cot, *small, *large)


def pick_kernel(held_count, meta, *refs):
    held_refs, out_ref = refs[:held_count], refs[held_count]
    for b, held in enumerate(held_refs):
        @pl.when(meta[0] == b)
        def _():
            for n in range(out_ref.shape[0]):
                out_ref[n] = held[meta[1 + n]]


def pick(which, index, held):
    count = index.shape[0]
    meta = jnp.concatenate([jnp.reshape(which, (1,)), index]).astype(jnp.int32)
    return pl.pallas_call(
        functools.partial(pick_kernel, len(held)),
        grid_spec=pltpu.PrefetchScalarGridSpec(
            num_scalar_prefetch=1,
            grid=(1,),
            in_specs=[pl.BlockSpec(memory_space=pltpu.VMEM)] * len(held),
            out_specs=pl.BlockSpec(memory_space=pltpu.VMEM),
        ),
        out_shape=jax.ShapeDtypeStruct((count,) + held[0].shape[1:], held[0].dtype),
        compiler_params=pltpu.CompilerParams(vmem_limit_bytes=16 * 2**20),
    )(meta, *held)


def place_requests(owners, per_device, pool_count, lanes):
    half = pool_count // 2
    count = owners.shape[1]
    order = jnp.arange(count, dtype=jnp.int32)
    side = (order // per_device) // half
    mate = side[:, None] == side[None, :]
    before = order[None, :] < order[:, None]
    same = owners[:, :, None] == owners[:, None, :]
    lower = owners[:, None, :] < owners[:, :, None]
    total = lambda mask: jnp.sum(mask.astype(jnp.int32), axis=2)
    rank = total(same & (mate & before)[None])
    crosses = rank >= lanes
    far = crosses[:, None, :]
    number = total(far & mate[None] & (lower | (same & before[None])))
    first = total(far & ~mate[None] & lower)
    guests = total(far & ~mate[None] & same)
    lane = jnp.where(crosses, number, first + guests + rank) % lanes
    row = jnp.where(crosses, 1 - side[None, :], side[None, :]) * half + lane % half
    return row, lane // half, crosses, number // half


def scatter_sum(total, axes):
    width = total.shape[1]
    sizes = [lax.axis_size(axis) for axis in axes]
    total = total.reshape(tuple(sizes) + (-1, width)).astype(jnp.float32)
    for at, axis in enumerate(axes):
        size, index = sizes[at], lax.axis_index(axis)
        if size & (size - 1):
            lead = (size,) + tuple(d for i, d in enumerate(total.shape) if i != at)
            parts = jnp.moveaxis(total, at, 0).astype(jnp.bfloat16)
            parts = lax.all_to_all(parts, axis, split_axis=0, concat_axis=0, tiled=True)
            total = jnp.sum(parts.reshape(lead).astype(jnp.float32), axis=0)
            total = jnp.expand_dims(total, at)
            continue
        bit = 1
        while bit < size:
            shape = total.shape
            split = total.reshape(shape[:at] + (shape[at] // 2, 2) + shape[at + 1 :])
            mine = (index // bit) % 2
            keep = lax.dynamic_index_in_dim(split, mine, at + 1, keepdims=False)
            give = lax.dynamic_index_in_dim(split, 1 - mine, at + 1, keepdims=False)
            got = lax.ppermute(
                give.astype(jnp.bfloat16), axis, [(i, i ^ bit) for i in range(size)]
            )
            total = keep + got.astype(jnp.float32)
            bit *= 2
    return total.reshape(-1, width)


def body(
    queries, cotangent, cond, nbr_owner, nbr_block, database, lengths, gain, w_down, w_up, w_kv
):
    axes = ("pool", "dp")
    pool_count = lax.axis_size("pool")
    columns = lax.axis_size("dp")
    relay_row = pool_count - 1
    half = pool_count // 2
    row = lax.axis_index("pool")
    me = lax.axis_index("dp")
    span_count, width = cond.shape[2:]
    nbr_count = nbr_owner.shape[3]
    per_device = span_count * nbr_count
    block_count, slot_len = database.shape[2:4]
    live_count = relay_row * per_device
    capacity = max(2, live_count // columns + 1)
    slots = -(-capacity // pool_count)
    lanes = half * slots
    most = 0
    if capacity > lanes:
        for rows in (half, relay_row - half):
            full, left = divmod(rows * per_device, capacity)
            most = max(most, full * (capacity - lanes) + max(0, left - lanes))
    crossing = -(-most // half)
    token_count, head_cols = queries.shape[2:]

    def hop(array, pairs):
        return lax.ppermute(
            array, axes, [(a * columns + j, b * columns + j) for a, b in pairs for j in range(columns)]
        )

    first = slot_len // 16 * 3 // 4 * 16
    bounds = [0, first, slot_len] if 0 < first < slot_len else [0, slot_len]
    parts = len(bounds) - 1
    full_store = database.reshape(block_count, slot_len, width)
    cut = lambda i: full_store[:, bounds[i] : bounds[i + 1]]
    store = [cut(0)]

    def to_all(array, axis):
        copies = jnp.broadcast_to(array[None], (lax.axis_size(axis),) + array.shape)
        return lax.all_to_all(copies, axis, split_axis=0, concat_axis=0, tiled=True)

    info = jnp.concatenate([nbr_owner.reshape(-1), nbr_block.reshape(-1), lengths.reshape(-1)])
    info = jnp.pad(info, (0, -info.shape[0] % 128))
    over = lambda a: hop(a, [(relay_row, relay_row - half)])
    across = [over(store[0])]
    table = to_all(info.reshape(-1, 128), axes)
    full_store, across, table = lax.optimization_barrier((full_store, across, table))
    store += [cut(i) for i in range(1, parts)]
    across += [over(a) for a in store[1:]]
    table = table.reshape(pool_count, columns, -1)
    by_column = jnp.swapaxes(table[:relay_row], 0, 1)
    owners = by_column[:, :, :per_device].reshape(columns, live_count)
    blocks = by_column[:, :, per_device : 2 * per_device].reshape(columns, live_count)
    store_len = table[relay_row, :, 2 * per_device : 2 * per_device + block_count]
    carrier, slot, crosses, number = place_requests(owners, per_device, pool_count, lanes)

    ring = jnp.arange(slots, dtype=jnp.int32)
    mine = ((owners == me) & (carrier == row))[:, None, :] & (slot[:, None, :] == ring[None, :, None])
    slot_block = jnp.sum(jnp.where(mine, blocks[:, None, :], 0), axis=2).reshape(-1)

    mine_of = lambda a: lax.dynamic_index_in_dim(a, me, 0, keepdims=False)
    my_owner, my_block, my_carrier, my_slot, my_cross, my_number = map(
        mine_of, (owners, blocks, carrier, slot, crosses, number)
    )
    place = my_owner * slots + my_slot
    ring = jnp.arange(crossing, dtype=jnp.int32)
    mine = (my_cross & (my_carrier == row))[None, :] & (my_number[None, :] == ring[:, None])
    leaving_place = jnp.sum(jnp.where(mine, place[None, :], 0), axis=1)

    def share(array, step):
        return hop(array, [(p, p // half * half + (p + step) % half) for p in range(pool_count)])

    held = []
    weight, weight_t = w_kv, None
    for i in range(parts):
        near = jnp.where(row == relay_row, store[i], across[i])
        stores = [near]
        held_by = jnp.where(row % half == half - 1, 0, 1)
        for step in range(1, half):
            stores.append(hop(near, [(p, p - step) for p in (relay_row, relay_row - half)]))
            held_by = jnp.where(row % half == half - 1 - step, step, held_by)
        wanted = slot_block
        if i == 1:
            weight_t, wanted = lax.optimization_barrier((weight.T, wanted))
        sends = pick(held_by, wanted, stores)
        if i == 0:
            weight, sends = lax.optimization_barrier((weight, sends))
        arrived = lax.all_to_all(sends, "dp", split_axis=0, concat_axis=0, tiled=True)
        here = [arrived] + [share(arrived, step) for step in range(1, half)]
        if crossing:
            leaving = pick(0, leaving_place, [arrived])
            landed = hop(leaving, [(p, (p + half) % pool_count) for p in range(pool_count)])
            here += [landed] + [share(landed, step) for step in range(1, half)]
        held.append(here)
    weight_t = weight.T if weight_t is None else weight_t
    origin = jnp.where(my_cross, (my_carrier + half) % pool_count, my_carrier)
    which = (row - origin) % half + jnp.where(my_cross, half, 0)
    index = jnp.where(my_cross, my_number, place)
    held = [here[b] for b in range(len(held[0])) for here in held]

    own_row = jnp.minimum(row, relay_row - 1)
    hot = (my_owner * block_count + my_block)[:, None] == jnp.arange(
        columns * block_count, dtype=jnp.int32
    )[None, :]
    wanted_len = jnp.sum(jnp.where(hot, store_len.reshape(1, -1), 0), axis=1)
    own = lambda a: lax.dynamic_index_in_dim(
        a.reshape(relay_row, per_device), own_row, 0, keepdims=False
    )
    live = (row < relay_row).astype(jnp.int32)
    meta = jnp.concatenate([live[None], own(wanted_len), own(which), own(index)]).astype(jnp.int32)

    attn_out, q_grad, cond_grad, terms = run_spans(
        meta,
        queries.reshape(token_count, head_cols),
        cotangent.reshape(token_count, head_cols),
        cond.reshape(span_count, width).astype(jnp.float32),
        held,
        bounds,
        gain,
        w_down,
        w_up,
        w_kv,
        weight_t,
        nbr_count,
    )

    adapter_grad = scatter_sum(terms, axes)
    return (
        attn_out.reshape(1, 1, token_count, head_cols),
        q_grad.reshape(1, 1, token_count, head_cols),
        cond_grad.reshape(1, 1, span_count, width),
        adapter_grad,
    )


def solution(mesh):
    return jax.shard_map(
        body,
        mesh=mesh,
        in_specs=(
            P("pool", "dp", None, None),
            P("pool", "dp", None, None),
            P("pool", "dp", None, None),
            P("pool", "dp", None, None),
            P("pool", "dp", None, None),
            P("pool", "dp", None, None, None),
            P("pool", "dp", None),
            P(),
            P(),
            P(),
            P(),
        ),
        out_specs=(
            P("pool", "dp", None, None),
            P("pool", "dp", None, None),
            P("pool", "dp", None, None),
            P(("pool", "dp"), None),
        ),
        check_vma=False,
    )
```

```python
import functools

import jax
import jax.numpy as jnp
from jax import lax
from jax.experimental import pallas as pl
from jax.experimental.pallas import tpu as pltpu
from jax.sharding import PartitionSpec as P

HEADS = 16
HEAD = 128
SPAN = 64
GROUP = 2

EPSILON = 1e-06
FLOOR = -1e30
LOG2E = 1.4426950408889634

NT = (((1,), (1,)), ((), ()))
TN = (((0,), (0,)), ((), ()))


def dot(a, b, dims=(((1,), (0,)), ((), ()))):
    return lax.dot_general(a, b, dims, preferred_element_type=jnp.float32)


def span_kernel(
    held_count, nbr_count, bounds, meta,
    q_ref, cot_ref, cond_ref, gain_ref, down_ref, up_ref, upt_ref, downt_ref, *rest,
):
    held_refs = rest[:held_count]
    (kv_hbm, kvt_hbm, out_ref, qg_ref, cg_ref, ad_ref,
     raw_ref, kv_ref, kvt_ref, proj_ref, grad_ref, score_ref, dprob_ref,
     q2_ref, cot2_ref, acc_ref, sems, kv_sem) = rest[held_count:]
    step = pl.program_id(0)
    per_device, slot_len, width = raw_ref.shape
    key_count = nbr_count * slot_len
    span_count = per_device // nbr_count
    group = span_count // pl.num_programs(0)
    head_cols = q_ref.shape[1]
    rank = down_ref.shape[1]
    scaling = HEAD ** (-0.5)
    live = meta[0] == 1
    lens, which, index = 1, 1 + per_device, 1 + 2 * per_device
    parts = len(bounds) - 1
    cuts = [pl.ds(low, high - low) for low, high in zip(bounds, bounds[1:])]
    pairs = [pl.ds(i * 2 * HEAD, 2 * HEAD) for i in range(HEADS // 2)]
    value_pairs = [pl.ds(head_cols + i * 2 * HEAD, 2 * HEAD) for i in range(HEADS // 2)]
    lanes = [pl.ds(i * 2 * SPAN, 2 * SPAN) for i in range(HEADS // 2)]
    keys = [pl.ds(g * key_count, key_count) for g in range(group)]
    tokens = [pl.ds(g * SPAN, SPAN) for g in range(group)]
    double = [pl.ds(g * 2 * SPAN, 2 * SPAN) for g in range(group)]
    spots = [
        (g, cols, value_cols, lane)
        for g in range(group)
        for cols, value_cols, lane in zip(pairs, value_pairs, lanes)
    ]
    kv_copy = pltpu.make_async_copy(kv_hbm, kv_ref, kv_sem.at[0])
    kvt_copy = pltpu.make_async_copy(kvt_hbm, kvt_ref, kv_sem.at[1])

    @pl.when(step == 0)
    def _():
        for n in range(per_device):
            for b, held in enumerate(held_refs):
                @pl.when(meta[which + n] == b // parts)
                def _():
                    part = b % parts
                    pltpu.make_async_copy(
                        held.at[meta[index + n]],
                        raw_ref.at[n, cuts[part]],
                        sems.at[n * parts + part],
                    ).start()
        kv_copy.start()
        kvt_copy.start()
        q2_ref[...] = jnp.zeros_like(q2_ref)
        cot2_ref[...] = jnp.zeros_like(cot2_ref)

    for g in range(group):
        for i in range(HEADS):
            cols = pl.ds(i * HEAD, HEAD)
            part = pl.ds((2 * g + i % 2) * SPAN, SPAN)
            q2_ref[part, cols] = q_ref[tokens[g], cols]
            cot2_ref[part, cols] = cot_ref[tokens[g], cols]

    for n in range(group * nbr_count):
        for part in range(parts):
            item = step * group * nbr_count + n
            pltpu.make_async_copy(
                held_refs[part].at[0],
                raw_ref.at[item, cuts[part]],
                sems.at[item * parts + part],
            ).wait()
    x_full = jnp.concatenate(
        [
            raw_ref[pl.ds((step * group + g) * nbr_count, nbr_count)]
            .reshape(key_count, width)
            .astype(jnp.float32)
            + cond_ref[pl.ds(step * group + g, 1), :]
            for g in range(group)
        ],
        axis=0,
    )
    inv_rms = lax.rsqrt(jnp.mean(x_full * x_full, axis=-1, keepdims=True) + EPSILON)
    gain = gain_ref[...]
    hidden = (x_full * inv_rms * gain).astype(jnp.bfloat16)
    latent = dot(hidden, down_ref[...]).astype(jnp.bfloat16)
    encoded = (x_full + dot(latent, up_ref[...])).astype(jnp.bfloat16)

    @pl.when(step == 0)
    def _():
        kv_copy.wait()

    for cols in pairs + value_pairs:
        proj_ref[:, cols] = dot(encoded, kv_ref[:, cols]).astype(jnp.bfloat16)

    for g, cols, value_cols, lane in spots:
        score_ref[keys[g], lane] = dot(proj_ref[keys[g], cols], q2_ref[double[g], cols], NT)
        dprob_ref[keys[g], lane] = dot(proj_ref[keys[g], value_cols], cot2_ref[double[g], cols], NT)

    def diagonal(both):
        return jnp.concatenate([both[:SPAN, :HEAD], both[SPAN:, HEAD:]], axis=1)

    slot = lax.broadcasted_iota(jnp.int32, (key_count, 2 * SPAN), 0)
    for g in range(group):
        limit = jnp.zeros((key_count, 2 * SPAN), jnp.int32)
        for n in range(nbr_count):
            here = jnp.logical_and(slot >= n * slot_len, slot < (n + 1) * slot_len)
            item = (step * group + g) * nbr_count + n
            limit = jnp.where(here, n * slot_len + meta[lens + item], limit)
        usable = slot < limit
        for cols, value_cols, lane in zip(pairs, value_pairs, lanes):
            scores = jnp.where(usable, score_ref[keys[g], lane], FLOOR)
            row_max = jnp.max(scores, axis=0, keepdims=True)
            raised = jnp.exp2((scores - row_max) * (scaling * LOG2E))
            probs = raised * (1.0 / jnp.sum(raised, axis=0, keepdims=True))
            d_probs = dprob_ref[keys[g], lane]
            delta = jnp.sum(probs * d_probs, axis=0, keepdims=True)
            probs_b = probs.astype(jnp.bfloat16)
            d_scores = (probs * (d_probs - delta) * scaling).astype(jnp.bfloat16)
            grad_ref[keys[g], cols] = dot(d_scores, q2_ref[double[g], cols]).astype(jnp.bfloat16)
            grad_ref[keys[g], value_cols] = dot(probs_b, cot2_ref[double[g], cols]).astype(
                jnp.bfloat16
            )
            out = diagonal(dot(probs_b.T, proj_ref[keys[g], value_cols]))
            grad = diagonal(dot(d_scores.T, proj_ref[keys[g], cols]))
            out_ref[tokens[g], cols] = jnp.where(live, out, 0.0).astype(jnp.bfloat16)
            qg_ref[tokens[g], cols] = jnp.where(live, grad, 0.0).astype(jnp.bfloat16)

    @pl.when(step == 0)
    def _():
        kvt_copy.wait()
        acc_ref[...] = jnp.zeros_like(acc_ref)

    enc_grad = dot(grad_ref[...], kvt_ref[...]).astype(jnp.bfloat16)
    lat_grad = dot(enc_grad, upt_ref[...]).astype(jnp.bfloat16)
    scaled = dot(lat_grad, downt_ref[...]) * gain
    normed = x_full * inv_rms
    x_grad = enc_grad.astype(jnp.float32) + inv_rms * (
        scaled - normed * jnp.mean(scaled * normed, axis=-1, keepdims=True)
    )
    for g in range(group):
        span_grad = jnp.sum(
            x_grad[g * key_count : (g + 1) * key_count], axis=0, keepdims=True
        )
        cg_ref[pl.ds(step * group + g, 1), :] = jnp.where(live, span_grad, 0.0)
    acc_ref[:, :rank] += dot(hidden, lat_grad, TN)
    acc_ref[:, rank:] += dot(enc_grad, latent, TN)

    @pl.when(step == pl.num_programs(0) - 1)
    def _():
        ad_ref[...] = jnp.where(live, acc_ref[...], 0.0).astype(ad_ref.dtype)


def run_spans(meta, query, cot, cond, held, bounds, gain, w_down, w_up, w_kv, w_kv_t, nbr_count):
    span_count, width = cond.shape
    token_count, head_cols = query.shape
    slot_len = bounds[-1]
    parts = len(bounds) - 1
    rank = w_down.shape[1]
    whole = lambda a: pl.BlockSpec(a.shape, lambda s, m: (0,) * a.ndim, pipeline_mode=pl.Buffered(1))
    group = GROUP if span_count % GROUP == 0 else 1
    tokens = pl.BlockSpec((group * SPAN, head_cols), lambda s, m: (s, 0))
    small = [cond, gain.reshape(1, width), w_down, w_up, w_up.T, w_down.T]
    large = list(held) + [w_kv, w_kv_t]
    per_device = span_count * nbr_count
    keys = group * nbr_count * slot_len
    rows = per_device * slot_len
    lanes = SPAN * HEADS
    flops = 2 * rows * (2 * width * 2 * head_cols + 6 * width * rank + 6 * SPAN * head_cols)
    return pl.pallas_call(
        functools.partial(span_kernel, len(held), nbr_count, bounds),
        grid_spec=pltpu.PrefetchScalarGridSpec(
            num_scalar_prefetch=1,
            grid=(span_count // group,),
            in_specs=[tokens, tokens]
            + [whole(a) for a in small]
            + [pl.BlockSpec(memory_space=pltpu.HBM)] * len(large),
            out_specs=[
                tokens,
                tokens,
                pl.BlockSpec((span_count, width), lambda s, m: (0, 0)),
                pl.BlockSpec((width, 2 * rank), lambda s, m: (0, 0)),
            ],
            scratch_shapes=[
                pltpu.VMEM((per_device, slot_len, width), jnp.bfloat16),
                pltpu.VMEM((width, 2 * head_cols), jnp.bfloat16),
                pltpu.VMEM((2 * head_cols, width), jnp.bfloat16),
                pltpu.VMEM((keys, 2 * head_cols), jnp.bfloat16),
                pltpu.VMEM((keys, 2 * head_cols), jnp.bfloat16),
                pltpu.VMEM((keys, lanes), jnp.float32),
                pltpu.VMEM((keys, lanes), jnp.float32),
                pltpu.VMEM((group * 2 * SPAN, head_cols), jnp.bfloat16),
                pltpu.VMEM((group * 2 * SPAN, head_cols), jnp.bfloat16),
                pltpu.VMEM((width, 2 * rank), jnp.float32),
                pltpu.SemaphoreType.DMA((per_device * parts,)),
                pltpu.SemaphoreType.DMA((2,)),
            ],
        ),
        out_shape=[
            jax.ShapeDtypeStruct((token_count, head_cols), jnp.bfloat16),
            jax.ShapeDtypeStruct((token_count, head_cols), jnp.bfloat16),
            jax.ShapeDtypeStruct((span_count, width), jnp.float32),
            jax.ShapeDtypeStruct((width, 2 * rank), jnp.float32),
        ],
        compiler_params=pltpu.CompilerParams(vmem_limit_bytes=60 * 2**20),
        cost_estimate=pl.CostEstimate(
            flops=flops, bytes_accessed=16 * 2**20, transcendentals=rows * SPAN * HEADS
        ),
    )(meta, query, cot, *small, *large)


def pick_kernel(held_count, meta, *refs):
    held_refs, out_ref = refs[:held_count], refs[held_count]
    for b, held in enumerate(held_refs):
        @pl.when(meta[0] == b)
        def _():
            for n in range(out_ref.shape[0]):
                out_ref[n] = held[meta[1 + n]]


def pick(which, index, held):
    count = index.shape[0]
    meta = jnp.concatenate([jnp.reshape(which, (1,)), index]).astype(jnp.int32)
    return pl.pallas_call(
        functools.partial(pick_kernel, len(held)),
        grid_spec=pltpu.PrefetchScalarGridSpec(
            num_scalar_prefetch=1,
            grid=(1,),
            in_specs=[pl.BlockSpec(memory_space=pltpu.VMEM)] * len(held),
            out_specs=pl.BlockSpec(memory_space=pltpu.VMEM),
        ),
        out_shape=jax.ShapeDtypeStruct((count,) + held[0].shape[1:], held[0].dtype),
        compiler_params=pltpu.CompilerParams(vmem_limit_bytes=16 * 2**20),
    )(meta, *held)


def place_requests(owners, per_device, pool_count, lanes):
    half = pool_count // 2
    count = owners.shape[1]
    order = jnp.arange(count, dtype=jnp.int32)
    side = (order // per_device) // half
    mate = side[:, None] == side[None, :]
    before = order[None, :] < order[:, None]
    same = owners[:, :, None] == owners[:, None, :]
    lower = owners[:, None, :] < owners[:, :, None]
    total = lambda mask: jnp.sum(mask.astype(jnp.int32), axis=2)
    rank = total(same & (mate & before)[None])
    crosses = rank >= lanes
    far = crosses[:, None, :]
    number = total(far & mate[None] & (lower | (same & before[None])))
    first = total(far & ~mate[None] & lower)
    guests = total(far & ~mate[None] & same)
    lane = jnp.where(crosses, number, first + guests + rank) % lanes
    row = jnp.where(crosses, 1 - side[None, :], side[None, :]) * half + lane % half
    return row, lane // half, crosses, number // half


def scatter_sum(total, axes):
    width = total.shape[1]
    sizes = [lax.axis_size(axis) for axis in axes]
    total = total.reshape(tuple(sizes) + (-1, width)).astype(jnp.float32)
    for at, axis in enumerate(axes):
        size, index = sizes[at], lax.axis_index(axis)
        if size & (size - 1):
            lead = (size,) + tuple(d for i, d in enumerate(total.shape) if i != at)
            parts = jnp.moveaxis(total, at, 0).astype(jnp.bfloat16)
            parts = lax.all_to_all(parts, axis, split_axis=0, concat_axis=0, tiled=True)
            total = jnp.sum(parts.reshape(lead).astype(jnp.float32), axis=0)
            total = jnp.expand_dims(total, at)
            continue
        bit = 1
        while bit < size:
            shape = total.shape
            split = total.reshape(shape[:at] + (shape[at] // 2, 2) + shape[at + 1 :])
            mine = (index // bit) % 2
            keep = lax.dynamic_index_in_dim(split, mine, at + 1, keepdims=False)
            give = lax.dynamic_index_in_dim(split, 1 - mine, at + 1, keepdims=False)
            got = lax.ppermute(
                give.astype(jnp.bfloat16), axis, [(i, i ^ bit) for i in range(size)]
            )
            total = keep + got.astype(jnp.float32)
            bit *= 2
    return total.reshape(-1, width)


def body(
    queries, cotangent, cond, nbr_owner, nbr_block, database, lengths, gain, w_down, w_up, w_kv
):
    axes = ("pool", "dp")
    pool_count = lax.axis_size("pool")
    columns = lax.axis_size("dp")
    relay_row = pool_count - 1
    half = pool_count // 2
    row = lax.axis_index("pool")
    me = lax.axis_index("dp")
    span_count, width = cond.shape[2:]
    nbr_count = nbr_owner.shape[3]
    per_device = span_count * nbr_count
    block_count, slot_len = database.shape[2:4]
    live_count = relay_row * per_device
    capacity = max(2, live_count // columns + 1)
    slots = -(-capacity // pool_count)
    lanes = half * slots
    most = 0
    if capacity > lanes:
        for rows in (half, relay_row - half):
            full, left = divmod(rows * per_device, capacity)
            most = max(most, full * (capacity - lanes) + max(0, left - lanes))
    crossing = -(-most // half)
    token_count, head_cols = queries.shape[2:]

    def hop(array, pairs):
        return lax.ppermute(
            array, axes, [(a * columns + j, b * columns + j) for a, b in pairs for j in range(columns)]
        )

    first = slot_len // 16 * 3 // 4 * 16
    bounds = [0, first, slot_len] if 0 < first < slot_len else [0, slot_len]
    parts = len(bounds) - 1
    full_store = database.reshape(block_count, slot_len, width)
    cut = lambda i: full_store[:, bounds[i] : bounds[i + 1]]
    store = [cut(0)]

    def to_all(array, axis):
        copies = jnp.broadcast_to(array[None], (lax.axis_size(axis),) + array.shape)
        return lax.all_to_all(copies, axis, split_axis=0, concat_axis=0, tiled=True)

    info = jnp.concatenate([nbr_owner.reshape(-1), nbr_block.reshape(-1), lengths.reshape(-1)])
    info = jnp.pad(info, (0, -info.shape[0] % 128))
    over = lambda a: hop(a, [(relay_row, relay_row - half)])
    across = [over(store[0])]
    table = to_all(info.reshape(-1, 128), axes)
    w_kv_t = w_kv.T
    full_store, across, table, w_kv_t = lax.optimization_barrier(
        (full_store, across, table, w_kv_t)
    )
    store += [cut(i) for i in range(1, parts)]
    across += [over(a) for a in store[1:]]
    table = table.reshape(pool_count, columns, -1)
    by_column = jnp.swapaxes(table[:relay_row], 0, 1)
    owners = by_column[:, :, :per_device].reshape(columns, live_count)
    blocks = by_column[:, :, per_device : 2 * per_device].reshape(columns, live_count)
    store_len = table[relay_row, :, 2 * per_device : 2 * per_device + block_count]
    carrier, slot, crosses, number = place_requests(owners, per_device, pool_count, lanes)

    ring = jnp.arange(slots, dtype=jnp.int32)
    mine = ((owners == me) & (carrier == row))[:, None, :] & (slot[:, None, :] == ring[None, :, None])
    slot_block = jnp.sum(jnp.where(mine, blocks[:, None, :], 0), axis=2).reshape(-1)

    mine_of = lambda a: lax.dynamic_index_in_dim(a, me, 0, keepdims=False)
    my_owner, my_block, my_carrier, my_slot, my_cross, my_number = map(
        mine_of, (owners, blocks, carrier, slot, crosses, number)
    )
    place = my_owner * slots + my_slot
    ring = jnp.arange(crossing, dtype=jnp.int32)
    mine = (my_cross & (my_carrier == row))[None, :] & (my_number[None, :] == ring[:, None])
    leaving_place = jnp.sum(jnp.where(mine, place[None, :], 0), axis=1)

    def share(array, step):
        return hop(array, [(p, p // half * half + (p + step) % half) for p in range(pool_count)])

    held = []
    for i in range(parts):
        near = jnp.where(row == relay_row, store[i], across[i])
        stores = [near]
        held_by = jnp.where(row % half == half - 1, 0, 1)
        for step in range(1, half):
            stores.append(hop(near, [(p, p - step) for p in (relay_row, relay_row - half)]))
            held_by = jnp.where(row % half == half - 1 - step, step, held_by)
        sends = pick(held_by, slot_block, stores)
        arrived = lax.all_to_all(sends, "dp", split_axis=0, concat_axis=0, tiled=True)
        here = [arrived] + [share(arrived, step) for step in range(1, half)]
        if crossing:
            leaving = pick(0, leaving_place, [arrived])
            landed = hop(leaving, [(p, (p + half) % pool_count) for p in range(pool_count)])
            here += [landed] + [share(landed, step) for step in range(1, half)]
        held.append(here)
    origin = jnp.where(my_cross, (my_carrier + half) % pool_count, my_carrier)
    which = (row - origin) % half + jnp.where(my_cross, half, 0)
    index = jnp.where(my_cross, my_number, place)
    held = [here[b] for b in range(len(held[0])) for here in held]

    own_row = jnp.minimum(row, relay_row - 1)
    hot = (my_owner * block_count + my_block)[:, None] == jnp.arange(
        columns * block_count, dtype=jnp.int32
    )[None, :]
    wanted_len = jnp.sum(jnp.where(hot, store_len.reshape(1, -1), 0), axis=1)
    own = lambda a: lax.dynamic_index_in_dim(
        a.reshape(relay_row, per_device), own_row, 0, keepdims=False
    )
    live = (row < relay_row).astype(jnp.int32)
    meta = jnp.concatenate([live[None], own(wanted_len), own(which), own(index)]).astype(jnp.int32)

    attn_out, q_grad, cond_grad, terms = run_spans(
        meta,
        queries.reshape(token_count, head_cols),
        cotangent.reshape(token_count, head_cols),
        cond.reshape(span_count, width).astype(jnp.float32),
        held,
        bounds,
        gain,
        w_down,
        w_up,
        w_kv,
        w_kv_t,
        nbr_count,
    )

    adapter_grad = scatter_sum(terms, axes)
    return (
        attn_out.reshape(1, 1, token_count, head_cols),
        q_grad.reshape(1, 1, token_count, head_cols),
        cond_grad.reshape(1, 1, span_count, width),
        adapter_grad,
    )


def solution(mesh):
    return jax.shard_map(
        body,
        mesh=mesh,
        in_specs=(
            P("pool", "dp", None, None),
            P("pool", "dp", None, None),
            P("pool", "dp", None, None),
            P("pool", "dp", None, None),
            P("pool", "dp", None, None),
            P("pool", "dp", None, None, None),
            P("pool", "dp", None),
            P(),
            P(),
            P(),
            P(),
        ),
        out_specs=(
            P("pool", "dp", None, None),
            P("pool", "dp", None, None),
            P("pool", "dp", None, None),
            P(("pool", "dp"), None),
        ),
        check_vma=False,
    )
```

```python
import functools

import jax
import jax.numpy as jnp
from jax import lax
from jax.experimental import pallas as pl
from jax.experimental.pallas import tpu as pltpu
from jax.sharding import PartitionSpec as P

HEADS = 16
HEAD = 128
SPAN = 64
GROUP = 2

EPSILON = 1e-06
FLOOR = -1e30
LOG2E = 1.4426950408889634

NT = (((1,), (1,)), ((), ()))
TN = (((0,), (0,)), ((), ()))


def dot(a, b, dims=(((1,), (0,)), ((), ()))):
    return lax.dot_general(a, b, dims, preferred_element_type=jnp.float32)


def span_kernel(
    held_count, nbr_count, bounds, meta,
    q_ref, cot_ref, cond_ref, gain_ref, down_ref, up_ref, upt_ref, downt_ref, *rest,
):
    held_refs = rest[:held_count]
    (kv_hbm, kvt_hbm, out_ref, qg_ref, cg_ref, ad_ref,
     raw_ref, kv_ref, kvt_ref, proj_ref, grad_ref,
     q2_ref, cot2_ref, acc_ref, sems, kv_sem) = rest[held_count:]
    step = pl.program_id(0)
    per_device, slot_len, width = raw_ref.shape
    key_count = nbr_count * slot_len
    span_count = per_device // nbr_count
    group = span_count // pl.num_programs(0)
    head_cols = q_ref.shape[1]
    rank = down_ref.shape[1]
    scaling = HEAD ** (-0.5)
    live = meta[0] == 1
    lens, which, index = 1, 1 + per_device, 1 + 2 * per_device
    parts = len(bounds) - 1
    cuts = [pl.ds(low, high - low) for low, high in zip(bounds, bounds[1:])]
    pairs = [pl.ds(i * 2 * HEAD, 2 * HEAD) for i in range(HEADS // 2)]
    value_pairs = [pl.ds(head_cols + i * 2 * HEAD, 2 * HEAD) for i in range(HEADS // 2)]
    keys = [pl.ds(g * key_count, key_count) for g in range(group)]
    tokens = [pl.ds(g * SPAN, SPAN) for g in range(group)]
    double = [pl.ds(g * 2 * SPAN, 2 * SPAN) for g in range(group)]
    kv_copy = pltpu.make_async_copy(kv_hbm, kv_ref, kv_sem.at[0])
    kvt_copy = pltpu.make_async_copy(kvt_hbm, kvt_ref, kv_sem.at[1])

    @pl.when(step == 0)
    def _():
        for n in range(per_device):
            for b, held in enumerate(held_refs):
                @pl.when(meta[which + n] == b // parts)
                def _():
                    part = b % parts
                    pltpu.make_async_copy(
                        held.at[meta[index + n]],
                        raw_ref.at[n, cuts[part]],
                        sems.at[n * parts + part],
                    ).start()
        kv_copy.start()
        kvt_copy.start()
        q2_ref[...] = jnp.zeros_like(q2_ref)
        cot2_ref[...] = jnp.zeros_like(cot2_ref)

    for g in range(group):
        for i in range(HEADS):
            cols = pl.ds(i * HEAD, HEAD)
            part = pl.ds((2 * g + i % 2) * SPAN, SPAN)
            q2_ref[part, cols] = q_ref[tokens[g], cols]
            cot2_ref[part, cols] = cot_ref[tokens[g], cols]

    for n in range(group * nbr_count):
        for part in range(parts):
            item = step * group * nbr_count + n
            pltpu.make_async_copy(
                held_refs[part].at[0],
                raw_ref.at[item, cuts[part]],
                sems.at[item * parts + part],
            ).wait()
    x_full = jnp.concatenate(
        [
            raw_ref[pl.ds((step * group + g) * nbr_count, nbr_count)]
            .reshape(key_count, width)
            .astype(jnp.float32)
            + cond_ref[pl.ds(step * group + g, 1), :]
            for g in range(group)
        ],
        axis=0,
    )
    inv_rms = lax.rsqrt(jnp.mean(x_full * x_full, axis=-1, keepdims=True) + EPSILON)
    gain = gain_ref[...]
    hidden = (x_full * inv_rms * gain).astype(jnp.bfloat16)
    latent = dot(hidden, down_ref[...]).astype(jnp.bfloat16)
    encoded = (x_full + dot(latent, up_ref[...])).astype(jnp.bfloat16)

    @pl.when(step == 0)
    def _():
        kv_copy.wait()

    for cols in pairs + value_pairs:
        proj_ref[:, cols] = dot(encoded, kv_ref[:, cols]).astype(jnp.bfloat16)

    def diagonal(both):
        return jnp.concatenate([both[:SPAN, :HEAD], both[SPAN:, HEAD:]], axis=1)

    slot = lax.broadcasted_iota(jnp.int32, (key_count, 2 * SPAN), 0)
    for g in range(group):
        limit = jnp.zeros((key_count, 2 * SPAN), jnp.int32)
        for n in range(nbr_count):
            here = jnp.logical_and(slot >= n * slot_len, slot < (n + 1) * slot_len)
            item = (step * group + g) * nbr_count + n
            limit = jnp.where(here, n * slot_len + meta[lens + item], limit)
        usable = slot < limit
        for cols, value_cols in zip(pairs, value_pairs):
            q2 = q2_ref[double[g], cols]
            cot2 = cot2_ref[double[g], cols]
            key_rows = proj_ref[keys[g], cols]
            value_rows = proj_ref[keys[g], value_cols]
            scores = jnp.where(usable, dot(key_rows, q2, NT), FLOOR)
            row_max = jnp.max(scores, axis=0, keepdims=True)
            raised = jnp.exp2((scores - row_max) * (scaling * LOG2E))
            probs = raised * (1.0 / jnp.sum(raised, axis=0, keepdims=True))
            d_probs = dot(value_rows, cot2, NT)
            delta = jnp.sum(probs * d_probs, axis=0, keepdims=True)
            probs_b = probs.astype(jnp.bfloat16)
            d_scores = (probs * (d_probs - delta) * scaling).astype(jnp.bfloat16)
            grad_ref[keys[g], cols] = dot(d_scores, q2).astype(jnp.bfloat16)
            grad_ref[keys[g], value_cols] = dot(probs_b, cot2).astype(jnp.bfloat16)
            out = diagonal(dot(probs_b.T, value_rows))
            grad = diagonal(dot(d_scores.T, key_rows))
            out_ref[tokens[g], cols] = jnp.where(live, out, 0.0).astype(jnp.bfloat16)
            qg_ref[tokens[g], cols] = jnp.where(live, grad, 0.0).astype(jnp.bfloat16)

    @pl.when(step == 0)
    def _():
        kvt_copy.wait()
        acc_ref[...] = jnp.zeros_like(acc_ref)

    enc_grad = dot(grad_ref[...], kvt_ref[...]).astype(jnp.bfloat16)
    lat_grad = dot(enc_grad, upt_ref[...]).astype(jnp.bfloat16)
    scaled = dot(lat_grad, downt_ref[...]) * gain
    normed = x_full * inv_rms
    x_grad = enc_grad.astype(jnp.float32) + inv_rms * (
        scaled - normed * jnp.mean(scaled * normed, axis=-1, keepdims=True)
    )
    for g in range(group):
        span_grad = jnp.sum(
            x_grad[g * key_count : (g + 1) * key_count], axis=0, keepdims=True
        )
        cg_ref[pl.ds(step * group + g, 1), :] = jnp.where(live, span_grad, 0.0)
    acc_ref[:, :rank] += dot(hidden, lat_grad, TN)
    acc_ref[:, rank:] += dot(enc_grad, latent, TN)

    @pl.when(step == pl.num_programs(0) - 1)
    def _():
        ad_ref[...] = jnp.where(live, acc_ref[...], 0.0).astype(ad_ref.dtype)


def run_spans(meta, query, cot, cond, held, bounds, gain, w_down, w_up, w_kv, w_kv_t, nbr_count):
    span_count, width = cond.shape
    token_count, head_cols = query.shape
    slot_len = bounds[-1]
    parts = len(bounds) - 1
    rank = w_down.shape[1]
    whole = lambda a: pl.BlockSpec(a.shape, lambda s, m: (0,) * a.ndim, pipeline_mode=pl.Buffered(1))
    group = GROUP if span_count % GROUP == 0 else 1
    tokens = pl.BlockSpec((group * SPAN, head_cols), lambda s, m: (s, 0))
    small = [cond, gain.reshape(1, width), w_down, w_up, w_up.T, w_down.T]
    large = list(held) + [w_kv, w_kv_t]
    per_device = span_count * nbr_count
    keys = group * nbr_count * slot_len
    rows = per_device * slot_len
    flops = 2 * rows * (2 * width * 2 * head_cols + 6 * width * rank + 6 * SPAN * head_cols)
    return pl.pallas_call(
        functools.partial(span_kernel, len(held), nbr_count, bounds),
        grid_spec=pltpu.PrefetchScalarGridSpec(
            num_scalar_prefetch=1,
            grid=(span_count // group,),
            in_specs=[tokens, tokens]
            + [whole(a) for a in small]
            + [pl.BlockSpec(memory_space=pltpu.HBM)] * len(large),
            out_specs=[
                tokens,
                tokens,
                pl.BlockSpec((span_count, width), lambda s, m: (0, 0)),
                pl.BlockSpec((width, 2 * rank), lambda s, m: (0, 0)),
            ],
            scratch_shapes=[
                pltpu.VMEM((per_device, slot_len, width), jnp.bfloat16),
                pltpu.VMEM((width, 2 * head_cols), jnp.bfloat16),
                pltpu.VMEM((2 * head_cols, width), jnp.bfloat16),
                pltpu.VMEM((keys, 2 * head_cols), jnp.bfloat16),
                pltpu.VMEM((keys, 2 * head_cols), jnp.bfloat16),
                pltpu.VMEM((group * 2 * SPAN, head_cols), jnp.bfloat16),
                pltpu.VMEM((group * 2 * SPAN, head_cols), jnp.bfloat16),
                pltpu.VMEM((width, 2 * rank), jnp.float32),
                pltpu.SemaphoreType.DMA((per_device * parts,)),
                pltpu.SemaphoreType.DMA((2,)),
            ],
        ),
        out_shape=[
            jax.ShapeDtypeStruct((token_count, head_cols), jnp.bfloat16),
            jax.ShapeDtypeStruct((token_count, head_cols), jnp.bfloat16),
            jax.ShapeDtypeStruct((span_count, width), jnp.float32),
            jax.ShapeDtypeStruct((width, 2 * rank), jnp.float32),
        ],
        compiler_params=pltpu.CompilerParams(vmem_limit_bytes=60 * 2**20),
        cost_estimate=pl.CostEstimate(
            flops=flops, bytes_accessed=16 * 2**20, transcendentals=rows * SPAN * HEADS
        ),
    )(meta, query, cot, *small, *large)


def pick_kernel(held_count, meta, *refs):
    held_refs, out_ref = refs[:held_count], refs[held_count]
    for b, held in enumerate(held_refs):
        @pl.when(meta[0] == b)
        def _():
            for n in range(out_ref.shape[0]):
                out_ref[n] = held[meta[1 + n]]


def pick(which, index, held):
    count = index.shape[0]
    meta = jnp.concatenate([jnp.reshape(which, (1,)), index]).astype(jnp.int32)
    return pl.pallas_call(
        functools.partial(pick_kernel, len(held)),
        grid_spec=pltpu.PrefetchScalarGridSpec(
            num_scalar_prefetch=1,
            grid=(1,),
            in_specs=[pl.BlockSpec(memory_space=pltpu.VMEM)] * len(held),
            out_specs=pl.BlockSpec(memory_space=pltpu.VMEM),
        ),
        out_shape=jax.ShapeDtypeStruct((count,) + held[0].shape[1:], held[0].dtype),
        compiler_params=pltpu.CompilerParams(vmem_limit_bytes=16 * 2**20),
    )(meta, *held)


def place_requests(owners, per_device, pool_count, lanes):
    half = pool_count // 2
    count = owners.shape[1]
    order = jnp.arange(count, dtype=jnp.int32)
    side = (order // per_device) // half
    mate = side[:, None] == side[None, :]
    before = order[None, :] < order[:, None]
    same = owners[:, :, None] == owners[:, None, :]
    lower = owners[:, None, :] < owners[:, :, None]
    total = lambda mask: jnp.sum(mask.astype(jnp.int32), axis=2)
    rank = total(same & (mate & before)[None])
    crosses = rank >= lanes
    far = crosses[:, None, :]
    number = total(far & mate[None] & (lower | (same & before[None])))
    first = total(far & ~mate[None] & lower)
    guests = total(far & ~mate[None] & same)
    lane = jnp.where(crosses, number, first + guests + rank) % lanes
    row = jnp.where(crosses, 1 - side[None, :], side[None, :]) * half + lane % half
    return row, lane // half, crosses, number // half


def scatter_sum(total, axes):
    width = total.shape[1]
    sizes = [lax.axis_size(axis) for axis in axes]
    total = total.reshape(tuple(sizes) + (-1, width)).astype(jnp.float32)
    for at, axis in enumerate(axes):
        size, index = sizes[at], lax.axis_index(axis)
        if size > 4 or size & (size - 1):
            lead = (size,) + tuple(d for i, d in enumerate(total.shape) if i != at)
            parts = jnp.moveaxis(total, at, 0).astype(jnp.bfloat16)
            parts = lax.all_to_all(parts, axis, split_axis=0, concat_axis=0, tiled=True)
            total = jnp.sum(parts.reshape(lead).astype(jnp.float32), axis=0)
            total = jnp.expand_dims(total, at)
            continue
        bit = 1
        while bit < size:
            shape = total.shape
            split = total.reshape(shape[:at] + (shape[at] // 2, 2) + shape[at + 1 :])
            mine = (index // bit) % 2
            keep = lax.dynamic_index_in_dim(split, mine, at + 1, keepdims=False)
            give = lax.dynamic_index_in_dim(split, 1 - mine, at + 1, keepdims=False)
            got = lax.ppermute(
                give.astype(jnp.bfloat16), axis, [(i, i ^ bit) for i in range(size)]
            )
            total = keep + got.astype(jnp.float32)
            bit *= 2
    return total.reshape(-1, width)


def body(
    queries, cotangent, cond, nbr_owner, nbr_block, database, lengths, gain, w_down, w_up, w_kv
):
    axes = ("pool", "dp")
    pool_count = lax.axis_size("pool")
    columns = lax.axis_size("dp")
    relay_row = pool_count - 1
    half = pool_count // 2
    row = lax.axis_index("pool")
    me = lax.axis_index("dp")
    span_count, width = cond.shape[2:]
    nbr_count = nbr_owner.shape[3]
    per_device = span_count * nbr_count
    block_count, slot_len = database.shape[2:4]
    live_count = relay_row * per_device
    capacity = max(2, live_count // columns + 1)
    slots = -(-capacity // pool_count)
    lanes = half * slots
    most = 0
    if capacity > lanes:
        for rows in (half, relay_row - half):
            full, left = divmod(rows * per_device, capacity)
            most = max(most, full * (capacity - lanes) + max(0, left - lanes))
    crossing = -(-most // half)
    token_count, head_cols = queries.shape[2:]

    def hop(array, pairs):
        return lax.ppermute(
            array, axes, [(a * columns + j, b * columns + j) for a, b in pairs for j in range(columns)]
        )

    first = slot_len // 16 * 5 // 8 * 16
    bounds = [0, first, slot_len] if 0 < first < slot_len else [0, slot_len]
    parts = len(bounds) - 1
    full_store = database.reshape(block_count, slot_len, width)
    cut = lambda i: full_store[:, bounds[i] : bounds[i + 1]]
    store = [cut(0)]

    def to_all(array, axis):
        copies = jnp.broadcast_to(array[None], (lax.axis_size(axis),) + array.shape)
        return lax.all_to_all(copies, axis, split_axis=0, concat_axis=0, tiled=True)

    info = jnp.concatenate([nbr_owner.reshape(-1), nbr_block.reshape(-1), lengths.reshape(-1)])
    info = jnp.pad(info, (0, -info.shape[0] % 128))
    over = lambda a: hop(a, [(relay_row, relay_row - half)])
    across = [over(store[0])]
    table = to_all(info.reshape(-1, 128), axes)
    w_kv_t = w_kv.T
    full_store, across, table, w_kv_t = lax.optimization_barrier(
        (full_store, across, table, w_kv_t)
    )
    store += [cut(i) for i in range(1, parts)]
    across += [over(a) for a in store[1:]]
    table = table.reshape(pool_count, columns, -1)
    by_column = jnp.swapaxes(table[:relay_row], 0, 1)
    owners = by_column[:, :, :per_device].reshape(columns, live_count)
    blocks = by_column[:, :, per_device : 2 * per_device].reshape(columns, live_count)
    store_len = table[relay_row, :, 2 * per_device : 2 * per_device + block_count]
    carrier, slot, crosses, number = place_requests(owners, per_device, pool_count, lanes)

    ring = jnp.arange(slots, dtype=jnp.int32)
    mine = ((owners == me) & (carrier == row))[:, None, :] & (slot[:, None, :] == ring[None, :, None])
    slot_block = jnp.sum(jnp.where(mine, blocks[:, None, :], 0), axis=2).reshape(-1)

    mine_of = lambda a: lax.dynamic_index_in_dim(a, me, 0, keepdims=False)
    my_owner, my_block, my_carrier, my_slot, my_cross, my_number = map(
        mine_of, (owners, blocks, carrier, slot, crosses, number)
    )
    place = my_owner * slots + my_slot
    ring = jnp.arange(crossing, dtype=jnp.int32)
    mine = (my_cross & (my_carrier == row))[None, :] & (my_number[None, :] == ring[:, None])
    leaving_place = jnp.sum(jnp.where(mine, place[None, :], 0), axis=1)

    def share(array, step):
        return hop(array, [(p, p // half * half + (p + step) % half) for p in range(pool_count)])

    held = []
    for i in range(parts):
        near = jnp.where(row == relay_row, store[i], across[i])
        stores = [near]
        held_by = jnp.where(row % half == half - 1, 0, 1)
        for step in range(1, half):
            stores.append(hop(near, [(p, p - step) for p in (relay_row, relay_row - half)]))
            held_by = jnp.where(row % half == half - 1 - step, step, held_by)
        sends = pick(held_by, slot_block, stores)
        arrived = lax.all_to_all(sends, "dp", split_axis=0, concat_axis=0, tiled=True)
        here = [arrived] + [share(arrived, step) for step in range(1, half)]
        if crossing:
            leaving = pick(0, leaving_place, [arrived])
            landed = hop(leaving, [(p, (p + half) % pool_count) for p in range(pool_count)])
            here += [landed] + [share(landed, step) for step in range(1, half)]
        held.append(here)
    origin = jnp.where(my_cross, (my_carrier + half) % pool_count, my_carrier)
    which = (row - origin) % half + jnp.where(my_cross, half, 0)
    index = jnp.where(my_cross, my_number, place)
    held = [here[b] for b in range(len(held[0])) for here in held]

    own_row = jnp.minimum(row, relay_row - 1)
    hot = (my_owner * block_count + my_block)[:, None] == jnp.arange(
        columns * block_count, dtype=jnp.int32
    )[None, :]
    wanted_len = jnp.sum(jnp.where(hot, store_len.reshape(1, -1), 0), axis=1)
    own = lambda a: lax.dynamic_index_in_dim(
        a.reshape(relay_row, per_device), own_row, 0, keepdims=False
    )
    live = (row < relay_row).astype(jnp.int32)
    meta = jnp.concatenate([live[None], own(wanted_len), own(which), own(index)]).astype(jnp.int32)

    attn_out, q_grad, cond_grad, terms = run_spans(
        meta,
        queries.reshape(token_count, head_cols),
        cotangent.reshape(token_count, head_cols),
        cond.reshape(span_count, width).astype(jnp.float32),
        held,
        bounds,
        gain,
        w_down,
        w_up,
        w_kv,
        w_kv_t,
        nbr_count,
    )

    adapter_grad = scatter_sum(terms, axes)
    return (
        attn_out.reshape(1, 1, token_count, head_cols),
        q_grad.reshape(1, 1, token_count, head_cols),
        cond_grad.reshape(1, 1, span_count, width),
        adapter_grad,
    )


def solution(mesh):
    return jax.shard_map(
        body,
        mesh=mesh,
        in_specs=(
            P("pool", "dp", None, None),
            P("pool", "dp", None, None),
            P("pool", "dp", None, None),
            P("pool", "dp", None, None),
            P("pool", "dp", None, None),
            P("pool", "dp", None, None, None),
            P("pool", "dp", None),
            P(),
            P(),
            P(),
            P(),
        ),
        out_specs=(
            P("pool", "dp", None, None),
            P("pool", "dp", None, None),
            P("pool", "dp", None, None),
            P(("pool", "dp"), None),
        ),
        check_vma=False,
    )
```

```python
import functools

import jax
import jax.numpy as jnp
from jax import lax
from jax.experimental import pallas as pl
from jax.experimental.pallas import tpu as pltpu
from jax.sharding import PartitionSpec as P

HEADS = 16
HEAD = 128
SPAN = 64
GROUP = 2

EPSILON = 1e-06
FLOOR = -1e30
LOG2E = 1.4426950408889634

NT = (((1,), (1,)), ((), ()))
TN = (((0,), (0,)), ((), ()))


def dot(a, b, dims=(((1,), (0,)), ((), ()))):
    return lax.dot_general(a, b, dims, preferred_element_type=jnp.float32)


def span_kernel(
    held_count, nbr_count, bounds, pool_count, meta,
    q_ref, cot_ref, cond_ref, gain_ref, down_ref, up_ref, upt_ref, downt_ref, *rest,
):
    held_refs = rest[:held_count]
    (kv_hbm, kvt_hbm, out_ref, qg_ref, cg_ref, keep_ref, give_ref,
     raw_ref, kv_ref, kvt_ref, proj_ref, grad_ref, score_ref, dprob_ref, prob_ref, dscore_ref,
     q2_ref, cot2_ref, acc_ref, sems, kv_sem) = rest[held_count:]
    step = pl.program_id(0)
    per_device, slot_len, width = raw_ref.shape
    key_count = nbr_count * slot_len
    span_count = per_device // nbr_count
    group = span_count // pl.num_programs(0)
    head_cols = q_ref.shape[1]
    rank = down_ref.shape[1]
    scaling = HEAD ** (-0.5)
    live = meta[0] == 1
    lens, which, index = 2, 2 + per_device, 2 + 2 * per_device
    parts = len(bounds) - 1
    cuts = [pl.ds(low, high - low) for low, high in zip(bounds, bounds[1:])]
    pairs = [pl.ds(i * 2 * HEAD, 2 * HEAD) for i in range(HEADS // 2)]
    value_pairs = [pl.ds(head_cols + i * 2 * HEAD, 2 * HEAD) for i in range(HEADS // 2)]
    lanes = [pl.ds(i * 2 * SPAN, 2 * SPAN) for i in range(HEADS // 2)]
    keys = [pl.ds(g * key_count, key_count) for g in range(group)]
    tokens = [pl.ds(g * SPAN, SPAN) for g in range(group)]
    double = [pl.ds(g * 2 * SPAN, 2 * SPAN) for g in range(group)]
    kv_copy = pltpu.make_async_copy(kv_hbm, kv_ref, kv_sem.at[0])
    kvt_copy = pltpu.make_async_copy(kvt_hbm, kvt_ref, kv_sem.at[1])

    @pl.when(step == 0)
    def _():
        for n in range(per_device):
            for b, held in enumerate(held_refs):
                @pl.when(meta[which + n] == b // parts)
                def _():
                    part = b % parts
                    pltpu.make_async_copy(
                        held.at[meta[index + n]],
                        raw_ref.at[n, cuts[part]],
                        sems.at[n * parts + part],
                    ).start()
        kv_copy.start()
        kvt_copy.start()
        q2_ref[...] = jnp.zeros_like(q2_ref)
        cot2_ref[...] = jnp.zeros_like(cot2_ref)

    for g in range(group):
        for i in range(HEADS):
            cols = pl.ds(i * HEAD, HEAD)
            part = pl.ds((2 * g + i % 2) * SPAN, SPAN)
            q2_ref[part, cols] = q_ref[tokens[g], cols]
            cot2_ref[part, cols] = cot_ref[tokens[g], cols]

    for n in range(group * nbr_count):
        for part in range(parts):
            item = step * group * nbr_count + n
            pltpu.make_async_copy(
                held_refs[part].at[0],
                raw_ref.at[item, cuts[part]],
                sems.at[item * parts + part],
            ).wait()
    x_full = jnp.concatenate(
        [
            raw_ref[pl.ds((step * group + g) * nbr_count, nbr_count)]
            .reshape(key_count, width)
            .astype(jnp.float32)
            + cond_ref[pl.ds(step * group + g, 1), :]
            for g in range(group)
        ],
        axis=0,
    )
    inv_rms = lax.rsqrt(jnp.mean(x_full * x_full, axis=-1, keepdims=True) + EPSILON)
    gain = gain_ref[...]
    hidden = (x_full * inv_rms * gain).astype(jnp.bfloat16)
    latent = dot(hidden, down_ref[...]).astype(jnp.bfloat16)
    encoded = (x_full + dot(latent, up_ref[...])).astype(jnp.bfloat16)

    @pl.when(step == 0)
    def _():
        kv_copy.wait()

    slot = lax.broadcasted_iota(jnp.int32, (key_count, 2 * SPAN), 0)
    usable = []
    for g in range(group):
        limit = jnp.zeros((key_count, 2 * SPAN), jnp.int32)
        for n in range(nbr_count):
            here = jnp.logical_and(slot >= n * slot_len, slot < (n + 1) * slot_len)
            item = (step * group + g) * nbr_count + n
            limit = jnp.where(here, n * slot_len + meta[lens + item], limit)
        usable.append(limit)

    def diagonal(both):
        return jnp.concatenate([both[:SPAN, :HEAD], both[SPAN:, HEAD:]], axis=1)

    def project(i):
        for cols in (pairs[i], value_pairs[i]):
            proj_ref[:, cols] = dot(encoded, kv_ref[:, cols]).astype(jnp.bfloat16)

    def score(i, g):
        score_ref[keys[g], lanes[i]] = dot(proj_ref[keys[g], pairs[i]], q2_ref[double[g], pairs[i]], NT)
        dprob_ref[keys[g], lanes[i]] = dot(
            proj_ref[keys[g], value_pairs[i]], cot2_ref[double[g], pairs[i]], NT
        )

    def soften(i, g):
        scores = jnp.where(slot < usable[g], score_ref[keys[g], lanes[i]], FLOOR)
        row_max = jnp.max(scores, axis=0, keepdims=True)
        raised = jnp.exp2((scores - row_max) * (scaling * LOG2E))
        probs = raised * (1.0 / jnp.sum(raised, axis=0, keepdims=True))
        d_probs = dprob_ref[keys[g], lanes[i]]
        delta = jnp.sum(probs * d_probs, axis=0, keepdims=True)
        prob_ref[keys[g], lanes[i]] = probs.astype(jnp.bfloat16)
        dscore_ref[keys[g], lanes[i]] = (probs * (d_probs - delta) * scaling).astype(jnp.bfloat16)

    def multiply(i, g):
        probs, d_scores = prob_ref[keys[g], lanes[i]], dscore_ref[keys[g], lanes[i]]
        grad_ref[keys[g], pairs[i]] = dot(d_scores, q2_ref[double[g], pairs[i]]).astype(jnp.bfloat16)
        grad_ref[keys[g], value_pairs[i]] = dot(probs, cot2_ref[double[g], pairs[i]]).astype(
            jnp.bfloat16
        )
        out = diagonal(dot(probs.T, proj_ref[keys[g], value_pairs[i]]))
        grad = diagonal(dot(d_scores.T, proj_ref[keys[g], pairs[i]]))
        out_ref[tokens[g], pairs[i]] = jnp.where(live, out, 0.0).astype(jnp.bfloat16)
        qg_ref[tokens[g], pairs[i]] = jnp.where(live, grad, 0.0).astype(jnp.bfloat16)

    spots = [(i, g) for i in range(HEADS // 2) for g in range(group)]
    project(0)
    score(*spots[0])
    for k, spot in enumerate(spots):
        if spot[1] == 0 and spot[0] + 1 < HEADS // 2:
            project(spot[0] + 1)
        if k + 1 < len(spots):
            score(*spots[k + 1])
        soften(*spot)
        if k:
            multiply(*spots[k - 1])
    multiply(*spots[-1])

    @pl.when(step == 0)
    def _():
        kvt_copy.wait()
        acc_ref[...] = jnp.zeros_like(acc_ref)

    enc_grad = dot(grad_ref[...], kvt_ref[...]).astype(jnp.bfloat16)
    lat_grad = dot(enc_grad, upt_ref[...]).astype(jnp.bfloat16)
    scaled = dot(lat_grad, downt_ref[...]) * gain
    normed = x_full * inv_rms
    x_grad = enc_grad.astype(jnp.float32) + inv_rms * (
        scaled - normed * jnp.mean(scaled * normed, axis=-1, keepdims=True)
    )
    for g in range(group):
        span_grad = jnp.sum(
            x_grad[g * key_count : (g + 1) * key_count], axis=0, keepdims=True
        )
        cg_ref[pl.ds(step * group + g, 1), :] = jnp.where(live, span_grad, 0.0)
    acc_ref[:, :rank] += dot(hidden, lat_grad, TN)
    acc_ref[:, rank:] += dot(enc_grad, latent, TN)

    @pl.when(step == pl.num_programs(0) - 1)
    def _():
        chunk = width // pool_count
        for k in range(pool_count // 2):
            part = pl.ds(k * chunk, chunk)
            for ref, own in ((keep_ref, meta[1]), (give_ref, 1 - meta[1])):
                rows = acc_ref[pl.ds(pl.multiple_of((2 * k + own) * chunk, chunk), chunk), :]
                ref[part, :] = jnp.where(live, rows, 0.0).astype(ref.dtype)


def run_spans(meta, query, cot, cond, held, bounds, gain, w_down, w_up, w_kv, w_kv_t, nbr_count, pool_count):
    span_count, width = cond.shape
    token_count, head_cols = query.shape
    slot_len = bounds[-1]
    parts = len(bounds) - 1
    rank = w_down.shape[1]
    whole = lambda a: pl.BlockSpec(a.shape, lambda s, m: (0,) * a.ndim, pipeline_mode=pl.Buffered(1))
    group = GROUP if span_count % GROUP == 0 else 1
    tokens = pl.BlockSpec((group * SPAN, head_cols), lambda s, m: (s, 0))
    small = [cond, gain.reshape(1, width), w_down, w_up, w_up.T, w_down.T]
    large = list(held) + [w_kv, w_kv_t]
    per_device = span_count * nbr_count
    keys = group * nbr_count * slot_len
    rows = per_device * slot_len
    flops = 2 * rows * (2 * width * 2 * head_cols + 6 * width * rank + 6 * SPAN * head_cols)
    return pl.pallas_call(
        functools.partial(span_kernel, len(held), nbr_count, bounds, pool_count),
        grid_spec=pltpu.PrefetchScalarGridSpec(
            num_scalar_prefetch=1,
            grid=(span_count // group,),
            in_specs=[tokens, tokens]
            + [whole(a) for a in small]
            + [pl.BlockSpec(memory_space=pltpu.HBM)] * len(large),
            out_specs=[
                tokens,
                tokens,
                pl.BlockSpec((span_count, width), lambda s, m: (0, 0)),
                pl.BlockSpec((width // 2, 2 * rank), lambda s, m: (0, 0)),
                pl.BlockSpec((width // 2, 2 * rank), lambda s, m: (0, 0)),
            ],
            scratch_shapes=[
                pltpu.VMEM((per_device, slot_len, width), jnp.bfloat16),
                pltpu.VMEM((width, 2 * head_cols), jnp.bfloat16),
                pltpu.VMEM((2 * head_cols, width), jnp.bfloat16),
                pltpu.VMEM((keys, 2 * head_cols), jnp.bfloat16),
                pltpu.VMEM((keys, 2 * head_cols), jnp.bfloat16),
                pltpu.VMEM((keys, SPAN * HEADS), jnp.float32),
                pltpu.VMEM((keys, SPAN * HEADS), jnp.float32),
                pltpu.VMEM((keys, SPAN * HEADS), jnp.bfloat16),
                pltpu.VMEM((keys, SPAN * HEADS), jnp.bfloat16),
                pltpu.VMEM((group * 2 * SPAN, head_cols), jnp.bfloat16),
                pltpu.VMEM((group * 2 * SPAN, head_cols), jnp.bfloat16),
                pltpu.VMEM((width, 2 * rank), jnp.float32),
                pltpu.SemaphoreType.DMA((per_device * parts,)),
                pltpu.SemaphoreType.DMA((2,)),
            ],
        ),
        out_shape=[
            jax.ShapeDtypeStruct((token_count, head_cols), jnp.bfloat16),
            jax.ShapeDtypeStruct((token_count, head_cols), jnp.bfloat16),
            jax.ShapeDtypeStruct((span_count, width), jnp.float32),
            jax.ShapeDtypeStruct((width // 2, 2 * rank), jnp.float32),
            jax.ShapeDtypeStruct((width // 2, 2 * rank), jnp.bfloat16),
        ],
        compiler_params=pltpu.CompilerParams(vmem_limit_bytes=60 * 2**20),
        cost_estimate=pl.CostEstimate(
            flops=flops, bytes_accessed=16 * 2**20, transcendentals=rows * SPAN * HEADS
        ),
    )(meta, query, cot, *small, *large)


def pick_kernel(held_count, meta, *refs):
    held_refs, out_ref = refs[:held_count], refs[held_count]
    for b, held in enumerate(held_refs):
        @pl.when(meta[0] == b)
        def _():
            for n in range(out_ref.shape[0]):
                out_ref[n] = held[meta[1 + n]]


def pick(which, index, held):
    count = index.shape[0]
    meta = jnp.concatenate([jnp.reshape(which, (1,)), index]).astype(jnp.int32)
    return pl.pallas_call(
        functools.partial(pick_kernel, len(held)),
        grid_spec=pltpu.PrefetchScalarGridSpec(
            num_scalar_prefetch=1,
            grid=(1,),
            in_specs=[pl.BlockSpec(memory_space=pltpu.VMEM)] * len(held),
            out_specs=pl.BlockSpec(memory_space=pltpu.VMEM),
        ),
        out_shape=jax.ShapeDtypeStruct((count,) + held[0].shape[1:], held[0].dtype),
        compiler_params=pltpu.CompilerParams(vmem_limit_bytes=16 * 2**20),
    )(meta, *held)


def place_requests(owners, per_device, pool_count, lanes):
    half = pool_count // 2
    count = owners.shape[1]
    order = jnp.arange(count, dtype=jnp.int32)
    side = (order // per_device) // half
    mate = side[:, None] == side[None, :]
    before = order[None, :] < order[:, None]
    same = owners[:, :, None] == owners[:, None, :]
    lower = owners[:, None, :] < owners[:, :, None]
    total = lambda mask: jnp.sum(mask.astype(jnp.int32), axis=2)
    rank = total(same & (mate & before)[None])
    crosses = rank >= lanes
    far = crosses[:, None, :]
    number = total(far & mate[None] & (lower | (same & before[None])))
    first = total(far & ~mate[None] & lower)
    guests = total(far & ~mate[None] & same)
    lane = jnp.where(crosses, number, first + guests + rank) % lanes
    row = jnp.where(crosses, 1 - side[None, :], side[None, :]) * half + lane % half
    return row, lane // half, crosses, number // half


def scatter_sum(keep, give, axes):
    width = keep.shape[1]
    size, columns = (lax.axis_size(axis) for axis in axes)
    index = lax.axis_index(axes[0])
    swap = lambda a, bit: lax.ppermute(a, axes[0], [(i, i ^ bit) for i in range(size)])
    total = keep + swap(give, 1).astype(jnp.float32)
    bit = 2
    while bit < size:
        split = total.reshape(size // bit // 2, 2, -1, width)
        mine = (index // bit) % 2
        keep = lax.dynamic_index_in_dim(split, mine, 1, keepdims=False)
        give = lax.dynamic_index_in_dim(split, 1 - mine, 1, keepdims=False)
        total = keep + swap(give.astype(jnp.bfloat16), bit).astype(jnp.float32)
        bit *= 2
    parts = total.reshape(columns, -1, width).astype(jnp.bfloat16)
    parts = lax.all_to_all(parts, axes[1], split_axis=0, concat_axis=0, tiled=True)
    return jnp.sum(parts.astype(jnp.float32), axis=0)


def body(
    queries, cotangent, cond, nbr_owner, nbr_block, database, lengths, gain, w_down, w_up, w_kv
):
    axes = ("pool", "dp")
    pool_count = lax.axis_size("pool")
    columns = lax.axis_size("dp")
    relay_row = pool_count - 1
    half = pool_count // 2
    row = lax.axis_index("pool")
    me = lax.axis_index("dp")
    span_count, width = cond.shape[2:]
    nbr_count = nbr_owner.shape[3]
    per_device = span_count * nbr_count
    block_count, slot_len = database.shape[2:4]
    live_count = relay_row * per_device
    capacity = max(2, live_count // columns + 1)
    slots = -(-capacity // pool_count)
    lanes = half * slots
    most = 0
    if capacity > lanes:
        for rows in (half, relay_row - half):
            full, left = divmod(rows * per_device, capacity)
            most = max(most, full * (capacity - lanes) + max(0, left - lanes))
    crossing = -(-most // half)
    token_count, head_cols = queries.shape[2:]

    def hop(array, pairs):
        return lax.ppermute(
            array, axes, [(a * columns + j, b * columns + j) for a, b in pairs for j in range(columns)]
        )

    first = slot_len // 16 * 3 // 4 * 16
    bounds = [0, first, slot_len] if 0 < first < slot_len else [0, slot_len]
    parts = len(bounds) - 1
    full_store = database.reshape(block_count, slot_len, width)
    cut = lambda i: full_store[:, bounds[i] : bounds[i + 1]]
    store = [cut(0)]

    def to_all(array, axis):
        copies = jnp.broadcast_to(array[None], (lax.axis_size(axis),) + array.shape)
        return lax.all_to_all(copies, axis, split_axis=0, concat_axis=0, tiled=True)

    info = jnp.concatenate([nbr_owner.reshape(-1), nbr_block.reshape(-1), lengths.reshape(-1)])
    info = jnp.pad(info, (0, -info.shape[0] % 128))
    over = lambda a: hop(a, [(relay_row, relay_row - half)])
    across = [over(store[0])]
    table = to_all(info.reshape(-1, 128), axes)
    w_kv_t = w_kv.T
    full_store, across, table, w_kv_t = lax.optimization_barrier(
        (full_store, across, table, w_kv_t)
    )
    store += [cut(i) for i in range(1, parts)]
    across += [over(a) for a in store[1:]]
    table = table.reshape(pool_count, columns, -1)
    by_column = jnp.swapaxes(table[:relay_row], 0, 1)
    owners = by_column[:, :, :per_device].reshape(columns, live_count)
    blocks = by_column[:, :, per_device : 2 * per_device].reshape(columns, live_count)
    store_len = table[relay_row, :, 2 * per_device : 2 * per_device + block_count]
    carrier, slot, crosses, number = place_requests(owners, per_device, pool_count, lanes)

    ring = jnp.arange(slots, dtype=jnp.int32)
    mine = ((owners == me) & (carrier == row))[:, None, :] & (slot[:, None, :] == ring[None, :, None])
    slot_block = jnp.sum(jnp.where(mine, blocks[:, None, :], 0), axis=2).reshape(-1)

    mine_of = lambda a: lax.dynamic_index_in_dim(a, me, 0, keepdims=False)
    my_owner, my_block, my_carrier, my_slot, my_cross, my_number = map(
        mine_of, (owners, blocks, carrier, slot, crosses, number)
    )
    place = my_owner * slots + my_slot
    ring = jnp.arange(crossing, dtype=jnp.int32)
    mine = (my_cross & (my_carrier == row))[None, :] & (my_number[None, :] == ring[:, None])
    leaving_place = jnp.sum(jnp.where(mine, place[None, :], 0), axis=1)

    def share(array, step):
        return hop(array, [(p, p // half * half + (p + step) % half) for p in range(pool_count)])

    origin = jnp.where(my_cross, (my_carrier + half) % pool_count, my_carrier)
    which = (row - origin) % half + jnp.where(my_cross, half, 0)
    index = jnp.where(my_cross, my_number, place)
    own_row = jnp.minimum(row, relay_row - 1)
    hot = (my_owner * block_count + my_block)[:, None] == jnp.arange(
        columns * block_count, dtype=jnp.int32
    )[None, :]
    wanted_len = jnp.sum(jnp.where(hot, store_len.reshape(1, -1), 0), axis=1)
    own = lambda a: lax.dynamic_index_in_dim(
        a.reshape(relay_row, per_device), own_row, 0, keepdims=False
    )
    flags = jnp.stack([(row < relay_row).astype(jnp.int32), row % 2])
    meta = jnp.concatenate([flags, own(wanted_len), own(which), own(index)]).astype(jnp.int32)

    held = []
    for i in range(parts):
        near = jnp.where(row == relay_row, store[i], across[i])
        stores = [near]
        held_by = jnp.where(row % half == half - 1, 0, 1)
        for step in range(1, half):
            stores.append(hop(near, [(p, p - step) for p in (relay_row, relay_row - half)]))
            held_by = jnp.where(row % half == half - 1 - step, step, held_by)
        if i:
            slot_block, meta = lax.optimization_barrier((slot_block, meta))
        sends = pick(held_by, slot_block, stores)
        arrived = lax.all_to_all(sends, "dp", split_axis=0, concat_axis=0, tiled=True)
        here = [arrived] + [share(arrived, step) for step in range(1, half)]
        if crossing:
            leaving = pick(0, leaving_place, [arrived])
            landed = hop(leaving, [(p, (p + half) % pool_count) for p in range(pool_count)])
            here += [landed] + [share(landed, step) for step in range(1, half)]
        held.append(here)
    held = [here[b] for b in range(len(held[0])) for here in held]

    attn_out, q_grad, cond_grad, keep, give = run_spans(
        meta,
        queries.reshape(token_count, head_cols),
        cotangent.reshape(token_count, head_cols),
        cond.reshape(span_count, width).astype(jnp.float32),
        held,
        bounds,
        gain,
        w_down,
        w_up,
        w_kv,
        w_kv_t,
        nbr_count,
        pool_count,
    )

    adapter_grad = scatter_sum(keep, give, axes)
    return (
        attn_out.reshape(1, 1, token_count, head_cols),
        q_grad.reshape(1, 1, token_count, head_cols),
        cond_grad.reshape(1, 1, span_count, width),
        adapter_grad,
    )


def solution(mesh):
    return jax.shard_map(
        body,
        mesh=mesh,
        in_specs=(
            P("pool", "dp", None, None),
            P("pool", "dp", None, None),
            P("pool", "dp", None, None),
            P("pool", "dp", None, None),
            P("pool", "dp", None, None),
            P("pool", "dp", None, None, None),
            P("pool", "dp", None),
            P(),
            P(),
            P(),
            P(),
        ),
        out_specs=(
            P("pool", "dp", None, None),
            P("pool", "dp", None, None),
            P("pool", "dp", None, None),
            P(("pool", "dp"), None),
        ),
        check_vma=False,
    )
```

```python
import functools

import jax
import jax.numpy as jnp
from jax import lax
from jax.experimental import pallas as pl
from jax.experimental.pallas import tpu as pltpu
from jax.sharding import PartitionSpec as P

HEADS = 16
HEAD = 128
SPAN = 64
GROUP = 2

EPSILON = 1e-06
FLOOR = -1e30
LOG2E = 1.4426950408889634

NT = (((1,), (1,)), ((), ()))
TN = (((0,), (0,)), ((), ()))


def dot(a, b, dims=(((1,), (0,)), ((), ()))):
    return lax.dot_general(a, b, dims, preferred_element_type=jnp.float32)


def span_kernel(
    held_count, nbr_count, bounds, pool_count, meta,
    q_ref, cot_ref, cond_ref, gain_ref, down_ref, up_ref, upt_ref, downt_ref, *rest,
):
    held_refs = rest[:held_count]
    (kv_hbm, kvt_hbm, proj_hbm, prob_hbm, dscore_hbm, cg_ref, keep_ref, give_ref,
     raw_ref, kv_ref, kvt_ref, proj_ref, grad_ref, score_ref, dprob_ref, prob_ref, dscore_ref,
     q2_ref, cot2_ref, acc_ref, sems, kv_sem) = rest[held_count:]
    step = pl.program_id(0)
    per_device, slot_len, width = raw_ref.shape
    key_count = nbr_count * slot_len
    span_count = per_device // nbr_count
    group = span_count // pl.num_programs(0)
    head_cols = q_ref.shape[1]
    rank = down_ref.shape[1]
    scaling = HEAD ** (-0.5)
    live = meta[0] == 1
    lens, which, index = 2, 2 + per_device, 2 + 2 * per_device
    parts = len(bounds) - 1
    cuts = [pl.ds(low, high - low) for low, high in zip(bounds, bounds[1:])]
    pairs = [pl.ds(i * 2 * HEAD, 2 * HEAD) for i in range(HEADS // 2)]
    value_pairs = [pl.ds(head_cols + i * 2 * HEAD, 2 * HEAD) for i in range(HEADS // 2)]
    lanes = [pl.ds(i * 2 * SPAN, 2 * SPAN) for i in range(HEADS // 2)]
    keys = [pl.ds(g * key_count, key_count) for g in range(group)]
    tokens = [pl.ds(g * SPAN, SPAN) for g in range(group)]
    double = [pl.ds(g * 2 * SPAN, 2 * SPAN) for g in range(group)]
    spots = [
        (g, cols, value_cols, lane)
        for g in range(group)
        for cols, value_cols, lane in zip(pairs, value_pairs, lanes)
    ]
    kv_copy = pltpu.make_async_copy(kv_hbm, kv_ref, kv_sem.at[0])
    kvt_copy = pltpu.make_async_copy(kvt_hbm, kvt_ref, kv_sem.at[1])

    @pl.when(step == 0)
    def _():
        for n in range(per_device):
            for b, held in enumerate(held_refs):
                @pl.when(meta[which + n] == b // parts)
                def _():
                    part = b % parts
                    pltpu.make_async_copy(
                        held.at[meta[index + n]],
                        raw_ref.at[n, cuts[part]],
                        sems.at[n * parts + part],
                    ).start()
        kv_copy.start()
        kvt_copy.start()
        q2_ref[...] = jnp.zeros_like(q2_ref)
        cot2_ref[...] = jnp.zeros_like(cot2_ref)

    for g in range(group):
        for i in range(HEADS):
            cols = pl.ds(i * HEAD, HEAD)
            part = pl.ds((2 * g + i % 2) * SPAN, SPAN)
            q2_ref[part, cols] = q_ref[tokens[g], cols]
            cot2_ref[part, cols] = cot_ref[tokens[g], cols]

    for n in range(group * nbr_count):
        for part in range(parts):
            item = step * group * nbr_count + n
            pltpu.make_async_copy(
                held_refs[part].at[0],
                raw_ref.at[item, cuts[part]],
                sems.at[item * parts + part],
            ).wait()
    x_full = jnp.concatenate(
        [
            raw_ref[pl.ds((step * group + g) * nbr_count, nbr_count)]
            .reshape(key_count, width)
            .astype(jnp.float32)
            + cond_ref[pl.ds(step * group + g, 1), :]
            for g in range(group)
        ],
        axis=0,
    )
    inv_rms = lax.rsqrt(jnp.mean(x_full * x_full, axis=-1, keepdims=True) + EPSILON)
    gain = gain_ref[...]
    hidden = (x_full * inv_rms * gain).astype(jnp.bfloat16)
    latent = dot(hidden, down_ref[...]).astype(jnp.bfloat16)
    encoded = (x_full + dot(latent, up_ref[...])).astype(jnp.bfloat16)

    @pl.when(step == 0)
    def _():
        kv_copy.wait()

    for cols in pairs + value_pairs:
        proj_ref[:, cols] = dot(encoded, kv_ref[:, cols]).astype(jnp.bfloat16)

    for g, cols, value_cols, lane in spots:
        score_ref[keys[g], lane] = dot(proj_ref[keys[g], cols], q2_ref[double[g], cols], NT)
        dprob_ref[keys[g], lane] = dot(proj_ref[keys[g], value_cols], cot2_ref[double[g], cols], NT)

    slot = lax.broadcasted_iota(jnp.int32, (key_count, 2 * SPAN), 0)
    for g in range(group):
        limit = jnp.zeros((key_count, 2 * SPAN), jnp.int32)
        for n in range(nbr_count):
            here = jnp.logical_and(slot >= n * slot_len, slot < (n + 1) * slot_len)
            item = (step * group + g) * nbr_count + n
            limit = jnp.where(here, n * slot_len + meta[lens + item], limit)
        usable = slot < limit
        for cols, value_cols, lane in zip(pairs, value_pairs, lanes):
            scores = jnp.where(usable, score_ref[keys[g], lane], FLOOR)
            row_max = jnp.max(scores, axis=0, keepdims=True)
            raised = jnp.exp2((scores - row_max) * (scaling * LOG2E))
            probs = raised * (1.0 / jnp.sum(raised, axis=0, keepdims=True))
            d_probs = dprob_ref[keys[g], lane]
            delta = jnp.sum(probs * d_probs, axis=0, keepdims=True)
            probs_b = probs.astype(jnp.bfloat16)
            d_scores = (probs * (d_probs - delta) * scaling).astype(jnp.bfloat16)
            grad_ref[keys[g], cols] = dot(d_scores, q2_ref[double[g], cols]).astype(jnp.bfloat16)
            grad_ref[keys[g], value_cols] = dot(probs_b, cot2_ref[double[g], cols]).astype(
                jnp.bfloat16
            )
            prob_ref[keys[g], lane] = probs_b
            dscore_ref[keys[g], lane] = d_scores

    rows = proj_ref.shape[0]
    mine = pl.ds(pl.multiple_of(step * rows, rows), rows)
    leaving = [
        pltpu.make_async_copy(ref, hbm.at[mine], kv_sem.at[2 + i])
        for i, (ref, hbm) in enumerate(
            ((proj_ref, proj_hbm), (prob_ref, prob_hbm), (dscore_ref, dscore_hbm))
        )
    ]
    for copy in leaving:
        copy.start()

    @pl.when(step == 0)
    def _():
        kvt_copy.wait()
        acc_ref[...] = jnp.zeros_like(acc_ref)

    enc_grad = dot(grad_ref[...], kvt_ref[...]).astype(jnp.bfloat16)
    lat_grad = dot(enc_grad, upt_ref[...]).astype(jnp.bfloat16)
    scaled = dot(lat_grad, downt_ref[...]) * gain
    normed = x_full * inv_rms
    x_grad = enc_grad.astype(jnp.float32) + inv_rms * (
        scaled - normed * jnp.mean(scaled * normed, axis=-1, keepdims=True)
    )
    for g in range(group):
        span_grad = jnp.sum(
            x_grad[g * key_count : (g + 1) * key_count], axis=0, keepdims=True
        )
        cg_ref[pl.ds(step * group + g, 1), :] = jnp.where(live, span_grad, 0.0)
    acc_ref[:, :rank] += dot(hidden, lat_grad, TN)
    acc_ref[:, rank:] += dot(enc_grad, latent, TN)
    for copy in leaving:
        copy.wait()

    @pl.when(step == pl.num_programs(0) - 1)
    def _():
        chunk = width // pool_count
        for k in range(pool_count // 2):
            part = pl.ds(k * chunk, chunk)
            for ref, own in ((keep_ref, meta[1]), (give_ref, 1 - meta[1])):
                rows = acc_ref[pl.ds(pl.multiple_of((2 * k + own) * chunk, chunk), chunk), :]
                ref[part, :] = jnp.where(live, rows, 0.0).astype(ref.dtype)


def out_kernel(meta, proj_ref, prob_ref, dscore_ref, out_ref, qg_ref):
    live = meta[0] == 1
    head_cols = out_ref.shape[1]

    def diagonal(both):
        return jnp.concatenate([both[:SPAN, :HEAD], both[SPAN:, HEAD:]], axis=1)

    for i in range(HEADS // 2):
        cols = pl.ds(i * 2 * HEAD, 2 * HEAD)
        value_cols = pl.ds(head_cols + i * 2 * HEAD, 2 * HEAD)
        lane = pl.ds(i * 2 * SPAN, 2 * SPAN)
        out = diagonal(dot(prob_ref[:, lane].T, proj_ref[:, value_cols]))
        grad = diagonal(dot(dscore_ref[:, lane].T, proj_ref[:, cols]))
        out_ref[:, cols] = jnp.where(live, out, 0.0).astype(jnp.bfloat16)
        qg_ref[:, cols] = jnp.where(live, grad, 0.0).astype(jnp.bfloat16)


def run_outs(meta, proj, prob, dscore, span_count):
    rows = proj.shape[0]
    head_cols = proj.shape[1] // 2
    keys = rows // span_count
    blocks = lambda a: pl.BlockSpec((a.shape[0] // span_count, a.shape[1]), lambda s, m: (s, 0))
    out = jax.ShapeDtypeStruct((span_count * SPAN, head_cols), jnp.bfloat16)
    return pl.pallas_call(
        out_kernel,
        grid_spec=pltpu.PrefetchScalarGridSpec(
            num_scalar_prefetch=1,
            grid=(span_count,),
            in_specs=[blocks(proj), blocks(prob), blocks(dscore)],
            out_specs=[blocks(out), blocks(out)],
        ),
        out_shape=[out, out],
        compiler_params=pltpu.CompilerParams(vmem_limit_bytes=48 * 2**20),
        cost_estimate=pl.CostEstimate(
            flops=8 * rows * SPAN * head_cols, bytes_accessed=14 * 2**20, transcendentals=0
        ),
    )(meta, proj, prob, dscore)


def run_spans(meta, query, cot, cond, held, bounds, gain, w_down, w_up, w_kv, w_kv_t, nbr_count, pool_count):
    span_count, width = cond.shape
    token_count, head_cols = query.shape
    slot_len = bounds[-1]
    parts = len(bounds) - 1
    rank = w_down.shape[1]
    whole = lambda a: pl.BlockSpec(a.shape, lambda s, m: (0,) * a.ndim, pipeline_mode=pl.Buffered(1))
    group = GROUP if span_count % GROUP == 0 else 1
    tokens = pl.BlockSpec((group * SPAN, head_cols), lambda s, m: (s, 0))
    small = [cond, gain.reshape(1, width), w_down, w_up, w_up.T, w_down.T]
    large = list(held) + [w_kv, w_kv_t]
    per_device = span_count * nbr_count
    keys = group * nbr_count * slot_len
    rows = per_device * slot_len
    lanes = SPAN * HEADS
    flops = 2 * rows * (2 * width * 2 * head_cols + 6 * width * rank + 6 * SPAN * head_cols)
    return pl.pallas_call(
        functools.partial(span_kernel, len(held), nbr_count, bounds, pool_count),
        grid_spec=pltpu.PrefetchScalarGridSpec(
            num_scalar_prefetch=1,
            grid=(span_count // group,),
            in_specs=[tokens, tokens]
            + [whole(a) for a in small]
            + [pl.BlockSpec(memory_space=pltpu.HBM)] * len(large),
            out_specs=[pl.BlockSpec(memory_space=pltpu.HBM)] * 3
            + [
                pl.BlockSpec((span_count, width), lambda s, m: (0, 0)),
                pl.BlockSpec((width // 2, 2 * rank), lambda s, m: (0, 0)),
                pl.BlockSpec((width // 2, 2 * rank), lambda s, m: (0, 0)),
            ],
            scratch_shapes=[
                pltpu.VMEM((per_device, slot_len, width), jnp.bfloat16),
                pltpu.VMEM((width, 2 * head_cols), jnp.bfloat16),
                pltpu.VMEM((2 * head_cols, width), jnp.bfloat16),
                pltpu.VMEM((keys, 2 * head_cols), jnp.bfloat16),
                pltpu.VMEM((keys, 2 * head_cols), jnp.bfloat16),
                pltpu.VMEM((keys, lanes), jnp.float32),
                pltpu.VMEM((keys, lanes), jnp.float32),
                pltpu.VMEM((keys, lanes), jnp.bfloat16),
                pltpu.VMEM((keys, lanes), jnp.bfloat16),
                pltpu.VMEM((group * 2 * SPAN, head_cols), jnp.bfloat16),
                pltpu.VMEM((group * 2 * SPAN, head_cols), jnp.bfloat16),
                pltpu.VMEM((width, 2 * rank), jnp.float32),
                pltpu.SemaphoreType.DMA((per_device * parts,)),
                pltpu.SemaphoreType.DMA((5,)),
            ],
        ),
        out_shape=[
            jax.ShapeDtypeStruct((rows, 2 * head_cols), jnp.bfloat16),
            jax.ShapeDtypeStruct((rows, lanes), jnp.bfloat16),
            jax.ShapeDtypeStruct((rows, lanes), jnp.bfloat16),
            jax.ShapeDtypeStruct((span_count, width), jnp.float32),
            jax.ShapeDtypeStruct((width // 2, 2 * rank), jnp.float32),
            jax.ShapeDtypeStruct((width // 2, 2 * rank), jnp.bfloat16),
        ],
        compiler_params=pltpu.CompilerParams(vmem_limit_bytes=60 * 2**20),
        cost_estimate=pl.CostEstimate(
            flops=flops, bytes_accessed=16 * 2**20, transcendentals=rows * SPAN * HEADS
        ),
    )(meta, query, cot, *small, *large)


def pick_kernel(held_count, meta, *refs):
    held_refs, out_ref = refs[:held_count], refs[held_count]
    for b, held in enumerate(held_refs):
        @pl.when(meta[0] == b)
        def _():
            for n in range(out_ref.shape[0]):
                out_ref[n] = held[meta[1 + n]]


def pick(which, index, held):
    count = index.shape[0]
    meta = jnp.concatenate([jnp.reshape(which, (1,)), index]).astype(jnp.int32)
    return pl.pallas_call(
        functools.partial(pick_kernel, len(held)),
        grid_spec=pltpu.PrefetchScalarGridSpec(
            num_scalar_prefetch=1,
            grid=(1,),
            in_specs=[pl.BlockSpec(memory_space=pltpu.VMEM)] * len(held),
            out_specs=pl.BlockSpec(memory_space=pltpu.VMEM),
        ),
        out_shape=jax.ShapeDtypeStruct((count,) + held[0].shape[1:], held[0].dtype),
        compiler_params=pltpu.CompilerParams(vmem_limit_bytes=16 * 2**20),
    )(meta, *held)


def place_requests(owners, per_device, pool_count, lanes):
    half = pool_count // 2
    count = owners.shape[1]
    order = jnp.arange(count, dtype=jnp.int32)
    side = (order // per_device) // half
    mate = side[:, None] == side[None, :]
    before = order[None, :] < order[:, None]
    same = owners[:, :, None] == owners[:, None, :]
    lower = owners[:, None, :] < owners[:, :, None]
    total = lambda mask: jnp.sum(mask.astype(jnp.int32), axis=2)
    rank = total(same & (mate & before)[None])
    crosses = rank >= lanes
    far = crosses[:, None, :]
    number = total(far & mate[None] & (lower | (same & before[None])))
    first = total(far & ~mate[None] & lower)
    guests = total(far & ~mate[None] & same)
    lane = jnp.where(crosses, number, first + guests + rank) % lanes
    row = jnp.where(crosses, 1 - side[None, :], side[None, :]) * half + lane % half
    return row, lane // half, crosses, number // half


def scatter_sum(keep, give, axes, beside):
    width = keep.shape[1]
    size, columns = (lax.axis_size(axis) for axis in axes)
    index = lax.axis_index(axes[0])
    swap = lambda a, bit: lax.ppermute(a, axes[0], [(i, i ^ bit) for i in range(size)])
    total = keep + swap(give, 1).astype(jnp.float32)
    bit = 2
    while bit < size:
        split = total.reshape(size // bit // 2, 2, -1, width)
        mine = (index // bit) % 2
        keep = lax.dynamic_index_in_dim(split, mine, 1, keepdims=False)
        give = lax.dynamic_index_in_dim(split, 1 - mine, 1, keepdims=False)
        total = keep + swap(give.astype(jnp.bfloat16), bit).astype(jnp.float32)
        bit *= 2
    parts = total.reshape(columns, -1, width).astype(jnp.bfloat16)
    parts, tied = lax.optimization_barrier((parts, beside[1]))
    parts = lax.all_to_all(parts, axes[1], split_axis=0, concat_axis=0, tiled=True)
    return jnp.sum(parts.astype(jnp.float32), axis=0), beside[0](tied)


def body(
    queries, cotangent, cond, nbr_owner, nbr_block, database, lengths, gain, w_down, w_up, w_kv
):
    axes = ("pool", "dp")
    pool_count = lax.axis_size("pool")
    columns = lax.axis_size("dp")
    relay_row = pool_count - 1
    half = pool_count // 2
    row = lax.axis_index("pool")
    me = lax.axis_index("dp")
    span_count, width = cond.shape[2:]
    nbr_count = nbr_owner.shape[3]
    per_device = span_count * nbr_count
    block_count, slot_len = database.shape[2:4]
    live_count = relay_row * per_device
    capacity = max(2, live_count // columns + 1)
    slots = -(-capacity // pool_count)
    lanes = half * slots
    most = 0
    if capacity > lanes:
        for rows in (half, relay_row - half):
            full, left = divmod(rows * per_device, capacity)
            most = max(most, full * (capacity - lanes) + max(0, left - lanes))
    crossing = -(-most // half)
    token_count, head_cols = queries.shape[2:]

    def hop(array, pairs):
        return lax.ppermute(
            array, axes, [(a * columns + j, b * columns + j) for a, b in pairs for j in range(columns)]
        )

    first = slot_len // 16 * 3 // 4 * 16
    bounds = [0, first, slot_len] if 0 < first < slot_len else [0, slot_len]
    parts = len(bounds) - 1
    full_store = database.reshape(block_count, slot_len, width)
    cut = lambda i: full_store[:, bounds[i] : bounds[i + 1]]
    store = [cut(0)]

    def to_all(array, axis):
        copies = jnp.broadcast_to(array[None], (lax.axis_size(axis),) + array.shape)
        return lax.all_to_all(copies, axis, split_axis=0, concat_axis=0, tiled=True)

    info = jnp.concatenate([nbr_owner.reshape(-1), nbr_block.reshape(-1), lengths.reshape(-1)])
    info = jnp.pad(info, (0, -info.shape[0] % 128))
    over = lambda a: hop(a, [(relay_row, relay_row - half)])
    across = [over(store[0])]
    table = to_all(info.reshape(-1, 128), axes)
    w_kv_t = w_kv.T
    full_store, across, table, w_kv_t = lax.optimization_barrier(
        (full_store, across, table, w_kv_t)
    )
    store += [cut(i) for i in range(1, parts)]
    across += [over(a) for a in store[1:]]
    table = table.reshape(pool_count, columns, -1)
    by_column = jnp.swapaxes(table[:relay_row], 0, 1)
    owners = by_column[:, :, :per_device].reshape(columns, live_count)
    blocks = by_column[:, :, per_device : 2 * per_device].reshape(columns, live_count)
    store_len = table[relay_row, :, 2 * per_device : 2 * per_device + block_count]
    carrier, slot, crosses, number = place_requests(owners, per_device, pool_count, lanes)

    ring = jnp.arange(slots, dtype=jnp.int32)
    mine = ((owners == me) & (carrier == row))[:, None, :] & (slot[:, None, :] == ring[None, :, None])
    slot_block = jnp.sum(jnp.where(mine, blocks[:, None, :], 0), axis=2).reshape(-1)

    mine_of = lambda a: lax.dynamic_index_in_dim(a, me, 0, keepdims=False)
    my_owner, my_block, my_carrier, my_slot, my_cross, my_number = map(
        mine_of, (owners, blocks, carrier, slot, crosses, number)
    )
    place = my_owner * slots + my_slot
    ring = jnp.arange(crossing, dtype=jnp.int32)
    mine = (my_cross & (my_carrier == row))[None, :] & (my_number[None, :] == ring[:, None])
    leaving_place = jnp.sum(jnp.where(mine, place[None, :], 0), axis=1)

    def share(array, step):
        return hop(array, [(p, p // half * half + (p + step) % half) for p in range(pool_count)])

    held = []
    for i in range(parts):
        near = jnp.where(row == relay_row, store[i], across[i])
        stores = [near]
        held_by = jnp.where(row % half == half - 1, 0, 1)
        for step in range(1, half):
            stores.append(hop(near, [(p, p - step) for p in (relay_row, relay_row - half)]))
            held_by = jnp.where(row % half == half - 1 - step, step, held_by)
        sends = pick(held_by, slot_block, stores)
        arrived = lax.all_to_all(sends, "dp", split_axis=0, concat_axis=0, tiled=True)
        here = [arrived] + [share(arrived, step) for step in range(1, half)]
        if crossing:
            leaving = pick(0, leaving_place, [arrived])
            landed = hop(leaving, [(p, (p + half) % pool_count) for p in range(pool_count)])
            here += [landed] + [share(landed, step) for step in range(1, half)]
        held.append(here)
    origin = jnp.where(my_cross, (my_carrier + half) % pool_count, my_carrier)
    which = (row - origin) % half + jnp.where(my_cross, half, 0)
    index = jnp.where(my_cross, my_number, place)
    held = [here[b] for b in range(len(held[0])) for here in held]

    own_row = jnp.minimum(row, relay_row - 1)
    hot = (my_owner * block_count + my_block)[:, None] == jnp.arange(
        columns * block_count, dtype=jnp.int32
    )[None, :]
    wanted_len = jnp.sum(jnp.where(hot, store_len.reshape(1, -1), 0), axis=1)
    own = lambda a: lax.dynamic_index_in_dim(
        a.reshape(relay_row, per_device), own_row, 0, keepdims=False
    )
    flags = jnp.stack([(row < relay_row).astype(jnp.int32), row % 2])
    meta = jnp.concatenate([flags, own(wanted_len), own(which), own(index)]).astype(jnp.int32)

    proj, prob, dscore, cond_grad, keep, give = run_spans(
        meta,
        queries.reshape(token_count, head_cols),
        cotangent.reshape(token_count, head_cols),
        cond.reshape(span_count, width).astype(jnp.float32),
        held,
        bounds,
        gain,
        w_down,
        w_up,
        w_kv,
        w_kv_t,
        nbr_count,
        pool_count,
    )

    outs = lambda tied: run_outs(tied, proj, prob, dscore, span_count)
    adapter_grad, (attn_out, q_grad) = scatter_sum(keep, give, axes, (outs, meta))
    return (
        attn_out.reshape(1, 1, token_count, head_cols),
        q_grad.reshape(1, 1, token_count, head_cols),
        cond_grad.reshape(1, 1, span_count, width),
        adapter_grad,
    )


def solution(mesh):
    return jax.shard_map(
        body,
        mesh=mesh,
        in_specs=(
            P("pool", "dp", None, None),
            P("pool", "dp", None, None),
            P("pool", "dp", None, None),
            P("pool", "dp", None, None),
            P("pool", "dp", None, None),
            P("pool", "dp", None, None, None),
            P("pool", "dp", None),
            P(),
            P(),
            P(),
            P(),
        ),
        out_specs=(
            P("pool", "dp", None, None),
            P("pool", "dp", None, None),
            P("pool", "dp", None, None),
            P(("pool", "dp"), None),
        ),
        check_vma=False,
    )
```

```python
import functools

import jax
import jax.numpy as jnp
from jax import lax
from jax.experimental import pallas as pl
from jax.experimental.pallas import tpu as pltpu
from jax.sharding import PartitionSpec as P

HEADS = 16
HEAD = 128
SPAN = 64
GROUP = 2

EPSILON = 1e-06
FLOOR = -1e30
LOG2E = 1.4426950408889634

NT = (((1,), (1,)), ((), ()))
TN = (((0,), (0,)), ((), ()))


def dot(a, b, dims=(((1,), (0,)), ((), ()))):
    return lax.dot_general(a, b, dims, preferred_element_type=jnp.float32)


def span_kernel(
    held_count, nbr_count, bounds, pool_count, meta,
    q_ref, cot_ref, cond_ref, gain_ref, down_ref, up_ref, upt_ref, downt_ref, *rest,
):
    held_refs = rest[:held_count]
    (kv_hbm, kvt_hbm, out_ref, qg_ref, cg_ref, keep_ref, give_ref,
     raw_ref, kv_ref, kvt_ref, proj_ref, grad_ref, score_ref, dprob_ref, stat_ref,
     q2_ref, cot2_ref, acc_ref, sems, kv_sem) = rest[held_count:]
    step = pl.program_id(0)
    per_device, slot_len, width = raw_ref.shape
    key_count = nbr_count * slot_len
    span_count = per_device // nbr_count
    group = span_count // pl.num_programs(0)
    head_cols = q_ref.shape[1]
    rank = down_ref.shape[1]
    scaling = HEAD ** (-0.5)
    live = meta[0] % 2 == 1
    odd = meta[0] // 2
    lens, which, index = 1, 1 + per_device, 1 + 2 * per_device
    parts = len(bounds) - 1
    cuts = [pl.ds(low, high - low) for low, high in zip(bounds, bounds[1:])]
    pairs = [pl.ds(i * 2 * HEAD, 2 * HEAD) for i in range(HEADS // 2)]
    value_pairs = [pl.ds(head_cols + i * 2 * HEAD, 2 * HEAD) for i in range(HEADS // 2)]
    lanes = [pl.ds(i * 2 * SPAN, 2 * SPAN) for i in range(HEADS // 2)]
    keys = [pl.ds(g * key_count, key_count) for g in range(group)]
    tokens = [pl.ds(g * SPAN, SPAN) for g in range(group)]
    double = [pl.ds(g * 2 * SPAN, 2 * SPAN) for g in range(group)]
    spots = [
        (g, cols, value_cols, lane)
        for g in range(group)
        for cols, value_cols, lane in zip(pairs, value_pairs, lanes)
    ]
    kv_copy = pltpu.make_async_copy(kv_hbm, kv_ref, kv_sem.at[0])
    kvt_copy = pltpu.make_async_copy(kvt_hbm, kvt_ref, kv_sem.at[1])

    @pl.when(step == 0)
    def _():
        for n in range(per_device):
            for b, held in enumerate(held_refs):
                @pl.when(meta[which + n] == b // parts)
                def _():
                    part = b % parts
                    pltpu.make_async_copy(
                        held.at[meta[index + n]],
                        raw_ref.at[n, cuts[part]],
                        sems.at[n * parts + part],
                    ).start()
        kv_copy.start()
        kvt_copy.start()
        q2_ref[...] = jnp.zeros_like(q2_ref)
        cot2_ref[...] = jnp.zeros_like(cot2_ref)

    for g in range(group):
        for i in range(HEADS):
            cols = pl.ds(i * HEAD, HEAD)
            part = pl.ds((2 * g + i % 2) * SPAN, SPAN)
            q2_ref[part, cols] = q_ref[tokens[g], cols]
            cot2_ref[part, cols] = cot_ref[tokens[g], cols]

    for n in range(group * nbr_count):
        for part in range(parts):
            item = step * group * nbr_count + n
            pltpu.make_async_copy(
                held_refs[part].at[0],
                raw_ref.at[item, cuts[part]],
                sems.at[item * parts + part],
            ).wait()
    x_full = jnp.concatenate(
        [
            raw_ref[pl.ds((step * group + g) * nbr_count, nbr_count)]
            .reshape(key_count, width)
            .astype(jnp.float32)
            + cond_ref[pl.ds(step * group + g, 1), :]
            for g in range(group)
        ],
        axis=0,
    )
    inv_rms = lax.rsqrt(jnp.mean(x_full * x_full, axis=-1, keepdims=True) + EPSILON)
    gain = gain_ref[...]
    hidden = (x_full * inv_rms * gain).astype(jnp.bfloat16)
    latent = dot(hidden, down_ref[...]).astype(jnp.bfloat16)
    encoded = (x_full + dot(latent, up_ref[...])).astype(jnp.bfloat16)

    @pl.when(step == 0)
    def _():
        kv_copy.wait()

    for cols in pairs + value_pairs:
        proj_ref[:, cols] = dot(encoded, kv_ref[:, cols]).astype(jnp.bfloat16)

    slot = lax.broadcasted_iota(jnp.int32, (key_count, 2 * SPAN), 0)
    usable = []
    for g in range(group):
        limit = jnp.zeros((key_count, 2 * SPAN), jnp.int32)
        for n in range(nbr_count):
            here = jnp.logical_and(slot >= n * slot_len, slot < (n + 1) * slot_len)
            item = (step * group + g) * nbr_count + n
            limit = jnp.where(here, n * slot_len + meta[lens + item], limit)
        usable.append(slot < limit)

    def diagonal(both):
        return jnp.concatenate([both[:SPAN, :HEAD], both[SPAN:, HEAD:]], axis=1)

    for g, cols, value_cols, lane in spots:
        scores = jnp.where(usable[g], dot(proj_ref[keys[g], cols], q2_ref[double[g], cols], NT), FLOOR)
        score_ref[keys[g], lane] = scores
        stat_ref[g, 0:1, lane] = jnp.max(scores, axis=0, keepdims=True)
        dprob_ref[keys[g], lane] = dot(proj_ref[keys[g], value_cols], cot2_ref[double[g], cols], NT)

    for g, cols, value_cols, lane in spots:
        raised = jnp.exp2((score_ref[keys[g], lane] - stat_ref[g, 0:1, lane]) * (scaling * LOG2E))
        inv_sum = 1.0 / jnp.sum(raised, axis=0, keepdims=True)
        score_ref[keys[g], lane] = raised
        stat_ref[g, 1:2, lane] = inv_sum
        stat_ref[g, 2:3, lane] = inv_sum * jnp.sum(
            raised * dprob_ref[keys[g], lane], axis=0, keepdims=True
        )

    for g, cols, value_cols, lane in spots:
        probs = score_ref[keys[g], lane] * stat_ref[g, 1:2, lane]
        d_scores = probs * (dprob_ref[keys[g], lane] - stat_ref[g, 2:3, lane]) * scaling
        probs_b, d_scores = probs.astype(jnp.bfloat16), d_scores.astype(jnp.bfloat16)
        grad_ref[keys[g], cols] = dot(d_scores, q2_ref[double[g], cols]).astype(jnp.bfloat16)
        grad_ref[keys[g], value_cols] = dot(probs_b, cot2_ref[double[g], cols]).astype(jnp.bfloat16)
        out = diagonal(dot(probs_b.T, proj_ref[keys[g], value_cols]))
        grad = diagonal(dot(d_scores.T, proj_ref[keys[g], cols]))
        out_ref[tokens[g], cols] = jnp.where(live, out, 0.0).astype(jnp.bfloat16)
        qg_ref[tokens[g], cols] = jnp.where(live, grad, 0.0).astype(jnp.bfloat16)

    @pl.when(step == 0)
    def _():
        kvt_copy.wait()
        acc_ref[...] = jnp.zeros_like(acc_ref)

    enc_grad = dot(grad_ref[...], kvt_ref[...]).astype(jnp.bfloat16)
    lat_grad = dot(enc_grad, upt_ref[...]).astype(jnp.bfloat16)
    scaled = dot(lat_grad, downt_ref[...]) * gain
    normed = x_full * inv_rms
    x_grad = enc_grad.astype(jnp.float32) + inv_rms * (
        scaled - normed * jnp.mean(scaled * normed, axis=-1, keepdims=True)
    )
    for g in range(group):
        span_grad = jnp.sum(
            x_grad[g * key_count : (g + 1) * key_count], axis=0, keepdims=True
        )
        cg_ref[pl.ds(step * group + g, 1), :] = jnp.where(live, span_grad, 0.0)
    acc_ref[:, :rank] += dot(hidden, lat_grad, TN)
    acc_ref[:, rank:] += dot(enc_grad, latent, TN)

    @pl.when(step == pl.num_programs(0) - 1)
    def _():
        chunk = width // pool_count
        for k in range(pool_count // 2):
            part = pl.ds(k * chunk, chunk)
            for ref, own in ((keep_ref, odd), (give_ref, 1 - odd)):
                rows = acc_ref[pl.ds(pl.multiple_of((2 * k + own) * chunk, chunk), chunk), :]
                ref[part, :] = jnp.where(live, rows, 0.0).astype(ref.dtype)


def run_spans(meta, query, cot, cond, held, bounds, gain, w_down, w_up, w_kv, w_kv_t, nbr_count, pool_count):
    span_count, width = cond.shape
    token_count, head_cols = query.shape
    slot_len = bounds[-1]
    parts = len(bounds) - 1
    rank = w_down.shape[1]
    whole = lambda a: pl.BlockSpec(a.shape, lambda s, m: (0,) * a.ndim, pipeline_mode=pl.Buffered(1))
    group = GROUP if span_count % GROUP == 0 else 1
    tokens = pl.BlockSpec((group * SPAN, head_cols), lambda s, m: (s, 0))
    small = [cond, gain.reshape(1, width), w_down, w_up, w_up.T, w_down.T]
    large = list(held) + [w_kv, w_kv_t]
    per_device = span_count * nbr_count
    keys = group * nbr_count * slot_len
    rows = per_device * slot_len
    lanes = SPAN * HEADS
    flops = 2 * rows * (2 * width * 2 * head_cols + 6 * width * rank + 6 * SPAN * head_cols)
    return pl.pallas_call(
        functools.partial(span_kernel, len(held), nbr_count, bounds, pool_count),
        grid_spec=pltpu.PrefetchScalarGridSpec(
            num_scalar_prefetch=1,
            grid=(span_count // group,),
            in_specs=[tokens, tokens]
            + [whole(a) for a in small]
            + [pl.BlockSpec(memory_space=pltpu.HBM)] * len(large),
            out_specs=[
                tokens,
                tokens,
                pl.BlockSpec((span_count, width), lambda s, m: (0, 0)),
                pl.BlockSpec((width // 2, 2 * rank), lambda s, m: (0, 0)),
                pl.BlockSpec((width // 2, 2 * rank), lambda s, m: (0, 0)),
            ],
            scratch_shapes=[
                pltpu.VMEM((per_device, slot_len, width), jnp.bfloat16),
                pltpu.VMEM((width, 2 * head_cols), jnp.bfloat16),
                pltpu.VMEM((2 * head_cols, width), jnp.bfloat16),
                pltpu.VMEM((keys, 2 * head_cols), jnp.bfloat16),
                pltpu.VMEM((keys, 2 * head_cols), jnp.bfloat16),
                pltpu.VMEM((keys, lanes), jnp.float32),
                pltpu.VMEM((keys, lanes), jnp.float32),
                pltpu.VMEM((group, 8, lanes), jnp.float32),
                pltpu.VMEM((group * 2 * SPAN, head_cols), jnp.bfloat16),
                pltpu.VMEM((group * 2 * SPAN, head_cols), jnp.bfloat16),
                pltpu.VMEM((width, 2 * rank), jnp.float32),
                pltpu.SemaphoreType.DMA((per_device * parts,)),
                pltpu.SemaphoreType.DMA((2,)),
            ],
        ),
        out_shape=[
            jax.ShapeDtypeStruct((token_count, head_cols), jnp.bfloat16),
            jax.ShapeDtypeStruct((token_count, head_cols), jnp.bfloat16),
            jax.ShapeDtypeStruct((span_count, width), jnp.float32),
            jax.ShapeDtypeStruct((width // 2, 2 * rank), jnp.float32),
            jax.ShapeDtypeStruct((width // 2, 2 * rank), jnp.bfloat16),
        ],
        compiler_params=pltpu.CompilerParams(vmem_limit_bytes=60 * 2**20),
        cost_estimate=pl.CostEstimate(
            flops=flops, bytes_accessed=16 * 2**20, transcendentals=rows * SPAN * HEADS
        ),
    )(meta, query, cot, *small, *large)


def pick_kernel(held_count, meta, *refs):
    held_refs, out_ref = refs[:held_count], refs[held_count]
    for b, held in enumerate(held_refs):
        @pl.when(meta[0] == b)
        def _():
            for n in range(out_ref.shape[0]):
                out_ref[n] = held[meta[1 + n]]


def pick(which, index, held):
    count = index.shape[0]
    meta = jnp.concatenate([jnp.reshape(which, (1,)), index]).astype(jnp.int32)
    return pl.pallas_call(
        functools.partial(pick_kernel, len(held)),
        grid_spec=pltpu.PrefetchScalarGridSpec(
            num_scalar_prefetch=1,
            grid=(1,),
            in_specs=[pl.BlockSpec(memory_space=pltpu.VMEM)] * len(held),
            out_specs=pl.BlockSpec(memory_space=pltpu.VMEM),
        ),
        out_shape=jax.ShapeDtypeStruct((count,) + held[0].shape[1:], held[0].dtype),
        compiler_params=pltpu.CompilerParams(vmem_limit_bytes=16 * 2**20),
    )(meta, *held)


def place_requests(owners, per_device, pool_count, lanes):
    half = pool_count // 2
    count = owners.shape[1]
    order = jnp.arange(count, dtype=jnp.int32)
    side = (order // per_device) // half
    mate = side[:, None] == side[None, :]
    before = order[None, :] < order[:, None]
    same = owners[:, :, None] == owners[:, None, :]
    lower = owners[:, None, :] < owners[:, :, None]
    total = lambda mask: jnp.sum(mask.astype(jnp.int32), axis=2)
    rank = total(same & (mate & before)[None])
    crosses = rank >= lanes
    far = crosses[:, None, :]
    number = total(far & mate[None] & (lower | (same & before[None])))
    first = total(far & ~mate[None] & lower)
    guests = total(far & ~mate[None] & same)
    lane = jnp.where(crosses, number, first + guests + rank) % lanes
    row = jnp.where(crosses, 1 - side[None, :], side[None, :]) * half + lane % half
    return row, lane // half, crosses, number // half


def scatter_sum(keep, give, axes):
    width = keep.shape[1]
    size, columns = (lax.axis_size(axis) for axis in axes)
    index = lax.axis_index(axes[0])
    swap = lambda a, bit: lax.ppermute(a, axes[0], [(i, i ^ bit) for i in range(size)])
    total = keep + swap(give, 1).astype(jnp.float32)
    bit = 2
    while bit < size:
        split = total.reshape(size // bit // 2, 2, -1, width)
        mine = (index // bit) % 2
        keep = lax.dynamic_index_in_dim(split, mine, 1, keepdims=False)
        give = lax.dynamic_index_in_dim(split, 1 - mine, 1, keepdims=False)
        total = keep + swap(give.astype(jnp.bfloat16), bit).astype(jnp.float32)
        bit *= 2
    parts = total.reshape(columns, -1, width).astype(jnp.bfloat16)
    parts = lax.all_to_all(parts, axes[1], split_axis=0, concat_axis=0, tiled=True)
    return jnp.sum(parts.astype(jnp.float32), axis=0)


def body(
    queries, cotangent, cond, nbr_owner, nbr_block, database, lengths, gain, w_down, w_up, w_kv
):
    axes = ("pool", "dp")
    pool_count = lax.axis_size("pool")
    columns = lax.axis_size("dp")
    relay_row = pool_count - 1
    half = pool_count // 2
    row = lax.axis_index("pool")
    me = lax.axis_index("dp")
    span_count, width = cond.shape[2:]
    nbr_count = nbr_owner.shape[3]
    per_device = span_count * nbr_count
    block_count, slot_len = database.shape[2:4]
    live_count = relay_row * per_device
    capacity = max(2, live_count // columns + 1)
    slots = -(-capacity // pool_count)
    lanes = half * slots
    most = 0
    if capacity > lanes:
        for rows in (half, relay_row - half):
            full, left = divmod(rows * per_device, capacity)
            most = max(most, full * (capacity - lanes) + max(0, left - lanes))
    crossing = -(-most // half)
    token_count, head_cols = queries.shape[2:]

    def hop(array, pairs):
        return lax.ppermute(
            array, axes, [(a * columns + j, b * columns + j) for a, b in pairs for j in range(columns)]
        )

    first = slot_len // 16 * 3 // 4 * 16
    bounds = [0, first, slot_len] if 0 < first < slot_len else [0, slot_len]
    parts = len(bounds) - 1
    full_store = database.reshape(block_count, slot_len, width)
    cut = lambda i: full_store[:, bounds[i] : bounds[i + 1]]
    store = [cut(0)]

    def to_all(array, axis):
        copies = jnp.broadcast_to(array[None], (lax.axis_size(axis),) + array.shape)
        return lax.all_to_all(copies, axis, split_axis=0, concat_axis=0, tiled=True)

    info = jnp.concatenate([nbr_owner.reshape(-1), nbr_block.reshape(-1), lengths.reshape(-1)])
    info = jnp.pad(info, (0, -info.shape[0] % 128))
    over = lambda a: hop(a, [(relay_row, relay_row - half)])
    across = [over(store[0])]
    table = to_all(info.reshape(-1, 128), axes)
    w_kv_t = w_kv.T
    full_store, across, table, w_kv_t = lax.optimization_barrier(
        (full_store, across, table, w_kv_t)
    )
    store += [cut(i) for i in range(1, parts)]
    across += [over(a) for a in store[1:]]
    table = table.reshape(pool_count, columns, -1)
    by_column = jnp.swapaxes(table[:relay_row], 0, 1)
    owners = by_column[:, :, :per_device].reshape(columns, live_count)
    blocks = by_column[:, :, per_device : 2 * per_device].reshape(columns, live_count)
    store_len = table[relay_row, :, 2 * per_device : 2 * per_device + block_count]
    carrier, slot, crosses, number = place_requests(owners, per_device, pool_count, lanes)

    ring = jnp.arange(slots, dtype=jnp.int32)
    mine = ((owners == me) & (carrier == row))[:, None, :] & (slot[:, None, :] == ring[None, :, None])
    slot_block = jnp.sum(jnp.where(mine, blocks[:, None, :], 0), axis=2).reshape(-1)

    mine_of = lambda a: lax.dynamic_index_in_dim(a, me, 0, keepdims=False)
    my_owner, my_block, my_carrier, my_slot, my_cross, my_number = map(
        mine_of, (owners, blocks, carrier, slot, crosses, number)
    )
    place = my_owner * slots + my_slot
    ring = jnp.arange(crossing, dtype=jnp.int32)
    mine = (my_cross & (my_carrier == row))[None, :] & (my_number[None, :] == ring[:, None])
    leaving_place = jnp.sum(jnp.where(mine, place[None, :], 0), axis=1)

    def share(array, step):
        return hop(array, [(p, p // half * half + (p + step) % half) for p in range(pool_count)])

    held = []
    for i in range(parts):
        near = jnp.where(row == relay_row, store[i], across[i])
        stores = [near]
        held_by = jnp.where(row % half == half - 1, 0, 1)
        for step in range(1, half):
            stores.append(hop(near, [(p, p - step) for p in (relay_row, relay_row - half)]))
            held_by = jnp.where(row % half == half - 1 - step, step, held_by)
        sends = pick(held_by, slot_block, stores)
        arrived = lax.all_to_all(sends, "dp", split_axis=0, concat_axis=0, tiled=True)
        here = [arrived] + [share(arrived, step) for step in range(1, half)]
        if crossing:
            leaving = pick(0, leaving_place, [arrived])
            landed = hop(leaving, [(p, (p + half) % pool_count) for p in range(pool_count)])
            here += [landed] + [share(landed, step) for step in range(1, half)]
        held.append(here)
    origin = jnp.where(my_cross, (my_carrier + half) % pool_count, my_carrier)
    which = (row - origin) % half + jnp.where(my_cross, half, 0)
    index = jnp.where(my_cross, my_number, place)
    held = [here[b] for b in range(len(held[0])) for here in held]

    own_row = jnp.minimum(row, relay_row - 1)
    hot = (my_owner * block_count + my_block)[:, None] == jnp.arange(
        columns * block_count, dtype=jnp.int32
    )[None, :]
    wanted_len = jnp.sum(jnp.where(hot, store_len.reshape(1, -1), 0), axis=1)
    own = lambda a: lax.dynamic_index_in_dim(
        a.reshape(relay_row, per_device), own_row, 0, keepdims=False
    )
    live = (row < relay_row).astype(jnp.int32) + row % 2 * 2
    meta = jnp.concatenate([live[None], own(wanted_len), own(which), own(index)]).astype(jnp.int32)

    attn_out, q_grad, cond_grad, keep, give = run_spans(
        meta,
        queries.reshape(token_count, head_cols),
        cotangent.reshape(token_count, head_cols),
        cond.reshape(span_count, width).astype(jnp.float32),
        held,
        bounds,
        gain,
        w_down,
        w_up,
        w_kv,
        w_kv_t,
        nbr_count,
        pool_count,
    )

    adapter_grad = scatter_sum(keep, give, axes)
    return (
        attn_out.reshape(1, 1, token_count, head_cols),
        q_grad.reshape(1, 1, token_count, head_cols),
        cond_grad.reshape(1, 1, span_count, width),
        adapter_grad,
    )


def solution(mesh):
    return jax.shard_map(
        body,
        mesh=mesh,
        in_specs=(
            P("pool", "dp", None, None),
            P("pool", "dp", None, None),
            P("pool", "dp", None, None),
            P("pool", "dp", None, None),
            P("pool", "dp", None, None),
            P("pool", "dp", None, None, None),
            P("pool", "dp", None),
            P(),
            P(),
            P(),
            P(),
        ),
        out_specs=(
            P("pool", "dp", None, None),
            P("pool", "dp", None, None),
            P("pool", "dp", None, None),
            P(("pool", "dp"), None),
        ),
        check_vma=False,
    )
```

```python
import functools

import jax
import jax.numpy as jnp
from jax import lax
from jax.experimental import pallas as pl
from jax.experimental.pallas import tpu as pltpu
from jax.sharding import PartitionSpec as P

HEADS = 16
HEAD = 128
SPAN = 64
GROUP = 2

EPSILON = 1e-06
FLOOR = -1e30
LOG2E = 1.4426950408889634

NT = (((1,), (1,)), ((), ()))
TN = (((0,), (0,)), ((), ()))


def dot(a, b, dims=(((1,), (0,)), ((), ()))):
    return lax.dot_general(a, b, dims, preferred_element_type=jnp.float32)


def span_kernel(
    held_count, nbr_count, bounds, pool_count, meta,
    cond_ref, gain_ref, down_ref, up_ref, upt_ref, downt_ref, *rest,
):
    held_refs = rest[:held_count]
    (q_hbm, cot_hbm, kv_hbm, kvt_hbm, out_hbm, qg_hbm, cg_ref, keep_ref, give_ref,
     q_ref, cot_ref, out_ref, qg_ref,
     raw_ref, kv_ref, kvt_ref, proj_ref, grad_ref, score_ref, dprob_ref, stat_ref,
     q2_ref, cot2_ref, acc_ref, sems, kv_sem) = rest[held_count:]
    step = pl.program_id(0)
    per_device, slot_len, width = raw_ref.shape
    key_count = nbr_count * slot_len
    span_count = per_device // nbr_count
    group = span_count // pl.num_programs(0)
    head_cols = q_ref.shape[1]
    rank = down_ref.shape[1]
    scaling = HEAD ** (-0.5)
    live = meta[0] % 2 == 1
    odd = meta[0] // 2
    lens, which, index = 1, 1 + per_device, 1 + 2 * per_device
    parts = len(bounds) - 1
    cuts = [pl.ds(low, high - low) for low, high in zip(bounds, bounds[1:])]
    pairs = [pl.ds(i * 2 * HEAD, 2 * HEAD) for i in range(HEADS // 2)]
    value_pairs = [pl.ds(head_cols + i * 2 * HEAD, 2 * HEAD) for i in range(HEADS // 2)]
    lanes = [pl.ds(i * 2 * SPAN, 2 * SPAN) for i in range(HEADS // 2)]
    keys = [pl.ds(g * key_count, key_count) for g in range(group)]
    tokens = [pl.ds(g * SPAN, SPAN) for g in range(group)]
    double = [pl.ds(g * 2 * SPAN, 2 * SPAN) for g in range(group)]
    spots = [
        (g, cols, value_cols, lane)
        for g in range(group)
        for cols, value_cols, lane in zip(pairs, value_pairs, lanes)
    ]
    kvt_copy = pltpu.make_async_copy(kvt_hbm, kvt_ref, kv_sem.at[0])
    token_copies = [
        pltpu.make_async_copy(q_hbm, q_ref, kv_sem.at[1]),
        pltpu.make_async_copy(cot_hbm, cot_ref, kv_sem.at[2]),
    ]
    own_rows = pl.ds(pl.multiple_of(step * group * SPAN, SPAN), group * SPAN)
    out_copies = [
        pltpu.make_async_copy(out_ref, out_hbm.at[own_rows], kv_sem.at[3]),
        pltpu.make_async_copy(qg_ref, qg_hbm.at[own_rows], kv_sem.at[4]),
    ]
    kv_piece = 4 * HEAD
    kv_copies = [
        pltpu.make_async_copy(
            kv_hbm.at[:, pl.ds(i * kv_piece, kv_piece)],
            kv_ref.at[:, pl.ds(i * kv_piece, kv_piece)],
            kv_sem.at[5 + i],
        )
        for i in range(2 * head_cols // kv_piece)
    ]

    @pl.when(step == 0)
    def _():
        for n in range(per_device):
            for b, held in enumerate(held_refs):
                @pl.when(meta[which + n] == b // parts)
                def _():
                    part = b % parts
                    pltpu.make_async_copy(
                        held.at[meta[index + n]],
                        raw_ref.at[n, cuts[part]],
                        sems.at[n * parts + part],
                    ).start()
        for copy in kv_copies + token_copies:
            copy.start()
        q2_ref[...] = jnp.zeros_like(q2_ref)
        cot2_ref[...] = jnp.zeros_like(cot2_ref)

    for n in range(group * nbr_count):
        for part in range(parts):
            item = step * group * nbr_count + n
            pltpu.make_async_copy(
                held_refs[part].at[0],
                raw_ref.at[item, cuts[part]],
                sems.at[item * parts + part],
            ).wait()
    x_full = jnp.concatenate(
        [
            raw_ref[pl.ds((step * group + g) * nbr_count, nbr_count)]
            .reshape(key_count, width)
            .astype(jnp.float32)
            + cond_ref[pl.ds(step * group + g, 1), :]
            for g in range(group)
        ],
        axis=0,
    )
    inv_rms = lax.rsqrt(jnp.mean(x_full * x_full, axis=-1, keepdims=True) + EPSILON)
    gain = gain_ref[...]
    hidden = (x_full * inv_rms * gain).astype(jnp.bfloat16)
    latent = dot(hidden, down_ref[...]).astype(jnp.bfloat16)
    encoded = (x_full + dot(latent, up_ref[...])).astype(jnp.bfloat16)

    for i, cols in enumerate(pairs + value_pairs):
        if i % 2 == 0:
            @pl.when(step == 0)
            def _():
                kv_copies[i // 2].wait()

        proj_ref[:, cols] = dot(encoded, kv_ref[:, cols]).astype(jnp.bfloat16)

    @pl.when(step == 0)
    def _():
        kvt_copy.start()
        for copy in token_copies:
            copy.wait()

    for g in range(group):
        for i in range(HEADS):
            cols = pl.ds(i * HEAD, HEAD)
            part = pl.ds((2 * g + i % 2) * SPAN, SPAN)
            q2_ref[part, cols] = q_ref[pl.ds(pl.multiple_of((step * group + g) * SPAN, SPAN), SPAN), cols]
            cot2_ref[part, cols] = cot_ref[pl.ds(pl.multiple_of((step * group + g) * SPAN, SPAN), SPAN), cols]

    slot = lax.broadcasted_iota(jnp.int32, (key_count, 2 * SPAN), 0)
    usable = []
    for g in range(group):
        limit = jnp.zeros((key_count, 2 * SPAN), jnp.int32)
        for n in range(nbr_count):
            here = jnp.logical_and(slot >= n * slot_len, slot < (n + 1) * slot_len)
            item = (step * group + g) * nbr_count + n
            limit = jnp.where(here, n * slot_len + meta[lens + item], limit)
        usable.append(slot < limit)

    def diagonal(both):
        return jnp.concatenate([both[:SPAN, :HEAD], both[SPAN:, HEAD:]], axis=1)

    for g, cols, value_cols, lane in spots:
        scores = jnp.where(usable[g], dot(proj_ref[keys[g], cols], q2_ref[double[g], cols], NT), FLOOR)
        score_ref[keys[g], lane] = scores
        stat_ref[g, 0:1, lane] = jnp.max(scores, axis=0, keepdims=True)
        dprob_ref[keys[g], lane] = dot(proj_ref[keys[g], value_cols], cot2_ref[double[g], cols], NT)

    for g, cols, value_cols, lane in spots:
        raised = jnp.exp2((score_ref[keys[g], lane] - stat_ref[g, 0:1, lane]) * (scaling * LOG2E))
        inv_sum = 1.0 / jnp.sum(raised, axis=0, keepdims=True)
        score_ref[keys[g], lane] = raised
        stat_ref[g, 1:2, lane] = inv_sum
        stat_ref[g, 2:3, lane] = inv_sum * jnp.sum(
            raised * dprob_ref[keys[g], lane], axis=0, keepdims=True
        )

    for g, cols, value_cols, lane in spots:
        probs = score_ref[keys[g], lane] * stat_ref[g, 1:2, lane]
        d_scores = probs * (dprob_ref[keys[g], lane] - stat_ref[g, 2:3, lane]) * scaling
        probs_b, d_scores = probs.astype(jnp.bfloat16), d_scores.astype(jnp.bfloat16)
        grad_ref[keys[g], cols] = dot(d_scores, q2_ref[double[g], cols]).astype(jnp.bfloat16)
        grad_ref[keys[g], value_cols] = dot(probs_b, cot2_ref[double[g], cols]).astype(jnp.bfloat16)
        out = diagonal(dot(probs_b.T, proj_ref[keys[g], value_cols]))
        grad = diagonal(dot(d_scores.T, proj_ref[keys[g], cols]))
        out_ref[tokens[g], cols] = jnp.where(live, out, 0.0).astype(jnp.bfloat16)
        qg_ref[tokens[g], cols] = jnp.where(live, grad, 0.0).astype(jnp.bfloat16)

    for copy in out_copies:
        copy.start()

    @pl.when(step == 0)
    def _():
        kvt_copy.wait()
        acc_ref[...] = jnp.zeros_like(acc_ref)

    enc_grad = dot(grad_ref[...], kvt_ref[...]).astype(jnp.bfloat16)
    lat_grad = dot(enc_grad, upt_ref[...]).astype(jnp.bfloat16)
    scaled = dot(lat_grad, downt_ref[...]) * gain
    normed = x_full * inv_rms
    x_grad = enc_grad.astype(jnp.float32) + inv_rms * (
        scaled - normed * jnp.mean(scaled * normed, axis=-1, keepdims=True)
    )
    for g in range(group):
        span_grad = jnp.sum(
            x_grad[g * key_count : (g + 1) * key_count], axis=0, keepdims=True
        )
        cg_ref[pl.ds(step * group + g, 1), :] = jnp.where(live, span_grad, 0.0)
    acc_ref[:, :rank] += dot(hidden, lat_grad, TN)
    acc_ref[:, rank:] += dot(enc_grad, latent, TN)
    for copy in out_copies:
        copy.wait()

    @pl.when(step == pl.num_programs(0) - 1)
    def _():
        chunk = width // pool_count
        for k in range(pool_count // 2):
            part = pl.ds(k * chunk, chunk)
            for ref, own in ((keep_ref, odd), (give_ref, 1 - odd)):
                rows = acc_ref[pl.ds(pl.multiple_of((2 * k + own) * chunk, chunk), chunk), :]
                ref[part, :] = jnp.where(live, rows, 0.0).astype(ref.dtype)


def run_spans(meta, query, cot, cond, held, bounds, gain, w_down, w_up, w_kv, w_kv_t, nbr_count, pool_count):
    span_count, width = cond.shape
    token_count, head_cols = query.shape
    slot_len = bounds[-1]
    parts = len(bounds) - 1
    rank = w_down.shape[1]
    whole = lambda a: pl.BlockSpec(a.shape, lambda s, m: (0,) * a.ndim, pipeline_mode=pl.Buffered(1))
    group = GROUP if span_count % GROUP == 0 else 1
    small = [cond, gain.reshape(1, width), w_down, w_up, w_up.T, w_down.T]
    large = list(held) + [query, cot, w_kv, w_kv_t]
    per_device = span_count * nbr_count
    keys = group * nbr_count * slot_len
    rows = per_device * slot_len
    lanes = SPAN * HEADS
    flops = 2 * rows * (2 * width * 2 * head_cols + 6 * width * rank + 6 * SPAN * head_cols)
    return pl.pallas_call(
        functools.partial(span_kernel, len(held), nbr_count, bounds, pool_count),
        grid_spec=pltpu.PrefetchScalarGridSpec(
            num_scalar_prefetch=1,
            grid=(span_count // group,),
            in_specs=[whole(a) for a in small]
            + [pl.BlockSpec(memory_space=pltpu.HBM)] * len(large),
            out_specs=[pl.BlockSpec(memory_space=pltpu.HBM)] * 2
            + [
                pl.BlockSpec((span_count, width), lambda s, m: (0, 0)),
                pl.BlockSpec((width // 2, 2 * rank), lambda s, m: (0, 0)),
                pl.BlockSpec((width // 2, 2 * rank), lambda s, m: (0, 0)),
            ],
            scratch_shapes=[
                pltpu.VMEM((token_count, head_cols), jnp.bfloat16),
                pltpu.VMEM((token_count, head_cols), jnp.bfloat16),
                pltpu.VMEM((group * SPAN, head_cols), jnp.bfloat16),
                pltpu.VMEM((group * SPAN, head_cols), jnp.bfloat16),
                pltpu.VMEM((per_device, slot_len, width), jnp.bfloat16),
                pltpu.VMEM((width, 2 * head_cols), jnp.bfloat16),
                pltpu.VMEM((2 * head_cols, width), jnp.bfloat16),
                pltpu.VMEM((keys, 2 * head_cols), jnp.bfloat16),
                pltpu.VMEM((keys, 2 * head_cols), jnp.bfloat16),
                pltpu.VMEM((keys, lanes), jnp.float32),
                pltpu.VMEM((keys, lanes), jnp.float32),
                pltpu.VMEM((group, 8, lanes), jnp.float32),
                pltpu.VMEM((group * 2 * SPAN, head_cols), jnp.bfloat16),
                pltpu.VMEM((group * 2 * SPAN, head_cols), jnp.bfloat16),
                pltpu.VMEM((width, 2 * rank), jnp.float32),
                pltpu.SemaphoreType.DMA((per_device * parts,)),
                pltpu.SemaphoreType.DMA((5 + head_cols // (2 * HEAD),)),
            ],
        ),
        out_shape=[
            jax.ShapeDtypeStruct((token_count, head_cols), jnp.bfloat16),
            jax.ShapeDtypeStruct((token_count, head_cols), jnp.bfloat16),
            jax.ShapeDtypeStruct((span_count, width), jnp.float32),
            jax.ShapeDtypeStruct((width // 2, 2 * rank), jnp.float32),
            jax.ShapeDtypeStruct((width // 2, 2 * rank), jnp.bfloat16),
        ],
        compiler_params=pltpu.CompilerParams(vmem_limit_bytes=60 * 2**20),
        cost_estimate=pl.CostEstimate(
            flops=flops, bytes_accessed=16 * 2**20, transcendentals=rows * SPAN * HEADS
        ),
    )(meta, *small, *large)


def pick_kernel(held_count, meta, *refs):
    held_refs, out_ref = refs[:held_count], refs[held_count]
    for b, held in enumerate(held_refs):
        @pl.when(meta[0] == b)
        def _():
            for n in range(out_ref.shape[0]):
                out_ref[n] = held[meta[1 + n]]


def pick(which, index, held):
    count = index.shape[0]
    meta = jnp.concatenate([jnp.reshape(which, (1,)), index]).astype(jnp.int32)
    return pl.pallas_call(
        functools.partial(pick_kernel, len(held)),
        grid_spec=pltpu.PrefetchScalarGridSpec(
            num_scalar_prefetch=1,
            grid=(1,),
            in_specs=[pl.BlockSpec(memory_space=pltpu.VMEM)] * len(held),
            out_specs=pl.BlockSpec(memory_space=pltpu.VMEM),
        ),
        out_shape=jax.ShapeDtypeStruct((count,) + held[0].shape[1:], held[0].dtype),
        compiler_params=pltpu.CompilerParams(vmem_limit_bytes=16 * 2**20),
    )(meta, *held)


def place_requests(owners, per_device, pool_count, lanes):
    half = pool_count // 2
    count = owners.shape[1]
    order = jnp.arange(count, dtype=jnp.int32)
    side = (order // per_device) // half
    mate = side[:, None] == side[None, :]
    before = order[None, :] < order[:, None]
    same = owners[:, :, None] == owners[:, None, :]
    lower = owners[:, None, :] < owners[:, :, None]
    total = lambda mask: jnp.sum(mask.astype(jnp.int32), axis=2)
    rank = total(same & (mate & before)[None])
    crosses = rank >= lanes
    far = crosses[:, None, :]
    number = total(far & mate[None] & (lower | (same & before[None])))
    first = total(far & ~mate[None] & lower)
    guests = total(far & ~mate[None] & same)
    lane = jnp.where(crosses, number, first + guests + rank) % lanes
    row = jnp.where(crosses, 1 - side[None, :], side[None, :]) * half + lane % half
    return row, lane // half, crosses, number // half


def scatter_sum(keep, give, axes):
    width = keep.shape[1]
    size, columns = (lax.axis_size(axis) for axis in axes)
    index = lax.axis_index(axes[0])
    swap = lambda a, bit: lax.ppermute(a, axes[0], [(i, i ^ bit) for i in range(size)])
    total = keep + swap(give, 1).astype(jnp.float32)
    bit = 2
    while bit < size:
        split = total.reshape(size // bit // 2, 2, -1, width)
        mine = (index // bit) % 2
        keep = lax.dynamic_index_in_dim(split, mine, 1, keepdims=False)
        give = lax.dynamic_index_in_dim(split, 1 - mine, 1, keepdims=False)
        total = keep + swap(give.astype(jnp.bfloat16), bit).astype(jnp.float32)
        bit *= 2
    parts = total.reshape(columns, -1, width).astype(jnp.bfloat16)
    parts = lax.all_to_all(parts, axes[1], split_axis=0, concat_axis=0, tiled=True)
    return jnp.sum(parts.astype(jnp.float32), axis=0)


def body(
    queries, cotangent, cond, nbr_owner, nbr_block, database, lengths, gain, w_down, w_up, w_kv
):
    axes = ("pool", "dp")
    pool_count = lax.axis_size("pool")
    columns = lax.axis_size("dp")
    relay_row = pool_count - 1
    half = pool_count // 2
    row = lax.axis_index("pool")
    me = lax.axis_index("dp")
    span_count, width = cond.shape[2:]
    nbr_count = nbr_owner.shape[3]
    per_device = span_count * nbr_count
    block_count, slot_len = database.shape[2:4]
    live_count = relay_row * per_device
    capacity = max(2, live_count // columns + 1)
    slots = -(-capacity // pool_count)
    lanes = half * slots
    most = 0
    if capacity > lanes:
        for rows in (half, relay_row - half):
            full, left = divmod(rows * per_device, capacity)
            most = max(most, full * (capacity - lanes) + max(0, left - lanes))
    crossing = -(-most // half)
    token_count, head_cols = queries.shape[2:]

    def hop(array, pairs):
        return lax.ppermute(
            array, axes, [(a * columns + j, b * columns + j) for a, b in pairs for j in range(columns)]
        )

    first = slot_len // 16 * 3 // 4 * 16
    bounds = [0, first, slot_len] if 0 < first < slot_len else [0, slot_len]
    parts = len(bounds) - 1
    full_store = database.reshape(block_count, slot_len, width)
    cut = lambda i: full_store[:, bounds[i] : bounds[i + 1]]
    store = [cut(0)]

    def to_all(array, axis):
        copies = jnp.broadcast_to(array[None], (lax.axis_size(axis),) + array.shape)
        return lax.all_to_all(copies, axis, split_axis=0, concat_axis=0, tiled=True)

    info = jnp.concatenate([nbr_owner.reshape(-1), nbr_block.reshape(-1), lengths.reshape(-1)])
    info = jnp.pad(info, (0, -info.shape[0] % 128))
    over = lambda a: hop(a, [(relay_row, relay_row - half)])
    across = [over(store[0])]
    table = to_all(info.reshape(-1, 128), axes)
    w_kv_t = w_kv.T
    full_store, across, table, w_kv_t = lax.optimization_barrier(
        (full_store, across, table, w_kv_t)
    )
    store += [cut(i) for i in range(1, parts)]
    across += [over(a) for a in store[1:]]
    table = table.reshape(pool_count, columns, -1)
    by_column = jnp.swapaxes(table[:relay_row], 0, 1)
    owners = by_column[:, :, :per_device].reshape(columns, live_count)
    blocks = by_column[:, :, per_device : 2 * per_device].reshape(columns, live_count)
    store_len = table[relay_row, :, 2 * per_device : 2 * per_device + block_count]
    carrier, slot, crosses, number = place_requests(owners, per_device, pool_count, lanes)

    ring = jnp.arange(slots, dtype=jnp.int32)
    mine = ((owners == me) & (carrier == row))[:, None, :] & (slot[:, None, :] == ring[None, :, None])
    slot_block = jnp.sum(jnp.where(mine, blocks[:, None, :], 0), axis=2).reshape(-1)

    mine_of = lambda a: lax.dynamic_index_in_dim(a, me, 0, keepdims=False)
    my_owner, my_block, my_carrier, my_slot, my_cross, my_number = map(
        mine_of, (owners, blocks, carrier, slot, crosses, number)
    )
    place = my_owner * slots + my_slot
    ring = jnp.arange(crossing, dtype=jnp.int32)
    mine = (my_cross & (my_carrier == row))[None, :] & (my_number[None, :] == ring[:, None])
    leaving_place = jnp.sum(jnp.where(mine, place[None, :], 0), axis=1)

    def share(array, step):
        return hop(array, [(p, p // half * half + (p + step) % half) for p in range(pool_count)])

    held = []
    for i in range(parts):
        near = jnp.where(row == relay_row, store[i], across[i])
        stores = [near]
        held_by = jnp.where(row % half == half - 1, 0, 1)
        for step in range(1, half):
            stores.append(hop(near, [(p, p - step) for p in (relay_row, relay_row - half)]))
            held_by = jnp.where(row % half == half - 1 - step, step, held_by)
        sends = pick(held_by, slot_block, stores)
        arrived = lax.all_to_all(sends, "dp", split_axis=0, concat_axis=0, tiled=True)
        here = [arrived] + [share(arrived, step) for step in range(1, half)]
        if crossing:
            leaving = pick(0, leaving_place, [arrived])
            landed = hop(leaving, [(p, (p + half) % pool_count) for p in range(pool_count)])
            here += [landed] + [share(landed, step) for step in range(1, half)]
        held.append(here)
    origin = jnp.where(my_cross, (my_carrier + half) % pool_count, my_carrier)
    which = (row - origin) % half + jnp.where(my_cross, half, 0)
    index = jnp.where(my_cross, my_number, place)
    held = [here[b] for b in range(len(held[0])) for here in held]

    own_row = jnp.minimum(row, relay_row - 1)
    hot = (my_owner * block_count + my_block)[:, None] == jnp.arange(
        columns * block_count, dtype=jnp.int32
    )[None, :]
    wanted_len = jnp.sum(jnp.where(hot, store_len.reshape(1, -1), 0), axis=1)
    own = lambda a: lax.dynamic_index_in_dim(
        a.reshape(relay_row, per_device), own_row, 0, keepdims=False
    )
    live = (row < relay_row).astype(jnp.int32) + row % 2 * 2
    meta = jnp.concatenate([live[None], own(wanted_len), own(which), own(index)]).astype(jnp.int32)

    attn_out, q_grad, cond_grad, keep, give = run_spans(
        meta,
        queries.reshape(token_count, head_cols),
        cotangent.reshape(token_count, head_cols),
        cond.reshape(span_count, width).astype(jnp.float32),
        held,
        bounds,
        gain,
        w_down,
        w_up,
        w_kv,
        w_kv_t,
        nbr_count,
        pool_count,
    )

    adapter_grad = scatter_sum(keep, give, axes)
    return (
        attn_out.reshape(1, 1, token_count, head_cols),
        q_grad.reshape(1, 1, token_count, head_cols),
        cond_grad.reshape(1, 1, span_count, width),
        adapter_grad,
    )


def solution(mesh):
    return jax.shard_map(
        body,
        mesh=mesh,
        in_specs=(
            P("pool", "dp", None, None),
            P("pool", "dp", None, None),
            P("pool", "dp", None, None),
            P("pool", "dp", None, None),
            P("pool", "dp", None, None),
            P("pool", "dp", None, None, None),
            P("pool", "dp", None),
            P(),
            P(),
            P(),
            P(),
        ),
        out_specs=(
            P("pool", "dp", None, None),
            P("pool", "dp", None, None),
            P("pool", "dp", None, None),
            P(("pool", "dp"), None),
        ),
        check_vma=False,
    )
```

```python
import functools

import jax
import jax.numpy as jnp
from jax import lax
from jax.experimental import pallas as pl
from jax.experimental.pallas import tpu as pltpu
from jax.sharding import PartitionSpec as P

HEADS = 16
HEAD = 128
SPAN = 64
GROUP = 2

EPSILON = 1e-06
FLOOR = -1e30
LOG2E = 1.4426950408889634

NT = (((1,), (1,)), ((), ()))
TN = (((0,), (0,)), ((), ()))


def dot(a, b, dims=(((1,), (0,)), ((), ()))):
    return lax.dot_general(a, b, dims, preferred_element_type=jnp.float32)


def span_kernel(
    held_count, nbr_count, bounds, pool_count, meta,
    q_ref, cot_ref, cond_ref, gain_ref, down_ref, up_ref, upt_ref, downt_ref, *rest,
):
    held_refs = rest[:held_count]
    (kv_hbm, kvt_hbm, out_ref, qg_ref, cg_ref, keep_ref, give_ref,
     raw_ref, kv_ref, kvt_ref, proj_ref, grad_ref, score_ref, dprob_ref, stat_ref,
     q2_ref, cot2_ref, acc_ref, sems, kv_sem) = rest[held_count:]
    step = pl.program_id(0)
    per_device, slot_len, width = raw_ref.shape
    key_count = nbr_count * slot_len
    span_count = per_device // nbr_count
    group = span_count // pl.num_programs(0)
    head_cols = q_ref.shape[1]
    rank = down_ref.shape[1]
    scaling = HEAD ** (-0.5)
    live = meta[0] % 2 == 1
    odd = meta[0] // 2
    lens, which, index = 1, 1 + per_device, 1 + 2 * per_device
    parts = len(bounds) - 1
    cuts = [pl.ds(low, high - low) for low, high in zip(bounds, bounds[1:])]
    pairs = [pl.ds(i * 2 * HEAD, 2 * HEAD) for i in range(HEADS // 2)]
    value_pairs = [pl.ds(head_cols + i * 2 * HEAD, 2 * HEAD) for i in range(HEADS // 2)]
    lanes = [pl.ds(i * 2 * SPAN, 2 * SPAN) for i in range(HEADS // 2)]
    keys = [pl.ds(g * key_count, key_count) for g in range(group)]
    tokens = [pl.ds(g * SPAN, SPAN) for g in range(group)]
    double = [pl.ds(g * 2 * SPAN, 2 * SPAN) for g in range(group)]
    spots = [
        (g, cols, value_cols, lane)
        for g in range(group)
        for cols, value_cols, lane in zip(pairs, value_pairs, lanes)
    ]
    kv_copy = pltpu.make_async_copy(kv_hbm, kv_ref, kv_sem.at[0])
    kvt_copy = pltpu.make_async_copy(kvt_hbm, kvt_ref, kv_sem.at[1])

    @pl.when(step == 0)
    def _():
        for n in range(per_device):
            for b, held in enumerate(held_refs):
                @pl.when(meta[which + n] == b // parts)
                def _():
                    part = b % parts
                    pltpu.make_async_copy(
                        held.at[meta[index + n]],
                        raw_ref.at[n, cuts[part]],
                        sems.at[n * parts + part],
                    ).start()
        kv_copy.start()
        kvt_copy.start()
        q2_ref[...] = jnp.zeros_like(q2_ref)
        cot2_ref[...] = jnp.zeros_like(cot2_ref)

    for g in range(group):
        for i in range(HEADS):
            cols = pl.ds(i * HEAD, HEAD)
            part = pl.ds((2 * g + i % 2) * SPAN, SPAN)
            q2_ref[part, cols] = q_ref[tokens[g], cols]
            cot2_ref[part, cols] = cot_ref[tokens[g], cols]

    for n in range(group * nbr_count):
        for part in range(parts):
            item = step * group * nbr_count + n
            pltpu.make_async_copy(
                held_refs[part].at[0],
                raw_ref.at[item, cuts[part]],
                sems.at[item * parts + part],
            ).wait()
    x_full = jnp.concatenate(
        [
            raw_ref[pl.ds((step * group + g) * nbr_count, nbr_count)]
            .reshape(key_count, width)
            .astype(jnp.float32)
            + cond_ref[pl.ds(step * group + g, 1), :]
            for g in range(group)
        ],
        axis=0,
    )
    inv_rms = lax.rsqrt(jnp.mean(x_full * x_full, axis=-1, keepdims=True) + EPSILON)
    gain = gain_ref[...]
    hidden = (x_full * inv_rms * gain).astype(jnp.bfloat16)
    latent = dot(hidden, down_ref[...]).astype(jnp.bfloat16)
    encoded = (x_full + dot(latent, up_ref[...])).astype(jnp.bfloat16)

    @pl.when(step == 0)
    def _():
        kv_copy.wait()

    for cols in pairs + value_pairs:
        proj_ref[:, cols] = dot(encoded, kv_ref[:, cols]).astype(jnp.bfloat16)

    slot = lax.broadcasted_iota(jnp.int32, (key_count, 2 * SPAN), 0)
    usable = []
    for g in range(group):
        limit = jnp.zeros((key_count, 2 * SPAN), jnp.int32)
        for n in range(nbr_count):
            here = jnp.logical_and(slot >= n * slot_len, slot < (n + 1) * slot_len)
            item = (step * group + g) * nbr_count + n
            limit = jnp.where(here, n * slot_len + meta[lens + item], limit)
        usable.append(slot < limit)

    def diagonal(both):
        return jnp.concatenate([both[:SPAN, :HEAD], both[SPAN:, HEAD:]], axis=1)

    for g, cols, value_cols, lane in spots:
        scores = jnp.where(usable[g], dot(proj_ref[keys[g], cols], q2_ref[double[g], cols], NT), FLOOR)
        score_ref[keys[g], lane] = scores
        stat_ref[g, 0:1, lane] = jnp.max(scores, axis=0, keepdims=True)
        dprob_ref[keys[g], lane] = dot(proj_ref[keys[g], value_cols], cot2_ref[double[g], cols], NT)

    for g, cols, value_cols, lane in spots:
        raised = jnp.exp2((score_ref[keys[g], lane] - stat_ref[g, 0:1, lane]) * (scaling * LOG2E))
        inv_sum = 1.0 / jnp.sum(raised, axis=0, keepdims=True)
        score_ref[keys[g], lane] = raised
        stat_ref[g, 1:2, lane] = inv_sum
        stat_ref[g, 2:3, lane] = inv_sum * jnp.sum(
            raised * dprob_ref[keys[g], lane], axis=0, keepdims=True
        )

    for g, cols, value_cols, lane in spots:
        probs = score_ref[keys[g], lane] * stat_ref[g, 1:2, lane]
        d_scores = probs * (dprob_ref[keys[g], lane] - stat_ref[g, 2:3, lane]) * scaling
        probs_b, d_scores = probs.astype(jnp.bfloat16), d_scores.astype(jnp.bfloat16)
        grad_ref[keys[g], cols] = dot(d_scores, q2_ref[double[g], cols]).astype(jnp.bfloat16)
        grad_ref[keys[g], value_cols] = dot(probs_b, cot2_ref[double[g], cols]).astype(jnp.bfloat16)
        out = diagonal(dot(probs_b.T, proj_ref[keys[g], value_cols]))
        grad = diagonal(dot(d_scores.T, proj_ref[keys[g], cols]))
        out_ref[tokens[g], cols] = jnp.where(live, out, 0.0).astype(jnp.bfloat16)
        qg_ref[tokens[g], cols] = jnp.where(live, grad, 0.0).astype(jnp.bfloat16)

    @pl.when(step == 0)
    def _():
        kvt_copy.wait()
        acc_ref[...] = jnp.zeros_like(acc_ref)

    enc_grad = dot(grad_ref[...], kvt_ref[...]).astype(jnp.bfloat16)
    lat_grad = dot(enc_grad, upt_ref[...]).astype(jnp.bfloat16)
    scaled = dot(lat_grad, downt_ref[...]) * gain
    normed = x_full * inv_rms
    x_grad = enc_grad.astype(jnp.float32) + inv_rms * (
        scaled - normed * jnp.mean(scaled * normed, axis=-1, keepdims=True)
    )
    for g in range(group):
        span_grad = jnp.sum(
            x_grad[g * key_count : (g + 1) * key_count], axis=0, keepdims=True
        )
        cg_ref[pl.ds(step * group + g, 1), :] = jnp.where(live, span_grad, 0.0)
    acc_ref[:, :rank] += dot(hidden, lat_grad, TN)
    acc_ref[:, rank:] += dot(enc_grad, latent, TN)

    @pl.when(step == pl.num_programs(0) - 1)
    def _():
        chunk = width // pool_count
        for k in range(pool_count // 2):
            part = pl.ds(k * chunk, chunk)
            for ref, own in ((keep_ref, odd), (give_ref, 1 - odd)):
                rows = acc_ref[pl.ds(pl.multiple_of((2 * k + own) * chunk, chunk), chunk), :]
                ref[part, :] = jnp.where(live, rows, 0.0).astype(ref.dtype)


def run_spans(meta, query, cot, cond, held, bounds, gain, w_down, w_up, w_kv, w_kv_t, nbr_count, pool_count):
    span_count, width = cond.shape
    token_count, head_cols = query.shape
    slot_len = bounds[-1]
    parts = len(bounds) - 1
    rank = w_down.shape[1]
    whole = lambda a: pl.BlockSpec(a.shape, lambda s, m: (0,) * a.ndim, pipeline_mode=pl.Buffered(1))
    group = GROUP if span_count % GROUP == 0 else 1
    tokens = pl.BlockSpec((group * SPAN, head_cols), lambda s, m: (s, 0))
    small = [cond, gain.reshape(1, width), w_down, w_up, w_up.T, w_down.T]
    large = list(held) + [w_kv, w_kv_t]
    per_device = span_count * nbr_count
    keys = group * nbr_count * slot_len
    rows = per_device * slot_len
    lanes = SPAN * HEADS
    flops = 2 * rows * (2 * width * 2 * head_cols + 6 * width * rank + 6 * SPAN * head_cols)
    return pl.pallas_call(
        functools.partial(span_kernel, len(held), nbr_count, bounds, pool_count),
        grid_spec=pltpu.PrefetchScalarGridSpec(
            num_scalar_prefetch=1,
            grid=(span_count // group,),
            in_specs=[tokens, tokens]
            + [whole(a) for a in small]
            + [pl.BlockSpec(memory_space=pltpu.HBM)] * len(large),
            out_specs=[
                tokens,
                tokens,
                pl.BlockSpec((span_count, width), lambda s, m: (0, 0)),
                pl.BlockSpec((width // 2, 2 * rank), lambda s, m: (0, 0)),
                pl.BlockSpec((width // 2, 2 * rank), lambda s, m: (0, 0)),
            ],
            scratch_shapes=[
                pltpu.VMEM((per_device, slot_len, width), jnp.bfloat16),
                pltpu.VMEM((width, 2 * head_cols), jnp.bfloat16),
                pltpu.VMEM((2 * head_cols, width), jnp.bfloat16),
                pltpu.VMEM((keys, 2 * head_cols), jnp.bfloat16),
                pltpu.VMEM((keys, 2 * head_cols), jnp.bfloat16),
                pltpu.VMEM((keys, lanes), jnp.float32),
                pltpu.VMEM((keys, lanes), jnp.float32),
                pltpu.VMEM((group, 8, lanes), jnp.float32),
                pltpu.VMEM((group * 2 * SPAN, head_cols), jnp.bfloat16),
                pltpu.VMEM((group * 2 * SPAN, head_cols), jnp.bfloat16),
                pltpu.VMEM((width, 2 * rank), jnp.float32),
                pltpu.SemaphoreType.DMA((per_device * parts,)),
                pltpu.SemaphoreType.DMA((2,)),
            ],
        ),
        out_shape=[
            jax.ShapeDtypeStruct((token_count, head_cols), jnp.bfloat16),
            jax.ShapeDtypeStruct((token_count, head_cols), jnp.bfloat16),
            jax.ShapeDtypeStruct((span_count, width), jnp.float32),
            jax.ShapeDtypeStruct((width // 2, 2 * rank), jnp.float32),
            jax.ShapeDtypeStruct((width // 2, 2 * rank), jnp.bfloat16),
        ],
        compiler_params=pltpu.CompilerParams(vmem_limit_bytes=60 * 2**20),
        cost_estimate=pl.CostEstimate(
            flops=flops, bytes_accessed=16 * 2**20, transcendentals=rows * SPAN * HEADS
        ),
    )(meta, query, cot, *small, *large)


def pick_kernel(held_count, meta, *refs):
    held_refs, out_ref = refs[:held_count], refs[held_count]
    for b, held in enumerate(held_refs):
        @pl.when(meta[0] == b)
        def _():
            for n in range(out_ref.shape[0]):
                out_ref[n] = held[meta[1 + n]]


def pick(which, index, held):
    count = index.shape[0]
    meta = jnp.concatenate([jnp.reshape(which, (1,)), index]).astype(jnp.int32)
    return pl.pallas_call(
        functools.partial(pick_kernel, len(held)),
        grid_spec=pltpu.PrefetchScalarGridSpec(
            num_scalar_prefetch=1,
            grid=(1,),
            in_specs=[pl.BlockSpec(memory_space=pltpu.VMEM)] * len(held),
            out_specs=pl.BlockSpec(memory_space=pltpu.VMEM),
        ),
        out_shape=jax.ShapeDtypeStruct((count,) + held[0].shape[1:], held[0].dtype),
        compiler_params=pltpu.CompilerParams(vmem_limit_bytes=16 * 2**20),
    )(meta, *held)


def place_requests(owners, per_device, pool_count, lanes):
    half = pool_count // 2
    count = owners.shape[1]
    order = jnp.arange(count, dtype=jnp.int32)
    side = (order // per_device) // half
    mate = side[:, None] == side[None, :]
    before = order[None, :] < order[:, None]
    same = owners[:, :, None] == owners[:, None, :]
    lower = owners[:, None, :] < owners[:, :, None]
    total = lambda mask: jnp.sum(mask.astype(jnp.int32), axis=2)
    rank = total(same & (mate & before)[None])
    crosses = rank >= lanes
    far = crosses[:, None, :]
    number = total(far & mate[None] & (lower | (same & before[None])))
    first = total(far & ~mate[None] & lower)
    guests = total(far & ~mate[None] & same)
    lane = jnp.where(crosses, number, first + guests + rank) % lanes
    row = jnp.where(crosses, 1 - side[None, :], side[None, :]) * half + lane % half
    return row, lane // half, crosses, number // half


def scatter_sum(keep, give, axes):
    width = keep.shape[1]
    size, columns = (lax.axis_size(axis) for axis in axes)
    index = lax.axis_index(axes[0])
    swap = lambda a, bit: lax.ppermute(a, axes[0], [(i, i ^ bit) for i in range(size)])
    total = keep + swap(give, 1).astype(jnp.float32)
    bit = 2
    while bit < size:
        split = total.reshape(size // bit // 2, 2, -1, width)
        mine = (index // bit) % 2
        keep = lax.dynamic_index_in_dim(split, mine, 1, keepdims=False)
        give = lax.dynamic_index_in_dim(split, 1 - mine, 1, keepdims=False)
        total = keep + swap(give.astype(jnp.bfloat16), bit).astype(jnp.float32)
        bit *= 2
    parts = total.reshape(columns, -1, width).astype(jnp.bfloat16)
    parts = lax.all_to_all(parts, axes[1], split_axis=0, concat_axis=0, tiled=True)
    return jnp.sum(parts.astype(jnp.float32), axis=0)


def body(
    queries, cotangent, cond, nbr_owner, nbr_block, database, lengths, gain, w_down, w_up, w_kv
):
    axes = ("pool", "dp")
    pool_count = lax.axis_size("pool")
    columns = lax.axis_size("dp")
    relay_row = pool_count - 1
    half = pool_count // 2
    row = lax.axis_index("pool")
    me = lax.axis_index("dp")
    span_count, width = cond.shape[2:]
    nbr_count = nbr_owner.shape[3]
    per_device = span_count * nbr_count
    block_count, slot_len = database.shape[2:4]
    live_count = relay_row * per_device
    capacity = max(2, live_count // columns + 1)
    slots = -(-capacity // pool_count)
    lanes = half * slots
    most = 0
    if capacity > lanes:
        for rows in (half, relay_row - half):
            full, left = divmod(rows * per_device, capacity)
            most = max(most, full * (capacity - lanes) + max(0, left - lanes))
    crossing = -(-most // half)
    token_count, head_cols = queries.shape[2:]

    def hop(array, pairs):
        return lax.ppermute(
            array, axes, [(a * columns + j, b * columns + j) for a, b in pairs for j in range(columns)]
        )

    first = slot_len // 16 * 3 // 4 * 16
    bounds = [0, first, slot_len] if 0 < first < slot_len else [0, slot_len]
    parts = len(bounds) - 1
    full_store = database.reshape(block_count, slot_len, width)
    cut = lambda i: full_store[:, bounds[i] : bounds[i + 1]]
    store = [cut(0)]

    def to_all(array, axis):
        copies = jnp.broadcast_to(array[None], (lax.axis_size(axis),) + array.shape)
        return lax.all_to_all(copies, axis, split_axis=0, concat_axis=0, tiled=True)

    info = jnp.concatenate([nbr_owner.reshape(-1), nbr_block.reshape(-1), lengths.reshape(-1)])
    info = jnp.pad(info, (0, -info.shape[0] % 128))
    over = lambda a: hop(a, [(relay_row, relay_row - half)])
    across = [over(store[0])]
    table = to_all(info.reshape(-1, 128), axes)
    w_kv_t = w_kv.T
    full_store, table, w_kv_t = lax.optimization_barrier((full_store, table, w_kv_t))
    store += [cut(i) for i in range(1, parts)]
    across += [over(a) for a in store[1:]]
    table = table.reshape(pool_count, columns, -1)
    by_column = jnp.swapaxes(table[:relay_row], 0, 1)
    owners = by_column[:, :, :per_device].reshape(columns, live_count)
    blocks = by_column[:, :, per_device : 2 * per_device].reshape(columns, live_count)
    store_len = table[relay_row, :, 2 * per_device : 2 * per_device + block_count]
    carrier, slot, crosses, number = place_requests(owners, per_device, pool_count, lanes)

    ring = jnp.arange(slots, dtype=jnp.int32)
    mine = ((owners == me) & (carrier == row))[:, None, :] & (slot[:, None, :] == ring[None, :, None])
    slot_block = jnp.sum(jnp.where(mine, blocks[:, None, :], 0), axis=2).reshape(-1)

    mine_of = lambda a: lax.dynamic_index_in_dim(a, me, 0, keepdims=False)
    my_owner, my_block, my_carrier, my_slot, my_cross, my_number = map(
        mine_of, (owners, blocks, carrier, slot, crosses, number)
    )
    place = my_owner * slots + my_slot
    ring = jnp.arange(crossing, dtype=jnp.int32)
    mine = (my_cross & (my_carrier == row))[None, :] & (my_number[None, :] == ring[:, None])
    leaving_place = jnp.sum(jnp.where(mine, place[None, :], 0), axis=1)

    def share(array, step):
        return hop(array, [(p, p // half * half + (p + step) % half) for p in range(pool_count)])

    origin = jnp.where(my_cross, (my_carrier + half) % pool_count, my_carrier)
    which = (row - origin) % half + jnp.where(my_cross, half, 0)
    index = jnp.where(my_cross, my_number, place)
    own_row = jnp.minimum(row, relay_row - 1)
    hot = (my_owner * block_count + my_block)[:, None] == jnp.arange(
        columns * block_count, dtype=jnp.int32
    )[None, :]
    wanted_len = jnp.sum(jnp.where(hot, store_len.reshape(1, -1), 0), axis=1)
    own = lambda a: lax.dynamic_index_in_dim(
        a.reshape(relay_row, per_device), own_row, 0, keepdims=False
    )
    live = (row < relay_row).astype(jnp.int32) + row % 2 * 2
    meta = jnp.concatenate([live[None], own(wanted_len), own(which), own(index)]).astype(jnp.int32)

    held = []
    for i in range(parts):
        near = jnp.where(row == relay_row, store[i], across[i])
        stores = [near]
        held_by = jnp.where(row % half == half - 1, 0, 1)
        for step in range(1, half):
            stores.append(hop(near, [(p, p - step) for p in (relay_row, relay_row - half)]))
            held_by = jnp.where(row % half == half - 1 - step, step, held_by)
        sends = pick(held_by, slot_block, stores)
        arrived = lax.all_to_all(sends, "dp", split_axis=0, concat_axis=0, tiled=True)
        here = [arrived] + [share(arrived, step) for step in range(1, half)]
        if crossing:
            if i:
                leaving_place, meta = lax.optimization_barrier((leaving_place, meta))
            leaving = pick(0, leaving_place, [arrived])
            landed = hop(leaving, [(p, (p + half) % pool_count) for p in range(pool_count)])
            here += [landed] + [share(landed, step) for step in range(1, half)]
        held.append(here)
    held = [here[b] for b in range(len(held[0])) for here in held]

    attn_out, q_grad, cond_grad, keep, give = run_spans(
        meta,
        queries.reshape(token_count, head_cols),
        cotangent.reshape(token_count, head_cols),
        cond.reshape(span_count, width).astype(jnp.float32),
        held,
        bounds,
        gain,
        w_down,
        w_up,
        w_kv,
        w_kv_t,
        nbr_count,
        pool_count,
    )

    adapter_grad = scatter_sum(keep, give, axes)
    return (
        attn_out.reshape(1, 1, token_count, head_cols),
        q_grad.reshape(1, 1, token_count, head_cols),
        cond_grad.reshape(1, 1, span_count, width),
        adapter_grad,
    )


def solution(mesh):
    return jax.shard_map(
        body,
        mesh=mesh,
        in_specs=(
            P("pool", "dp", None, None),
            P("pool", "dp", None, None),
            P("pool", "dp", None, None),
            P("pool", "dp", None, None),
            P("pool", "dp", None, None),
            P("pool", "dp", None, None, None),
            P("pool", "dp", None),
            P(),
            P(),
            P(),
            P(),
        ),
        out_specs=(
            P("pool", "dp", None, None),
            P("pool", "dp", None, None),
            P("pool", "dp", None, None),
            P(("pool", "dp"), None),
        ),
        check_vma=False,
    )
```

```python
import functools

import jax
import jax.numpy as jnp
from jax import lax
from jax.experimental import pallas as pl
from jax.experimental.pallas import tpu as pltpu
from jax.sharding import PartitionSpec as P

HEADS = 16
HEAD = 128
SPAN = 64
GROUP = 2

EPSILON = 1e-06
FLOOR = -1e30
LOG2E = 1.4426950408889634

NT = (((1,), (1,)), ((), ()))
TN = (((0,), (0,)), ((), ()))


def dot(a, b, dims=(((1,), (0,)), ((), ()))):
    return lax.dot_general(a, b, dims, preferred_element_type=jnp.float32)


def span_kernel(
    held_count, nbr_count, bounds, pool_count, meta,
    q_ref, cot_ref, cond_ref, gain_ref, down_ref, up_ref, upt_ref, downt_ref, *rest,
):
    held_refs = rest[:held_count]
    (kv_hbm, kvt_hbm, out_ref, qg_ref, cg_ref, keep_ref, give_ref,
     raw_ref, kv_ref, kvt_ref, proj_ref, grad_ref, score_ref, dprob_ref, stat_ref,
     q2_ref, cot2_ref, acc_ref, sems, kv_sem) = rest[held_count:]
    step = pl.program_id(0)
    per_device, slot_len, width = raw_ref.shape
    key_count = nbr_count * slot_len
    span_count = per_device // nbr_count
    group = span_count // pl.num_programs(0)
    head_cols = q_ref.shape[1]
    rank = down_ref.shape[1]
    scaling = HEAD ** (-0.5)
    live = meta[0] % 2 == 1
    odd = meta[0] // 2
    lens, which, index = 1, 1 + per_device, 1 + 2 * per_device
    parts = len(bounds) - 1
    cuts = [pl.ds(low, high - low) for low, high in zip(bounds, bounds[1:])]
    pairs = [pl.ds(i * 2 * HEAD, 2 * HEAD) for i in range(HEADS // 2)]
    value_pairs = [pl.ds(head_cols + i * 2 * HEAD, 2 * HEAD) for i in range(HEADS // 2)]
    lanes = [pl.ds(i * 2 * SPAN, 2 * SPAN) for i in range(HEADS // 2)]
    keys = [pl.ds(g * key_count, key_count) for g in range(group)]
    tokens = [pl.ds(g * SPAN, SPAN) for g in range(group)]
    double = [pl.ds(g * 2 * SPAN, 2 * SPAN) for g in range(group)]
    spots = [
        (g, cols, value_cols, lane)
        for g in range(group)
        for cols, value_cols, lane in zip(pairs, value_pairs, lanes)
    ]
    kv_copy = pltpu.make_async_copy(kv_hbm, kv_ref, kv_sem.at[0])
    kvt_copy = pltpu.make_async_copy(kvt_hbm, kvt_ref, kv_sem.at[1])

    @pl.when(step == 0)
    def _():
        for n in range(per_device):
            for b, held in enumerate(held_refs):
                @pl.when(meta[which + n] == b // parts)
                def _():
                    part = b % parts
                    pltpu.make_async_copy(
                        held.at[meta[index + n]],
                        raw_ref.at[n, cuts[part]],
                        sems.at[n * parts + part],
                    ).start()
        kv_copy.start()
        kvt_copy.start()
        q2_ref[...] = jnp.zeros_like(q2_ref)
        cot2_ref[...] = jnp.zeros_like(cot2_ref)

    for g in range(group):
        for i in range(HEADS):
            cols = pl.ds(i * HEAD, HEAD)
            part = pl.ds((2 * g + i % 2) * SPAN, SPAN)
            q2_ref[part, cols] = q_ref[tokens[g], cols]
            cot2_ref[part, cols] = cot_ref[tokens[g], cols]

    for n in range(group * nbr_count):
        for part in range(parts):
            item = step * group * nbr_count + n
            pltpu.make_async_copy(
                held_refs[part].at[0],
                raw_ref.at[item, cuts[part]],
                sems.at[item * parts + part],
            ).wait()
    x_full = jnp.concatenate(
        [
            raw_ref[pl.ds((step * group + g) * nbr_count, nbr_count)]
            .reshape(key_count, width)
            .astype(jnp.float32)
            + cond_ref[pl.ds(step * group + g, 1), :]
            for g in range(group)
        ],
        axis=0,
    )
    inv_rms = lax.rsqrt(jnp.mean(x_full * x_full, axis=-1, keepdims=True) + EPSILON)
    gain = gain_ref[...]
    hidden = (x_full * inv_rms * gain).astype(jnp.bfloat16)
    latent = dot(hidden, down_ref[...]).astype(jnp.bfloat16)
    encoded = (x_full + dot(latent, up_ref[...])).astype(jnp.bfloat16)

    @pl.when(step == 0)
    def _():
        kv_copy.wait()

    for cols in pairs + value_pairs:
        proj_ref[:, cols] = dot(encoded, kv_ref[:, cols]).astype(jnp.bfloat16)

    slot = lax.broadcasted_iota(jnp.int32, (key_count, 2 * SPAN), 0)
    usable = []
    for g in range(group):
        limit = jnp.zeros((key_count, 2 * SPAN), jnp.int32)
        for n in range(nbr_count):
            here = jnp.logical_and(slot >= n * slot_len, slot < (n + 1) * slot_len)
            item = (step * group + g) * nbr_count + n
            limit = jnp.where(here, n * slot_len + meta[lens + item], limit)
        usable.append(slot < limit)

    def diagonal(both):
        return jnp.concatenate([both[:SPAN, :HEAD], both[SPAN:, HEAD:]], axis=1)

    for g, cols, value_cols, lane in spots:
        scores = jnp.where(usable[g], dot(proj_ref[keys[g], cols], q2_ref[double[g], cols], NT), FLOOR)
        score_ref[keys[g], lane] = scores
        stat_ref[g, 0:1, lane] = jnp.max(scores, axis=0, keepdims=True)
        dprob_ref[keys[g], lane] = dot(proj_ref[keys[g], value_cols], cot2_ref[double[g], cols], NT)

    for g, cols, value_cols, lane in spots:
        raised = jnp.exp2((score_ref[keys[g], lane] - stat_ref[g, 0:1, lane]) * (scaling * LOG2E))
        inv_sum = 1.0 / jnp.sum(raised, axis=0, keepdims=True)
        score_ref[keys[g], lane] = raised
        stat_ref[g, 1:2, lane] = inv_sum
        stat_ref[g, 2:3, lane] = inv_sum * jnp.sum(
            raised * dprob_ref[keys[g], lane], axis=0, keepdims=True
        )

    for g, cols, value_cols, lane in spots:
        probs = score_ref[keys[g], lane] * stat_ref[g, 1:2, lane]
        d_scores = probs * (dprob_ref[keys[g], lane] - stat_ref[g, 2:3, lane]) * scaling
        probs_b, d_scores = probs.astype(jnp.bfloat16), d_scores.astype(jnp.bfloat16)
        grad_ref[keys[g], cols] = dot(d_scores, q2_ref[double[g], cols]).astype(jnp.bfloat16)
        grad_ref[keys[g], value_cols] = dot(probs_b, cot2_ref[double[g], cols]).astype(jnp.bfloat16)
        out = diagonal(dot(probs_b.T, proj_ref[keys[g], value_cols]))
        grad = diagonal(dot(d_scores.T, proj_ref[keys[g], cols]))
        out_ref[tokens[g], cols] = jnp.where(live, out, 0.0).astype(jnp.bfloat16)
        qg_ref[tokens[g], cols] = jnp.where(live, grad, 0.0).astype(jnp.bfloat16)

    @pl.when(step == 0)
    def _():
        kvt_copy.wait()
        acc_ref[...] = jnp.zeros_like(acc_ref)

    enc_grad = dot(grad_ref[...], kvt_ref[...]).astype(jnp.bfloat16)
    lat_grad = dot(enc_grad, upt_ref[...]).astype(jnp.bfloat16)
    scaled = dot(lat_grad, downt_ref[...]) * gain
    normed = x_full * inv_rms
    x_grad = enc_grad.astype(jnp.float32) + inv_rms * (
        scaled - normed * jnp.mean(scaled * normed, axis=-1, keepdims=True)
    )
    for g in range(group):
        span_grad = jnp.sum(
            x_grad[g * key_count : (g + 1) * key_count], axis=0, keepdims=True
        )
        cg_ref[pl.ds(step * group + g, 1), :] = jnp.where(live, span_grad, 0.0)
    acc_ref[:, :rank] += dot(hidden, lat_grad, TN)
    acc_ref[:, rank:] += dot(enc_grad, latent, TN)

    @pl.when(step == pl.num_programs(0) - 1)
    def _():
        chunk = width // pool_count
        for k in range(pool_count // 2):
            part = pl.ds(k * chunk, chunk)
            for ref, own in ((keep_ref, odd), (give_ref, 1 - odd)):
                rows = acc_ref[pl.ds(pl.multiple_of((2 * k + own) * chunk, chunk), chunk), :]
                ref[part, :] = jnp.where(live, rows, 0.0).astype(ref.dtype)


def run_spans(meta, query, cot, cond, held, bounds, gain, w_down, w_up, w_kv, w_kv_t, nbr_count, pool_count):
    span_count, width = cond.shape
    token_count, head_cols = query.shape
    slot_len = bounds[-1]
    parts = len(bounds) - 1
    rank = w_down.shape[1]
    whole = lambda a: pl.BlockSpec(a.shape, lambda s, m: (0,) * a.ndim, pipeline_mode=pl.Buffered(1))
    group = GROUP if span_count % GROUP == 0 else 1
    tokens = pl.BlockSpec((group * SPAN, head_cols), lambda s, m: (s, 0))
    small = [cond, gain.reshape(1, width), w_down, w_up, w_up.T, w_down.T]
    large = list(held) + [w_kv, w_kv_t]
    per_device = span_count * nbr_count
    keys = group * nbr_count * slot_len
    rows = per_device * slot_len
    lanes = SPAN * HEADS
    flops = 2 * rows * (2 * width * 2 * head_cols + 6 * width * rank + 6 * SPAN * head_cols)
    return pl.pallas_call(
        functools.partial(span_kernel, len(held), nbr_count, bounds, pool_count),
        grid_spec=pltpu.PrefetchScalarGridSpec(
            num_scalar_prefetch=1,
            grid=(span_count // group,),
            in_specs=[tokens, tokens]
            + [whole(a) for a in small]
            + [pl.BlockSpec(memory_space=pltpu.HBM)] * len(large),
            out_specs=[
                tokens,
                tokens,
                pl.BlockSpec((span_count, width), lambda s, m: (0, 0)),
                pl.BlockSpec((width // 2, 2 * rank), lambda s, m: (0, 0)),
                pl.BlockSpec((width // 2, 2 * rank), lambda s, m: (0, 0)),
            ],
            scratch_shapes=[
                pltpu.VMEM((per_device, slot_len, width), jnp.bfloat16),
                pltpu.VMEM((width, 2 * head_cols), jnp.bfloat16),
                pltpu.VMEM((2 * head_cols, width), jnp.bfloat16),
                pltpu.VMEM((keys, 2 * head_cols), jnp.bfloat16),
                pltpu.VMEM((keys, 2 * head_cols), jnp.bfloat16),
                pltpu.VMEM((keys, lanes), jnp.float32),
                pltpu.VMEM((keys, lanes), jnp.float32),
                pltpu.VMEM((group, 8, lanes), jnp.float32),
                pltpu.VMEM((group * 2 * SPAN, head_cols), jnp.bfloat16),
                pltpu.VMEM((group * 2 * SPAN, head_cols), jnp.bfloat16),
                pltpu.VMEM((width, 2 * rank), jnp.float32),
                pltpu.SemaphoreType.DMA((per_device * parts,)),
                pltpu.SemaphoreType.DMA((2,)),
            ],
        ),
        out_shape=[
            jax.ShapeDtypeStruct((token_count, head_cols), jnp.bfloat16),
            jax.ShapeDtypeStruct((token_count, head_cols), jnp.bfloat16),
            jax.ShapeDtypeStruct((span_count, width), jnp.float32),
            jax.ShapeDtypeStruct((width // 2, 2 * rank), jnp.float32),
            jax.ShapeDtypeStruct((width // 2, 2 * rank), jnp.bfloat16),
        ],
        compiler_params=pltpu.CompilerParams(vmem_limit_bytes=60 * 2**20),
        cost_estimate=pl.CostEstimate(
            flops=flops, bytes_accessed=16 * 2**20, transcendentals=rows * SPAN * HEADS
        ),
    )(meta, query, cot, *small, *large)


def pick_kernel(held_count, meta, *refs):
    held_refs, out_ref = refs[:held_count], refs[held_count]
    for b, held in enumerate(held_refs):
        @pl.when(meta[0] == b)
        def _():
            for n in range(out_ref.shape[0]):
                out_ref[n] = held[meta[1 + n]]


def pick(which, index, held):
    count = index.shape[0]
    meta = jnp.concatenate([jnp.reshape(which, (1,)), index]).astype(jnp.int32)
    return pl.pallas_call(
        functools.partial(pick_kernel, len(held)),
        grid_spec=pltpu.PrefetchScalarGridSpec(
            num_scalar_prefetch=1,
            grid=(1,),
            in_specs=[pl.BlockSpec(memory_space=pltpu.VMEM)] * len(held),
            out_specs=pl.BlockSpec(memory_space=pltpu.VMEM),
        ),
        out_shape=jax.ShapeDtypeStruct((count,) + held[0].shape[1:], held[0].dtype),
        compiler_params=pltpu.CompilerParams(vmem_limit_bytes=16 * 2**20),
    )(meta, *held)


def place_requests(owners, per_device, pool_count, lanes):
    half = pool_count // 2
    count = owners.shape[1]
    order = jnp.arange(count, dtype=jnp.int32)
    side = (order // per_device) // half
    mate = side[:, None] == side[None, :]
    before = order[None, :] < order[:, None]
    same = owners[:, :, None] == owners[:, None, :]
    lower = owners[:, None, :] < owners[:, :, None]
    total = lambda mask: jnp.sum(mask.astype(jnp.int32), axis=2)
    rank = total(same & (mate & before)[None])
    crosses = rank >= lanes
    far = crosses[:, None, :]
    number = total(far & mate[None] & (lower | (same & before[None])))
    first = total(far & ~mate[None] & lower)
    guests = total(far & ~mate[None] & same)
    lane = jnp.where(crosses, number, first + guests + rank) % lanes
    row = jnp.where(crosses, 1 - side[None, :], side[None, :]) * half + lane % half
    return row, lane // half, crosses, number // half


def scatter_sum(keep, give, axes):
    width = keep.shape[1]
    size, columns = (lax.axis_size(axis) for axis in axes)
    index = lax.axis_index(axes[0])
    swap = lambda a, bit: lax.ppermute(a, axes[0], [(i, i ^ bit) for i in range(size)])
    total = keep + swap(give, 1).astype(jnp.float32)
    bit = 2
    while bit < size:
        split = total.reshape(size // bit // 2, 2, -1, width)
        mine = (index // bit) % 2
        keep = lax.dynamic_index_in_dim(split, mine, 1, keepdims=False)
        give = lax.dynamic_index_in_dim(split, 1 - mine, 1, keepdims=False)
        total = keep + swap(give.astype(jnp.bfloat16), bit).astype(jnp.float32)
        bit *= 2
    parts = total.reshape(columns, -1, width).astype(jnp.bfloat16)
    parts = lax.all_to_all(parts, axes[1], split_axis=0, concat_axis=0, tiled=True)
    return jnp.sum(parts.astype(jnp.float32), axis=0)


def body(
    queries, cotangent, cond, nbr_owner, nbr_block, database, lengths, gain, w_down, w_up, w_kv
):
    axes = ("pool", "dp")
    pool_count = lax.axis_size("pool")
    columns = lax.axis_size("dp")
    relay_row = pool_count - 1
    half = pool_count // 2
    row = lax.axis_index("pool")
    me = lax.axis_index("dp")
    span_count, width = cond.shape[2:]
    nbr_count = nbr_owner.shape[3]
    per_device = span_count * nbr_count
    block_count, slot_len = database.shape[2:4]
    live_count = relay_row * per_device
    capacity = max(2, live_count // columns + 1)
    slots = -(-capacity // pool_count)
    lanes = half * slots
    most = 0
    if capacity > lanes:
        for rows in (half, relay_row - half):
            full, left = divmod(rows * per_device, capacity)
            most = max(most, full * (capacity - lanes) + max(0, left - lanes))
    crossing = -(-most // half)
    token_count, head_cols = queries.shape[2:]

    def hop(array, pairs):
        return lax.ppermute(
            array, axes, [(a * columns + j, b * columns + j) for a, b in pairs for j in range(columns)]
        )

    first = slot_len // 16 * 3 // 4 * 16
    bounds = [0, first, slot_len] if 0 < first < slot_len else [0, slot_len]
    parts = len(bounds) - 1
    full_store = database.reshape(block_count, slot_len, width)
    cut = lambda i: full_store[:, bounds[i] : bounds[i + 1]]
    store = [cut(0)]

    def to_all(array, axis):
        copies = jnp.broadcast_to(array[None], (lax.axis_size(axis),) + array.shape)
        return lax.all_to_all(copies, axis, split_axis=0, concat_axis=0, tiled=True)

    info = jnp.concatenate([nbr_owner.reshape(-1), nbr_block.reshape(-1), lengths.reshape(-1)])
    info = jnp.pad(info, (0, -info.shape[0] % 128))
    over = lambda a: hop(a, [(relay_row, relay_row - half)])
    across = [over(store[0])]
    table = to_all(info.reshape(-1, 128), axes)
    w_kv_t = w_kv.T
    full_store, across, table, w_kv_t = lax.optimization_barrier(
        (full_store, across, table, w_kv_t)
    )
    store += [cut(i) for i in range(1, parts)]
    across += [over(a) for a in store[1:]]
    table = table.reshape(pool_count, columns, -1)
    by_column = jnp.swapaxes(table[:relay_row], 0, 1)
    owners = by_column[:, :, :per_device].reshape(columns, live_count)
    blocks = by_column[:, :, per_device : 2 * per_device].reshape(columns, live_count)
    store_len = table[relay_row, :, 2 * per_device : 2 * per_device + block_count]
    carrier, slot, crosses, number = place_requests(owners, per_device, pool_count, lanes)

    ring = jnp.arange(slots, dtype=jnp.int32)
    mine = ((owners == me) & (carrier == row))[:, None, :] & (slot[:, None, :] == ring[None, :, None])
    slot_block = jnp.sum(jnp.where(mine, blocks[:, None, :], 0), axis=2).reshape(-1)

    mine_of = lambda a: lax.dynamic_index_in_dim(a, me, 0, keepdims=False)
    my_owner, my_block, my_carrier, my_slot, my_cross, my_number = map(
        mine_of, (owners, blocks, carrier, slot, crosses, number)
    )
    place = my_owner * slots + my_slot
    spare = crossing // 4
    usual = crossing - spare
    ring = jnp.arange(crossing, dtype=jnp.int32)
    mine = (my_cross & (my_carrier == row))[None, :] & (my_number[None, :] == ring[:, None])
    leaving_place = jnp.sum(jnp.where(mine, place[None, :], 0), axis=1)

    def share(array, step):
        return hop(array, [(p, p // half * half + (p + step) % half) for p in range(pool_count)])

    def cross(arrived, places):
        leaving = pick(0, places, [arrived])
        landed = hop(leaving, [(p, (p + half) % pool_count) for p in range(pool_count)])
        return [landed] + [share(landed, step) for step in range(1, half)]

    held = []
    for i in range(parts):
        near = jnp.where(row == relay_row, store[i], across[i])
        stores = [near]
        held_by = jnp.where(row % half == half - 1, 0, 1)
        for step in range(1, half):
            stores.append(hop(near, [(p, p - step) for p in (relay_row, relay_row - half)]))
            held_by = jnp.where(row % half == half - 1 - step, step, held_by)
        sends = pick(held_by, slot_block, stores)
        arrived = lax.all_to_all(sends, "dp", split_axis=0, concat_axis=0, tiled=True)
        here = [arrived] + [share(arrived, step) for step in range(1, half)]
        if crossing:
            here += cross(arrived, leaving_place[:usual])
        held.append(here)
    if spare:
        first = [here[0] for here in held]
        extra = lax.cond(
            jnp.any(crosses & (number >= usual)),
            lambda arrays: [cross(a, leaving_place[usual:]) for a in arrays],
            lambda arrays: [
                [jnp.zeros((spare,) + a.shape[1:], a.dtype)] * half for a in arrays
            ],
            first,
        )
        held = [here + more for here, more in zip(held, extra)]
    origin = jnp.where(my_cross, (my_carrier + half) % pool_count, my_carrier)
    late = my_cross & (my_number >= usual)
    which = (row - origin) % half + jnp.where(my_cross, half, 0) + jnp.where(late, half, 0)
    index = jnp.where(my_cross, my_number - jnp.where(late, usual, 0), place)
    held = [here[b] for b in range(len(held[0])) for here in held]

    own_row = jnp.minimum(row, relay_row - 1)
    hot = (my_owner * block_count + my_block)[:, None] == jnp.arange(
        columns * block_count, dtype=jnp.int32
    )[None, :]
    wanted_len = jnp.sum(jnp.where(hot, store_len.reshape(1, -1), 0), axis=1)
    own = lambda a: lax.dynamic_index_in_dim(
        a.reshape(relay_row, per_device), own_row, 0, keepdims=False
    )
    live = (row < relay_row).astype(jnp.int32) + row % 2 * 2
    meta = jnp.concatenate([live[None], own(wanted_len), own(which), own(index)]).astype(jnp.int32)

    attn_out, q_grad, cond_grad, keep, give = run_spans(
        meta,
        queries.reshape(token_count, head_cols),
        cotangent.reshape(token_count, head_cols),
        cond.reshape(span_count, width).astype(jnp.float32),
        held,
        bounds,
        gain,
        w_down,
        w_up,
        w_kv,
        w_kv_t,
        nbr_count,
        pool_count,
    )

    adapter_grad = scatter_sum(keep, give, axes)
    return (
        attn_out.reshape(1, 1, token_count, head_cols),
        q_grad.reshape(1, 1, token_count, head_cols),
        cond_grad.reshape(1, 1, span_count, width),
        adapter_grad,
    )


def solution(mesh):
    return jax.shard_map(
        body,
        mesh=mesh,
        in_specs=(
            P("pool", "dp", None, None),
            P("pool", "dp", None, None),
            P("pool", "dp", None, None),
            P("pool", "dp", None, None),
            P("pool", "dp", None, None),
            P("pool", "dp", None, None, None),
            P("pool", "dp", None),
            P(),
            P(),
            P(),
            P(),
        ),
        out_specs=(
            P("pool", "dp", None, None),
            P("pool", "dp", None, None),
            P("pool", "dp", None, None),
            P(("pool", "dp"), None),
        ),
        check_vma=False,
    )
```

```python
import functools

import jax
import jax.numpy as jnp
from jax import lax
from jax.experimental import pallas as pl
from jax.experimental.pallas import tpu as pltpu
from jax.sharding import PartitionSpec as P

HEADS = 16
HEAD = 128
SPAN = 64
GROUP = 4

EPSILON = 1e-06
FLOOR = -1e30
LOG2E = 1.4426950408889634

NT = (((1,), (1,)), ((), ()))
TN = (((0,), (0,)), ((), ()))


def dot(a, b, dims=(((1,), (0,)), ((), ()))):
    return lax.dot_general(a, b, dims, preferred_element_type=jnp.float32)


def span_kernel(
    held_count, nbr_count, bounds, pool_count, meta,
    q_ref, cot_ref, cond_ref, gain_ref, down_ref, up_ref, upt_ref, downt_ref, *rest,
):
    held_refs = rest[:held_count]
    (kv_hbm, kvt_hbm, out_ref, qg_ref, cg_ref, keep_ref, give_ref,
     raw_ref, kv_ref, kvt_ref, proj_ref, grad_ref, score_ref, dprob_ref, stat_ref,
     q2_ref, cot2_ref, acc_ref, sems, kv_sem) = rest[held_count:]
    step = pl.program_id(0)
    per_device, slot_len, width = raw_ref.shape
    key_count = nbr_count * slot_len
    span_count = per_device // nbr_count
    group = span_count // pl.num_programs(0)
    head_cols = q_ref.shape[1]
    rank = down_ref.shape[1]
    scaling = HEAD ** (-0.5)
    live = meta[0] % 2 == 1
    odd = meta[0] // 2
    lens, which, index = 1, 1 + per_device, 1 + 2 * per_device
    parts = len(bounds) - 1
    cuts = [pl.ds(low, high - low) for low, high in zip(bounds, bounds[1:])]
    pairs = [pl.ds(i * 2 * HEAD, 2 * HEAD) for i in range(HEADS // 2)]
    value_pairs = [pl.ds(head_cols + i * 2 * HEAD, 2 * HEAD) for i in range(HEADS // 2)]
    lanes = [pl.ds(i * 2 * SPAN, 2 * SPAN) for i in range(HEADS // 2)]
    keys = [pl.ds(g * key_count, key_count) for g in range(group)]
    tokens = [pl.ds(g * SPAN, SPAN) for g in range(group)]
    double = [pl.ds(g * 2 * SPAN, 2 * SPAN) for g in range(group)]
    spots = [
        (g, cols, value_cols, lane)
        for g in range(group)
        for cols, value_cols, lane in zip(pairs, value_pairs, lanes)
    ]
    kv_copy = pltpu.make_async_copy(kv_hbm, kv_ref, kv_sem.at[0])
    kvt_copy = pltpu.make_async_copy(kvt_hbm, kvt_ref, kv_sem.at[1])

    @pl.when(step == 0)
    def _():
        for n in range(per_device):
            for b, held in enumerate(held_refs):
                @pl.when(meta[which + n] == b // parts)
                def _():
                    part = b % parts
                    pltpu.make_async_copy(
                        held.at[meta[index + n]],
                        raw_ref.at[n, cuts[part]],
                        sems.at[n * parts + part],
                    ).start()
        kv_copy.start()
        kvt_copy.start()
        q2_ref[...] = jnp.zeros_like(q2_ref)
        cot2_ref[...] = jnp.zeros_like(cot2_ref)

    for g in range(group):
        for i in range(HEADS):
            cols = pl.ds(i * HEAD, HEAD)
            part = pl.ds((2 * g + i % 2) * SPAN, SPAN)
            q2_ref[part, cols] = q_ref[tokens[g], cols]
            cot2_ref[part, cols] = cot_ref[tokens[g], cols]

    for n in range(group * nbr_count):
        for part in range(parts):
            item = step * group * nbr_count + n
            pltpu.make_async_copy(
                held_refs[part].at[0],
                raw_ref.at[item, cuts[part]],
                sems.at[item * parts + part],
            ).wait()
    x_full = jnp.concatenate(
        [
            raw_ref[pl.ds((step * group + g) * nbr_count, nbr_count)]
            .reshape(key_count, width)
            .astype(jnp.float32)
            + cond_ref[pl.ds(step * group + g, 1), :]
            for g in range(group)
        ],
        axis=0,
    )
    inv_rms = lax.rsqrt(jnp.mean(x_full * x_full, axis=-1, keepdims=True) + EPSILON)
    gain = gain_ref[...]
    hidden = (x_full * inv_rms * gain).astype(jnp.bfloat16)
    latent = dot(hidden, down_ref[...]).astype(jnp.bfloat16)
    encoded = (x_full + dot(latent, up_ref[...])).astype(jnp.bfloat16)

    @pl.when(step == 0)
    def _():
        kv_copy.wait()

    for cols in pairs + value_pairs:
        proj_ref[:, cols] = dot(encoded, kv_ref[:, cols]).astype(jnp.bfloat16)

    slot = lax.broadcasted_iota(jnp.int32, (key_count, 2 * SPAN), 0)
    usable = []
    for g in range(group):
        limit = jnp.zeros((key_count, 2 * SPAN), jnp.int32)
        for n in range(nbr_count):
            here = jnp.logical_and(slot >= n * slot_len, slot < (n + 1) * slot_len)
            item = (step * group + g) * nbr_count + n
            limit = jnp.where(here, n * slot_len + meta[lens + item], limit)
        usable.append(slot < limit)

    def diagonal(both):
        return jnp.concatenate([both[:SPAN, :HEAD], both[SPAN:, HEAD:]], axis=1)

    for g, cols, value_cols, lane in spots:
        scores = jnp.where(usable[g], dot(proj_ref[keys[g], cols], q2_ref[double[g], cols], NT), FLOOR)
        score_ref[keys[g], lane] = scores
        stat_ref[g, 0:1, lane] = jnp.max(scores, axis=0, keepdims=True)
        dprob_ref[keys[g], lane] = dot(proj_ref[keys[g], value_cols], cot2_ref[double[g], cols], NT)

    for g, cols, value_cols, lane in spots:
        raised = jnp.exp2((score_ref[keys[g], lane] - stat_ref[g, 0:1, lane]) * (scaling * LOG2E))
        inv_sum = 1.0 / jnp.sum(raised, axis=0, keepdims=True)
        score_ref[keys[g], lane] = raised
        stat_ref[g, 1:2, lane] = inv_sum
        stat_ref[g, 2:3, lane] = inv_sum * jnp.sum(
            raised * dprob_ref[keys[g], lane], axis=0, keepdims=True
        )

    for g, cols, value_cols, lane in spots:
        probs = score_ref[keys[g], lane] * stat_ref[g, 1:2, lane]
        d_scores = probs * (dprob_ref[keys[g], lane] - stat_ref[g, 2:3, lane]) * scaling
        probs_b, d_scores = probs.astype(jnp.bfloat16), d_scores.astype(jnp.bfloat16)
        grad_ref[keys[g], cols] = dot(d_scores, q2_ref[double[g], cols]).astype(jnp.bfloat16)
        grad_ref[keys[g], value_cols] = dot(probs_b, cot2_ref[double[g], cols]).astype(jnp.bfloat16)
        out = diagonal(dot(probs_b.T, proj_ref[keys[g], value_cols]))
        grad = diagonal(dot(d_scores.T, proj_ref[keys[g], cols]))
        out_ref[tokens[g], cols] = jnp.where(live, out, 0.0).astype(jnp.bfloat16)
        qg_ref[tokens[g], cols] = jnp.where(live, grad, 0.0).astype(jnp.bfloat16)

    @pl.when(step == 0)
    def _():
        kvt_copy.wait()
        acc_ref[...] = jnp.zeros_like(acc_ref)

    enc_grad = dot(grad_ref[...], kvt_ref[...]).astype(jnp.bfloat16)
    lat_grad = dot(enc_grad, upt_ref[...]).astype(jnp.bfloat16)
    scaled = dot(lat_grad, downt_ref[...]) * gain
    normed = x_full * inv_rms
    x_grad = enc_grad.astype(jnp.float32) + inv_rms * (
        scaled - normed * jnp.mean(scaled * normed, axis=-1, keepdims=True)
    )
    for g in range(group):
        span_grad = jnp.sum(
            x_grad[g * key_count : (g + 1) * key_count], axis=0, keepdims=True
        )
        cg_ref[pl.ds(step * group + g, 1), :] = jnp.where(live, span_grad, 0.0)
    acc_ref[:, :rank] += dot(hidden, lat_grad, TN)
    acc_ref[:, rank:] += dot(enc_grad, latent, TN)

    @pl.when(step == pl.num_programs(0) - 1)
    def _():
        chunk = width // pool_count
        for k in range(pool_count // 2):
            part = pl.ds(k * chunk, chunk)
            for ref, own in ((keep_ref, odd), (give_ref, 1 - odd)):
                rows = acc_ref[pl.ds(pl.multiple_of((2 * k + own) * chunk, chunk), chunk), :]
                ref[part, :] = jnp.where(live, rows, 0.0).astype(ref.dtype)


def run_spans(meta, query, cot, cond, held, bounds, gain, w_down, w_up, w_kv, w_kv_t, nbr_count, pool_count):
    span_count, width = cond.shape
    token_count, head_cols = query.shape
    slot_len = bounds[-1]
    parts = len(bounds) - 1
    rank = w_down.shape[1]
    whole = lambda a: pl.BlockSpec(a.shape, lambda s, m: (0,) * a.ndim, pipeline_mode=pl.Buffered(1))
    group = GROUP if span_count % GROUP == 0 else 1
    tokens = pl.BlockSpec((group * SPAN, head_cols), lambda s, m: (s, 0))
    small = [cond, gain.reshape(1, width), w_down, w_up, w_up.T, w_down.T]
    large = list(held) + [w_kv, w_kv_t]
    per_device = span_count * nbr_count
    keys = group * nbr_count * slot_len
    rows = per_device * slot_len
    lanes = SPAN * HEADS
    flops = 2 * rows * (2 * width * 2 * head_cols + 6 * width * rank + 6 * SPAN * head_cols)
    return pl.pallas_call(
        functools.partial(span_kernel, len(held), nbr_count, bounds, pool_count),
        grid_spec=pltpu.PrefetchScalarGridSpec(
            num_scalar_prefetch=1,
            grid=(span_count // group,),
            in_specs=[tokens, tokens]
            + [whole(a) for a in small]
            + [pl.BlockSpec(memory_space=pltpu.HBM)] * len(large),
            out_specs=[
                tokens,
                tokens,
                pl.BlockSpec((span_count, width), lambda s, m: (0, 0)),
                pl.BlockSpec((width // 2, 2 * rank), lambda s, m: (0, 0)),
                pl.BlockSpec((width // 2, 2 * rank), lambda s, m: (0, 0)),
            ],
            scratch_shapes=[
                pltpu.VMEM((per_device, slot_len, width), jnp.bfloat16),
                pltpu.VMEM((width, 2 * head_cols), jnp.bfloat16),
                pltpu.VMEM((2 * head_cols, width), jnp.bfloat16),
                pltpu.VMEM((keys, 2 * head_cols), jnp.bfloat16),
                pltpu.VMEM((keys, 2 * head_cols), jnp.bfloat16),
                pltpu.VMEM((keys, lanes), jnp.float32),
                pltpu.VMEM((keys, lanes), jnp.float32),
                pltpu.VMEM((group, 8, lanes), jnp.float32),
                pltpu.VMEM((group * 2 * SPAN, head_cols), jnp.bfloat16),
                pltpu.VMEM((group * 2 * SPAN, head_cols), jnp.bfloat16),
                pltpu.VMEM((width, 2 * rank), jnp.float32),
                pltpu.SemaphoreType.DMA((per_device * parts,)),
                pltpu.SemaphoreType.DMA((2,)),
            ],
        ),
        out_shape=[
            jax.ShapeDtypeStruct((token_count, head_cols), jnp.bfloat16),
            jax.ShapeDtypeStruct((token_count, head_cols), jnp.bfloat16),
            jax.ShapeDtypeStruct((span_count, width), jnp.float32),
            jax.ShapeDtypeStruct((width // 2, 2 * rank), jnp.float32),
            jax.ShapeDtypeStruct((width // 2, 2 * rank), jnp.bfloat16),
        ],
        compiler_params=pltpu.CompilerParams(vmem_limit_bytes=60 * 2**20),
        cost_estimate=pl.CostEstimate(
            flops=flops, bytes_accessed=16 * 2**20, transcendentals=rows * SPAN * HEADS
        ),
    )(meta, query, cot, *small, *large)


def pick_kernel(held_count, meta, *refs):
    held_refs, out_ref = refs[:held_count], refs[held_count]
    for b, held in enumerate(held_refs):
        @pl.when(meta[0] == b)
        def _():
            for n in range(out_ref.shape[0]):
                out_ref[n] = held[meta[1 + n]]


def pick(which, index, held):
    count = index.shape[0]
    meta = jnp.concatenate([jnp.reshape(which, (1,)), index]).astype(jnp.int32)
    return pl.pallas_call(
        functools.partial(pick_kernel, len(held)),
        grid_spec=pltpu.PrefetchScalarGridSpec(
            num_scalar_prefetch=1,
            grid=(1,),
            in_specs=[pl.BlockSpec(memory_space=pltpu.VMEM)] * len(held),
            out_specs=pl.BlockSpec(memory_space=pltpu.VMEM),
        ),
        out_shape=jax.ShapeDtypeStruct((count,) + held[0].shape[1:], held[0].dtype),
        compiler_params=pltpu.CompilerParams(vmem_limit_bytes=16 * 2**20),
    )(meta, *held)


def place_requests(owners, per_device, pool_count, lanes):
    half = pool_count // 2
    count = owners.shape[1]
    order = jnp.arange(count, dtype=jnp.int32)
    side = (order // per_device) // half
    mate = side[:, None] == side[None, :]
    before = order[None, :] < order[:, None]
    same = owners[:, :, None] == owners[:, None, :]
    lower = owners[:, None, :] < owners[:, :, None]
    total = lambda mask: jnp.sum(mask.astype(jnp.int32), axis=2)
    rank = total(same & (mate & before)[None])
    crosses = rank >= lanes
    far = crosses[:, None, :]
    number = total(far & mate[None] & (lower | (same & before[None])))
    first = total(far & ~mate[None] & lower)
    guests = total(far & ~mate[None] & same)
    lane = jnp.where(crosses, number, first + guests + rank) % lanes
    row = jnp.where(crosses, 1 - side[None, :], side[None, :]) * half + lane % half
    return row, lane // half, crosses, number // half


def scatter_sum(keep, give, axes):
    width = keep.shape[1]
    size, columns = (lax.axis_size(axis) for axis in axes)
    index = lax.axis_index(axes[0])
    swap = lambda a, bit: lax.ppermute(a, axes[0], [(i, i ^ bit) for i in range(size)])
    total = keep + swap(give, 1).astype(jnp.float32)
    bit = 2
    while bit < size:
        split = total.reshape(size // bit // 2, 2, -1, width)
        mine = (index // bit) % 2
        keep = lax.dynamic_index_in_dim(split, mine, 1, keepdims=False)
        give = lax.dynamic_index_in_dim(split, 1 - mine, 1, keepdims=False)
        total = keep + swap(give.astype(jnp.bfloat16), bit).astype(jnp.float32)
        bit *= 2
    parts = total.reshape(columns, -1, width).astype(jnp.bfloat16)
    parts = lax.all_to_all(parts, axes[1], split_axis=0, concat_axis=0, tiled=True)
    return jnp.sum(parts.astype(jnp.float32), axis=0)


def body(
    queries, cotangent, cond, nbr_owner, nbr_block, database, lengths, gain, w_down, w_up, w_kv
):
    axes = ("pool", "dp")
    pool_count = lax.axis_size("pool")
    columns = lax.axis_size("dp")
    relay_row = pool_count - 1
    half = pool_count // 2
    row = lax.axis_index("pool")
    me = lax.axis_index("dp")
    span_count, width = cond.shape[2:]
    nbr_count = nbr_owner.shape[3]
    per_device = span_count * nbr_count
    block_count, slot_len = database.shape[2:4]
    live_count = relay_row * per_device
    capacity = max(2, live_count // columns + 1)
    slots = -(-capacity // pool_count)
    lanes = half * slots
    most = 0
    if capacity > lanes:
        for rows in (half, relay_row - half):
            full, left = divmod(rows * per_device, capacity)
            most = max(most, full * (capacity - lanes) + max(0, left - lanes))
    crossing = -(-most // half)
    token_count, head_cols = queries.shape[2:]

    def hop(array, pairs):
        return lax.ppermute(
            array, axes, [(a * columns + j, b * columns + j) for a, b in pairs for j in range(columns)]
        )

    first = slot_len // 16 * 3 // 4 * 16
    bounds = [0, first, slot_len] if 0 < first < slot_len else [0, slot_len]
    parts = len(bounds) - 1
    full_store = database.reshape(block_count, slot_len, width)
    cut = lambda i: full_store[:, bounds[i] : bounds[i + 1]]
    store = [cut(0)]

    def to_all(array, axis):
        copies = jnp.broadcast_to(array[None], (lax.axis_size(axis),) + array.shape)
        return lax.all_to_all(copies, axis, split_axis=0, concat_axis=0, tiled=True)

    info = jnp.concatenate([nbr_owner.reshape(-1), nbr_block.reshape(-1), lengths.reshape(-1)])
    info = jnp.pad(info, (0, -info.shape[0] % 128))
    over = lambda a: hop(a, [(relay_row, relay_row - half)])
    across = [over(store[0])]
    table = to_all(info.reshape(-1, 128), axes)
    w_kv_t = w_kv.T
    full_store, across, table, w_kv_t = lax.optimization_barrier(
        (full_store, across, table, w_kv_t)
    )
    store += [cut(i) for i in range(1, parts)]
    across += [over(a) for a in store[1:]]
    table = table.reshape(pool_count, columns, -1)
    by_column = jnp.swapaxes(table[:relay_row], 0, 1)
    owners = by_column[:, :, :per_device].reshape(columns, live_count)
    blocks = by_column[:, :, per_device : 2 * per_device].reshape(columns, live_count)
    store_len = table[relay_row, :, 2 * per_device : 2 * per_device + block_count]
    carrier, slot, crosses, number = place_requests(owners, per_device, pool_count, lanes)

    ring = jnp.arange(slots, dtype=jnp.int32)
    mine = ((owners == me) & (carrier == row))[:, None, :] & (slot[:, None, :] == ring[None, :, None])
    slot_block = jnp.sum(jnp.where(mine, blocks[:, None, :], 0), axis=2).reshape(-1)

    mine_of = lambda a: lax.dynamic_index_in_dim(a, me, 0, keepdims=False)
    my_owner, my_block, my_carrier, my_slot, my_cross, my_number = map(
        mine_of, (owners, blocks, carrier, slot, crosses, number)
    )
    place = my_owner * slots + my_slot
    ring = jnp.arange(crossing, dtype=jnp.int32)
    mine = (my_cross & (my_carrier == row))[None, :] & (my_number[None, :] == ring[:, None])
    leaving_place = jnp.sum(jnp.where(mine, place[None, :], 0), axis=1)

    def share(array, step):
        return hop(array, [(p, p // half * half + (p + step) % half) for p in range(pool_count)])

    held = []
    for i in range(parts):
        near = jnp.where(row == relay_row, store[i], across[i])
        stores = [near]
        held_by = jnp.where(row % half == half - 1, 0, 1)
        for step in range(1, half):
            stores.append(hop(near, [(p, p - step) for p in (relay_row, relay_row - half)]))
            held_by = jnp.where(row % half == half - 1 - step, step, held_by)
        sends = pick(held_by, slot_block, stores)
        arrived = lax.all_to_all(sends, "dp", split_axis=0, concat_axis=0, tiled=True)
        here = [arrived] + [share(arrived, step) for step in range(1, half)]
        if crossing:
            leaving = pick(0, leaving_place, [arrived])
            landed = hop(leaving, [(p, (p + half) % pool_count) for p in range(pool_count)])
            here += [landed] + [share(landed, step) for step in range(1, half)]
        held.append(here)
    origin = jnp.where(my_cross, (my_carrier + half) % pool_count, my_carrier)
    which = (row - origin) % half + jnp.where(my_cross, half, 0)
    index = jnp.where(my_cross, my_number, place)
    held = [here[b] for b in range(len(held[0])) for here in held]

    own_row = jnp.minimum(row, relay_row - 1)
    hot = (my_owner * block_count + my_block)[:, None] == jnp.arange(
        columns * block_count, dtype=jnp.int32
    )[None, :]
    wanted_len = jnp.sum(jnp.where(hot, store_len.reshape(1, -1), 0), axis=1)
    own = lambda a: lax.dynamic_index_in_dim(
        a.reshape(relay_row, per_device), own_row, 0, keepdims=False
    )
    live = (row < relay_row).astype(jnp.int32) + row % 2 * 2
    meta = jnp.concatenate([live[None], own(wanted_len), own(which), own(index)]).astype(jnp.int32)

    attn_out, q_grad, cond_grad, keep, give = run_spans(
        meta,
        queries.reshape(token_count, head_cols),
        cotangent.reshape(token_count, head_cols),
        cond.reshape(span_count, width).astype(jnp.float32),
        held,
        bounds,
        gain,
        w_down,
        w_up,
        w_kv,
        w_kv_t,
        nbr_count,
        pool_count,
    )

    adapter_grad = scatter_sum(keep, give, axes)
    return (
        attn_out.reshape(1, 1, token_count, head_cols),
        q_grad.reshape(1, 1, token_count, head_cols),
        cond_grad.reshape(1, 1, span_count, width),
        adapter_grad,
    )


def solution(mesh):
    return jax.shard_map(
        body,
        mesh=mesh,
        in_specs=(
            P("pool", "dp", None, None),
            P("pool", "dp", None, None),
            P("pool", "dp", None, None),
            P("pool", "dp", None, None),
            P("pool", "dp", None, None),
            P("pool", "dp", None, None, None),
            P("pool", "dp", None),
            P(),
            P(),
            P(),
            P(),
        ),
        out_specs=(
            P("pool", "dp", None, None),
            P("pool", "dp", None, None),
            P("pool", "dp", None, None),
            P(("pool", "dp"), None),
        ),
        check_vma=False,
    )
```

```python
import functools

import jax
import jax.numpy as jnp
from jax import lax
from jax.experimental import pallas as pl
from jax.experimental.pallas import tpu as pltpu
from jax.sharding import PartitionSpec as P

HEADS = 16
HEAD = 128
SPAN = 64
GROUP = 4

EPSILON = 1e-06
FLOOR = -1e30
LOG2E = 1.4426950408889634

NT = (((1,), (1,)), ((), ()))
TN = (((0,), (0,)), ((), ()))


def dot(a, b, dims=(((1,), (0,)), ((), ()))):
    return lax.dot_general(a, b, dims, preferred_element_type=jnp.float32)


def span_kernel(
    held_count, nbr_count, bounds, pool_count, meta,
    cond_ref, gain_ref, down_ref, up_ref, upt_ref, downt_ref, *rest,
):
    held_refs = rest[:held_count]
    (q_hbm, cot_hbm, kv_hbm, kvt_hbm, out_hbm, qg_hbm, cg_ref, keep_ref, give_ref,
     q_ref, cot_ref, out_ref, qg_ref,
     raw_ref, kv_ref, kvt_ref, proj_ref, grad_ref, score_ref, dprob_ref, stat_ref,
     q2_ref, cot2_ref, acc_ref, sems, kv_sem) = rest[held_count:]
    step = pl.program_id(0)
    per_device, slot_len, width = raw_ref.shape
    key_count = nbr_count * slot_len
    span_count = per_device // nbr_count
    group = span_count // pl.num_programs(0)
    head_cols = q_ref.shape[1]
    rank = down_ref.shape[1]
    scaling = HEAD ** (-0.5)
    live = meta[0] % 2 == 1
    odd = meta[0] // 2
    lens, which, index = 1, 1 + per_device, 1 + 2 * per_device
    parts = len(bounds) - 1
    cuts = [pl.ds(low, high - low) for low, high in zip(bounds, bounds[1:])]
    pairs = [pl.ds(i * 2 * HEAD, 2 * HEAD) for i in range(HEADS // 2)]
    value_pairs = [pl.ds(head_cols + i * 2 * HEAD, 2 * HEAD) for i in range(HEADS // 2)]
    lanes = [pl.ds(i * 2 * SPAN, 2 * SPAN) for i in range(HEADS // 2)]
    keys = [pl.ds(g * key_count, key_count) for g in range(group)]
    tokens = [pl.ds(g * SPAN, SPAN) for g in range(group)]
    double = [pl.ds(g * 2 * SPAN, 2 * SPAN) for g in range(group)]
    spots = [
        (g, cols, value_cols, lane)
        for g in range(group)
        for cols, value_cols, lane in zip(pairs, value_pairs, lanes)
    ]
    kvt_copy = pltpu.make_async_copy(kvt_hbm, kvt_ref, kv_sem.at[0])
    token_copies = [
        pltpu.make_async_copy(q_hbm, q_ref, kv_sem.at[1]),
        pltpu.make_async_copy(cot_hbm, cot_ref, kv_sem.at[2]),
    ]
    own_rows = pl.ds(pl.multiple_of(step * group * SPAN, SPAN), group * SPAN)
    out_copies = [
        pltpu.make_async_copy(out_ref, out_hbm.at[own_rows], kv_sem.at[3]),
        pltpu.make_async_copy(qg_ref, qg_hbm.at[own_rows], kv_sem.at[4]),
    ]
    kv_copy = pltpu.make_async_copy(kv_hbm, kv_ref, kv_sem.at[5])

    @pl.when(step == 0)
    def _():
        for n in range(per_device):
            for b, held in enumerate(held_refs):
                @pl.when(meta[which + n] == b // parts)
                def _():
                    part = b % parts
                    pltpu.make_async_copy(
                        held.at[meta[index + n]],
                        raw_ref.at[n, cuts[part]],
                        sems.at[n * parts + part],
                    ).start()
        for copy in [kv_copy] + token_copies:
            copy.start()
        q2_ref[...] = jnp.zeros_like(q2_ref)
        cot2_ref[...] = jnp.zeros_like(cot2_ref)

    for n in range(group * nbr_count):
        for part in range(parts):
            item = step * group * nbr_count + n
            pltpu.make_async_copy(
                held_refs[part].at[0],
                raw_ref.at[item, cuts[part]],
                sems.at[item * parts + part],
            ).wait()
    x_full = jnp.concatenate(
        [
            raw_ref[pl.ds((step * group + g) * nbr_count, nbr_count)]
            .reshape(key_count, width)
            .astype(jnp.float32)
            + cond_ref[pl.ds(step * group + g, 1), :]
            for g in range(group)
        ],
        axis=0,
    )
    inv_rms = lax.rsqrt(jnp.mean(x_full * x_full, axis=-1, keepdims=True) + EPSILON)
    gain = gain_ref[...]
    hidden = (x_full * inv_rms * gain).astype(jnp.bfloat16)
    latent = dot(hidden, down_ref[...]).astype(jnp.bfloat16)
    encoded = (x_full + dot(latent, up_ref[...])).astype(jnp.bfloat16)

    @pl.when(step == 0)
    def _():
        kv_copy.wait()

    for cols in pairs + value_pairs:
        proj_ref[:, cols] = dot(encoded, kv_ref[:, cols]).astype(jnp.bfloat16)

    @pl.when(step == 0)
    def _():
        kvt_copy.start()
        for copy in token_copies:
            copy.wait()

    for g in range(group):
        for i in range(HEADS):
            cols = pl.ds(i * HEAD, HEAD)
            part = pl.ds((2 * g + i % 2) * SPAN, SPAN)
            q2_ref[part, cols] = q_ref[pl.ds(pl.multiple_of((step * group + g) * SPAN, SPAN), SPAN), cols]
            cot2_ref[part, cols] = cot_ref[pl.ds(pl.multiple_of((step * group + g) * SPAN, SPAN), SPAN), cols]

    slot = lax.broadcasted_iota(jnp.int32, (key_count, 2 * SPAN), 0)
    usable = []
    for g in range(group):
        limit = jnp.zeros((key_count, 2 * SPAN), jnp.int32)
        for n in range(nbr_count):
            here = jnp.logical_and(slot >= n * slot_len, slot < (n + 1) * slot_len)
            item = (step * group + g) * nbr_count + n
            limit = jnp.where(here, n * slot_len + meta[lens + item], limit)
        usable.append(slot < limit)

    def diagonal(both):
        return jnp.concatenate([both[:SPAN, :HEAD], both[SPAN:, HEAD:]], axis=1)

    for g, cols, value_cols, lane in spots:
        scores = jnp.where(usable[g], dot(proj_ref[keys[g], cols], q2_ref[double[g], cols], NT), FLOOR)
        score_ref[keys[g], lane] = scores
        stat_ref[g, 0:1, lane] = jnp.max(scores, axis=0, keepdims=True)
        dprob_ref[keys[g], lane] = dot(proj_ref[keys[g], value_cols], cot2_ref[double[g], cols], NT)

    for g, cols, value_cols, lane in spots:
        raised = jnp.exp2((score_ref[keys[g], lane] - stat_ref[g, 0:1, lane]) * (scaling * LOG2E))
        inv_sum = 1.0 / jnp.sum(raised, axis=0, keepdims=True)
        score_ref[keys[g], lane] = raised
        stat_ref[g, 1:2, lane] = inv_sum
        stat_ref[g, 2:3, lane] = inv_sum * jnp.sum(
            raised * dprob_ref[keys[g], lane], axis=0, keepdims=True
        )

    for g, cols, value_cols, lane in spots:
        probs = score_ref[keys[g], lane] * stat_ref[g, 1:2, lane]
        d_scores = probs * (dprob_ref[keys[g], lane] - stat_ref[g, 2:3, lane]) * scaling
        probs_b, d_scores = probs.astype(jnp.bfloat16), d_scores.astype(jnp.bfloat16)
        grad_ref[keys[g], cols] = dot(d_scores, q2_ref[double[g], cols]).astype(jnp.bfloat16)
        grad_ref[keys[g], value_cols] = dot(probs_b, cot2_ref[double[g], cols]).astype(jnp.bfloat16)
        out = diagonal(dot(probs_b.T, proj_ref[keys[g], value_cols]))
        grad = diagonal(dot(d_scores.T, proj_ref[keys[g], cols]))
        out_ref[tokens[g], cols] = jnp.where(live, out, 0.0).astype(jnp.bfloat16)
        qg_ref[tokens[g], cols] = jnp.where(live, grad, 0.0).astype(jnp.bfloat16)

    for copy in out_copies:
        copy.start()

    @pl.when(step == 0)
    def _():
        kvt_copy.wait()
        acc_ref[...] = jnp.zeros_like(acc_ref)

    enc_grad = dot(grad_ref[...], kvt_ref[...]).astype(jnp.bfloat16)
    lat_grad = dot(enc_grad, upt_ref[...]).astype(jnp.bfloat16)
    scaled = dot(lat_grad, downt_ref[...]) * gain
    normed = x_full * inv_rms
    x_grad = enc_grad.astype(jnp.float32) + inv_rms * (
        scaled - normed * jnp.mean(scaled * normed, axis=-1, keepdims=True)
    )
    for g in range(group):
        span_grad = jnp.sum(
            x_grad[g * key_count : (g + 1) * key_count], axis=0, keepdims=True
        )
        cg_ref[pl.ds(step * group + g, 1), :] = jnp.where(live, span_grad, 0.0)
    acc_ref[:, :rank] += dot(hidden, lat_grad, TN)
    acc_ref[:, rank:] += dot(enc_grad, latent, TN)
    for copy in out_copies:
        copy.wait()

    @pl.when(step == pl.num_programs(0) - 1)
    def _():
        chunk = width // pool_count
        for k in range(pool_count // 2):
            part = pl.ds(k * chunk, chunk)
            for ref, own in ((keep_ref, odd), (give_ref, 1 - odd)):
                rows = acc_ref[pl.ds(pl.multiple_of((2 * k + own) * chunk, chunk), chunk), :]
                ref[part, :] = jnp.where(live, rows, 0.0).astype(ref.dtype)


def run_spans(meta, query, cot, cond, held, bounds, gain, w_down, w_up, w_kv, w_kv_t, nbr_count, pool_count):
    span_count, width = cond.shape
    token_count, head_cols = query.shape
    slot_len = bounds[-1]
    parts = len(bounds) - 1
    rank = w_down.shape[1]
    whole = lambda a: pl.BlockSpec(a.shape, lambda s, m: (0,) * a.ndim, pipeline_mode=pl.Buffered(1))
    group = GROUP if span_count % GROUP == 0 else 1
    small = [cond, gain.reshape(1, width), w_down, w_up, w_up.T, w_down.T]
    large = list(held) + [query, cot, w_kv, w_kv_t]
    per_device = span_count * nbr_count
    keys = group * nbr_count * slot_len
    rows = per_device * slot_len
    lanes = SPAN * HEADS
    flops = 2 * rows * (2 * width * 2 * head_cols + 6 * width * rank + 6 * SPAN * head_cols)
    return pl.pallas_call(
        functools.partial(span_kernel, len(held), nbr_count, bounds, pool_count),
        grid_spec=pltpu.PrefetchScalarGridSpec(
            num_scalar_prefetch=1,
            grid=(span_count // group,),
            in_specs=[whole(a) for a in small]
            + [pl.BlockSpec(memory_space=pltpu.HBM)] * len(large),
            out_specs=[pl.BlockSpec(memory_space=pltpu.HBM)] * 2
            + [
                pl.BlockSpec((span_count, width), lambda s, m: (0, 0)),
                pl.BlockSpec((width // 2, 2 * rank), lambda s, m: (0, 0)),
                pl.BlockSpec((width // 2, 2 * rank), lambda s, m: (0, 0)),
            ],
            scratch_shapes=[
                pltpu.VMEM((token_count, head_cols), jnp.bfloat16),
                pltpu.VMEM((token_count, head_cols), jnp.bfloat16),
                pltpu.VMEM((group * SPAN, head_cols), jnp.bfloat16),
                pltpu.VMEM((group * SPAN, head_cols), jnp.bfloat16),
                pltpu.VMEM((per_device, slot_len, width), jnp.bfloat16),
                pltpu.VMEM((width, 2 * head_cols), jnp.bfloat16),
                pltpu.VMEM((2 * head_cols, width), jnp.bfloat16),
                pltpu.VMEM((keys, 2 * head_cols), jnp.bfloat16),
                pltpu.VMEM((keys, 2 * head_cols), jnp.bfloat16),
                pltpu.VMEM((keys, lanes), jnp.float32),
                pltpu.VMEM((keys, lanes), jnp.float32),
                pltpu.VMEM((group, 8, lanes), jnp.float32),
                pltpu.VMEM((group * 2 * SPAN, head_cols), jnp.bfloat16),
                pltpu.VMEM((group * 2 * SPAN, head_cols), jnp.bfloat16),
                pltpu.VMEM((width, 2 * rank), jnp.float32),
                pltpu.SemaphoreType.DMA((per_device * parts,)),
                pltpu.SemaphoreType.DMA((6,)),
            ],
        ),
        out_shape=[
            jax.ShapeDtypeStruct((token_count, head_cols), jnp.bfloat16),
            jax.ShapeDtypeStruct((token_count, head_cols), jnp.bfloat16),
            jax.ShapeDtypeStruct((span_count, width), jnp.float32),
            jax.ShapeDtypeStruct((width // 2, 2 * rank), jnp.float32),
            jax.ShapeDtypeStruct((width // 2, 2 * rank), jnp.bfloat16),
        ],
        compiler_params=pltpu.CompilerParams(vmem_limit_bytes=60 * 2**20),
        cost_estimate=pl.CostEstimate(
            flops=flops, bytes_accessed=16 * 2**20, transcendentals=rows * SPAN * HEADS
        ),
    )(meta, *small, *large)


def pick_kernel(held_count, meta, *refs):
    held_refs, out_ref = refs[:held_count], refs[held_count]
    for b, held in enumerate(held_refs):
        @pl.when(meta[0] == b)
        def _():
            for n in range(out_ref.shape[0]):
                out_ref[n] = held[meta[1 + n]]


def pick(which, index, held):
    count = index.shape[0]
    meta = jnp.concatenate([jnp.reshape(which, (1,)), index]).astype(jnp.int32)
    return pl.pallas_call(
        functools.partial(pick_kernel, len(held)),
        grid_spec=pltpu.PrefetchScalarGridSpec(
            num_scalar_prefetch=1,
            grid=(1,),
            in_specs=[pl.BlockSpec(memory_space=pltpu.VMEM)] * len(held),
            out_specs=pl.BlockSpec(memory_space=pltpu.VMEM),
        ),
        out_shape=jax.ShapeDtypeStruct((count,) + held[0].shape[1:], held[0].dtype),
        compiler_params=pltpu.CompilerParams(vmem_limit_bytes=16 * 2**20),
    )(meta, *held)


def place_requests(owners, per_device, pool_count, lanes):
    half = pool_count // 2
    count = owners.shape[1]
    order = jnp.arange(count, dtype=jnp.int32)
    side = (order // per_device) // half
    mate = side[:, None] == side[None, :]
    before = order[None, :] < order[:, None]
    same = owners[:, :, None] == owners[:, None, :]
    lower = owners[:, None, :] < owners[:, :, None]
    total = lambda mask: jnp.sum(mask.astype(jnp.int32), axis=2)
    rank = total(same & (mate & before)[None])
    crosses = rank >= lanes
    far = crosses[:, None, :]
    number = total(far & mate[None] & (lower | (same & before[None])))
    first = total(far & ~mate[None] & lower)
    guests = total(far & ~mate[None] & same)
    lane = jnp.where(crosses, number, first + guests + rank) % lanes
    row = jnp.where(crosses, 1 - side[None, :], side[None, :]) * half + lane % half
    return row, lane // half, crosses, number // half


def scatter_sum(keep, give, axes):
    width = keep.shape[1]
    size, columns = (lax.axis_size(axis) for axis in axes)
    index = lax.axis_index(axes[0])
    swap = lambda a, bit: lax.ppermute(a, axes[0], [(i, i ^ bit) for i in range(size)])
    total = keep + swap(give, 1).astype(jnp.float32)
    bit = 2
    while bit < size:
        split = total.reshape(size // bit // 2, 2, -1, width)
        mine = (index // bit) % 2
        keep = lax.dynamic_index_in_dim(split, mine, 1, keepdims=False)
        give = lax.dynamic_index_in_dim(split, 1 - mine, 1, keepdims=False)
        total = keep + swap(give.astype(jnp.bfloat16), bit).astype(jnp.float32)
        bit *= 2
    parts = total.reshape(columns, -1, width).astype(jnp.bfloat16)
    parts = lax.all_to_all(parts, axes[1], split_axis=0, concat_axis=0, tiled=True)
    return jnp.sum(parts.astype(jnp.float32), axis=0)


def body(
    queries, cotangent, cond, nbr_owner, nbr_block, database, lengths, gain, w_down, w_up, w_kv
):
    axes = ("pool", "dp")
    pool_count = lax.axis_size("pool")
    columns = lax.axis_size("dp")
    relay_row = pool_count - 1
    half = pool_count // 2
    row = lax.axis_index("pool")
    me = lax.axis_index("dp")
    span_count, width = cond.shape[2:]
    nbr_count = nbr_owner.shape[3]
    per_device = span_count * nbr_count
    block_count, slot_len = database.shape[2:4]
    live_count = relay_row * per_device
    capacity = max(2, live_count // columns + 1)
    slots = -(-capacity // pool_count)
    lanes = half * slots
    most = 0
    if capacity > lanes:
        for rows in (half, relay_row - half):
            full, left = divmod(rows * per_device, capacity)
            most = max(most, full * (capacity - lanes) + max(0, left - lanes))
    crossing = -(-most // half)
    token_count, head_cols = queries.shape[2:]

    def hop(array, pairs):
        return lax.ppermute(
            array, axes, [(a * columns + j, b * columns + j) for a, b in pairs for j in range(columns)]
        )

    first = slot_len // 16 * 3 // 4 * 16
    bounds = [0, first, slot_len] if 0 < first < slot_len else [0, slot_len]
    parts = len(bounds) - 1
    full_store = database.reshape(block_count, slot_len, width)
    cut = lambda i: full_store[:, bounds[i] : bounds[i + 1]]
    store = [cut(0)]

    def to_all(array, axis):
        copies = jnp.broadcast_to(array[None], (lax.axis_size(axis),) + array.shape)
        return lax.all_to_all(copies, axis, split_axis=0, concat_axis=0, tiled=True)

    info = jnp.concatenate([nbr_owner.reshape(-1), nbr_block.reshape(-1), lengths.reshape(-1)])
    info = jnp.pad(info, (0, -info.shape[0] % 128))
    over = lambda a: hop(a, [(relay_row, relay_row - half)])
    across = [over(store[0])]
    table = to_all(info.reshape(-1, 128), axes)
    w_kv_t = w_kv.T
    full_store, across, table, w_kv_t = lax.optimization_barrier(
        (full_store, across, table, w_kv_t)
    )
    store += [cut(i) for i in range(1, parts)]
    across += [over(a) for a in store[1:]]
    table = table.reshape(pool_count, columns, -1)
    by_column = jnp.swapaxes(table[:relay_row], 0, 1)
    owners = by_column[:, :, :per_device].reshape(columns, live_count)
    blocks = by_column[:, :, per_device : 2 * per_device].reshape(columns, live_count)
    store_len = table[relay_row, :, 2 * per_device : 2 * per_device + block_count]
    carrier, slot, crosses, number = place_requests(owners, per_device, pool_count, lanes)

    ring = jnp.arange(slots, dtype=jnp.int32)
    mine = ((owners == me) & (carrier == row))[:, None, :] & (slot[:, None, :] == ring[None, :, None])
    slot_block = jnp.sum(jnp.where(mine, blocks[:, None, :], 0), axis=2).reshape(-1)

    mine_of = lambda a: lax.dynamic_index_in_dim(a, me, 0, keepdims=False)
    my_owner, my_block, my_carrier, my_slot, my_cross, my_number = map(
        mine_of, (owners, blocks, carrier, slot, crosses, number)
    )
    place = my_owner * slots + my_slot
    ring = jnp.arange(crossing, dtype=jnp.int32)
    mine = (my_cross & (my_carrier == row))[None, :] & (my_number[None, :] == ring[:, None])
    leaving_place = jnp.sum(jnp.where(mine, place[None, :], 0), axis=1)

    def share(array, step):
        return hop(array, [(p, p // half * half + (p + step) % half) for p in range(pool_count)])

    held = []
    for i in range(parts):
        near = jnp.where(row == relay_row, store[i], across[i])
        stores = [near]
        held_by = jnp.where(row % half == half - 1, 0, 1)
        for step in range(1, half):
            stores.append(hop(near, [(p, p - step) for p in (relay_row, relay_row - half)]))
            held_by = jnp.where(row % half == half - 1 - step, step, held_by)
        sends = pick(held_by, slot_block, stores)
        arrived = lax.all_to_all(sends, "dp", split_axis=0, concat_axis=0, tiled=True)
        here = [arrived] + [share(arrived, step) for step in range(1, half)]
        if crossing:
            leaving = pick(0, leaving_place, [arrived])
            landed = hop(leaving, [(p, (p + half) % pool_count) for p in range(pool_count)])
            here += [landed] + [share(landed, step) for step in range(1, half)]
        held.append(here)
    origin = jnp.where(my_cross, (my_carrier + half) % pool_count, my_carrier)
    which = (row - origin) % half + jnp.where(my_cross, half, 0)
    index = jnp.where(my_cross, my_number, place)
    held = [here[b] for b in range(len(held[0])) for here in held]

    own_row = jnp.minimum(row, relay_row - 1)
    hot = (my_owner * block_count + my_block)[:, None] == jnp.arange(
        columns * block_count, dtype=jnp.int32
    )[None, :]
    wanted_len = jnp.sum(jnp.where(hot, store_len.reshape(1, -1), 0), axis=1)
    own = lambda a: lax.dynamic_index_in_dim(
        a.reshape(relay_row, per_device), own_row, 0, keepdims=False
    )
    live = (row < relay_row).astype(jnp.int32) + row % 2 * 2
    meta = jnp.concatenate([live[None], own(wanted_len), own(which), own(index)]).astype(jnp.int32)

    attn_out, q_grad, cond_grad, keep, give = run_spans(
        meta,
        queries.reshape(token_count, head_cols),
        cotangent.reshape(token_count, head_cols),
        cond.reshape(span_count, width).astype(jnp.float32),
        held,
        bounds,
        gain,
        w_down,
        w_up,
        w_kv,
        w_kv_t,
        nbr_count,
        pool_count,
    )

    adapter_grad = scatter_sum(keep, give, axes)
    return (
        attn_out.reshape(1, 1, token_count, head_cols),
        q_grad.reshape(1, 1, token_count, head_cols),
        cond_grad.reshape(1, 1, span_count, width),
        adapter_grad,
    )


def solution(mesh):
    return jax.shard_map(
        body,
        mesh=mesh,
        in_specs=(
            P("pool", "dp", None, None),
            P("pool", "dp", None, None),
            P("pool", "dp", None, None),
            P("pool", "dp", None, None),
            P("pool", "dp", None, None),
            P("pool", "dp", None, None, None),
            P("pool", "dp", None),
            P(),
            P(),
            P(),
            P(),
        ),
        out_specs=(
            P("pool", "dp", None, None),
            P("pool", "dp", None, None),
            P("pool", "dp", None, None),
            P(("pool", "dp"), None),
        ),
        check_vma=False,
    )
```

```python
import functools

import jax
import jax.numpy as jnp
from jax import lax
from jax.experimental import pallas as pl
from jax.experimental.pallas import tpu as pltpu
from jax.sharding import PartitionSpec as P

HEADS = 16
HEAD = 128
SPAN = 64
GROUP = 4

EPSILON = 1e-06
FLOOR = -1e30
LOG2E = 1.4426950408889634

NT = (((1,), (1,)), ((), ()))
TN = (((0,), (0,)), ((), ()))


def dot(a, b, dims=(((1,), (0,)), ((), ()))):
    return lax.dot_general(a, b, dims, preferred_element_type=jnp.float32)


def span_kernel(
    held_count, nbr_count, bounds, pool_count, meta,
    q_ref, cot_ref, cond_ref, gain_ref, down_ref, up_ref, upt_ref, downt_ref, *rest,
):
    held_refs = rest[:held_count]
    (kv_hbm, kvt_hbm, out_ref, qg_ref, cg_ref, keep_ref, give_ref,
     raw_ref, kv_ref, kvt_ref, proj_ref, grad_ref, score_ref, dprob_ref, stat_ref,
     q2_ref, cot2_ref, acc_ref, sems, kv_sem) = rest[held_count:]
    step = pl.program_id(0)
    per_device, slot_len, width = raw_ref.shape
    key_count = nbr_count * slot_len
    span_count = per_device // nbr_count
    group = span_count // pl.num_programs(0)
    head_cols = q_ref.shape[1]
    rank = down_ref.shape[1]
    scaling = HEAD ** (-0.5)
    live = meta[0] % 2 == 1
    odd = meta[0] // 2
    lens, which, index = 1, 1 + per_device, 1 + 2 * per_device
    parts = len(bounds) - 1
    cuts = [pl.ds(low, high - low) for low, high in zip(bounds, bounds[1:])]
    pairs = [pl.ds(i * 2 * HEAD, 2 * HEAD) for i in range(HEADS // 2)]
    value_pairs = [pl.ds(head_cols + i * 2 * HEAD, 2 * HEAD) for i in range(HEADS // 2)]
    lanes = [pl.ds(i * 2 * SPAN, 2 * SPAN) for i in range(HEADS // 2)]
    keys = [pl.ds(g * key_count, key_count) for g in range(group)]
    tokens = [pl.ds(g * SPAN, SPAN) for g in range(group)]
    double = [pl.ds(g * 2 * SPAN, 2 * SPAN) for g in range(group)]
    spots = [
        (g, cols, value_cols, lane)
        for g in range(group)
        for cols, value_cols, lane in zip(pairs, value_pairs, lanes)
    ]
    kv_copy = pltpu.make_async_copy(kv_hbm, kv_ref, kv_sem.at[0])
    kvt_copy = pltpu.make_async_copy(kvt_hbm, kvt_ref, kv_sem.at[1])

    @pl.when(step == 0)
    def _():
        for n in range(per_device):
            for b, held in enumerate(held_refs):
                @pl.when(meta[which + n] == b // parts)
                def _():
                    part = b % parts
                    pltpu.make_async_copy(
                        held.at[meta[index + n]],
                        raw_ref.at[n, cuts[part]],
                        sems.at[n * parts + part],
                    ).start()
        kv_copy.start()
        kvt_copy.start()
        q2_ref[...] = jnp.zeros_like(q2_ref)
        cot2_ref[...] = jnp.zeros_like(cot2_ref)

    for g in range(group):
        for i in range(HEADS):
            cols = pl.ds(i * HEAD, HEAD)
            part = pl.ds((2 * g + i % 2) * SPAN, SPAN)
            q2_ref[part, cols] = q_ref[tokens[g], cols]
            cot2_ref[part, cols] = cot_ref[tokens[g], cols]

    for n in range(group * nbr_count):
        for part in range(parts):
            item = step * group * nbr_count + n
            pltpu.make_async_copy(
                held_refs[part].at[0],
                raw_ref.at[item, cuts[part]],
                sems.at[item * parts + part],
            ).wait()
    x_full = jnp.concatenate(
        [
            raw_ref[pl.ds((step * group + g) * nbr_count, nbr_count)]
            .reshape(key_count, width)
            .astype(jnp.float32)
            + cond_ref[pl.ds(step * group + g, 1), :]
            for g in range(group)
        ],
        axis=0,
    )
    inv_rms = lax.rsqrt(jnp.mean(x_full * x_full, axis=-1, keepdims=True) + EPSILON)
    gain = gain_ref[...]
    hidden = (x_full * inv_rms * gain).astype(jnp.bfloat16)
    latent = dot(hidden, down_ref[...]).astype(jnp.bfloat16)
    encoded = (x_full + dot(latent, up_ref[...])).astype(jnp.bfloat16)

    @pl.when(step == 0)
    def _():
        kv_copy.wait()

    for cols in pairs + value_pairs:
        proj_ref[:, cols] = dot(encoded, kv_ref[:, cols]).astype(jnp.bfloat16)

    slot = lax.broadcasted_iota(jnp.int32, (key_count, 2 * SPAN), 0)
    usable = []
    for g in range(group):
        limit = jnp.zeros((key_count, 2 * SPAN), jnp.int32)
        for n in range(nbr_count):
            here = jnp.logical_and(slot >= n * slot_len, slot < (n + 1) * slot_len)
            item = (step * group + g) * nbr_count + n
            limit = jnp.where(here, n * slot_len + meta[lens + item], limit)
        usable.append(slot < limit)

    def diagonal(both):
        return jnp.concatenate([both[:SPAN, :HEAD], both[SPAN:, HEAD:]], axis=1)

    for g, cols, value_cols, lane in spots:
        scores = jnp.where(usable[g], dot(proj_ref[keys[g], cols], q2_ref[double[g], cols], NT), FLOOR)
        score_ref[keys[g], lane] = scores
        stat_ref[g, 0:1, lane] = jnp.max(scores, axis=0, keepdims=True)
        dprob_ref[keys[g], lane] = dot(proj_ref[keys[g], value_cols], cot2_ref[double[g], cols], NT)

    for g, cols, value_cols, lane in spots:
        raised = jnp.exp2((score_ref[keys[g], lane] - stat_ref[g, 0:1, lane]) * (scaling * LOG2E))
        d_probs = dprob_ref[keys[g], lane]
        inv_sum = 1.0 / jnp.sum(raised, axis=0, keepdims=True)
        delta = inv_sum * jnp.sum(raised * d_probs, axis=0, keepdims=True)
        probs = raised * inv_sum
        d_scores = probs * (d_probs - delta) * scaling
        probs_b, d_scores = probs.astype(jnp.bfloat16), d_scores.astype(jnp.bfloat16)
        grad_ref[keys[g], cols] = dot(d_scores, q2_ref[double[g], cols]).astype(jnp.bfloat16)
        grad_ref[keys[g], value_cols] = dot(probs_b, cot2_ref[double[g], cols]).astype(jnp.bfloat16)
        out = diagonal(dot(probs_b.T, proj_ref[keys[g], value_cols]))
        grad = diagonal(dot(d_scores.T, proj_ref[keys[g], cols]))
        out_ref[tokens[g], cols] = jnp.where(live, out, 0.0).astype(jnp.bfloat16)
        qg_ref[tokens[g], cols] = jnp.where(live, grad, 0.0).astype(jnp.bfloat16)

    @pl.when(step == 0)
    def _():
        kvt_copy.wait()
        acc_ref[...] = jnp.zeros_like(acc_ref)

    enc_grad = dot(grad_ref[...], kvt_ref[...]).astype(jnp.bfloat16)
    lat_grad = dot(enc_grad, upt_ref[...]).astype(jnp.bfloat16)
    scaled = dot(lat_grad, downt_ref[...]) * gain
    normed = x_full * inv_rms
    x_grad = enc_grad.astype(jnp.float32) + inv_rms * (
        scaled - normed * jnp.mean(scaled * normed, axis=-1, keepdims=True)
    )
    for g in range(group):
        span_grad = jnp.sum(
            x_grad[g * key_count : (g + 1) * key_count], axis=0, keepdims=True
        )
        cg_ref[pl.ds(step * group + g, 1), :] = jnp.where(live, span_grad, 0.0)
    acc_ref[:, :rank] += dot(hidden, lat_grad, TN)
    acc_ref[:, rank:] += dot(enc_grad, latent, TN)

    @pl.when(step == pl.num_programs(0) - 1)
    def _():
        chunk = width // pool_count
        for k in range(pool_count // 2):
            part = pl.ds(k * chunk, chunk)
            for ref, own in ((keep_ref, odd), (give_ref, 1 - odd)):
                rows = acc_ref[pl.ds(pl.multiple_of((2 * k + own) * chunk, chunk), chunk), :]
                ref[part, :] = jnp.where(live, rows, 0.0).astype(ref.dtype)


def run_spans(meta, query, cot, cond, held, bounds, gain, w_down, w_up, w_kv, w_kv_t, nbr_count, pool_count):
    span_count, width = cond.shape
    token_count, head_cols = query.shape
    slot_len = bounds[-1]
    parts = len(bounds) - 1
    rank = w_down.shape[1]
    whole = lambda a: pl.BlockSpec(a.shape, lambda s, m: (0,) * a.ndim, pipeline_mode=pl.Buffered(1))
    group = GROUP if span_count % GROUP == 0 else 1
    tokens = pl.BlockSpec((group * SPAN, head_cols), lambda s, m: (s, 0))
    small = [cond, gain.reshape(1, width), w_down, w_up, w_up.T, w_down.T]
    large = list(held) + [w_kv, w_kv_t]
    per_device = span_count * nbr_count
    keys = group * nbr_count * slot_len
    rows = per_device * slot_len
    lanes = SPAN * HEADS
    flops = 2 * rows * (2 * width * 2 * head_cols + 6 * width * rank + 6 * SPAN * head_cols)
    return pl.pallas_call(
        functools.partial(span_kernel, len(held), nbr_count, bounds, pool_count),
        grid_spec=pltpu.PrefetchScalarGridSpec(
            num_scalar_prefetch=1,
            grid=(span_count // group,),
            in_specs=[tokens, tokens]
            + [whole(a) for a in small]
            + [pl.BlockSpec(memory_space=pltpu.HBM)] * len(large),
            out_specs=[
                tokens,
                tokens,
                pl.BlockSpec((span_count, width), lambda s, m: (0, 0)),
                pl.BlockSpec((width // 2, 2 * rank), lambda s, m: (0, 0)),
                pl.BlockSpec((width // 2, 2 * rank), lambda s, m: (0, 0)),
            ],
            scratch_shapes=[
                pltpu.VMEM((per_device, slot_len, width), jnp.bfloat16),
                pltpu.VMEM((width, 2 * head_cols), jnp.bfloat16),
                pltpu.VMEM((2 * head_cols, width), jnp.bfloat16),
                pltpu.VMEM((keys, 2 * head_cols), jnp.bfloat16),
                pltpu.VMEM((keys, 2 * head_cols), jnp.bfloat16),
                pltpu.VMEM((keys, lanes), jnp.float32),
                pltpu.VMEM((keys, lanes), jnp.float32),
                pltpu.VMEM((group, 8, lanes), jnp.float32),
                pltpu.VMEM((group * 2 * SPAN, head_cols), jnp.bfloat16),
                pltpu.VMEM((group * 2 * SPAN, head_cols), jnp.bfloat16),
                pltpu.VMEM((width, 2 * rank), jnp.float32),
                pltpu.SemaphoreType.DMA((per_device * parts,)),
                pltpu.SemaphoreType.DMA((2,)),
            ],
        ),
        out_shape=[
            jax.ShapeDtypeStruct((token_count, head_cols), jnp.bfloat16),
            jax.ShapeDtypeStruct((token_count, head_cols), jnp.bfloat16),
            jax.ShapeDtypeStruct((span_count, width), jnp.float32),
            jax.ShapeDtypeStruct((width // 2, 2 * rank), jnp.float32),
            jax.ShapeDtypeStruct((width // 2, 2 * rank), jnp.bfloat16),
        ],
        compiler_params=pltpu.CompilerParams(vmem_limit_bytes=60 * 2**20),
        cost_estimate=pl.CostEstimate(
            flops=flops, bytes_accessed=16 * 2**20, transcendentals=rows * SPAN * HEADS
        ),
    )(meta, query, cot, *small, *large)


def pick_kernel(held_count, meta, *refs):
    held_refs, out_ref = refs[:held_count], refs[held_count]
    for b, held in enumerate(held_refs):
        @pl.when(meta[0] == b)
        def _():
            for n in range(out_ref.shape[0]):
                out_ref[n] = held[meta[1 + n]]


def pick(which, index, held):
    count = index.shape[0]
    meta = jnp.concatenate([jnp.reshape(which, (1,)), index]).astype(jnp.int32)
    return pl.pallas_call(
        functools.partial(pick_kernel, len(held)),
        grid_spec=pltpu.PrefetchScalarGridSpec(
            num_scalar_prefetch=1,
            grid=(1,),
            in_specs=[pl.BlockSpec(memory_space=pltpu.VMEM)] * len(held),
            out_specs=pl.BlockSpec(memory_space=pltpu.VMEM),
        ),
        out_shape=jax.ShapeDtypeStruct((count,) + held[0].shape[1:], held[0].dtype),
        compiler_params=pltpu.CompilerParams(vmem_limit_bytes=16 * 2**20),
    )(meta, *held)


def place_requests(owners, per_device, pool_count, lanes):
    half = pool_count // 2
    count = owners.shape[1]
    order = jnp.arange(count, dtype=jnp.int32)
    side = (order // per_device) // half
    mate = side[:, None] == side[None, :]
    before = order[None, :] < order[:, None]
    same = owners[:, :, None] == owners[:, None, :]
    lower = owners[:, None, :] < owners[:, :, None]
    total = lambda mask: jnp.sum(mask.astype(jnp.int32), axis=2)
    rank = total(same & (mate & before)[None])
    crosses = rank >= lanes
    far = crosses[:, None, :]
    number = total(far & mate[None] & (lower | (same & before[None])))
    first = total(far & ~mate[None] & lower)
    guests = total(far & ~mate[None] & same)
    lane = jnp.where(crosses, number, first + guests + rank) % lanes
    row = jnp.where(crosses, 1 - side[None, :], side[None, :]) * half + lane % half
    return row, lane // half, crosses, number // half


def scatter_sum(keep, give, axes):
    width = keep.shape[1]
    size, columns = (lax.axis_size(axis) for axis in axes)
    index = lax.axis_index(axes[0])
    swap = lambda a, bit: lax.ppermute(a, axes[0], [(i, i ^ bit) for i in range(size)])
    total = keep + swap(give, 1).astype(jnp.float32)
    bit = 2
    while bit < size:
        split = total.reshape(size // bit // 2, 2, -1, width)
        mine = (index // bit) % 2
        keep = lax.dynamic_index_in_dim(split, mine, 1, keepdims=False)
        give = lax.dynamic_index_in_dim(split, 1 - mine, 1, keepdims=False)
        total = keep + swap(give.astype(jnp.bfloat16), bit).astype(jnp.float32)
        bit *= 2
    parts = total.reshape(columns, -1, width).astype(jnp.bfloat16)
    parts = lax.all_to_all(parts, axes[1], split_axis=0, concat_axis=0, tiled=True)
    return jnp.sum(parts.astype(jnp.float32), axis=0)


def body(
    queries, cotangent, cond, nbr_owner, nbr_block, database, lengths, gain, w_down, w_up, w_kv
):
    axes = ("pool", "dp")
    pool_count = lax.axis_size("pool")
    columns = lax.axis_size("dp")
    relay_row = pool_count - 1
    half = pool_count // 2
    row = lax.axis_index("pool")
    me = lax.axis_index("dp")
    span_count, width = cond.shape[2:]
    nbr_count = nbr_owner.shape[3]
    per_device = span_count * nbr_count
    block_count, slot_len = database.shape[2:4]
    live_count = relay_row * per_device
    capacity = max(2, live_count // columns + 1)
    slots = -(-capacity // pool_count)
    lanes = half * slots
    most = 0
    if capacity > lanes:
        for rows in (half, relay_row - half):
            full, left = divmod(rows * per_device, capacity)
            most = max(most, full * (capacity - lanes) + max(0, left - lanes))
    crossing = -(-most // half)
    token_count, head_cols = queries.shape[2:]

    def hop(array, pairs):
        return lax.ppermute(
            array, axes, [(a * columns + j, b * columns + j) for a, b in pairs for j in range(columns)]
        )

    first = slot_len // 16 * 3 // 4 * 16
    bounds = [0, first, slot_len] if 0 < first < slot_len else [0, slot_len]
    parts = len(bounds) - 1
    full_store = database.reshape(block_count, slot_len, width)
    cut = lambda i: full_store[:, bounds[i] : bounds[i + 1]]
    store = [cut(0)]

    def to_all(array, axis):
        copies = jnp.broadcast_to(array[None], (lax.axis_size(axis),) + array.shape)
        return lax.all_to_all(copies, axis, split_axis=0, concat_axis=0, tiled=True)

    info = jnp.concatenate([nbr_owner.reshape(-1), nbr_block.reshape(-1), lengths.reshape(-1)])
    info = jnp.pad(info, (0, -info.shape[0] % 128))
    over = lambda a: hop(a, [(relay_row, relay_row - half)])
    across = [over(store[0])]
    table = to_all(info.reshape(-1, 128), axes)
    w_kv_t = w_kv.T
    full_store, across, table, w_kv_t = lax.optimization_barrier(
        (full_store, across, table, w_kv_t)
    )
    store += [cut(i) for i in range(1, parts)]
    across += [over(a) for a in store[1:]]
    table = table.reshape(pool_count, columns, -1)
    by_column = jnp.swapaxes(table[:relay_row], 0, 1)
    owners = by_column[:, :, :per_device].reshape(columns, live_count)
    blocks = by_column[:, :, per_device : 2 * per_device].reshape(columns, live_count)
    store_len = table[relay_row, :, 2 * per_device : 2 * per_device + block_count]
    carrier, slot, crosses, number = place_requests(owners, per_device, pool_count, lanes)

    ring = jnp.arange(slots, dtype=jnp.int32)
    mine = ((owners == me) & (carrier == row))[:, None, :] & (slot[:, None, :] == ring[None, :, None])
    slot_block = jnp.sum(jnp.where(mine, blocks[:, None, :], 0), axis=2).reshape(-1)

    mine_of = lambda a: lax.dynamic_index_in_dim(a, me, 0, keepdims=False)
    my_owner, my_block, my_carrier, my_slot, my_cross, my_number = map(
        mine_of, (owners, blocks, carrier, slot, crosses, number)
    )
    place = my_owner * slots + my_slot
    ring = jnp.arange(crossing, dtype=jnp.int32)
    mine = (my_cross & (my_carrier == row))[None, :] & (my_number[None, :] == ring[:, None])
    leaving_place = jnp.sum(jnp.where(mine, place[None, :], 0), axis=1)

    def share(array, step):
        return hop(array, [(p, p // half * half + (p + step) % half) for p in range(pool_count)])

    held = []
    for i in range(parts):
        near = jnp.where(row == relay_row, store[i], across[i])
        stores = [near]
        held_by = jnp.where(row % half == half - 1, 0, 1)
        for step in range(1, half):
            stores.append(hop(near, [(p, p - step) for p in (relay_row, relay_row - half)]))
            held_by = jnp.where(row % half == half - 1 - step, step, held_by)
        sends = pick(held_by, slot_block, stores)
        arrived = lax.all_to_all(sends, "dp", split_axis=0, concat_axis=0, tiled=True)
        here = [arrived] + [share(arrived, step) for step in range(1, half)]
        if crossing:
            leaving = pick(0, leaving_place, [arrived])
            landed = hop(leaving, [(p, (p + half) % pool_count) for p in range(pool_count)])
            here += [landed] + [share(landed, step) for step in range(1, half)]
        held.append(here)
    origin = jnp.where(my_cross, (my_carrier + half) % pool_count, my_carrier)
    which = (row - origin) % half + jnp.where(my_cross, half, 0)
    index = jnp.where(my_cross, my_number, place)
    held = [here[b] for b in range(len(held[0])) for here in held]

    own_row = jnp.minimum(row, relay_row - 1)
    hot = (my_owner * block_count + my_block)[:, None] == jnp.arange(
        columns * block_count, dtype=jnp.int32
    )[None, :]
    wanted_len = jnp.sum(jnp.where(hot, store_len.reshape(1, -1), 0), axis=1)
    own = lambda a: lax.dynamic_index_in_dim(
        a.reshape(relay_row, per_device), own_row, 0, keepdims=False
    )
    live = (row < relay_row).astype(jnp.int32) + row % 2 * 2
    meta = jnp.concatenate([live[None], own(wanted_len), own(which), own(index)]).astype(jnp.int32)

    attn_out, q_grad, cond_grad, keep, give = run_spans(
        meta,
        queries.reshape(token_count, head_cols),
        cotangent.reshape(token_count, head_cols),
        cond.reshape(span_count, width).astype(jnp.float32),
        held,
        bounds,
        gain,
        w_down,
        w_up,
        w_kv,
        w_kv_t,
        nbr_count,
        pool_count,
    )

    adapter_grad = scatter_sum(keep, give, axes)
    return (
        attn_out.reshape(1, 1, token_count, head_cols),
        q_grad.reshape(1, 1, token_count, head_cols),
        cond_grad.reshape(1, 1, span_count, width),
        adapter_grad,
    )


def solution(mesh):
    return jax.shard_map(
        body,
        mesh=mesh,
        in_specs=(
            P("pool", "dp", None, None),
            P("pool", "dp", None, None),
            P("pool", "dp", None, None),
            P("pool", "dp", None, None),
            P("pool", "dp", None, None),
            P("pool", "dp", None, None, None),
            P("pool", "dp", None),
            P(),
            P(),
            P(),
            P(),
        ),
        out_specs=(
            P("pool", "dp", None, None),
            P("pool", "dp", None, None),
            P("pool", "dp", None, None),
            P(("pool", "dp"), None),
        ),
        check_vma=False,
    )
```

```python
import functools

import jax
import jax.numpy as jnp
from jax import lax
from jax.experimental import pallas as pl
from jax.experimental.pallas import tpu as pltpu
from jax.sharding import PartitionSpec as P

HEADS = 16
HEAD = 128
SPAN = 64
GROUP = 4

EPSILON = 1e-06
FLOOR = -1e30
LOG2E = 1.4426950408889634

NT = (((1,), (1,)), ((), ()))
TN = (((0,), (0,)), ((), ()))


def dot(a, b, dims=(((1,), (0,)), ((), ()))):
    return lax.dot_general(a, b, dims, preferred_element_type=jnp.float32)


def span_kernel(
    held_count, nbr_count, bounds, pool_count, meta,
    q_ref, cot_ref, cond_ref, gain_ref, down_ref, up_ref, upt_ref, downt_ref, *rest,
):
    held_refs = rest[:held_count]
    (kv_hbm, kvt_hbm, out_ref, qg_ref, cg_ref, keep_ref, give_ref,
     raw_ref, kv_ref, kvt_ref, proj_ref, grad_ref, score_ref, dprob_ref, stat_ref,
     q2_ref, cot2_ref, acc_ref, sems, kv_sem) = rest[held_count:]
    step = pl.program_id(0)
    per_device, slot_len, width = raw_ref.shape
    key_count = nbr_count * slot_len
    span_count = per_device // nbr_count
    group = span_count // pl.num_programs(0)
    head_cols = q_ref.shape[1]
    rank = down_ref.shape[1]
    scaling = HEAD ** (-0.5)
    live = meta[0] % 2 == 1
    odd = meta[0] // 2
    lens, which, index = 1, 1 + per_device, 1 + 2 * per_device
    parts = len(bounds) - 1
    cuts = [pl.ds(low, high - low) for low, high in zip(bounds, bounds[1:])]
    pairs = [pl.ds(i * 2 * HEAD, 2 * HEAD) for i in range(HEADS // 2)]
    value_pairs = [pl.ds(head_cols + i * 2 * HEAD, 2 * HEAD) for i in range(HEADS // 2)]
    lanes = [pl.ds(i * 2 * SPAN, 2 * SPAN) for i in range(HEADS // 2)]
    keys = [pl.ds(g * key_count, key_count) for g in range(group)]
    tokens = [pl.ds(g * SPAN, SPAN) for g in range(group)]
    double = [pl.ds(g * 2 * SPAN, 2 * SPAN) for g in range(group)]
    spots = [
        (g, cols, value_cols, lane)
        for g in range(group)
        for cols, value_cols, lane in zip(pairs, value_pairs, lanes)
    ]
    kv_copy = pltpu.make_async_copy(kv_hbm, kv_ref, kv_sem.at[0])
    kvt_copy = pltpu.make_async_copy(kvt_hbm, kvt_ref, kv_sem.at[1])

    @pl.when(step == 0)
    def _():
        kv_copy.start()
        for n in range(per_device):
            for b, held in enumerate(held_refs):
                @pl.when(meta[which + n] == b // parts)
                def _():
                    part = b % parts
                    pltpu.make_async_copy(
                        held.at[meta[index + n]],
                        raw_ref.at[n, cuts[part]],
                        sems.at[n * parts + part],
                    ).start()
        q2_ref[...] = jnp.zeros_like(q2_ref)
        cot2_ref[...] = jnp.zeros_like(cot2_ref)

    for g in range(group):
        for i in range(HEADS):
            cols = pl.ds(i * HEAD, HEAD)
            part = pl.ds((2 * g + i % 2) * SPAN, SPAN)
            q2_ref[part, cols] = q_ref[tokens[g], cols]
            cot2_ref[part, cols] = cot_ref[tokens[g], cols]

    for n in range(group * nbr_count):
        for part in range(parts):
            item = step * group * nbr_count + n
            pltpu.make_async_copy(
                held_refs[part].at[0],
                raw_ref.at[item, cuts[part]],
                sems.at[item * parts + part],
            ).wait()
    x_full = jnp.concatenate(
        [
            raw_ref[pl.ds((step * group + g) * nbr_count, nbr_count)]
            .reshape(key_count, width)
            .astype(jnp.float32)
            + cond_ref[pl.ds(step * group + g, 1), :]
            for g in range(group)
        ],
        axis=0,
    )
    inv_rms = lax.rsqrt(jnp.mean(x_full * x_full, axis=-1, keepdims=True) + EPSILON)
    gain = gain_ref[...]
    hidden = (x_full * inv_rms * gain).astype(jnp.bfloat16)
    latent = dot(hidden, down_ref[...]).astype(jnp.bfloat16)
    encoded = (x_full + dot(latent, up_ref[...])).astype(jnp.bfloat16)

    @pl.when(step == 0)
    def _():
        kv_copy.wait()
        kvt_copy.start()

    for cols in pairs + value_pairs:
        proj_ref[:, cols] = dot(encoded, kv_ref[:, cols]).astype(jnp.bfloat16)

    slot = lax.broadcasted_iota(jnp.int32, (key_count, 2 * SPAN), 0)
    usable = []
    for g in range(group):
        limit = jnp.zeros((key_count, 2 * SPAN), jnp.int32)
        for n in range(nbr_count):
            here = jnp.logical_and(slot >= n * slot_len, slot < (n + 1) * slot_len)
            item = (step * group + g) * nbr_count + n
            limit = jnp.where(here, n * slot_len + meta[lens + item], limit)
        usable.append(slot < limit)

    def diagonal(both):
        return jnp.concatenate([both[:SPAN, :HEAD], both[SPAN:, HEAD:]], axis=1)

    for g, cols, value_cols, lane in spots:
        scores = jnp.where(usable[g], dot(proj_ref[keys[g], cols], q2_ref[double[g], cols], NT), FLOOR)
        score_ref[keys[g], lane] = scores
        stat_ref[g, 0:1, lane] = jnp.max(scores, axis=0, keepdims=True)
        dprob_ref[keys[g], lane] = dot(proj_ref[keys[g], value_cols], cot2_ref[double[g], cols], NT)

    for g, cols, value_cols, lane in spots:
        raised = jnp.exp2((score_ref[keys[g], lane] - stat_ref[g, 0:1, lane]) * (scaling * LOG2E))
        inv_sum = 1.0 / jnp.sum(raised, axis=0, keepdims=True)
        score_ref[keys[g], lane] = raised
        stat_ref[g, 1:2, lane] = inv_sum
        stat_ref[g, 2:3, lane] = inv_sum * jnp.sum(
            raised * dprob_ref[keys[g], lane], axis=0, keepdims=True
        )

    for g, cols, value_cols, lane in spots:
        probs = score_ref[keys[g], lane] * stat_ref[g, 1:2, lane]
        d_scores = probs * (dprob_ref[keys[g], lane] - stat_ref[g, 2:3, lane]) * scaling
        probs_b, d_scores = probs.astype(jnp.bfloat16), d_scores.astype(jnp.bfloat16)
        grad_ref[keys[g], cols] = dot(d_scores, q2_ref[double[g], cols]).astype(jnp.bfloat16)
        grad_ref[keys[g], value_cols] = dot(probs_b, cot2_ref[double[g], cols]).astype(jnp.bfloat16)
        out = diagonal(dot(probs_b.T, proj_ref[keys[g], value_cols]))
        grad = diagonal(dot(d_scores.T, proj_ref[keys[g], cols]))
        out_ref[tokens[g], cols] = jnp.where(live, out, 0.0).astype(jnp.bfloat16)
        qg_ref[tokens[g], cols] = jnp.where(live, grad, 0.0).astype(jnp.bfloat16)

    @pl.when(step == 0)
    def _():
        kvt_copy.wait()
        acc_ref[...] = jnp.zeros_like(acc_ref)

    enc_grad = dot(grad_ref[...], kvt_ref[...]).astype(jnp.bfloat16)
    lat_grad = dot(enc_grad, upt_ref[...]).astype(jnp.bfloat16)
    scaled = dot(lat_grad, downt_ref[...]) * gain
    normed = x_full * inv_rms
    x_grad = enc_grad.astype(jnp.float32) + inv_rms * (
        scaled - normed * jnp.mean(scaled * normed, axis=-1, keepdims=True)
    )
    for g in range(group):
        span_grad = jnp.sum(
            x_grad[g * key_count : (g + 1) * key_count], axis=0, keepdims=True
        )
        cg_ref[pl.ds(step * group + g, 1), :] = jnp.where(live, span_grad, 0.0)
    acc_ref[:, :rank] += dot(hidden, lat_grad, TN)
    acc_ref[:, rank:] += dot(enc_grad, latent, TN)

    @pl.when(step == pl.num_programs(0) - 1)
    def _():
        chunk = width // pool_count
        for k in range(pool_count // 2):
            part = pl.ds(k * chunk, chunk)
            for ref, own in ((keep_ref, odd), (give_ref, 1 - odd)):
                rows = acc_ref[pl.ds(pl.multiple_of((2 * k + own) * chunk, chunk), chunk), :]
                ref[part, :] = jnp.where(live, rows, 0.0).astype(ref.dtype)


def run_spans(meta, query, cot, cond, held, bounds, gain, w_down, w_up, w_kv, w_kv_t, nbr_count, pool_count):
    span_count, width = cond.shape
    token_count, head_cols = query.shape
    slot_len = bounds[-1]
    parts = len(bounds) - 1
    rank = w_down.shape[1]
    whole = lambda a: pl.BlockSpec(a.shape, lambda s, m: (0,) * a.ndim, pipeline_mode=pl.Buffered(1))
    group = GROUP if span_count % GROUP == 0 else 1
    tokens = pl.BlockSpec((group * SPAN, head_cols), lambda s, m: (s, 0))
    small = [cond, gain.reshape(1, width), w_down, w_up, w_up.T, w_down.T]
    large = list(held) + [w_kv, w_kv_t]
    per_device = span_count * nbr_count
    keys = group * nbr_count * slot_len
    rows = per_device * slot_len
    lanes = SPAN * HEADS
    flops = 2 * rows * (2 * width * 2 * head_cols + 6 * width * rank + 6 * SPAN * head_cols)
    return pl.pallas_call(
        functools.partial(span_kernel, len(held), nbr_count, bounds, pool_count),
        grid_spec=pltpu.PrefetchScalarGridSpec(
            num_scalar_prefetch=1,
            grid=(span_count // group,),
            in_specs=[tokens, tokens]
            + [whole(a) for a in small]
            + [pl.BlockSpec(memory_space=pltpu.HBM)] * len(large),
            out_specs=[
                tokens,
                tokens,
                pl.BlockSpec((span_count, width), lambda s, m: (0, 0)),
                pl.BlockSpec((width // 2, 2 * rank), lambda s, m: (0, 0)),
                pl.BlockSpec((width // 2, 2 * rank), lambda s, m: (0, 0)),
            ],
            scratch_shapes=[
                pltpu.VMEM((per_device, slot_len, width), jnp.bfloat16),
                pltpu.VMEM((width, 2 * head_cols), jnp.bfloat16),
                pltpu.VMEM((2 * head_cols, width), jnp.bfloat16),
                pltpu.VMEM((keys, 2 * head_cols), jnp.bfloat16),
                pltpu.VMEM((keys, 2 * head_cols), jnp.bfloat16),
                pltpu.VMEM((keys, lanes), jnp.float32),
                pltpu.VMEM((keys, lanes), jnp.float32),
                pltpu.VMEM((group, 8, lanes), jnp.float32),
                pltpu.VMEM((group * 2 * SPAN, head_cols), jnp.bfloat16),
                pltpu.VMEM((group * 2 * SPAN, head_cols), jnp.bfloat16),
                pltpu.VMEM((width, 2 * rank), jnp.float32),
                pltpu.SemaphoreType.DMA((per_device * parts,)),
                pltpu.SemaphoreType.DMA((2,)),
            ],
        ),
        out_shape=[
            jax.ShapeDtypeStruct((token_count, head_cols), jnp.bfloat16),
            jax.ShapeDtypeStruct((token_count, head_cols), jnp.bfloat16),
            jax.ShapeDtypeStruct((span_count, width), jnp.float32),
            jax.ShapeDtypeStruct((width // 2, 2 * rank), jnp.float32),
            jax.ShapeDtypeStruct((width // 2, 2 * rank), jnp.bfloat16),
        ],
        compiler_params=pltpu.CompilerParams(vmem_limit_bytes=60 * 2**20),
        cost_estimate=pl.CostEstimate(
            flops=flops, bytes_accessed=16 * 2**20, transcendentals=rows * SPAN * HEADS
        ),
    )(meta, query, cot, *small, *large)


def pick_kernel(held_count, meta, *refs):
    held_refs, out_ref = refs[:held_count], refs[held_count]
    for b, held in enumerate(held_refs):
        @pl.when(meta[0] == b)
        def _():
            for n in range(out_ref.shape[0]):
                out_ref[n] = held[meta[1 + n]]


def pick(which, index, held):
    count = index.shape[0]
    meta = jnp.concatenate([jnp.reshape(which, (1,)), index]).astype(jnp.int32)
    return pl.pallas_call(
        functools.partial(pick_kernel, len(held)),
        grid_spec=pltpu.PrefetchScalarGridSpec(
            num_scalar_prefetch=1,
            grid=(1,),
            in_specs=[pl.BlockSpec(memory_space=pltpu.VMEM)] * len(held),
            out_specs=pl.BlockSpec(memory_space=pltpu.VMEM),
        ),
        out_shape=jax.ShapeDtypeStruct((count,) + held[0].shape[1:], held[0].dtype),
        compiler_params=pltpu.CompilerParams(vmem_limit_bytes=16 * 2**20),
    )(meta, *held)


def place_requests(owners, per_device, pool_count, lanes):
    half = pool_count // 2
    count = owners.shape[1]
    order = jnp.arange(count, dtype=jnp.int32)
    side = (order // per_device) // half
    mate = side[:, None] == side[None, :]
    before = order[None, :] < order[:, None]
    same = owners[:, :, None] == owners[:, None, :]
    lower = owners[:, None, :] < owners[:, :, None]
    total = lambda mask: jnp.sum(mask.astype(jnp.int32), axis=2)
    rank = total(same & (mate & before)[None])
    crosses = rank >= lanes
    far = crosses[:, None, :]
    number = total(far & mate[None] & (lower | (same & before[None])))
    first = total(far & ~mate[None] & lower)
    guests = total(far & ~mate[None] & same)
    lane = jnp.where(crosses, number, first + guests + rank) % lanes
    row = jnp.where(crosses, 1 - side[None, :], side[None, :]) * half + lane % half
    return row, lane // half, crosses, number // half


def scatter_sum(keep, give, axes):
    width = keep.shape[1]
    size, columns = (lax.axis_size(axis) for axis in axes)
    index = lax.axis_index(axes[0])
    swap = lambda a, bit: lax.ppermute(a, axes[0], [(i, i ^ bit) for i in range(size)])
    total = keep + swap(give, 1).astype(jnp.float32)
    bit = 2
    while bit < size:
        split = total.reshape(size // bit // 2, 2, -1, width)
        mine = (index // bit) % 2
        keep = lax.dynamic_index_in_dim(split, mine, 1, keepdims=False)
        give = lax.dynamic_index_in_dim(split, 1 - mine, 1, keepdims=False)
        total = keep + swap(give.astype(jnp.bfloat16), bit).astype(jnp.float32)
        bit *= 2
    parts = total.reshape(columns, -1, width).astype(jnp.bfloat16)
    parts = lax.all_to_all(parts, axes[1], split_axis=0, concat_axis=0, tiled=True)
    return jnp.sum(parts.astype(jnp.float32), axis=0)


def body(
    queries, cotangent, cond, nbr_owner, nbr_block, database, lengths, gain, w_down, w_up, w_kv
):
    axes = ("pool", "dp")
    pool_count = lax.axis_size("pool")
    columns = lax.axis_size("dp")
    relay_row = pool_count - 1
    half = pool_count // 2
    row = lax.axis_index("pool")
    me = lax.axis_index("dp")
    span_count, width = cond.shape[2:]
    nbr_count = nbr_owner.shape[3]
    per_device = span_count * nbr_count
    block_count, slot_len = database.shape[2:4]
    live_count = relay_row * per_device
    capacity = max(2, live_count // columns + 1)
    slots = -(-capacity // pool_count)
    lanes = half * slots
    most = 0
    if capacity > lanes:
        for rows in (half, relay_row - half):
            full, left = divmod(rows * per_device, capacity)
            most = max(most, full * (capacity - lanes) + max(0, left - lanes))
    crossing = -(-most // half)
    token_count, head_cols = queries.shape[2:]

    def hop(array, pairs):
        return lax.ppermute(
            array, axes, [(a * columns + j, b * columns + j) for a, b in pairs for j in range(columns)]
        )

    first = slot_len // 16 * 3 // 4 * 16
    bounds = [0, first, slot_len] if 0 < first < slot_len else [0, slot_len]
    parts = len(bounds) - 1
    full_store = database.reshape(block_count, slot_len, width)
    cut = lambda i: full_store[:, bounds[i] : bounds[i + 1]]
    store = [cut(0)]

    def to_all(array, axis):
        copies = jnp.broadcast_to(array[None], (lax.axis_size(axis),) + array.shape)
        return lax.all_to_all(copies, axis, split_axis=0, concat_axis=0, tiled=True)

    info = jnp.concatenate([nbr_owner.reshape(-1), nbr_block.reshape(-1), lengths.reshape(-1)])
    info = jnp.pad(info, (0, -info.shape[0] % 128))
    over = lambda a: hop(a, [(relay_row, relay_row - half)])
    across = [over(store[0])]
    table = to_all(info.reshape(-1, 128), axes)
    w_kv_t = w_kv.T
    full_store, across, table, w_kv_t = lax.optimization_barrier(
        (full_store, across, table, w_kv_t)
    )
    store += [cut(i) for i in range(1, parts)]
    across += [over(a) for a in store[1:]]
    table = table.reshape(pool_count, columns, -1)
    by_column = jnp.swapaxes(table[:relay_row], 0, 1)
    owners = by_column[:, :, :per_device].reshape(columns, live_count)
    blocks = by_column[:, :, per_device : 2 * per_device].reshape(columns, live_count)
    store_len = table[relay_row, :, 2 * per_device : 2 * per_device + block_count]
    carrier, slot, crosses, number = place_requests(owners, per_device, pool_count, lanes)

    ring = jnp.arange(slots, dtype=jnp.int32)
    mine = ((owners == me) & (carrier == row))[:, None, :] & (slot[:, None, :] == ring[None, :, None])
    slot_block = jnp.sum(jnp.where(mine, blocks[:, None, :], 0), axis=2).reshape(-1)

    mine_of = lambda a: lax.dynamic_index_in_dim(a, me, 0, keepdims=False)
    my_owner, my_block, my_carrier, my_slot, my_cross, my_number = map(
        mine_of, (owners, blocks, carrier, slot, crosses, number)
    )
    place = my_owner * slots + my_slot
    ring = jnp.arange(crossing, dtype=jnp.int32)
    mine = (my_cross & (my_carrier == row))[None, :] & (my_number[None, :] == ring[:, None])
    leaving_place = jnp.sum(jnp.where(mine, place[None, :], 0), axis=1)

    def share(array, step):
        return hop(array, [(p, p // half * half + (p + step) % half) for p in range(pool_count)])

    held = []
    for i in range(parts):
        near = jnp.where(row == relay_row, store[i], across[i])
        stores = [near]
        held_by = jnp.where(row % half == half - 1, 0, 1)
        for step in range(1, half):
            stores.append(hop(near, [(p, p - step) for p in (relay_row, relay_row - half)]))
            held_by = jnp.where(row % half == half - 1 - step, step, held_by)
        sends = pick(held_by, slot_block, stores)
        arrived = lax.all_to_all(sends, "dp", split_axis=0, concat_axis=0, tiled=True)
        here = [arrived] + [share(arrived, step) for step in range(1, half)]
        if crossing:
            leaving = pick(0, leaving_place, [arrived])
            landed = hop(leaving, [(p, (p + half) % pool_count) for p in range(pool_count)])
            here += [landed] + [share(landed, step) for step in range(1, half)]
        held.append(here)
    origin = jnp.where(my_cross, (my_carrier + half) % pool_count, my_carrier)
    which = (row - origin) % half + jnp.where(my_cross, half, 0)
    index = jnp.where(my_cross, my_number, place)
    held = [here[b] for b in range(len(held[0])) for here in held]

    own_row = jnp.minimum(row, relay_row - 1)
    hot = (my_owner * block_count + my_block)[:, None] == jnp.arange(
        columns * block_count, dtype=jnp.int32
    )[None, :]
    wanted_len = jnp.sum(jnp.where(hot, store_len.reshape(1, -1), 0), axis=1)
    own = lambda a: lax.dynamic_index_in_dim(
        a.reshape(relay_row, per_device), own_row, 0, keepdims=False
    )
    live = (row < relay_row).astype(jnp.int32) + row % 2 * 2
    meta = jnp.concatenate([live[None], own(wanted_len), own(which), own(index)]).astype(jnp.int32)

    attn_out, q_grad, cond_grad, keep, give = run_spans(
        meta,
        queries.reshape(token_count, head_cols),
        cotangent.reshape(token_count, head_cols),
        cond.reshape(span_count, width).astype(jnp.float32),
        held,
        bounds,
        gain,
        w_down,
        w_up,
        w_kv,
        w_kv_t,
        nbr_count,
        pool_count,
    )

    adapter_grad = scatter_sum(keep, give, axes)
    return (
        attn_out.reshape(1, 1, token_count, head_cols),
        q_grad.reshape(1, 1, token_count, head_cols),
        cond_grad.reshape(1, 1, span_count, width),
        adapter_grad,
    )


def solution(mesh):
    return jax.shard_map(
        body,
        mesh=mesh,
        in_specs=(
            P("pool", "dp", None, None),
            P("pool", "dp", None, None),
            P("pool", "dp", None, None),
            P("pool", "dp", None, None),
            P("pool", "dp", None, None),
            P("pool", "dp", None, None, None),
            P("pool", "dp", None),
            P(),
            P(),
            P(),
            P(),
        ),
        out_specs=(
            P("pool", "dp", None, None),
            P("pool", "dp", None, None),
            P("pool", "dp", None, None),
            P(("pool", "dp"), None),
        ),
        check_vma=False,
    )
```
